32 devices in a mesh: ta: 4 (over y, x), pa: 4 (over z), dev: 2 (over core).
Axes of the slice: x: 2, y: 2, z: 4, core: 2. Of those that a mesh axis runs over, the one named last changes fastest.
Arguments:
- latents: bfloat16 [4, 20, 1024, 384], P('dev', 'ta', 'pa'), may hold values from -6 to 6
- context: bfloat16 [4, 120, 384], P('dev'), may hold values from -6 to 6
- cotangent: bfloat16 [4, 20, 1024, 384], P('dev', 'ta', 'pa'), may hold values from -6 to 6
- timesteps: int32 [4], P('dev'), may hold values from 0 to 999
- frame_counts: int32 [4], P('dev'), may hold values from 6 to 20, as said below
- text_lengths: int32 [4], P('dev'), may hold values from 15 to 120, as said below
- step_proj: bfloat16 [256, 2304], replicated, may hold values from -0.1875 to 0.1875
- mod_table: bfloat16 [2, 6, 384], replicated, may hold values from -1.796875 to 1.796875
- patch_attn: bfloat16 [4, 384, 384], replicated
- cross_attn: bfloat16 [4, 384, 384], replicated
- patch_up: bfloat16 [384, 1536], replicated, may hold values from -0.3125 to 0.3125
- patch_down: bfloat16 [1536, 384], replicated, may hold values from -0.15625 to 0.15625
- frame_attn: bfloat16 [4, 384, 384], replicated
- frame_up: bfloat16 [384, 1536], replicated, may hold values from -0.3125 to 0.3125
- frame_down: bfloat16 [1536, 384], replicated, may hold values from -0.15625 to 0.15625
Outputs:
- output: bfloat16 [4, 20, 1024, 384], P('dev', 'ta', 'pa')
- latents_grad: float32 [4, 20, 1024, 384], P('dev', 'ta', 'pa')
- step_proj_grad: float32 [256, 2304], replicated
- mod_table_grad: float32 [2, 6, 384], replicated
- patch_attn_grad: float32 [4, 384, 384], replicated
- cross_attn_grad: float32 [4, 384, 384], replicated
- patch_up_grad: float32 [384, 1536], replicated
- patch_down_grad: float32 [1536, 384], replicated
- frame_attn_grad: float32 [4, 384, 384], replicated
- frame_up_grad: float32 [384, 1536], replicated
- frame_down_grad: float32 [1536, 384], replicated
The draws below stay inside these ranges and needn't reach their ends.
Inputs may be any that keep to these rules, and one draw needn't show every extreme that they name: `frame_counts`: in every aligned block of 2 clips one clip has all 20 frames valid. `text_lengths`: in every aligned block of 2 clips one clip has all 120 text tokens live.
All inputs are finite; a program needn't handle non-finite values.
Results may differ from the reference program's by a relative error of at most 0.02.
Values may be sent and summed in bfloat16 or wider, within the bound.
A program may use at most 320 MiB of HBM per device.

```python
import math
import jax
import jax.numpy as jnp
from jax import lax

D = 384
HEADS = 6
HDIM = 64
FF = 1536
TFREQ = 256
TXT = 120
FRAMES = 20
CLIP_DEV = 2
CLIPS = 4
FR_DEV = 5
NP = 1024


def attention_stack(key, factor):
    standard = jax.random.normal(key, (4, D, D), dtype=jnp.float32) * D ** (-0.5)
    booster = jnp.array([1.0, 1.0, 1.0, factor], dtype=jnp.float32)
    return (standard * booster[:, None, None]).astype(jnp.bfloat16)


def full_clip_counts(key, lowest, highest):
    first_key, second_key = jax.random.split(key)
    counts = jax.random.randint(first_key, (CLIPS,), lowest, highest + 1)
    chosen = jax.random.randint(second_key, (CLIPS // CLIP_DEV,), 0, CLIP_DEV)
    slot_ids = jnp.arange(CLIPS // CLIP_DEV, dtype=jnp.int32) * CLIP_DEV + chosen
    return counts.at[slot_ids].set(highest).astype(jnp.int32)


def draw_patch_attn(key, part):
    key = jax.random.fold_in(key, 11)
    return attention_stack(key, 2.0)


def draw_cross_attn(key, part):
    key = jax.random.fold_in(key, 12)
    return attention_stack(key, 1.5)


def draw_frame_attn(key, part):
    key = jax.random.fold_in(key, 13)
    return attention_stack(key, 1.5)


def draw_frame_counts(key, part):
    key = jax.random.fold_in(key, 14)
    return full_clip_counts(key, FR_DEV + 1, FRAMES)


def draw_text_lengths(key, part):
    key = jax.random.fold_in(key, 15)
    return full_clip_counts(key, TXT // 8, TXT)


def set_ends(drawn, stream_key, smallest, top_value):
    longest = drawn.shape.index(max(drawn.shape))
    spots = []
    for shift in (0, 1):
        where = [jax.random.randint(jax.random.fold_in(stream_key, axis), (), 0, length) for axis, length in enumerate(drawn.shape)]
        where[longest] = (where[longest] + shift) % drawn.shape[longest]
        spots.append(tuple(where))
    return drawn.at[spots[0]].set(smallest).at[spots[1]].set(top_value)


def shard_levels(stream_key, shape, cuts, low, top_value):
    gain, own = 1.0, jax.random.fold_in(stream_key, 6)
    for position, parts in cuts:
        steps = jnp.exp(jax.random.uniform(jax.random.fold_in(own, position), (parts,), jnp.float32, low / len(cuts), top_value / len(cuts)))
        gain = gain * jnp.repeat(steps, shape[position] // parts).reshape([-1 if axis == position else 1 for axis in range(len(shape))])
    return gain


def scatter_about(key, shape, width, reach, pieces=(), kind=jnp.bfloat16):
    drawn = width * jax.random.normal(key, shape, jnp.float32)
    if pieces:
        drawn = drawn * shard_levels(key, shape, pieces, -0.22, 0.18)
    return jnp.clip(drawn, -reach, reach).astype(kind)


def setup_inputs(seed: int = 0) -> dict:
    keys = jax.random.split(jax.random.key(seed), 16)
    latents = scatter_about(keys[0], (CLIPS, FRAMES, NP, D), 1.0, 6.0, ((0, 2), (1, 4), (2, 4)))
    context = scatter_about(keys[1], (CLIPS, TXT, D), 1.0, 6.0, ((0, 2),))
    cotangent = scatter_about(keys[2], (CLIPS, FRAMES, NP, D), 1.0, 6.0, ((0, 2), (1, 4), (2, 4)))
    timesteps = set_ends(jax.random.randint(keys[3], (CLIPS,), 0, 1000), jax.random.fold_in(keys[3], 1), 0, 999).astype(jnp.int32)
    frame_counts = draw_frame_counts(jax.random.fold_in(keys[15], 71), 0)
    text_lengths = draw_text_lengths(jax.random.fold_in(keys[15], 71), 0)
    step_proj = scatter_about(keys[6], (TFREQ, 6 * D), (4 * TFREQ) ** -0.5, 0.1875)
    mod_table = scatter_about(keys[7], (2, 6, D), 0.3, 1.796875)
    patch_attn = draw_patch_attn(jax.random.fold_in(keys[15], 71), 0)
    cross_attn = draw_cross_attn(jax.random.fold_in(keys[15], 71), 0)
    patch_up = scatter_about(keys[10], (D, FF), D ** -0.5, 0.3125)
    patch_down = scatter_about(keys[11], (FF, D), FF ** -0.5, 0.15625)
    frame_attn = draw_frame_attn(jax.random.fold_in(keys[15], 71), 0)
    frame_up = scatter_about(keys[13], (D, FF), D ** -0.5, 0.3125)
    frame_down = scatter_about(keys[14], (FF, D), FF ** -0.5, 0.15625)
    return dict(latents=latents, context=context, cotangent=cotangent, timesteps=timesteps, frame_counts=frame_counts, text_lengths=text_lengths, step_proj=step_proj, mod_table=mod_table, patch_attn=patch_attn, cross_attn=cross_attn, patch_up=patch_up, patch_down=patch_down, frame_attn=frame_attn, frame_up=frame_up, frame_down=frame_down)


EPSILON = 1e-06
MASKED_SCORE = -1e+30
HIGHEST = lax.Precision.HIGHEST

@jax.custom_vjp
def low(v):
    return lax.optimization_barrier(v.astype(jnp.bfloat16)).astype(jnp.float32)

@jax.custom_vjp
def low_back(v):
    return v

def low_keep(v):
    return (low(v), None)

def low_pass(kept, grad):
    return (grad,)

def back_keep(v):
    return (v, None)

def back_low(kept, grad):
    return (low(grad),)
low.defvjp(low_keep, low_pass)
low_back.defvjp(back_keep, back_low)

def layer_norm(values):
    centred = values - lax.optimization_barrier(jnp.mean(values, axis=-1, keepdims=True))
    return centred * lax.rsqrt(lax.optimization_barrier(jnp.mean(centred * centred, axis=-1, keepdims=True)) + EPSILON)

def modulate(values, shift_by, scale_by):
    return layer_norm(values) * (1.0 + scale_by) + shift_by

def sinusoid(step_ids):
    half_count = TFREQ // 2
    frequency = jnp.exp(-math.log(10000.0) * jnp.arange(half_count, dtype=jnp.float32) / half_count)
    angles = step_ids.astype(jnp.float32)[:, None] * frequency[None, :]
    return jnp.concatenate([jnp.cos(angles), jnp.sin(angles)], axis=1)

def project(values, matrix):
    return jnp.einsum('...d,de->...e', values, matrix, precision=HIGHEST)

def split_heads(values):
    return values.reshape(values.shape[:-1] + (HEADS, HDIM))

def attend(queries, key_rows, value_rows, live_mask):
    scores = jnp.einsum('qhe,khe->hqk', queries, key_rows, precision=HIGHEST) * HDIM ** (-0.5)
    scores = low_back(scores)
    scores = jnp.where(live_mask[None, None, :], scores, MASKED_SCORE)
    largest = lax.optimization_barrier(jnp.max(scores, axis=-1, keepdims=True))
    exponent = jnp.exp(scores - largest)
    normalized = low(exponent / lax.optimization_barrier(jnp.sum(exponent, axis=-1, keepdims=True)))
    return jnp.einsum('hqk,khe->qhe', normalized, value_rows, precision=HIGHEST)

def spatial_attend(queries, key_rows, value_rows):
    live_mask = jnp.ones((key_rows.shape[1],), dtype=bool)

    def one_frame(items):
        return attend(items[0], items[1], items[2], live_mask)
    return lax.map(jax.checkpoint(one_frame), (queries, key_rows, value_rows))

def temporal_attend(frame_live):

    def attend_frames(queries, key_rows, value_rows):

        def one_patch(query_seq, key_seq, value_seq):
            return attend(query_seq, key_seq, value_seq, frame_live)
        moved = jax.vmap(one_patch)(jnp.swapaxes(queries, 0, 1), jnp.swapaxes(key_rows, 0, 1), jnp.swapaxes(value_rows, 0, 1))
        return jnp.swapaxes(moved, 0, 1)
    return attend_frames

def self_branch(normed, stack, attend_all):
    queries = low_back(low(project(normed, stack[0])))
    key_rows = low_back(low(project(normed, stack[1])))
    value_rows = low_back(low(project(normed, stack[2])))
    attended = attend_all(split_heads(queries), split_heads(key_rows), split_heads(value_rows))
    attended = low_back(low(attended.reshape(normed.shape)))
    return low_back(project(attended, stack[3]))

def cross_branch(hidden, context, stack, text_live):
    queries = low_back(low(project(low(hidden), stack[0])))
    key_rows = low(project(context, stack[1]))
    value_rows = low(project(context, stack[2]))
    flat_queries = split_heads(queries).reshape((-1, HEADS, HDIM))
    attended = attend(flat_queries, split_heads(key_rows), split_heads(value_rows), text_live)
    attended = low_back(low(attended.reshape(hidden.shape)))
    return low_back(project(attended, stack[3]))

def mlp_branch(normed, up_weight, down_weight):
    lifted = low_back(project(normed, up_weight))
    activated = low(jax.nn.gelu(lifted, approximate=True))
    return low_back(project(activated, down_weight))

def clip_forward(hidden, context, embedding, frame_live, text_live, weights):
    step_proj, mod_table, patch_attn, cross_attn, patch_up, patch_down, frame_attn, frame_up, frame_down = weights
    timing = jnp.dot(embedding, step_proj, precision=HIGHEST).reshape(6, D)
    frame_keep = frame_live.astype(jnp.float32)[:, None, None]
    modulation = timing + mod_table[0]
    normed = low(modulate(hidden, modulation[0], modulation[1]))
    hidden = hidden + frame_keep * modulation[2] * self_branch(normed, patch_attn, spatial_attend)
    hidden = hidden + frame_keep * cross_branch(hidden, context, cross_attn, text_live)
    normed = low(modulate(hidden, modulation[3], modulation[4]))
    hidden = hidden + frame_keep * modulation[5] * mlp_branch(normed, patch_up, patch_down)
    modulation = timing + mod_table[1]
    normed = low(modulate(hidden, modulation[0], modulation[1]))
    hidden = hidden + frame_keep * modulation[2] * self_branch(normed, frame_attn, temporal_attend(frame_live))
    normed = low(modulate(hidden, modulation[3], modulation[4]))
    hidden = hidden + frame_keep * modulation[5] * mlp_branch(normed, frame_up, frame_down)
    return hidden

def reference(latents, context, cotangent, timesteps, frame_counts, text_lengths, step_proj, mod_table, patch_attn, cross_attn, patch_up, patch_down, frame_attn, frame_up, frame_down):
    weights = tuple((weight.astype(jnp.float32) for weight in (step_proj, mod_table, patch_attn, cross_attn, patch_up, patch_down, frame_attn, frame_up, frame_down)))
    embeddings = sinusoid(timesteps)

    def one_clip(totals, items):
        clip_tokens, clip_context, clip_cotangent, embedding, frame_count, text_count = items
        frame_live = jnp.arange(FRAMES, dtype=jnp.int32) < frame_count
        text_live = jnp.arange(TXT, dtype=jnp.int32) < text_count
        context_values = clip_context.astype(jnp.float32)

        def run(hidden, params):
            return clip_forward(hidden, context_values, embedding, frame_live, text_live, params)
        result, pullback = jax.vjp(run, clip_tokens.astype(jnp.float32), weights)
        input_grad, weight_grads = pullback(clip_cotangent.astype(jnp.float32))
        totals = jax.tree.map(jnp.add, totals, weight_grads)
        return (totals, (result.astype(jnp.bfloat16), input_grad))
    zeros = jax.tree.map(jnp.zeros_like, weights)
    totals, (outputs, input_grads) = lax.scan(one_clip, zeros, (latents, context, cotangent, embeddings, frame_counts, text_lengths))
    return (outputs, input_grads, totals[0], totals[1], totals[2], totals[3], totals[4], totals[5], totals[6], totals[7], totals[8])
```

```python
import math

import jax
import jax.numpy as jnp
from jax import lax
from jax.experimental import pallas as pl
from jax.experimental.pallas import tpu as pltpu
from jax.sharding import PartitionSpec as P

HEADS = 6
HDIM = 64
PAIRS = HEADS // 2
LANES = 2 * HDIM
EPSILON = 1e-06
MASKED_SCORE = -1e30
HIGHEST = lax.Precision.HIGHEST
F32 = jnp.float32
BF = jnp.bfloat16
VMEM_BYTES = 60 * 2**20
SUM_ROWS = 16
FRAME_GROUPS = ((0, 1, 2, 3, 4),)
BLOCK = 16


def dot(a, b):
    return jnp.dot(a, b, preferred_element_type=F32)


def dot_nt(a, b):
    return lax.dot_general(a, b, (((1,), (1,)), ((), ())), preferred_element_type=F32)


def norm_parts(values):
    centred = values - jnp.mean(values, axis=-1, keepdims=True)
    inverse = lax.rsqrt(jnp.mean(centred * centred, axis=-1, keepdims=True) + EPSILON)
    return centred * inverse, inverse


def norm_back(d_normed, hat, inverse, scale_by):
    d_hat = d_normed * (1.0 + scale_by)
    mean_d = jnp.mean(d_hat, axis=-1, keepdims=True)
    mean_dh = jnp.mean(d_hat * hat, axis=-1, keepdims=True)
    return inverse * (d_hat - mean_d - hat * mean_dh)


GELU_A = math.sqrt(2.0 / math.pi)
GELU_B = 0.044715


def gelu_parts(values):
    square = values * values
    bent = jnp.tanh(GELU_A * values * (1.0 + GELU_B * square))
    half = 0.5 * (1.0 + bent)
    slope = half + (0.5 * GELU_A) * values * (1.0 - bent * bent) * (1.0 + 3.0 * GELU_B * square)
    return values * half, slope


def row_sums(values):
    return jnp.sum(values, axis=0, keepdims=True)


def head_lanes(values, head):
    lane = lax.broadcasted_iota(jnp.int32, values.shape, 1)
    return jnp.where((lane >= HDIM) == (head % 2 == 1), values, jnp.zeros_like(values))


def pair_of(values, pair):
    return values[:, pair * LANES : (pair + 1) * LANES]


def head_rows(values, head):
    return values[head * HDIM : (head + 1) * HDIM, :]


def lone_rows(values, head):
    rows = head_rows(values, head)
    blank = jnp.zeros_like(rows)
    return jnp.concatenate([rows, blank] if head % 2 == 0 else [blank, rows], axis=0)


def attend(queries, keys, values_t, bias, keep_exponent):
    ones = jnp.ones((SUM_ROWS, values_t.shape[1]), BF)
    parts, inverses = [], []
    for head in range(HEADS):
        pair = head // 2
        scores = dot_nt(pair_of(keys, pair), head_lanes(pair_of(queries, pair), head))
        if bias is not None:
            scores = scores + bias
        largest = jnp.max(scores, axis=0, keepdims=True)
        exponent = jnp.exp(scores - largest).astype(BF)
        keep_exponent(head, exponent)
        lifted = jnp.concatenate([head_rows(values_t, head), ones], axis=0)
        summed = dot(lifted, exponent)
        inverse = 1.0 / summed[HDIM : HDIM + 1, :]
        parts.append(summed[:HDIM, :] * inverse)
        inverses.append(inverse)
    return jnp.concatenate(parts, axis=0), inverses


def attend_back(exponent_of, queries_of, keys_t_of, values_of, d_att_t, att_t, inverse_of, keys_chunk):
    n_keys, chunk = keys_chunk
    d_query_parts, d_key_pairs, d_value_pairs = [], [], []
    for pair in range(PAIRS):
        d_keys = [None] * (n_keys // chunk)
        d_values = [None] * (n_keys // chunk)
        for head in (2 * pair, 2 * pair + 1):
            inverse = inverse_of(head)
            d_att_head = head_rows(d_att_t, head)
            centre = row_sums(d_att_head * head_rows(att_t, head)) * inverse
            scaled = (d_att_head * inverse).astype(BF)
            blank = jnp.zeros_like(scaled)
            scaled_pair = jnp.concatenate([scaled, blank] if head % 2 == 0 else [blank, scaled], axis=0)
            query_pair = head_lanes(queries_of(pair), head)
            d_query = None
            for at in range(n_keys // chunk):
                rows = slice(at * chunk, (at + 1) * chunk)
                exponent = exponent_of(head, rows)
                d_chance = dot(values_of(pair, rows), scaled_pair)
                d_score = (exponent.astype(F32) * (d_chance - centre)).astype(BF)
                d_value = dot_nt(exponent, scaled_pair)
                d_key = dot(d_score, query_pair)
                part = dot(keys_t_of(head, rows), d_score)
                d_query = part if d_query is None else d_query + part
                d_keys[at] = d_key if d_keys[at] is None else d_keys[at] + d_key
                d_values[at] = d_value if d_values[at] is None else d_values[at] + d_value
            d_query_parts.append(d_query)
        d_key_pairs.append(jnp.concatenate(d_keys, axis=0))
        d_value_pairs.append(jnp.concatenate(d_values, axis=0))
    return (
        jnp.concatenate(d_query_parts, axis=0),
        jnp.concatenate(d_key_pairs, axis=1),
        jnp.concatenate(d_value_pairs, axis=1),
    )


def fold(ref):
    value = ref[...]
    return value.reshape(-1, value.shape[-1])


def space_forward_kernel(
    first_frame,
    counts_ref,
    own_ref,
    other_ref,
    mod_ref,
    attn_ref,
    turned_ref,
    cross_ref,
    text_keys_ref,
    text_values_t_ref,
    up_ref,
    down_ref,
    state_ref,
    normed_ref,
    query_ref,
    keys_t_ref,
    value_ref,
    exponent_ref,
    att_t_ref,
    att_ref,
    inverse_ref,
    cross_in_ref,
    cross_query_ref,
    cross_exponent_ref,
    cross_att_t_ref,
    cross_att_ref,
    cross_inverse_ref,
    middle_ref,
    normed2_ref,
    act_ref,
    slope_ref,
):
    scale_by = HDIM ** (-0.5)
    frame = counts_ref[2] + first_frame + pl.program_id(0)
    keep = (frame < counts_ref[0]).astype(F32)
    mod = mod_ref[...]
    own = fold(own_ref).astype(F32)
    rows = own.shape[0]
    normed_own = (norm_parts(own)[0] * (1.0 + mod[1:2]) + mod[0:1]).astype(BF)
    normed_other = (norm_parts(fold(other_ref).astype(F32))[0] * (1.0 + mod[1:2]) + mod[0:1]).astype(BF)
    normed = jnp.concatenate([normed_own, normed_other], axis=0)
    normed_ref[0] = normed
    queries = (dot(normed_own, attn_ref[0]).astype(BF) * scale_by).astype(BF)
    keys = dot(normed, attn_ref[1]).astype(BF)
    values = dot(normed, attn_ref[2]).astype(BF)
    query_ref[0] = queries
    value_ref[0] = values
    keys_t_ref[0] = dot_nt(turned_ref[0], normed).astype(BF)
    values_t = dot_nt(turned_ref[1], normed).astype(BF)

    def keep_exponent(head, exponent):
        exponent_ref[0, head] = exponent

    att_t, inverses = attend(queries, keys, values_t, None, keep_exponent)
    for head in range(HEADS):
        inverse_ref[0, head : head + 1, :] = inverses[head]
    att_t_ref[0] = att_t.astype(BF)
    att = att_t.T.astype(BF)
    att_ref[0] = att
    state = own + (keep * mod[2:3]) * dot(att, attn_ref[3])
    cross_in = state.astype(BF)
    cross_in_ref[0] = cross_in
    cross_queries = (dot(cross_in, cross_ref[0]).astype(BF) * scale_by).astype(BF)
    cross_query_ref[0] = cross_queries
    text_id = lax.broadcasted_iota(jnp.int32, (text_keys_ref.shape[0], rows), 0)
    bias = jnp.where(text_id < counts_ref[1], 0.0, MASKED_SCORE)

    def keep_cross(head, exponent):
        cross_exponent_ref[0, head] = exponent

    cross_t, inverses = attend(cross_queries, text_keys_ref[...], text_values_t_ref[...], bias, keep_cross)
    for head in range(HEADS):
        cross_inverse_ref[0, head : head + 1, :] = inverses[head]
    cross_att_t_ref[0] = cross_t.astype(BF)
    cross_att = cross_t.T.astype(BF)
    cross_att_ref[0] = cross_att
    state = state + keep * dot(cross_att, cross_ref[1])
    middle_ref[0] = state
    normed2 = (norm_parts(state)[0] * (1.0 + mod[4:5]) + mod[3:4]).astype(BF)
    normed2_ref[0] = normed2
    act, slope = gelu_parts(dot(normed2, up_ref[...]))
    act = act.astype(BF)
    act_ref[0] = act
    slope_ref[0] = slope.astype(BF)
    state = state + (keep * mod[5:6]) * dot(act, down_ref[...])
    state_ref[0] = state.astype(BF)


def space_backward_kernel(
    first_frame,
    counts_ref,
    grad_ref,
    mod_ref,
    attn_ref,
    cross_ref,
    text_keys_t_ref,
    text_values_ref,
    up_ref,
    down_ref,
    query_ref,
    keys_t_ref,
    value_ref,
    exponent_ref,
    att_t_ref,
    inverse_ref,
    cross_query_ref,
    cross_exponent_ref,
    cross_att_t_ref,
    cross_inverse_ref,
    middle_ref,
    slope_ref,
    state_grad_ref,
    own_grad_ref,
    other_grad_ref,
    kept3_ref,
    d_lifted_ref,
    kept2_ref,
    d_cross_query_ref,
    kept1_ref,
    d_query_ref,
    d_key_ref,
    d_value_ref,
    d_text_keys_ref,
    d_text_values_ref,
    mods_ref,
):
    scale_by = HDIM ** (-0.5)
    frame = counts_ref[2] + first_frame + pl.program_id(0)
    keep = (frame < counts_ref[0]).astype(F32)
    mod = mod_ref[...]
    grad = fold(grad_ref).astype(F32)
    rows = grad.shape[0]
    kept = keep * grad
    kept3_ref[0] = kept.astype(BF)
    d_act = dot_nt((kept * mod[5:6]).astype(BF), down_ref[...])
    d_lifted = (d_act * slope_ref[0].astype(F32)).astype(BF)
    d_lifted_ref[0] = d_lifted
    d_normed = dot_nt(d_lifted, up_ref[...])
    hat, inverse = norm_parts(middle_ref[0])
    grad = grad + norm_back(d_normed, hat, inverse, mod[4:5])
    mods_ref[0] = jnp.concatenate(
        [row_sums(d_normed), row_sums(d_normed * hat), jnp.zeros((6, hat.shape[1]), F32)], axis=0
    )
    kept = (keep * grad).astype(BF)
    kept2_ref[0] = kept
    d_att_t = dot_nt(cross_ref[1], kept)
    d_query_t, d_keys, d_values = attend_back(
        lambda head, at: cross_exponent_ref[0, head, at, :],
        lambda pair: cross_query_ref[0, :, pair * LANES : (pair + 1) * LANES],
        lambda head, at: text_keys_t_ref[head * HDIM : (head + 1) * HDIM, at],
        lambda pair, at: text_values_ref[at, pair * LANES : (pair + 1) * LANES],
        d_att_t,
        cross_att_t_ref[0].astype(F32),
        lambda head: cross_inverse_ref[0, head : head + 1, :],
        (text_values_ref.shape[0], text_values_ref.shape[0]),
    )
    d_text_keys_ref[0] = d_keys
    d_text_values_ref[0] = d_values
    d_query = (d_query_t.T * scale_by).astype(BF)
    d_cross_query_ref[0] = d_query
    grad = grad + dot_nt(d_query, cross_ref[0])
    state_grad_ref[0] = grad
    kept = keep * grad
    kept1_ref[0] = kept.astype(BF)
    d_att_t = dot_nt(attn_ref[3], (kept * mod[2:3]).astype(BF))
    n_keys = value_ref.shape[1]
    d_query_t, d_keys, d_values = attend_back(
        lambda head, at: exponent_ref[0, head, at, :],
        lambda pair: query_ref[0, :, pair * LANES : (pair + 1) * LANES],
        lambda head, at: keys_t_ref[0, head * HDIM : (head + 1) * HDIM, at],
        lambda pair, at: value_ref[0, at, pair * LANES : (pair + 1) * LANES],
        d_att_t,
        att_t_ref[0].astype(F32),
        lambda head: inverse_ref[0, head : head + 1, :],
        (n_keys, min(n_keys, 256)),
    )
    d_query = (d_query_t.T * scale_by).astype(BF)
    d_keys, d_values = d_keys.astype(BF), d_values.astype(BF)
    d_query_ref[0] = d_query
    d_key_ref[0] = d_keys
    d_value_ref[0] = d_values
    d_normed = dot_nt(d_keys, attn_ref[1]) + dot_nt(d_values, attn_ref[2])
    own_grad_ref[0] = d_normed[:rows] + dot_nt(d_query, attn_ref[0])
    other_grad_ref[0] = d_normed[rows:].astype(BF)


def space_finish_kernel(n_parts, own_ref, state_grad_ref, own_grad_ref, *rest):
    parts, (mod_ref, out_ref, mods_ref) = rest[:n_parts], rest[n_parts:]
    d_normed = own_grad_ref[0]
    for part in parts:
        d_normed = d_normed + part[0].astype(F32)
    hat, inverse = norm_parts(fold(own_ref).astype(F32))
    grad = state_grad_ref[0] + norm_back(d_normed, hat, inverse, mod_ref[1:2, :])
    out_ref[...] = grad.astype(BF).reshape(out_ref.shape)
    mods_ref[0] = jnp.concatenate(
        [row_sums(d_normed), row_sums(d_normed * hat), jnp.zeros((6, hat.shape[1]), F32)], axis=0
    )


def time_kernel(
    counts_ref,
    state_ref,
    cot_ref,
    mod_ref,
    bias_ref,
    attn_ref,
    turned_ref,
    up_ref,
    down_ref,
    out_ref,
    grad_ref,
    normed_ref,
    d_qkv_ref,
    att_ref,
    kept4_ref,
    normed2_ref,
    act_ref,
    d_lifted_ref,
    kept5_ref,
    mods_ref,
    exponent_ref,
):
    scale_by = HDIM ** (-0.5)
    block = state_ref.shape
    mod = mod_ref[...]

    def put(ref, value):
        ref[...] = value.reshape(ref.shape)

    state = fold(state_ref).astype(F32)
    rows = state.shape[0]
    frame = lax.broadcasted_iota(jnp.int32, (rows, 1), 0) // block[1]
    keep = (frame < counts_ref[0]).astype(F32)
    hat1, inverse1 = norm_parts(state)
    normed = (hat1 * (1.0 + mod[1:2]) + mod[0:1]).astype(BF)
    put(normed_ref, normed)
    queries = (dot(normed, attn_ref[0]).astype(BF) * scale_by).astype(BF)
    keys = dot(normed, attn_ref[1]).astype(BF)
    values = dot(normed, attn_ref[2]).astype(BF)
    keys_t = dot_nt(turned_ref[0], normed).astype(BF)
    values_t = dot_nt(turned_ref[1], normed).astype(BF)

    def keep_exponent(head, exponent):
        exponent_ref[head] = exponent

    att_t, inverses = attend(queries, keys, values_t, bias_ref[...], keep_exponent)
    att = att_t.T.astype(BF)
    put(att_ref, att)
    state = state + (keep * mod[2:3]) * dot(att, attn_ref[3])
    hat2, inverse2 = norm_parts(state)
    normed2 = (hat2 * (1.0 + mod[4:5]) + mod[3:4]).astype(BF)
    put(normed2_ref, normed2)
    act, slope = gelu_parts(dot(normed2, up_ref[...]))
    act = act.astype(BF)
    put(act_ref, act)
    put(out_ref, (state + (keep * mod[5:6]) * dot(act, down_ref[...])).astype(BF))
    grad = fold(cot_ref).astype(F32)
    kept = keep * grad
    put(kept5_ref, kept.astype(BF))
    d_act = dot_nt((kept * mod[5:6]).astype(BF), down_ref[...])
    d_lifted = (d_act * slope).astype(BF)
    put(d_lifted_ref, d_lifted)
    d_normed2 = dot_nt(d_lifted, up_ref[...])
    grad = grad + norm_back(d_normed2, hat2, inverse2, mod[4:5])
    kept = keep * grad
    put(kept4_ref, kept.astype(BF))
    d_att_t = dot_nt(attn_ref[3], (kept * mod[2:3]).astype(BF))
    d_query_t, d_keys, d_values = attend_back(
        lambda head, at: exponent_ref[head, at, :],
        lambda pair: pair_of(queries, pair),
        lambda head, at: head_rows(keys_t, head)[:, at],
        lambda pair, at: pair_of(values, pair)[at],
        d_att_t,
        att_t,
        lambda head: inverses[head],
        (rows, rows),
    )
    d_qkv = jnp.concatenate(
        [(d_query_t.T * scale_by).astype(BF), d_keys.astype(BF), d_values.astype(BF)], axis=1
    )
    put(d_qkv_ref, d_qkv)
    width = hat1.shape[1]
    d_normed1 = (
        dot_nt(d_qkv[:, :width], attn_ref[0])
        + dot_nt(d_qkv[:, width : 2 * width], attn_ref[1])
        + dot_nt(d_qkv[:, 2 * width :], attn_ref[2])
    )
    grad = grad + norm_back(d_normed1, hat1, inverse1, mod[1:2])
    put(grad_ref, grad.astype(BF))
    mods_ref[0] = jnp.concatenate(
        [
            row_sums(d_normed1),
            row_sums(d_normed1 * hat1),
            row_sums(d_normed2),
            row_sums(d_normed2 * hat2),
            jnp.zeros((4, width), F32),
        ],
        axis=0,
    )


def whole(array):
    zeros = (0,) * array.ndim
    return pl.BlockSpec(array.shape, lambda *grid: zeros)


def framed(array):
    tail = (0,) * (array.ndim - 1)
    return pl.BlockSpec((1,) + tuple(array.shape[1:]), lambda frame: (frame,) + tail)


SCALARS = pl.BlockSpec(memory_space=pltpu.SMEM)


def shape_of(shape, dtype):
    return jax.ShapeDtypeStruct(shape, dtype)


def call(kernel, grid, inputs, in_specs, outputs, out_specs, flops, scratch=()):
    moved = sum(math.prod(a.shape) * a.dtype.itemsize for a in (*inputs, *outputs))
    return pl.pallas_call(
        kernel,
        grid=grid,
        in_specs=in_specs,
        out_specs=out_specs,
        out_shape=outputs,
        scratch_shapes=list(scratch),
        compiler_params=pltpu.CompilerParams(vmem_limit_bytes=VMEM_BYTES),
        cost_estimate=pl.CostEstimate(flops=int(flops), bytes_accessed=int(moved), transcendentals=0),
    )(*inputs)


def make_per_device(n_ta, n_pa, n_dev):
    def per_device(
        latents,
        context,
        cotangent,
        timesteps,
        frame_counts,
        text_lengths,
        step_proj,
        mod_table,
        patch_attn,
        cross_attn,
        patch_up,
        patch_down,
        frame_attn,
        frame_up,
        frame_down,
    ):
        clips_dev, frames, patches, width = latents.shape
        clips = clips_dev * n_dev
        run = n_pa // clips
        group = run * n_dev
        near = n_pa // group
        space_rows = near * patches
        time_patches = space_rows // n_ta
        other_rows = (group - 1) * space_rows
        key_rows = group * space_rows
        all_frames = n_ta * frames
        ta, pa, dev = (lax.axis_index(name) for name in ("ta", "pa", "dev"))
        clip = pa // run
        member = dev * run + pa % run

        def place(clip_id, member_id):
            return (clip_id * run + member_id % run) * n_dev + member_id // run

        def space_pairs(step):
            pairs = []
            for p in range(n_pa):
                for d in range(n_dev):
                    k = d * clips_dev + (p + step) % clips_dev
                    pairs.append((p * n_dev + d, place(k, p // near)))
            return pairs

        halves = n_ta // near

        def time_pairs(step):
            u, w = step % halves, step // halves
            pairs = []
            for t in range(n_ta):
                for p in range(n_pa):
                    for d in range(n_dev):
                        s = (t % halves + u) % halves
                        j = (t // halves + w) % clips_dev
                        k = d * clips_dev + j
                        pairs.append(
                            (
                                (t * n_pa + p) * n_dev + d,
                                ((p % near) * halves + s) * n_pa * n_dev + place(k, p // near),
                            )
                        )
            return pairs

        def back(pairs):
            return [(b, a) for a, b in pairs]

        def group_pairs(step):
            return [
                (place(k, g), place(k, (g + step) % group)) for k in range(clips) for g in range(group)
            ]

        def ta_pairs(step):
            return [(t, t ^ step) for t in range(n_ta)]

        whole_axes = ("ta", "pa", "dev")
        pair_axes = ("pa", "dev")

        def of_clip(local):
            both = lax.all_gather(local, "dev", axis=0, tiled=True)
            return lax.dynamic_index_in_dim(both, clip, 0, keepdims=False)

        def sinusoid(steps):
            half = step_proj.shape[0] // 2
            frequency = jnp.exp(-math.log(10000.0) * jnp.arange(half, dtype=F32) / half)
            angles = steps.astype(F32)[:, None] * frequency[None, :]
            return jnp.concatenate([jnp.cos(angles), jnp.sin(angles)], axis=1)

        numbers = lax.all_gather(jnp.stack([timesteps, frame_counts, text_lengths], axis=1), "dev", axis=0, tiled=True)
        own_numbers = lax.dynamic_index_in_dim(numbers, clip, 0, keepdims=False)
        embeddings = sinusoid(numbers[:, 0])
        embedding = lax.dynamic_index_in_dim(embeddings, clip, 0, keepdims=True)
        timing = jnp.dot(embedding, step_proj.astype(F32), precision=HIGHEST).reshape(6, width)
        table = mod_table.astype(F32)
        pad = jnp.zeros((2, width), F32)
        space_mod = jnp.concatenate([timing + table[0], pad])
        frame_mod = jnp.concatenate([timing + table[1], pad])
        counts = jnp.stack([own_numbers[1], own_numbers[2], ta * frames, 0]).astype(jnp.int32)
        text = of_clip(context)
        text_count = text.shape[0]
        text_rows = -(-text_count // LANES) * LANES
        text_wide = jnp.pad(text, ((0, text_rows - text_count), (0, 0)))
        text_keys = dot(text_wide, cross_attn[1]).astype(BF)
        text_values = dot(text_wide, cross_attn[2]).astype(BF)
        cross_ends = jnp.stack([cross_attn[0], cross_attn[3]])
        patch_turned = jnp.swapaxes(patch_attn[1:3], 1, 2)
        frame_turned = jnp.swapaxes(frame_attn[1:3], 1, 2)

        def to_space(frame_ids):
            picked = latents[:, frame_ids[0] : frame_ids[-1] + 1]
            parts = []
            for step in range(clips_dev):
                sent = lax.dynamic_index_in_dim(picked, (pa + step) % clips_dev, 0, keepdims=False)
                parts.append(lax.ppermute(sent, pair_axes, space_pairs(step)))
            stacked = jnp.stack(parts)
            slots = [
                lax.dynamic_index_in_dim(stacked, (clip - b) % clips_dev, 0, keepdims=False) for b in range(near)
            ]
            own = jnp.concatenate(slots, axis=1)
            others = [lax.ppermute(own, pair_axes, group_pairs(step)) for step in range(1, group)]
            return own, jnp.concatenate(others, axis=1)

        def space_forward(frame_ids, own, other):
            count = len(frame_ids)

            def out(*shape, dtype=BF):
                return shape_of((count,) + shape, dtype)

            inputs = (
                counts, own, other, space_mod, patch_attn, patch_turned, cross_ends, text_keys, text_values.T,
                patch_up, patch_down,
            )
            hidden = patch_up.shape[1]
            outputs = (
                out(space_rows, width),
                out(key_rows, width),
                out(space_rows, width),
                out(width, key_rows),
                out(key_rows, width),
                out(HEADS, key_rows, space_rows),
                out(width, space_rows),
                out(space_rows, width),
                out(8, space_rows, dtype=F32),
                out(space_rows, width),
                out(space_rows, width),
                out(HEADS, text_rows, space_rows),
                out(width, space_rows),
                out(space_rows, width),
                out(8, space_rows, dtype=F32),
                out(space_rows, width, dtype=F32),
                out(space_rows, width),
                out(space_rows, hidden),
                out(space_rows, hidden),
            )
            dense = 2 * count * space_rows * width * (6 * width + 2 * hidden) + 8 * count * key_rows * width * width
            return call(
                lambda *refs: space_forward_kernel(frame_ids[0], *refs),
                (count,),
                inputs,
                [SCALARS, framed(own), framed(other)] + [whole(a) for a in inputs[3:]],
                outputs,
                [framed(a) for a in outputs],
                dense + 16 * count * space_rows * key_rows * width,
            )

        def space_backward(frame_ids, grad, saved):
            count = len(frame_ids)

            def out(*shape, dtype=BF):
                return shape_of((count,) + shape, dtype)

            (_, _, query, keys_t, value, exponent, att_t, _, inverse, _, cross_query, cross_exponent, cross_att_t, _,
             cross_inverse, middle, _, _, slope) = saved
            inputs = (
                counts, grad, space_mod, patch_attn, cross_ends, text_keys.T, text_values, patch_up, patch_down,
                query, keys_t, value, exponent, att_t, inverse, cross_query, cross_exponent, cross_att_t,
                cross_inverse, middle, slope,
            )
            hidden = patch_up.shape[1]
            outputs = (
                out(space_rows, width, dtype=F32),
                out(space_rows, width, dtype=F32),
                out(other_rows, width),
                out(space_rows, width),
                out(space_rows, hidden),
                out(space_rows, width),
                out(space_rows, width),
                out(space_rows, width),
                out(space_rows, width),
                out(key_rows, width),
                out(key_rows, width),
                out(text_rows, width, dtype=F32),
                out(text_rows, width, dtype=F32),
                out(8, width, dtype=F32),
            )
            grad_spec = pl.BlockSpec((n_ta, 1, time_patches, width), lambda frame: (0, frame, 0, 0))
            dense = 2 * count * space_rows * width * (6 * width + 2 * hidden) + 8 * count * key_rows * width * width
            return call(
                lambda *refs: space_backward_kernel(frame_ids[0], *refs),
                (count,),
                inputs,
                [SCALARS, grad_spec] + [whole(a) for a in inputs[2:9]] + [framed(a) for a in inputs[9:]],
                outputs,
                [framed(a) for a in outputs],
                dense + 32 * count * space_rows * key_rows * width,
            )

        def space_finish(own, state_grad, own_grad, parts):
            count = own.shape[0]
            inputs = (own, state_grad, own_grad, *parts, space_mod)
            outputs = (
                shape_of((count, near, patches, width), BF),
                shape_of((count, 8, width), F32),
            )
            return call(
                lambda *refs: space_finish_kernel(len(parts), *refs),
                (count,),
                inputs,
                [framed(a) for a in inputs[:-1]] + [whole(space_mod)],
                outputs,
                [framed(a) for a in outputs],
                count * space_rows * width * 30,
            )

        owns, saves, states = [], [], []
        for frame_ids in FRAME_GROUPS:
            own, other = to_space(frame_ids)
            saved = space_forward(frame_ids, own, other)
            owns.append(own)
            saves.append(saved)
            states.append(saved[0])

        n_steps = halves * clips_dev
        cot_parts = []
        for step in range(n_steps):
            u, w = step % halves, step // halves
            s = (ta % halves + u) % halves
            j = (ta // halves + w) % clips_dev
            sent = lax.dynamic_slice(
                cotangent, (j, 0, s * time_patches, 0), (1, frames, time_patches, width)
            )[0]
            cot_parts.append(lax.ppermute(sent, whole_axes, time_pairs(step)))
        cot_stack = jnp.stack(cot_parts)
        slot = ta % halves

        def step_from(source):
            u = (slot - source % halves) % halves
            w = (clip % clips_dev - source // halves) % clips_dev
            return w * halves + u

        cot = jnp.concatenate(
            [lax.dynamic_index_in_dim(cot_stack, step_from(t), 0, keepdims=False) for t in range(n_ta)]
        )

        def exchange(pieces):
            got = [lax.dynamic_index_in_dim(pieces, ta, 0, keepdims=False)]
            for step in range(1, n_ta):
                sent = lax.dynamic_index_in_dim(pieces, ta ^ step, 0, keepdims=False)
                got.append(lax.ppermute(sent, "ta", ta_pairs(step)))
            stacked = jnp.stack(got)
            return jnp.stack(
                [lax.dynamic_index_in_dim(stacked, ta ^ t, 0, keepdims=False) for t in range(n_ta)]
            )

        state_groups = []
        for state in states:
            pieces = state.reshape(state.shape[0], n_ta, time_patches, width).swapaxes(0, 1)
            state_groups.append(exchange(pieces))
        state = jnp.concatenate(state_groups, axis=1).reshape(all_frames, time_patches, width)

        block_rows = all_frames * BLOCK
        ids = jnp.arange(block_rows, dtype=jnp.int32)
        same = (ids[:, None] % BLOCK == ids[None, :] % BLOCK) & (ids[:, None] // BLOCK < counts[0])
        bias = jnp.where(same, 0.0, MASKED_SCORE).astype(F32)
        hidden = frame_up.shape[1]
        n_blocks = time_patches // BLOCK

        def tokens(features):
            return shape_of((all_frames, time_patches, features), BF)

        time_inputs = (counts, state, cot, frame_mod, bias, frame_attn, frame_turned, frame_up, frame_down)
        time_outputs = (
            tokens(width),
            tokens(width),
            tokens(width),
            tokens(3 * width),
            tokens(width),
            tokens(width),
            tokens(width),
            tokens(hidden),
            tokens(hidden),
            tokens(width),
            shape_of((n_blocks, 8, width), F32),
        )

        def blocked(array):
            return pl.BlockSpec((all_frames, BLOCK, array.shape[2]), lambda at: (0, at, 0))

        (out_t, grad_t, normed_t, d_qkv_t, att_tt, kept4, normed4, act4, d_lifted4, kept5, frame_mods) = call(
            time_kernel,
            (n_blocks,),
            time_inputs,
            [SCALARS, blocked(state), blocked(cot)] + [whole(a) for a in time_inputs[3:]],
            time_outputs,
            [blocked(a) for a in time_outputs[:-1]] + [framed(time_outputs[-1])],
            all_frames * time_patches * width * (24 * width + 12 * hidden),
            [pltpu.VMEM((HEADS, block_rows, block_rows), BF)],
        )

        out_pieces = out_t.reshape(n_ta, frames, time_patches, width)
        out_parts = []
        for step in range(n_steps):
            u, w = step % halves, step // halves
            source = (slot - u) % halves + halves * ((clip % clips_dev - w) % clips_dev)
            sent = lax.dynamic_index_in_dim(out_pieces, source, 0, keepdims=False)
            out_parts.append(lax.ppermute(sent, whole_axes, back(time_pairs(step))))
        out_stack = jnp.stack(out_parts)
        rows = []
        for j in range(clips_dev):
            runs = []
            for s in range(halves):
                step = ((j - ta // halves) % clips_dev) * halves + (s - ta % halves) % halves
                runs.append(lax.dynamic_index_in_dim(out_stack, step, 0, keepdims=False))
            rows.append(jnp.concatenate(runs, axis=1))
        output = jnp.stack(rows)

        grad_s = exchange(grad_t.reshape(n_ta, frames, time_patches, width))

        def weight_grad(left, right):
            n = left.ndim - 1
            axes = tuple(range(n))
            return lax.dot_general(left, right, ((axes, axes), ((), ())), preferred_element_type=F32)

        def gated(product, gate, weight):
            return product * gate, jnp.sum(weight.astype(F32) * product, axis=0)

        d_frame_qkv = weight_grad(normed_t, d_qkv_t).reshape(width, 3, width).swapaxes(0, 1)
        d_frame_proj, d_gate2_t = gated(weight_grad(att_tt, kept4), frame_mod[2], frame_attn[3])
        d_frame_up = weight_grad(normed4, d_lifted4)
        d_frame_down, d_gate5_t = gated(weight_grad(act4, kept5), frame_mod[5], frame_down)
        frame_mods = jnp.sum(frame_mods, axis=0)

        def summed(arrays):
            flat = jnp.concatenate([a.reshape(-1).astype(BF) for a in arrays])
            total = lax.psum(flat, whole_axes).astype(F32)
            results, at = [], 0
            for a in arrays:
                results.append(total[at : at + a.size].reshape(a.shape))
                at += a.size
            return results

        d_frame_attn = jnp.concatenate([d_frame_qkv, d_frame_proj[None]])
        d_frame_attn, d_frame_up, d_frame_down = summed([d_frame_attn, d_frame_up, d_frame_down])

        pieces = []
        finished, first_mods, backs = [], [], []
        for frame_ids, own, saved in zip(FRAME_GROUPS, owns, saves):
            grad = grad_s[:, frame_ids[0] : frame_ids[-1] + 1]
            backed = space_backward(frame_ids, grad, saved)
            backs.append(backed)
            other_grad = backed[2]
            parts = []
            for step in range(1, group):
                sent = other_grad[:, (step - 1) * space_rows : step * space_rows]
                parts.append(lax.ppermute(sent, pair_axes, back(group_pairs(step))))
            done, mods = space_finish(own, backed[0], backed[1], parts)
            finished.append(done)
            first_mods.append(jnp.sum(mods, axis=0))
            got = []
            for step in range(clips_dev):
                b = (clip - step) % clips_dev
                sent = lax.dynamic_index_in_dim(done, b, 1, keepdims=False)
                got.append(lax.ppermute(sent, pair_axes, back(space_pairs(step))))
            stacked = jnp.stack(got)
            pieces.append(
                jnp.stack(
                    [
                        lax.dynamic_index_in_dim(stacked, (j - pa) % clips_dev, 0, keepdims=False)
                        for j in range(clips_dev)
                    ]
                )
            )
        latents_grad = jnp.concatenate(pieces, axis=1).astype(F32)

        def over_frames(lists, index):
            picked = [entry[index] for entry in lists]
            return picked[0] if len(picked) == 1 else jnp.concatenate(picked)

        normed1, att1, cross_in, cross_att, normed2, act2 = (
            over_frames(saves, i) for i in (1, 7, 9, 13, 16, 17)
        )
        kept3, d_lifted2, kept2, d_cross_query, kept1, d_query, d_key, d_value, d_tk, d_tv, space_mods = (
            over_frames(backs, i) for i in range(3, 14)
        )
        d_patch_up = weight_grad(normed2, d_lifted2)
        d_patch_down, d_gate5 = gated(weight_grad(act2, kept3), space_mod[5], patch_down)
        d_cross_proj = weight_grad(cross_att, kept2)
        d_cross_q = weight_grad(cross_in, d_cross_query)
        text_t = text.astype(F32).T
        d_cross_k = jnp.dot(text_t, jnp.sum(d_tk, axis=0)[:text_count], precision=HIGHEST)
        d_cross_v = jnp.dot(text_t, jnp.sum(d_tv, axis=0)[:text_count], precision=HIGHEST)
        d_cross = jnp.stack([d_cross_q, d_cross_k, d_cross_v, d_cross_proj])
        d_patch_proj, d_gate2 = gated(weight_grad(att1, kept1), space_mod[2], patch_attn[3])
        d_patch_attn = jnp.stack(
            [
                weight_grad(normed1[:, :space_rows], d_query),
                weight_grad(normed1, d_key),
                weight_grad(normed1, d_value),
                d_patch_proj,
            ]
        )
        space_mods = jnp.sum(space_mods, axis=0)
        first_mods = sum(first_mods[1:], first_mods[0])
        d_cross, d_patch_up, d_patch_down = summed([d_cross, d_patch_up, d_patch_down])
        (d_patch_attn,) = summed([d_patch_attn])

        space_six = jnp.stack([first_mods[0], first_mods[1], d_gate2, space_mods[0], space_mods[1], d_gate5])
        frame_six = jnp.stack([frame_mods[0], frame_mods[1], d_gate2_t, frame_mods[2], frame_mods[3], d_gate5_t])
        mine = jnp.stack([space_six, frame_six])
        spread = jnp.where(jnp.arange(clips)[:, None, None, None] == clip, mine[None], 0.0)
        by_clip = lax.psum(spread, whole_axes)
        d_table = jnp.sum(by_clip, axis=0)
        d_step = lax.dot_general(
            embeddings,
            jnp.sum(by_clip, axis=1).reshape(clips, -1),
            (((0,), (0,)), ((), ())),
            precision=HIGHEST,
        )
        return (
            output,
            latents_grad,
            d_step,
            d_table,
            d_patch_attn,
            d_cross,
            d_patch_up,
            d_patch_down,
            d_frame_attn,
            d_frame_up,
            d_frame_down,
        )

    return per_device


def solution(mesh):
    sizes = dict(mesh.shape)
    tokens = P("dev", "ta", "pa", None)
    in_specs = (tokens, P("dev", None, None), tokens, P("dev"), P("dev"), P("dev")) + (P(),) * 9
    out_specs = (tokens, tokens) + (P(),) * 9
    return jax.shard_map(
        make_per_device(sizes["ta"], sizes["pa"], sizes["dev"]),
        mesh=mesh,
        in_specs=in_specs,
        out_specs=out_specs,
        check_vma=False,
    )
```

```python
import math

import jax
import jax.numpy as jnp
from jax import lax
from jax.experimental import pallas as pl
from jax.experimental.pallas import tpu as pltpu
from jax.sharding import PartitionSpec as P

HEADS = 6
HDIM = 64
PAIRS = HEADS // 2
LANES = 2 * HDIM
EPSILON = 1e-06
MASKED_SCORE = -1e30
HIGHEST = lax.Precision.HIGHEST
F32 = jnp.float32
BF = jnp.bfloat16
VMEM_BYTES = 60 * 2**20
SUM_ROWS = 16
BLOCK = 16
SUB = 8
TILE = 16
PARTS = (7, 5, 4, 3, 2, 1)
PATTERN = (0, 1, 2, 0, 1, 0, 1)


def dot(a, b):
    return jnp.dot(a, b, preferred_element_type=F32)


def dot_nt(a, b):
    return lax.dot_general(a, b, (((1,), (1,)), ((), ())), preferred_element_type=F32)


def norm_parts(values):
    centred = values - jnp.mean(values, axis=-1, keepdims=True)
    inverse = lax.rsqrt(jnp.mean(centred * centred, axis=-1, keepdims=True) + EPSILON)
    return centred * inverse, inverse


def norm_back(d_normed, hat, inverse, scale_by):
    d_hat = d_normed * (1.0 + scale_by)
    mean_d = jnp.mean(d_hat, axis=-1, keepdims=True)
    mean_dh = jnp.mean(d_hat * hat, axis=-1, keepdims=True)
    return inverse * (d_hat - mean_d - hat * mean_dh)


GELU_A = math.sqrt(2.0 / math.pi)
GELU_B = 0.044715


def gelu_parts(values):
    square = values * values
    bent = jnp.tanh(GELU_A * values * (1.0 + GELU_B * square))
    half = 0.5 * (1.0 + bent)
    slope = half + (0.5 * GELU_A) * values * (1.0 - bent * bent) * (1.0 + 3.0 * GELU_B * square)
    return values * half, slope


def row_sums(values):
    return jnp.sum(values, axis=0, keepdims=True)


def head_lanes(values, head):
    lane = lax.broadcasted_iota(jnp.int32, values.shape, 1)
    return jnp.where((lane >= HDIM) == (head % 2 == 1), values, jnp.zeros_like(values))


def pair_of(values, pair):
    return values[:, pair * LANES : (pair + 1) * LANES]


def head_rows(values, head):
    return values[head * HDIM : (head + 1) * HDIM, :]


def lone_rows(values, head):
    rows = head_rows(values, head)
    blank = jnp.zeros_like(rows)
    return jnp.concatenate([rows, blank] if head % 2 == 0 else [blank, rows], axis=0)


def attend(queries, keys, values_t, bias, keep_exponent):
    ones = jnp.ones((SUM_ROWS, values_t.shape[1]), BF)
    parts, inverses = [], []
    for head in range(HEADS):
        pair = head // 2
        scores = dot_nt(pair_of(keys, pair), head_lanes(pair_of(queries, pair), head))
        if bias is not None:
            scores = scores + bias
        largest = jnp.max(scores, axis=0, keepdims=True)
        exponent = jnp.exp(scores - largest).astype(BF)
        keep_exponent(head, exponent)
        lifted = jnp.concatenate([head_rows(values_t, head), ones], axis=0)
        summed = dot(lifted, exponent)
        inverse = 1.0 / summed[HDIM : HDIM + 1, :]
        parts.append(summed[:HDIM, :] * inverse)
        inverses.append(inverse)
    return jnp.concatenate(parts, axis=0), inverses


def attend_back(exponent_of, queries_of, keys_t_of, values_of, d_att_t, att_t, inverse_of, keys_chunk):
    n_keys, chunk = keys_chunk
    d_query_parts, d_key_pairs, d_value_pairs = [], [], []
    for pair in range(PAIRS):
        d_keys = [None] * (n_keys // chunk)
        d_values = [None] * (n_keys // chunk)
        for head in (2 * pair, 2 * pair + 1):
            inverse = inverse_of(head)
            d_att_head = head_rows(d_att_t, head)
            centre = row_sums(d_att_head * head_rows(att_t, head)) * inverse
            scaled = (d_att_head * inverse).astype(BF)
            blank = jnp.zeros_like(scaled)
            scaled_pair = jnp.concatenate([scaled, blank] if head % 2 == 0 else [blank, scaled], axis=0)
            query_pair = head_lanes(queries_of(pair), head)
            d_query = None
            for at in range(n_keys // chunk):
                rows = slice(at * chunk, (at + 1) * chunk)
                exponent = exponent_of(head, rows)
                d_chance = dot(values_of(pair, rows), scaled_pair)
                d_score = (exponent.astype(F32) * (d_chance - centre)).astype(BF)
                d_value = dot_nt(exponent, scaled_pair)
                d_key = dot(d_score, query_pair)
                part = dot(keys_t_of(head, rows), d_score)
                d_query = part if d_query is None else d_query + part
                d_keys[at] = d_key if d_keys[at] is None else d_keys[at] + d_key
                d_values[at] = d_value if d_values[at] is None else d_values[at] + d_value
            d_query_parts.append(d_query)
        d_key_pairs.append(jnp.concatenate(d_keys, axis=0))
        d_value_pairs.append(jnp.concatenate(d_values, axis=0))
    return (
        jnp.concatenate(d_query_parts, axis=0),
        jnp.concatenate(d_key_pairs, axis=1),
        jnp.concatenate(d_value_pairs, axis=1),
    )


def fold(ref):
    value = ref[...]
    return value.reshape(-1, value.shape[-1])


def space_forward_kernel(
    first_frame,
    counts_ref,
    own_ref,
    other_ref,
    mod_ref,
    attn_ref,
    turned_ref,
    cross_ref,
    text_keys_ref,
    text_values_t_ref,
    up_ref,
    down_ref,
    state_ref,
    normed_ref,
    query_ref,
    keys_t_ref,
    value_ref,
    exponent_ref,
    att_t_ref,
    att_ref,
    inverse_ref,
    cross_in_ref,
    cross_query_ref,
    cross_exponent_ref,
    cross_att_t_ref,
    cross_att_ref,
    cross_inverse_ref,
    middle_ref,
    normed2_ref,
    act_ref,
    slope_ref,
    branch2_ref,
    branch5_ref,
):
    scale_by = HDIM ** (-0.5)
    frame = counts_ref[2] + first_frame + pl.program_id(0)
    keep = (frame < counts_ref[0]).astype(F32)
    mod = mod_ref[...]
    own = fold(own_ref).astype(F32)
    rows = own.shape[0]
    normed_own = (norm_parts(own)[0] * (1.0 + mod[1:2]) + mod[0:1]).astype(BF)
    normed_other = (norm_parts(fold(other_ref).astype(F32))[0] * (1.0 + mod[1:2]) + mod[0:1]).astype(BF)
    normed = jnp.concatenate([normed_own, normed_other], axis=0)
    normed_ref[0] = normed
    queries = (dot(normed_own, attn_ref[0]).astype(BF) * scale_by).astype(BF)
    keys = dot(normed, attn_ref[1]).astype(BF)
    values = dot(normed, attn_ref[2]).astype(BF)
    query_ref[0] = queries
    value_ref[0] = values
    keys_t_ref[0] = dot_nt(turned_ref[0], normed).astype(BF)
    values_t = dot_nt(turned_ref[1], normed).astype(BF)

    def keep_exponent(head, exponent):
        exponent_ref[0, head] = exponent

    att_t, inverses = attend(queries, keys, values_t, None, keep_exponent)
    for head in range(HEADS):
        inverse_ref[0, head : head + 1, :] = inverses[head]
    att_t_ref[0] = att_t.astype(BF)
    att = att_t.T.astype(BF)
    att_ref[0] = att
    branch = dot(att, attn_ref[3])
    branch2_ref[0] = branch.astype(BF)
    state = own + (keep * mod[2:3]) * branch
    cross_in = state.astype(BF)
    cross_in_ref[0] = cross_in
    cross_queries = (dot(cross_in, cross_ref[0]).astype(BF) * scale_by).astype(BF)
    cross_query_ref[0] = cross_queries
    text_id = lax.broadcasted_iota(jnp.int32, (text_keys_ref.shape[0], rows), 0)
    bias = jnp.where(text_id < counts_ref[1], 0.0, MASKED_SCORE)

    def keep_cross(head, exponent):
        cross_exponent_ref[0, head] = exponent

    cross_t, inverses = attend(cross_queries, text_keys_ref[...], text_values_t_ref[...], bias, keep_cross)
    for head in range(HEADS):
        cross_inverse_ref[0, head : head + 1, :] = inverses[head]
    cross_att_t_ref[0] = cross_t.astype(BF)
    cross_att = cross_t.T.astype(BF)
    cross_att_ref[0] = cross_att
    state = state + keep * dot(cross_att, cross_ref[1])
    middle_ref[0] = state
    normed2 = (norm_parts(state)[0] * (1.0 + mod[4:5]) + mod[3:4]).astype(BF)
    normed2_ref[0] = normed2
    act, slope = gelu_parts(dot(normed2, up_ref[...]))
    act = act.astype(BF)
    act_ref[0] = act
    slope_ref[0] = slope.astype(BF)
    branch = dot(act, down_ref[...])
    branch5_ref[0] = branch.astype(BF)
    state = state + (keep * mod[5:6]) * branch
    state_ref[0] = state.astype(BF)


def space_backward_kernel(
    first_frame,
    counts_ref,
    grad_ref,
    mod_ref,
    attn_ref,
    cross_ref,
    text_keys_t_ref,
    text_values_ref,
    up_ref,
    down_ref,
    query_ref,
    keys_t_ref,
    value_ref,
    exponent_ref,
    att_t_ref,
    inverse_ref,
    cross_query_ref,
    cross_exponent_ref,
    cross_att_t_ref,
    cross_inverse_ref,
    middle_ref,
    slope_ref,
    branch2_ref,
    branch5_ref,
    state_grad_ref,
    own_grad_ref,
    other_grad_ref,
    kept3_ref,
    d_lifted_ref,
    kept2_ref,
    d_cross_query_ref,
    kept1_ref,
    d_query_ref,
    d_key_ref,
    d_value_ref,
    d_text_keys_ref,
    d_text_values_ref,
    mods_ref,
):
    scale_by = HDIM ** (-0.5)
    frame = counts_ref[2] + first_frame + pl.program_id(0)
    keep = (frame < counts_ref[0]).astype(F32)
    mod = mod_ref[...]
    grad = fold(grad_ref).astype(F32)
    rows = grad.shape[0]
    kept = keep * grad
    d_gate5 = row_sums(kept * branch5_ref[0].astype(F32))
    d_branch = (kept * mod[5:6]).astype(BF)
    kept3_ref[0] = d_branch
    d_act = dot_nt(d_branch, down_ref[...])
    d_lifted = (d_act * slope_ref[0].astype(F32)).astype(BF)
    d_lifted_ref[0] = d_lifted
    d_normed = dot_nt(d_lifted, up_ref[...])
    hat, inverse = norm_parts(middle_ref[0])
    grad = grad + norm_back(d_normed, hat, inverse, mod[4:5])
    d_shift, d_scale = row_sums(d_normed), row_sums(d_normed * hat)
    kept = (keep * grad).astype(BF)
    kept2_ref[0] = kept
    d_att_t = dot_nt(cross_ref[1], kept)
    d_query_t, d_keys, d_values = attend_back(
        lambda head, at: cross_exponent_ref[0, head, at, :],
        lambda pair: cross_query_ref[0, :, pair * LANES : (pair + 1) * LANES],
        lambda head, at: text_keys_t_ref[head * HDIM : (head + 1) * HDIM, at],
        lambda pair, at: text_values_ref[at, pair * LANES : (pair + 1) * LANES],
        d_att_t,
        cross_att_t_ref[0].astype(F32),
        lambda head: cross_inverse_ref[0, head : head + 1, :],
        (text_values_ref.shape[0], text_values_ref.shape[0]),
    )
    d_text_keys_ref[0] = d_keys
    d_text_values_ref[0] = d_values
    d_query = (d_query_t.T * scale_by).astype(BF)
    d_cross_query_ref[0] = d_query
    grad = grad + dot_nt(d_query, cross_ref[0])
    state_grad_ref[0] = grad
    kept = keep * grad
    d_gate2 = row_sums(kept * branch2_ref[0].astype(F32))
    mods_ref[0] = jnp.concatenate(
        [jnp.zeros((2, hat.shape[1]), F32), d_gate2, d_shift, d_scale, d_gate5, jnp.zeros((2, hat.shape[1]), F32)],
        axis=0,
    )
    d_branch = (kept * mod[2:3]).astype(BF)
    kept1_ref[0] = d_branch
    d_att_t = dot_nt(attn_ref[3], d_branch)
    n_keys = value_ref.shape[1]
    d_query_t, d_keys, d_values = attend_back(
        lambda head, at: exponent_ref[0, head, at, :],
        lambda pair: query_ref[0, :, pair * LANES : (pair + 1) * LANES],
        lambda head, at: keys_t_ref[0, head * HDIM : (head + 1) * HDIM, at],
        lambda pair, at: value_ref[0, at, pair * LANES : (pair + 1) * LANES],
        d_att_t,
        att_t_ref[0].astype(F32),
        lambda head: inverse_ref[0, head : head + 1, :],
        (n_keys, min(n_keys, 256)),
    )
    d_query = (d_query_t.T * scale_by).astype(BF)
    d_keys, d_values = d_keys.astype(BF), d_values.astype(BF)
    d_query_ref[0] = d_query
    d_key_ref[0] = d_keys
    d_value_ref[0] = d_values
    d_normed = dot_nt(d_keys, attn_ref[1]) + dot_nt(d_values, attn_ref[2])
    own_grad_ref[0] = d_normed[:rows] + dot_nt(d_query, attn_ref[0])
    other_grad_ref[0] = d_normed[rows:].astype(BF)


def space_finish_kernel(n_parts, own_ref, state_grad_ref, own_grad_ref, *rest):
    parts, (mod_ref, out_ref, mods_ref) = rest[:n_parts], rest[n_parts:]
    d_normed = own_grad_ref[0]
    for part in parts:
        d_normed = d_normed + part[0].astype(F32)
    hat, inverse = norm_parts(fold(own_ref).astype(F32))
    grad = state_grad_ref[0] + norm_back(d_normed, hat, inverse, mod_ref[1:2, :])
    out_ref[...] = grad.astype(BF).reshape(out_ref.shape)
    mods_ref[0] = jnp.concatenate(
        [row_sums(d_normed), row_sums(d_normed * hat), jnp.zeros((6, hat.shape[1]), F32)], axis=0
    )


def time_kernel(
    counts_ref,
    state_ref,
    cot_ref,
    mod_ref,
    bias_ref,
    attn_ref,
    turned_ref,
    up_ref,
    down_ref,
    out_ref,
    grad_ref,
    normed_ref,
    d_qkv_ref,
    att_ref,
    branch4_ref,
    normed2_ref,
    act_ref,
    d_lifted_ref,
    branch5_ref,
    mods_ref,
    exponent_ref,
):
    scale_by = HDIM ** (-0.5)
    frames, block, width = state_ref.shape
    run_rows = frames * SUB
    runs = block // SUB
    mod = mod_ref[...]

    def load(ref):
        cube = ref[...].astype(F32)
        parts = [cube[:, r * SUB : (r + 1) * SUB].reshape(run_rows, width) for r in range(runs)]
        return jnp.concatenate(parts, axis=0)

    def store(ref, value):
        parts = [value[r * run_rows : (r + 1) * run_rows].reshape(frames, SUB, width) for r in range(runs)]
        ref[...] = jnp.concatenate(parts, axis=1).astype(ref.dtype)

    def run_of(value, r):
        return value[r * run_rows : (r + 1) * run_rows]

    state = load(state_ref)
    rows = state.shape[0]
    frame = (lax.broadcasted_iota(jnp.int32, (rows, 1), 0) // SUB) % frames
    keep = (frame < counts_ref[0]).astype(F32)
    hat1, inverse1 = norm_parts(state)
    normed = (hat1 * (1.0 + mod[1:2]) + mod[0:1]).astype(BF)
    normed_ref[0] = normed
    queries = (dot(normed, attn_ref[0]).astype(BF) * scale_by).astype(BF)
    keys = dot(normed, attn_ref[1]).astype(BF)
    values = dot(normed, attn_ref[2]).astype(BF)
    att_parts, att_t_parts, inverse_parts, keys_t_parts = [], [], [], []
    for r in range(runs):
        normed_run = run_of(normed, r)
        keys_t_parts.append(dot_nt(turned_ref[0], normed_run).astype(BF))
        values_t = dot_nt(turned_ref[1], normed_run).astype(BF)

        def keep_exponent(head, exponent):
            exponent_ref[r, head] = exponent

        att_t, inverses = attend(
            run_of(queries, r), run_of(keys, r), values_t, bias_ref[...], keep_exponent
        )
        att_t_parts.append(att_t)
        inverse_parts.append(inverses)
        att_parts.append(att_t.T.astype(BF))
    att = jnp.concatenate(att_parts, axis=0)
    att_ref[0] = att
    branch2 = dot(att, attn_ref[3])
    state = state + (keep * mod[2:3]) * branch2
    hat2, inverse2 = norm_parts(state)
    normed2 = (hat2 * (1.0 + mod[4:5]) + mod[3:4]).astype(BF)
    normed2_ref[0] = normed2
    act, slope = gelu_parts(dot(normed2, up_ref[...]))
    act = act.astype(BF)
    act_ref[0] = act
    branch5 = dot(act, down_ref[...])
    store(out_ref, state + (keep * mod[5:6]) * branch5)
    grad = load(cot_ref)
    kept = keep * grad
    d_gate5 = row_sums(kept * branch5)
    d_branch = (kept * mod[5:6]).astype(BF)
    branch5_ref[0] = d_branch
    d_act = dot_nt(d_branch, down_ref[...])
    d_lifted = (d_act * slope).astype(BF)
    d_lifted_ref[0] = d_lifted
    d_normed2 = dot_nt(d_lifted, up_ref[...])
    grad = grad + norm_back(d_normed2, hat2, inverse2, mod[4:5])
    kept = keep * grad
    d_gate2 = row_sums(kept * branch2)
    d_branch = (kept * mod[2:3]).astype(BF)
    branch4_ref[0] = d_branch
    d_query_parts, d_key_parts, d_value_parts = [], [], []
    for r in range(runs):
        d_att_t = dot_nt(attn_ref[3], run_of(d_branch, r))
        query_run, value_run = run_of(queries, r), run_of(values, r)
        d_query_t, d_keys, d_values = attend_back(
            lambda head, at: exponent_ref[r, head, at, :],
            lambda pair: pair_of(query_run, pair),
            lambda head, at: head_rows(keys_t_parts[r], head)[:, at],
            lambda pair, at: pair_of(value_run, pair)[at],
            d_att_t,
            att_t_parts[r],
            lambda head: inverse_parts[r][head],
            (run_rows, run_rows),
        )
        d_query_parts.append((d_query_t.T * scale_by).astype(BF))
        d_key_parts.append(d_keys.astype(BF))
        d_value_parts.append(d_values.astype(BF))
    d_qkv = [jnp.concatenate(parts, axis=0) for parts in (d_query_parts, d_key_parts, d_value_parts)]
    d_normed1 = None
    for i in range(3):
        d_qkv_ref[0, :, i * width : (i + 1) * width] = d_qkv[i]
        part = dot_nt(d_qkv[i], attn_ref[i])
        d_normed1 = part if d_normed1 is None else d_normed1 + part
    grad = grad + norm_back(d_normed1, hat1, inverse1, mod[1:2])
    store(grad_ref, grad)
    mods_ref[0] = jnp.concatenate(
        [
            row_sums(d_normed1),
            row_sums(d_normed1 * hat1),
            d_gate2,
            row_sums(d_normed2),
            row_sums(d_normed2 * hat2),
            d_gate5,
            jnp.zeros((2, width), F32),
        ],
        axis=0,
    )


class Reducer:
    def __init__(self, shapes, small_rows, sizes):
        self.width = width = shapes[0][1]
        self.shapes = shapes
        bits = {name: [(name, 1 << i) for i in range(sizes[name].bit_length() - 1)] for name in ("ta", "pa")}
        kinds = [bits["ta"] + bits["pa"], bits["ta"][::-1] + bits["pa"], bits["pa"] + bits["ta"]]
        self.ways = [("dev", 1)] + kinds[0]
        self.loads, row = [], 0
        for i, shape in enumerate(shapes):
            for column in range(shape[1] // width):
                self.loads.append((i, row, column * width, shape[0]))
                row += shape[0]
        self.total = row
        self.parts = next(n for n in PARTS if row % (2 * n * TILE) == 0)
        self.part_rows = row // 2 // self.parts
        self.half_rows = row // 2
        self.orders = [[("dev", 1)] + kinds[PATTERN[p % len(PATTERN)]] for p in range(self.parts)]
        self.steps = len(self.ways)
        self.small_rows = small_rows
        self.counts, self.halves, self.boxes, at = [self.part_rows], [True], [], 0
        for _ in range(1, self.steps):
            halve = (self.counts[-1] // 2) % TILE == 0
            self.halves.append(halve)
            self.counts.append(self.counts[-1] // 2 if halve else self.counts[-1])
        for p in range(self.parts):
            self.boxes.append([])
            for count in self.counts:
                self.boxes[p].append(at)
                at += count
        self.box_rows = at
        self.phases = 2 * self.steps + 1

    def scratch(self):
        shapes = [
            pltpu.VMEM((self.total, self.width), BF),
            pltpu.VMEM((self.total, self.width), BF),
            pltpu.VMEM((self.box_rows, self.width), BF),
            pltpu.SemaphoreType.DMA((len(self.loads),)),
            pltpu.SemaphoreType.DMA((self.parts, 2)),
            pltpu.SemaphoreType.DMA((self.parts, 2 * self.steps)),
            pltpu.SemaphoreType.DMA((self.parts, 2 * self.steps)),
        ]
        if self.small_rows:
            shapes += [
                pltpu.VMEM((self.steps, self.small_rows, self.width), F32),
                pltpu.SemaphoreType.DMA((self.steps,)),
                pltpu.SemaphoreType.DMA((self.steps,)),
            ]
        return shapes

    def bind(self, sources, out, scratch, small_in=None, small_out=None):
        self.sources, self.out = sources, out
        self.work, self.whole, self.inbox, self.in_sem, self.out_sem, self.send_sem, self.recv_sem = scratch[:7]
        self.small_in, self.small_out = small_in, small_out
        if self.small_rows:
            self.small_box, self.small_send, self.small_recv = scratch[7:]

    def bit(self, way):
        return (lax.axis_index(way[0]) // way[1]) % 2

    def peer(self, way):
        return {way[0]: lax.axis_index(way[0]) + way[1] - 2 * way[1] * self.bit(way)}

    def greet(self):
        barrier = pltpu.get_barrier_semaphore()
        for way in self.ways:
            pl.semaphore_signal(barrier, inc=1, device_id=self.peer(way), device_id_type=pl.DeviceIdType.MESH)
        return len(self.ways)

    def base(self, p, step):
        row = self.bit(self.orders[p][0]) * self.half_rows + p * self.part_rows
        for s in range(1, step + 1):
            if self.halves[s]:
                row = row + self.bit(self.orders[p][s]) * self.counts[s]
        return row

    def rows(self, ref, row, count):
        return ref.at[pl.ds(pl.multiple_of(row, TILE), count)]

    def load(self, i):
        source, row, column, rows = self.loads[i]
        view = self.sources[source].at[:, column : column + self.width]
        return pltpu.make_async_copy(view, self.work.at[row : row + rows], self.in_sem.at[i])

    def remote(self, src, dst, p, step, way):
        return pltpu.make_async_remote_copy(
            src_ref=src,
            dst_ref=dst,
            send_sem=self.send_sem.at[p, step],
            recv_sem=self.recv_sem.at[p, step],
            device_id=self.peer(way),
            device_id_type=pl.DeviceIdType.MESH,
        )

    def down(self, p, step):
        way, count = self.orders[p][step], self.counts[step]
        if step == 0:
            row = (1 - self.bit(way)) * self.half_rows + p * self.part_rows
        else:
            row = self.base(p, step - 1)
            if self.halves[step]:
                row = row + (1 - self.bit(way)) * count
        box = self.boxes[p][step]
        return self.remote(self.rows(self.work, row, count), self.inbox.at[box : box + count], p, step, way)

    def end_down(self, p, step):
        self.down(p, step).wait()
        count, base, box = self.counts[step], self.base(p, step), self.boxes[p][step]
        chunk = next(c for c in (96, 64, 48, 32, TILE) if count % c == 0)

        def body(i, carry):
            at = pl.ds(pl.multiple_of(base + i * chunk, TILE), chunk)
            got = self.inbox[pl.ds(pl.multiple_of(box + i * chunk, TILE), chunk), :]
            total = (self.work[at, :].astype(F32) + got.astype(F32)).astype(BF)
            if step == self.steps - 1:
                self.whole[at, :] = total
            else:
                self.work[at, :] = total
            return carry

        lax.fori_loop(0, count // chunk, body, 0)

    def up(self, p, turn):
        step = self.steps - 1 - turn
        if not self.halves[step]:
            return None
        rows = self.rows(self.whole, self.base(p, step), self.counts[step])
        return self.remote(rows, rows, p, self.steps + turn, self.orders[p][step])

    def store(self, p, side):
        rows = pl.ds(side * self.half_rows + p * self.part_rows, self.part_rows)
        return pltpu.make_async_copy(self.whole.at[rows], self.out.at[rows], self.out_sem.at[p, side])

    def small(self, step):
        return pltpu.make_async_remote_copy(
            src_ref=self.small_out,
            dst_ref=self.small_box.at[step],
            send_sem=self.small_send.at[step],
            recv_sem=self.small_recv.at[step],
            device_id=self.peer(self.ways[step]),
            device_id_type=pl.DeviceIdType.MESH,
        )

    def prepare(self):
        for i in range(len(self.loads)):
            self.load(i).start()
        if self.small_rows:
            self.small_out[...] = self.small_in[...]

    def phase(self, k):
        n = self.steps
        if k == 0:
            for i in range(len(self.loads)):
                self.load(i).wait()
        for p in range(self.parts):
            if 1 <= k <= n:
                self.end_down(p, k - 1)
            elif k > n:
                before = self.up(p, k - n - 1)
                if before is not None:
                    before.wait()
            if k < n:
                self.down(p, k).start()
            elif k < 2 * n:
                after = self.up(p, k - n)
                if after is not None:
                    after.start()
            else:
                self.store(p, 0).start()
                self.store(p, 1).start()
        if k == 2 * n:
            for p in range(self.parts):
                self.store(p, 0).wait()
                self.store(p, 1).wait()
        if self.small_rows and k <= n:
            if k > 0:
                self.small(k - 1).wait()
                self.small_out[...] = self.small_out[...] + self.small_box[k - 1]
            if k < n:
                self.small(k).start()

    def unpack(self, reduced):
        results, at = [], 0
        for rows, columns in self.shapes:
            turns = columns // self.width
            blocks = [reduced[at + i * rows : at + (i + 1) * rows] for i in range(turns)]
            at += turns * rows
            results.append((blocks[0] if turns == 1 else jnp.concatenate(blocks, axis=1)).astype(F32))
        return results


def reduce_all(arrays, small, sizes):
    reducer = Reducer([a.shape for a in arrays], small.shape[0], sizes)
    n = len(arrays)

    def kernel(*refs):
        reducer.bind(refs[:n], refs[n + 1], refs[n + 3 :], refs[n], refs[n + 2])
        reducer.prepare()
        pl.semaphore_wait(pltpu.get_barrier_semaphore(), reducer.greet())
        for k in range(reducer.phases):
            reducer.phase(k)

    any_spec, vmem_spec = pl.BlockSpec(memory_space=pl.ANY), pl.BlockSpec(memory_space=pltpu.VMEM)
    reduced, small_sum = pl.pallas_call(
        kernel,
        in_specs=[any_spec] * n + [vmem_spec],
        out_specs=[any_spec, vmem_spec],
        out_shape=[shape_of((reducer.total, reducer.width), BF), shape_of(small.shape, F32)],
        scratch_shapes=reducer.scratch(),
        compiler_params=pltpu.CompilerParams(collective_id=0, has_side_effects=True, vmem_limit_bytes=VMEM_BYTES),
        cost_estimate=pl.CostEstimate(
            flops=8 * reducer.total * reducer.width, bytes_accessed=4 * reducer.total * reducer.width, transcendentals=0
        ),
    )(*arrays, small)
    return reducer.unpack(reduced), small_sum


def whole(array):
    zeros = (0,) * array.ndim
    return pl.BlockSpec(array.shape, lambda *grid: zeros)


def framed(array):
    tail = (0,) * (array.ndim - 1)
    return pl.BlockSpec((1,) + tuple(array.shape[1:]), lambda frame: (frame,) + tail)


SCALARS = pl.BlockSpec(memory_space=pltpu.SMEM)


def shape_of(shape, dtype):
    return jax.ShapeDtypeStruct(shape, dtype)


def call(kernel, grid, inputs, in_specs, outputs, out_specs, flops, scratch=()):
    moved = sum(math.prod(a.shape) * a.dtype.itemsize for a in (*inputs, *outputs))
    return pl.pallas_call(
        kernel,
        grid=grid,
        in_specs=in_specs,
        out_specs=out_specs,
        out_shape=outputs,
        scratch_shapes=list(scratch),
        compiler_params=pltpu.CompilerParams(vmem_limit_bytes=VMEM_BYTES),
        cost_estimate=pl.CostEstimate(flops=int(flops), bytes_accessed=int(moved), transcendentals=0),
    )(*inputs)


def make_per_device(sizes):
    n_ta, n_pa, n_dev = sizes["ta"], sizes["pa"], sizes["dev"]

    def per_device(
        latents,
        context,
        cotangent,
        timesteps,
        frame_counts,
        text_lengths,
        step_proj,
        mod_table,
        patch_attn,
        cross_attn,
        patch_up,
        patch_down,
        frame_attn,
        frame_up,
        frame_down,
    ):
        clips_dev, frames, patches, width = latents.shape
        clips = clips_dev * n_dev
        run = n_pa // clips
        group = run * n_dev
        near = n_pa // group
        space_rows = near * patches
        time_patches = space_rows // n_ta
        other_rows = (group - 1) * space_rows
        key_rows = group * space_rows
        all_frames = n_ta * frames
        ta, pa, dev = (lax.axis_index(name) for name in ("ta", "pa", "dev"))
        clip = pa // run
        member = dev * run + pa % run

        def place(clip_id, member_id):
            return (clip_id * run + member_id % run) * n_dev + member_id // run

        def space_pairs(step):
            pairs = []
            for p in range(n_pa):
                for d in range(n_dev):
                    k = d * clips_dev + (p + step) % clips_dev
                    pairs.append((p * n_dev + d, place(k, p // near)))
            return pairs

        halves = n_ta // near

        def time_pairs(step):
            u, w = step % halves, step // halves
            pairs = []
            for t in range(n_ta):
                for p in range(n_pa):
                    for d in range(n_dev):
                        s = (t % halves + u) % halves
                        j = (t // halves + w) % clips_dev
                        k = d * clips_dev + j
                        pairs.append(
                            (
                                (t * n_pa + p) * n_dev + d,
                                ((p % near) * halves + s) * n_pa * n_dev + place(k, p // near),
                            )
                        )
            return pairs

        def back(pairs):
            return [(b, a) for a, b in pairs]

        def group_pairs(step):
            return [
                (place(k, g), place(k, (g + step) % group)) for k in range(clips) for g in range(group)
            ]

        def ta_pairs(step):
            return [(t, t ^ step) for t in range(n_ta)]

        whole_axes = ("ta", "pa", "dev")
        pair_axes = ("pa", "dev")

        def of_clip(local):
            both = lax.all_gather(local, "dev", axis=0, tiled=True)
            return lax.dynamic_index_in_dim(both, clip, 0, keepdims=False)

        def sinusoid(steps):
            half = step_proj.shape[0] // 2
            frequency = jnp.exp(-math.log(10000.0) * jnp.arange(half, dtype=F32) / half)
            angles = steps.astype(F32)[:, None] * frequency[None, :]
            return jnp.concatenate([jnp.cos(angles), jnp.sin(angles)], axis=1)

        numbers = lax.all_gather(jnp.stack([timesteps, frame_counts, text_lengths], axis=1), "dev", axis=0, tiled=True)
        own_numbers = lax.dynamic_index_in_dim(numbers, clip, 0, keepdims=False)
        embeddings = sinusoid(numbers[:, 0])
        embedding = lax.dynamic_index_in_dim(embeddings, clip, 0, keepdims=True)
        timing = jnp.dot(embedding, step_proj.astype(F32), precision=HIGHEST).reshape(6, width)
        table = mod_table.astype(F32)
        pad = jnp.zeros((2, width), F32)
        space_mod = jnp.concatenate([timing + table[0], pad])
        frame_mod = jnp.concatenate([timing + table[1], pad])
        counts = jnp.stack([own_numbers[1], own_numbers[2], ta * frames, 0]).astype(jnp.int32)
        text = of_clip(context)
        text_count = text.shape[0]
        text_rows = -(-text_count // LANES) * LANES
        text_wide = jnp.pad(text, ((0, text_rows - text_count), (0, 0)))
        text_keys = dot(text_wide, cross_attn[1]).astype(BF)
        text_values = dot(text_wide, cross_attn[2]).astype(BF)
        cross_ends = jnp.stack([cross_attn[0], cross_attn[3]])
        patch_turned = jnp.swapaxes(patch_attn[1:3], 1, 2)
        frame_turned = jnp.swapaxes(frame_attn[1:3], 1, 2)

        def to_space(frame_ids):
            picked = latents[:, frame_ids[0] : frame_ids[-1] + 1]
            parts = []
            for step in range(clips_dev):
                sent = lax.dynamic_index_in_dim(picked, (pa + step) % clips_dev, 0, keepdims=False)
                parts.append(lax.ppermute(sent, pair_axes, space_pairs(step)))
            stacked = jnp.stack(parts)
            slots = [
                lax.dynamic_index_in_dim(stacked, (clip - b) % clips_dev, 0, keepdims=False) for b in range(near)
            ]
            own = jnp.concatenate(slots, axis=1)
            others = [lax.ppermute(own, pair_axes, group_pairs(step)) for step in range(1, group)]
            return own, jnp.concatenate(others, axis=1)

        def space_forward(frame_ids, own, other):
            count = len(frame_ids)

            def out(*shape, dtype=BF):
                return shape_of((count,) + shape, dtype)

            inputs = (
                counts, own, other, space_mod, patch_attn, patch_turned, cross_ends, text_keys, text_values.T,
                patch_up, patch_down,
            )
            hidden = patch_up.shape[1]
            outputs = (
                out(space_rows, width),
                out(key_rows, width),
                out(space_rows, width),
                out(width, key_rows),
                out(key_rows, width),
                out(HEADS, key_rows, space_rows),
                out(width, space_rows),
                out(space_rows, width),
                out(8, space_rows, dtype=F32),
                out(space_rows, width),
                out(space_rows, width),
                out(HEADS, text_rows, space_rows),
                out(width, space_rows),
                out(space_rows, width),
                out(8, space_rows, dtype=F32),
                out(space_rows, width, dtype=F32),
                out(space_rows, width),
                out(space_rows, hidden),
                out(space_rows, hidden),
                out(space_rows, width),
                out(space_rows, width),
            )
            dense = 2 * count * space_rows * width * (6 * width + 2 * hidden) + 8 * count * key_rows * width * width
            return call(
                lambda *refs: space_forward_kernel(frame_ids[0], *refs),
                (count,),
                inputs,
                [SCALARS, framed(own), framed(other)] + [whole(a) for a in inputs[3:]],
                outputs,
                [framed(a) for a in outputs],
                dense + 16 * count * space_rows * key_rows * width,
            )

        def space_backward(frame_ids, grad, saved):
            count = len(frame_ids)

            def out(*shape, dtype=BF):
                return shape_of((count,) + shape, dtype)

            (_, _, query, keys_t, value, exponent, att_t, _, inverse, _, cross_query, cross_exponent, cross_att_t, _,
             cross_inverse, middle, _, _, slope, branch2, branch5) = saved
            inputs = (
                counts, grad, space_mod, patch_attn, cross_ends, text_keys.T, text_values, patch_up, patch_down,
                query, keys_t, value, exponent, att_t, inverse, cross_query, cross_exponent, cross_att_t,
                cross_inverse, middle, slope, branch2, branch5,
            )
            hidden = patch_up.shape[1]
            outputs = (
                out(space_rows, width, dtype=F32),
                out(space_rows, width, dtype=F32),
                out(other_rows, width),
                out(space_rows, width),
                out(space_rows, hidden),
                out(space_rows, width),
                out(space_rows, width),
                out(space_rows, width),
                out(space_rows, width),
                out(key_rows, width),
                out(key_rows, width),
                out(text_rows, width, dtype=F32),
                out(text_rows, width, dtype=F32),
                out(8, width, dtype=F32),
            )
            grad_spec = pl.BlockSpec((n_ta, 1, time_patches, width), lambda frame: (0, frame, 0, 0))
            dense = 2 * count * space_rows * width * (6 * width + 2 * hidden) + 8 * count * key_rows * width * width
            return call(
                lambda *refs: space_backward_kernel(frame_ids[0], *refs),
                (count,),
                inputs,
                [SCALARS, grad_spec] + [whole(a) for a in inputs[2:9]] + [framed(a) for a in inputs[9:]],
                outputs,
                [framed(a) for a in outputs],
                dense + 32 * count * space_rows * key_rows * width,
            )

        def space_finish(own, state_grad, own_grad, parts):
            count = own.shape[0]
            inputs = (own, state_grad, own_grad, *parts, space_mod)
            outputs = (
                shape_of((count, near, patches, width), BF),
                shape_of((count, 8, width), F32),
            )
            return call(
                lambda *refs: space_finish_kernel(len(parts), *refs),
                (count,),
                inputs,
                [framed(a) for a in inputs[:-1]] + [whole(space_mod)],
                outputs,
                [framed(a) for a in outputs],
                count * space_rows * width * 30,
            )

        near_frames = min(2, frames)
        frame_groups = [tuple(range(near_frames)), tuple(range(near_frames, frames))]
        frame_groups = [ids for ids in frame_groups if ids]
        arrived = [to_space(ids) for ids in frame_groups]
        owns = [own for own, _ in arrived]
        cotangent, owns[-1] = lax.optimization_barrier((cotangent, owns[-1]))
        saves = [
            space_forward(ids, own, other) for ids, own, (_, other) in zip(frame_groups, owns, arrived)
        ]
        states = [saved[0] for saved in saves]

        n_steps = halves * clips_dev
        cot_parts = []
        for step in range(n_steps):
            u, w = step % halves, step // halves
            s = (ta % halves + u) % halves
            j = (ta // halves + w) % clips_dev
            sent = lax.dynamic_slice(
                cotangent, (j, 0, s * time_patches, 0), (1, frames, time_patches, width)
            )[0]
            cot_parts.append(lax.ppermute(sent, whole_axes, time_pairs(step)))
        cot_stack = jnp.stack(cot_parts)
        slot = ta % halves

        def step_from(source):
            u = (slot - source % halves) % halves
            w = (clip % clips_dev - source // halves) % clips_dev
            return w * halves + u

        cot = jnp.concatenate(
            [lax.dynamic_index_in_dim(cot_stack, step_from(t), 0, keepdims=False) for t in range(n_ta)]
        )

        def exchange(pieces):
            got = [lax.dynamic_index_in_dim(pieces, ta, 0, keepdims=False)]
            for step in range(1, n_ta):
                sent = lax.dynamic_index_in_dim(pieces, ta ^ step, 0, keepdims=False)
                got.append(lax.ppermute(sent, "ta", ta_pairs(step)))
            stacked = jnp.stack(got)
            return jnp.stack(
                [lax.dynamic_index_in_dim(stacked, ta ^ t, 0, keepdims=False) for t in range(n_ta)]
            )

        state_groups = []
        for state in states:
            pieces = state.reshape(state.shape[0], n_ta, time_patches, width).swapaxes(0, 1)
            state_groups.append(exchange(pieces))
        state = jnp.concatenate(state_groups, axis=1).reshape(all_frames, time_patches, width)

        block_rows = all_frames * BLOCK
        run_rows = all_frames * SUB
        ids = jnp.arange(run_rows, dtype=jnp.int32)
        same = (ids[:, None] % SUB == ids[None, :] % SUB) & (ids[:, None] // SUB < counts[0])
        bias = jnp.where(same, 0.0, MASKED_SCORE).astype(F32)
        hidden = frame_up.shape[1]
        n_blocks = time_patches // BLOCK

        def tokens(features):
            return shape_of((n_blocks, block_rows, features), BF)

        time_inputs = (counts, state, cot, frame_mod, bias, frame_attn, frame_turned, frame_up, frame_down)
        time_outputs = (
            shape_of((all_frames, time_patches, width), BF),
            shape_of((all_frames, time_patches, width), BF),
            tokens(width),
            tokens(3 * width),
            tokens(width),
            tokens(width),
            tokens(width),
            tokens(hidden),
            tokens(hidden),
            tokens(width),
            shape_of((n_blocks, 8, width), F32),
        )

        def blocked(array):
            return pl.BlockSpec((all_frames, BLOCK, array.shape[2]), lambda at: (0, at, 0))

        (out_t, grad_t, normed_t, d_qkv_t, att_tt, branch4, normed4, act4, d_lifted4, branch5, frame_six) = call(
            time_kernel,
            (n_blocks,),
            time_inputs,
            [SCALARS, blocked(state), blocked(cot)] + [whole(a) for a in time_inputs[3:]],
            time_outputs,
            [blocked(a) for a in time_outputs[:2]] + [framed(a) for a in time_outputs[2:]],
            all_frames * time_patches * width * (24 * width + 12 * hidden),
            [pltpu.VMEM((BLOCK // SUB, HEADS, run_rows, run_rows), BF)],
        )

        grad_s = exchange(grad_t.reshape(n_ta, frames, time_patches, width))

        out_t, grad_s = lax.optimization_barrier((out_t, grad_s))
        out_pieces = out_t.reshape(n_ta, frames, time_patches, width)
        out_parts = []
        for step in range(n_steps):
            u, w = step % halves, step // halves
            source = (slot - u) % halves + halves * ((clip % clips_dev - w) % clips_dev)
            sent = lax.dynamic_index_in_dim(out_pieces, source, 0, keepdims=False)
            out_parts.append(lax.ppermute(sent, whole_axes, back(time_pairs(step))))
        out_stack = jnp.stack(out_parts)
        rows = []
        for j in range(clips_dev):
            runs = []
            for s in range(halves):
                step = ((j - ta // halves) % clips_dev) * halves + (s - ta % halves) % halves
                runs.append(lax.dynamic_index_in_dim(out_stack, step, 0, keepdims=False))
            rows.append(jnp.concatenate(runs, axis=1))
        output = jnp.stack(rows)

        def weight_grad(left, right):
            left, right = left.reshape(-1, left.shape[-1]), right.reshape(-1, right.shape[-1])
            return lax.dot_general(left, right, (((0,), (0,)), ((), ())), preferred_element_type=F32).astype(BF)

        d_frame_qkv = weight_grad(normed_t, d_qkv_t)
        d_frame_proj = weight_grad(att_tt, branch4)
        d_frame_up = weight_grad(normed4, d_lifted4)
        d_frame_down = weight_grad(act4, branch5)

        pieces, backs, finish_six = [], [], []
        for i, (frame_ids, own, saved) in enumerate(zip(frame_groups, owns, saves)):
            grad = grad_s[:, frame_ids[0] : frame_ids[-1] + 1]
            if i == 1:
                grad, output = lax.optimization_barrier((grad, output))
            backed = space_backward(frame_ids, grad, saved)
            backs.append(backed)
            other_grad = backed[2]
            parts = []
            for step in range(1, group):
                sent = other_grad[:, (step - 1) * space_rows : step * space_rows]
                parts.append(lax.ppermute(sent, pair_axes, back(group_pairs(step))))
            done, mods = space_finish(own, backed[0], backed[1], parts)
            finish_six.append(mods)
            got = []
            for step in range(clips_dev):
                b = (clip - step) % clips_dev
                sent = lax.dynamic_index_in_dim(done, b, 1, keepdims=False)
                got.append(lax.ppermute(sent, pair_axes, back(space_pairs(step))))
            stacked = jnp.stack(got)
            pieces.append(
                jnp.stack(
                    [
                        lax.dynamic_index_in_dim(stacked, (j - pa) % clips_dev, 0, keepdims=False)
                        for j in range(clips_dev)
                    ]
                )
            )
        latents_grad = jnp.concatenate(pieces, axis=1).astype(F32)

        def over_frames(lists, index):
            picked = [entry[index] for entry in lists]
            return picked[0] if len(picked) == 1 else jnp.concatenate(picked)

        def grad_over(lists, index, others, other_index):
            total = None
            for one, two in zip(lists, others):
                left, right = one[index], two[other_index]
                left, right = left.reshape(-1, left.shape[-1]), right.reshape(-1, right.shape[-1])
                part = lax.dot_general(left, right, (((0,), (0,)), ((), ())), preferred_element_type=F32)
                total = part if total is None else total + part
            return total.astype(BF)

        d_patch_up = grad_over(saves, 16, backs, 4)
        d_patch_down = grad_over(saves, 17, backs, 3)
        d_cross_proj = grad_over(saves, 13, backs, 5)
        d_cross_q = grad_over(saves, 9, backs, 6)
        text_t = text.astype(F32).T
        d_tk, d_tv = (over_frames(backs, i) for i in (11, 12))
        d_cross_k = jnp.dot(text_t, jnp.sum(d_tk, axis=0)[:text_count], precision=HIGHEST).astype(BF)
        d_cross_v = jnp.dot(text_t, jnp.sum(d_tv, axis=0)[:text_count], precision=HIGHEST).astype(BF)
        d_patch_proj = grad_over(saves, 7, backs, 7)
        near_saves = [(saved[1][:, :space_rows],) for saved in saves]
        d_patch_q = grad_over(near_saves, 0, backs, 8)
        d_patch_k = grad_over(saves, 1, backs, 9)
        d_patch_v = grad_over(saves, 1, backs, 10)
        six = jnp.sum(over_frames(backs, 13), axis=0) + jnp.sum(jnp.concatenate(finish_six), axis=0)
        mine = jnp.stack([six, jnp.sum(frame_six, axis=0)])
        spread = jnp.where(jnp.arange(clips)[:, None, None, None] == clip, mine[None], 0.0)
        arrays = [
            d_patch_q, d_patch_k, d_patch_v, d_patch_proj, d_cross_q, d_cross_k, d_cross_v, d_cross_proj,
            d_patch_up, d_patch_down, d_frame_qkv, d_frame_proj, d_frame_up, d_frame_down,
        ]
        results, by_clip = reduce_all(arrays, spread.reshape(-1, width), sizes)
        by_clip = by_clip.reshape(clips, 2, 8, width)[:, :, :6]
        d_patch_attn = jnp.stack(results[0:4])
        d_cross = jnp.stack(results[4:8])
        d_patch_up, d_patch_down = results[8:10]
        d_frame_qkv = results[10].reshape(width, 3, width).swapaxes(0, 1)
        d_frame_attn = jnp.concatenate([d_frame_qkv, results[11][None]])
        d_frame_up, d_frame_down = results[12:14]
        d_table = jnp.sum(by_clip, axis=0)
        d_step = lax.dot_general(
            embeddings,
            jnp.sum(by_clip, axis=1).reshape(clips, -1),
            (((0,), (0,)), ((), ())),
            precision=HIGHEST,
        )
        return (
            output,
            latents_grad,
            d_step,
            d_table,
            d_patch_attn,
            d_cross,
            d_patch_up,
            d_patch_down,
            d_frame_attn,
            d_frame_up,
            d_frame_down,
        )

    return per_device


def solution(mesh):
    sizes = dict(mesh.shape)
    tokens = P("dev", "ta", "pa", None)
    in_specs = (tokens, P("dev", None, None), tokens, P("dev"), P("dev"), P("dev")) + (P(),) * 9
    out_specs = (tokens, tokens) + (P(),) * 9
    return jax.shard_map(
        make_per_device(sizes),
        mesh=mesh,
        in_specs=in_specs,
        out_specs=out_specs,
        check_vma=False,
    )
```

```python
import math

import jax
import jax.numpy as jnp
from jax import lax
from jax.experimental import pallas as pl
from jax.experimental.pallas import tpu as pltpu
from jax.sharding import PartitionSpec as P

HEADS = 6
HDIM = 64
PAIRS = HEADS // 2
LANES = 2 * HDIM
EPSILON = 1e-06
MASKED_SCORE = -1e30
HIGHEST = lax.Precision.HIGHEST
F32 = jnp.float32
BF = jnp.bfloat16
VMEM_BYTES = 60 * 2**20
SUM_ROWS = 16
BLOCK = 16
SUB = 8
TILE = 16
PARTS = (7, 5, 4, 3, 2, 1)
PATTERN = (0, 1, 2, 0, 1, 0, 1)


def dot(a, b):
    return jnp.dot(a, b, preferred_element_type=F32)


def dot_nt(a, b):
    return lax.dot_general(a, b, (((1,), (1,)), ((), ())), preferred_element_type=F32)


def norm_parts(values):
    centred = values - jnp.mean(values, axis=-1, keepdims=True)
    inverse = lax.rsqrt(jnp.mean(centred * centred, axis=-1, keepdims=True) + EPSILON)
    return centred * inverse, inverse


def norm_back(d_normed, hat, inverse, scale_by):
    d_hat = d_normed * (1.0 + scale_by)
    mean_d = jnp.mean(d_hat, axis=-1, keepdims=True)
    mean_dh = jnp.mean(d_hat * hat, axis=-1, keepdims=True)
    return inverse * (d_hat - mean_d - hat * mean_dh)


GELU_A = math.sqrt(2.0 / math.pi)
GELU_B = 0.044715


def gelu_parts(values):
    square = values * values
    bent = jnp.tanh(GELU_A * values * (1.0 + GELU_B * square))
    half = 0.5 * (1.0 + bent)
    slope = half + (0.5 * GELU_A) * values * (1.0 - bent * bent) * (1.0 + 3.0 * GELU_B * square)
    return values * half, slope


def row_sums(values):
    return jnp.sum(values, axis=0, keepdims=True)


def head_lanes(values, head):
    lane = lax.broadcasted_iota(jnp.int32, values.shape, 1)
    return jnp.where((lane >= HDIM) == (head % 2 == 1), values, jnp.zeros_like(values))


def pair_of(values, pair):
    return values[:, pair * LANES : (pair + 1) * LANES]


def head_rows(values, head):
    return values[head * HDIM : (head + 1) * HDIM, :]


def lone_rows(values, head):
    rows = head_rows(values, head)
    blank = jnp.zeros_like(rows)
    return jnp.concatenate([rows, blank] if head % 2 == 0 else [blank, rows], axis=0)


def attend(queries, keys, values_t, bias, keep_exponent):
    ones = jnp.ones((SUM_ROWS, values_t.shape[1]), BF)
    parts, inverses = [], []
    for head in range(HEADS):
        pair = head // 2
        scores = dot_nt(pair_of(keys, pair), head_lanes(pair_of(queries, pair), head))
        if bias is not None:
            scores = scores + bias
        largest = jnp.max(scores, axis=0, keepdims=True)
        exponent = jnp.exp(scores - largest).astype(BF)
        keep_exponent(head, exponent)
        lifted = jnp.concatenate([head_rows(values_t, head), ones], axis=0)
        summed = dot(lifted, exponent)
        inverse = 1.0 / summed[HDIM : HDIM + 1, :]
        parts.append(summed[:HDIM, :] * inverse)
        inverses.append(inverse)
    return jnp.concatenate(parts, axis=0), inverses


def attend_back(exponent_of, queries_of, keys_t_of, values_of, d_att_t, att_t, inverse_of, keys_chunk):
    n_keys, chunk = keys_chunk
    d_query_parts, d_key_pairs, d_value_pairs = [], [], []
    for pair in range(PAIRS):
        d_keys = [None] * (n_keys // chunk)
        d_values = [None] * (n_keys // chunk)
        for head in (2 * pair, 2 * pair + 1):
            inverse = inverse_of(head)
            d_att_head = head_rows(d_att_t, head)
            centre = row_sums(d_att_head * head_rows(att_t, head)) * inverse
            scaled = (d_att_head * inverse).astype(BF)
            blank = jnp.zeros_like(scaled)
            scaled_pair = jnp.concatenate([scaled, blank] if head % 2 == 0 else [blank, scaled], axis=0)
            query_pair = head_lanes(queries_of(pair), head)
            d_query = None
            for at in range(n_keys // chunk):
                rows = slice(at * chunk, (at + 1) * chunk)
                exponent = exponent_of(head, rows)
                d_chance = dot(values_of(pair, rows), scaled_pair)
                d_score = (exponent.astype(F32) * (d_chance - centre)).astype(BF)
                d_value = dot_nt(exponent, scaled_pair)
                d_key = dot(d_score, query_pair)
                part = dot(keys_t_of(head, rows), d_score)
                d_query = part if d_query is None else d_query + part
                d_keys[at] = d_key if d_keys[at] is None else d_keys[at] + d_key
                d_values[at] = d_value if d_values[at] is None else d_values[at] + d_value
            d_query_parts.append(d_query)
        d_key_pairs.append(jnp.concatenate(d_keys, axis=0))
        d_value_pairs.append(jnp.concatenate(d_values, axis=0))
    return (
        jnp.concatenate(d_query_parts, axis=0),
        jnp.concatenate(d_key_pairs, axis=1),
        jnp.concatenate(d_value_pairs, axis=1),
    )


def fold(ref):
    value = ref[...]
    return value.reshape(-1, value.shape[-1])


class Layout:
    def __init__(self, sizes, latents_shape):
        self.clips_dev, self.frames, self.patches, self.width = latents_shape
        self.n_ta, self.n_pa, self.n_dev = sizes["ta"], sizes["pa"], sizes["dev"]
        self.clips = self.clips_dev * self.n_dev
        self.run = self.n_pa // self.clips
        self.group = self.run * self.n_dev
        self.near = self.n_pa // self.group
        self.halves = self.n_ta // self.near
        self.space_rows = self.near * self.patches
        self.time_patches = self.space_rows // self.n_ta
        self.other_rows = (self.group - 1) * self.space_rows
        self.key_rows = self.group * self.space_rows
        self.all_frames = self.n_ta * self.frames

    def here(self):
        return {name: lax.axis_index(name) for name in ("ta", "pa", "dev")}

    def clip(self, me):
        return me["pa"] // self.run

    def member(self, me):
        return me["dev"] * self.run + me["pa"] % self.run

    def space_place(self, ta, clip, member):
        return {"ta": ta, "pa": clip * self.run + member % self.run, "dev": member // self.run}

    def space_target(self, me, j):
        return self.space_place(me["ta"], me["dev"] * self.clips_dev + j, me["pa"] // self.near)

    def owner(self, me, ta, slot):
        return {"ta": ta, "pa": self.near * self.member(me) + slot, "dev": self.clip(me) // self.clips_dev}

    def time_target(self, me, j, s):
        place = self.space_target(me, j)
        return {**place, "ta": (me["pa"] % self.near) * self.halves + s}

    def fellow(self, me, step):
        return self.space_place(me["ta"], self.clip(me), (self.member(me) + step) % self.group)

    def across(self, me, step):
        return {**me, "ta": (me["ta"] + step) % self.n_ta}


def is_me(me, place):
    same = None
    for name, index in place.items():
        if index is not me[name]:
            equal = index == me[name]
            same = equal if same is None else same & equal
    return same


def greet(me, place):
    @pl.when(jnp.logical_not(is_me(me, place)))
    def _():
        pl.semaphore_signal(
            pltpu.get_barrier_semaphore(), inc=1, device_id=place, device_id_type=pl.DeviceIdType.MESH
        )


def await_greetings(me, places):
    amount = jnp.int32(0)
    for place in places:
        amount = amount + jnp.logical_not(is_me(me, place)).astype(jnp.int32)
    pl.semaphore_wait(pltpu.get_barrier_semaphore(), amount)


def push(src, dst, send_sem, recv_sem, place):
    return pltpu.make_async_remote_copy(
        src_ref=src,
        dst_ref=dst,
        send_sem=send_sem,
        recv_sem=recv_sem,
        device_id=place,
        device_id_type=pl.DeviceIdType.MESH,
    )


def start_push(me, src, dst, send_sem, recv_sem, place):
    same = is_me(me, place)

    @pl.when(same)
    def _():
        pltpu.make_async_copy(src, dst, recv_sem).start()

    @pl.when(jnp.logical_not(same))
    def _():
        push(src, dst, send_sem, recv_sem, place).start()


def end_push(me, src, dst, send_sem, recv_sem, place):
    @pl.when(jnp.logical_not(is_me(me, place)))
    def _():
        push(src, dst, send_sem, recv_sem, place).wait_send()


def arrived(dst, recv_sem):
    pltpu.make_async_copy(dst, dst, recv_sem).wait()


def space_forward_kernel(
    lay,
    counts_ref,
    latents_ref,
    cot_ref,
    mod_ref,
    attn_ref,
    turned_ref,
    cross_ref,
    text_keys_ref,
    text_values_t_ref,
    up_ref,
    down_ref,
    state_ref,
    moved_ref,
    own_ref,
    normed_ref,
    query_ref,
    keys_t_ref,
    value_ref,
    exponent_ref,
    att_t_ref,
    att_ref,
    inverse_ref,
    cross_in_ref,
    cross_query_ref,
    cross_exponent_ref,
    cross_att_t_ref,
    cross_att_ref,
    cross_inverse_ref,
    middle_ref,
    normed2_ref,
    act_ref,
    slope_ref,
    branch2_ref,
    branch5_ref,
    own_buf,
    other_buf,
    sent_buf,
    lat_send,
    lat_recv,
    fellow_send,
    fellow_recv,
    state_send,
    state_recv,
    cot_send,
    cot_recv,
):
    scale_by = HDIM ** (-0.5)
    me = lay.here()
    step = pl.program_id(0)
    frames, near = lay.frames, lay.near
    last = step == frames - 1

    def latent_copy(j, f):
        slot = me["pa"] % near
        return (
            latents_ref.at[j, f], own_buf.at[f, slot], lat_send.at[j, f], lat_recv.at[f, slot], lay.space_target(me, j),
        )

    def fellow_copy(turn, f):
        return (
            own_buf.at[f], other_buf.at[f, turn - 1], fellow_send.at[turn - 1, f], fellow_recv.at[turn - 1, f],
            lay.fellow(me, turn),
        )

    def state_copy(turn, f):
        place = lay.across(me, turn)
        row = pl.multiple_of(place["ta"] * lay.time_patches, TILE)
        return (
            sent_buf.at[f, pl.ds(row, lay.time_patches)], state_ref.at[me["ta"] * frames + f], state_send.at[turn, f],
            state_recv.at[turn, f], place,
        )

    def cot_copy(j, s):
        return (
            cot_ref.at[j, :, pl.ds(s * lay.time_patches, lay.time_patches)],
            moved_ref.at[pl.ds(me["ta"] * frames, frames)],
            cot_send.at[j, s], cot_recv.at[me["ta"]], lay.time_target(me, j, s),
        )

    def start_latents(f):
        for j in range(lay.clips_dev):
            start_push(me, *latent_copy(j, f))

    def pass_on(f):
        for slot in range(near):
            arrived(own_buf.at[f, slot], lat_recv.at[f, slot])
        for turn in range(1, lay.group):
            push(*fellow_copy(turn, f)).start()

    @pl.when(step == 0)
    def _():
        for slot in range(near):
            greet(me, lay.owner(me, me["ta"], slot))
        for t in range(lay.n_ta):
            greet(me, lay.owner(me, t, me["ta"] // lay.halves))
        friends = [lay.fellow(me, turn) for turn in range(1, lay.group)]
        friends += [lay.across(me, turn) for turn in range(1, lay.n_ta)]
        for friend in friends:
            greet(me, friend)
        targets = [lay.space_target(me, j) for j in range(lay.clips_dev)]
        targets += [lay.time_target(me, j, s) for j in range(lay.clips_dev) for s in range(lay.halves)]
        await_greetings(me, targets + friends)
        start_latents(0)
        if frames > 1:
            start_latents(1)
        pass_on(0)

    @pl.when(step + 2 < frames)
    def _():
        start_latents(step + 2)

    @pl.when(step == min(1, frames - 1))
    def _():
        for j in range(lay.clips_dev):
            for s in range(lay.halves):
                start_push(me, *cot_copy(j, s))

    for turn in range(1, lay.group):
        arrived(other_buf.at[step, turn - 1], fellow_recv.at[turn - 1, step])
    frame = counts_ref[2] + step
    keep = (frame < counts_ref[0]).astype(F32)
    mod = mod_ref[...]
    own_low = own_buf[step].reshape(lay.space_rows, lay.width)
    own_ref[0] = own_low
    own = own_low.astype(F32)
    rows = lay.space_rows
    normed_own = (norm_parts(own)[0] * (1.0 + mod[1:2]) + mod[0:1]).astype(BF)
    other = other_buf[step].reshape(lay.other_rows, lay.width).astype(F32)
    normed_other = (norm_parts(other)[0] * (1.0 + mod[1:2]) + mod[0:1]).astype(BF)
    normed = jnp.concatenate([normed_own, normed_other], axis=0)
    normed_ref[0] = normed
    queries = (dot(normed_own, attn_ref[0]).astype(BF) * scale_by).astype(BF)
    keys = dot(normed, attn_ref[1]).astype(BF)
    values = dot(normed, attn_ref[2]).astype(BF)
    query_ref[0] = queries
    value_ref[0] = values
    keys_t_ref[0] = dot_nt(turned_ref[0], normed).astype(BF)
    values_t = dot_nt(turned_ref[1], normed).astype(BF)

    def keep_exponent(head, exponent):
        exponent_ref[0, head] = exponent

    att_t, inverses = attend(queries, keys, values_t, None, keep_exponent)
    for head in range(HEADS):
        inverse_ref[0, head : head + 1, :] = inverses[head]
    att_t_ref[0] = att_t.astype(BF)
    att = att_t.T.astype(BF)
    att_ref[0] = att

    @pl.when(jnp.logical_not(last))
    def _():
        pass_on(step + 1)

    branch = dot(att_ref[0], attn_ref[3])
    branch2_ref[0] = branch.astype(BF)
    state = own_ref[0].astype(F32) + (keep * mod[2:3]) * branch
    cross_in = state.astype(BF)
    cross_in_ref[0] = cross_in
    cross_queries = (dot(cross_in, cross_ref[0]).astype(BF) * scale_by).astype(BF)
    cross_query_ref[0] = cross_queries
    text_id = lax.broadcasted_iota(jnp.int32, (text_keys_ref.shape[0], rows), 0)
    bias = jnp.where(text_id < counts_ref[1], 0.0, MASKED_SCORE)

    def keep_cross(head, exponent):
        cross_exponent_ref[0, head] = exponent

    cross_t, inverses = attend(cross_queries, text_keys_ref[...], text_values_t_ref[...], bias, keep_cross)
    for head in range(HEADS):
        cross_inverse_ref[0, head : head + 1, :] = inverses[head]
    cross_att_t_ref[0] = cross_t.astype(BF)
    cross_att = cross_t.T.astype(BF)
    cross_att_ref[0] = cross_att
    state = state + keep * dot(cross_att, cross_ref[1])
    middle_ref[0] = state
    normed2 = (norm_parts(state)[0] * (1.0 + mod[4:5]) + mod[3:4]).astype(BF)
    normed2_ref[0] = normed2
    act, slope = gelu_parts(dot(normed2, up_ref[...]))
    act = act.astype(BF)
    act_ref[0] = act
    slope_ref[0] = slope.astype(BF)
    branch = dot(act, down_ref[...])
    branch5_ref[0] = branch.astype(BF)
    state = state + (keep * mod[5:6]) * branch
    sent_buf[step] = state.astype(BF)
    src, dst, _, sem, _ = state_copy(0, step)
    pltpu.make_async_copy(src, dst, sem).start()
    for turn in range(1, lay.n_ta):
        push(*state_copy(turn, step)).start()

    @pl.when(last)
    def _():
        for f in range(frames):
            for j in range(lay.clips_dev):
                end_push(me, *latent_copy(j, f))
            for turn in range(1, lay.group):
                push(*fellow_copy(turn, f)).wait_send()
            for turn in range(1, lay.n_ta):
                push(*state_copy(turn, f)).wait_send()
            for turn in range(lay.n_ta):
                src, dst, _, sem, _ = state_copy(turn, f)
                arrived(dst, sem)
        for j in range(lay.clips_dev):
            for s in range(lay.halves):
                end_push(me, *cot_copy(j, s))
        for t in range(lay.n_ta):
            arrived(moved_ref.at[pl.ds(t * frames, frames)], cot_recv.at[t])


def space_backward_kernel(
    first_frame,
    counts_ref,
    grad_ref,
    mod_ref,
    attn_ref,
    cross_ref,
    text_keys_t_ref,
    text_values_ref,
    up_ref,
    down_ref,
    query_ref,
    keys_t_ref,
    value_ref,
    exponent_ref,
    att_t_ref,
    inverse_ref,
    cross_query_ref,
    cross_exponent_ref,
    cross_att_t_ref,
    cross_inverse_ref,
    middle_ref,
    slope_ref,
    branch2_ref,
    branch5_ref,
    state_grad_ref,
    own_grad_ref,
    other_grad_ref,
    kept3_ref,
    d_lifted_ref,
    kept2_ref,
    d_cross_query_ref,
    kept1_ref,
    d_query_ref,
    d_key_ref,
    d_value_ref,
    d_text_keys_ref,
    d_text_values_ref,
    mods_ref,
):
    scale_by = HDIM ** (-0.5)
    frame = counts_ref[2] + first_frame + pl.program_id(0)
    keep = (frame < counts_ref[0]).astype(F32)
    mod = mod_ref[...]
    grad = fold(grad_ref).astype(F32)
    rows = grad.shape[0]
    kept = keep * grad
    d_gate5 = row_sums(kept * branch5_ref[0].astype(F32))
    d_branch = (kept * mod[5:6]).astype(BF)
    kept3_ref[0] = d_branch
    d_act = dot_nt(d_branch, down_ref[...])
    d_lifted = (d_act * slope_ref[0].astype(F32)).astype(BF)
    d_lifted_ref[0] = d_lifted
    d_normed = dot_nt(d_lifted, up_ref[...])
    hat, inverse = norm_parts(middle_ref[0])
    grad = grad + norm_back(d_normed, hat, inverse, mod[4:5])
    d_shift, d_scale = row_sums(d_normed), row_sums(d_normed * hat)
    kept = (keep * grad).astype(BF)
    kept2_ref[0] = kept
    d_att_t = dot_nt(cross_ref[1], kept)
    d_query_t, d_keys, d_values = attend_back(
        lambda head, at: cross_exponent_ref[0, head, at, :],
        lambda pair: cross_query_ref[0, :, pair * LANES : (pair + 1) * LANES],
        lambda head, at: text_keys_t_ref[head * HDIM : (head + 1) * HDIM, at],
        lambda pair, at: text_values_ref[at, pair * LANES : (pair + 1) * LANES],
        d_att_t,
        cross_att_t_ref[0].astype(F32),
        lambda head: cross_inverse_ref[0, head : head + 1, :],
        (text_values_ref.shape[0], text_values_ref.shape[0]),
    )
    d_text_keys_ref[0] = d_keys
    d_text_values_ref[0] = d_values
    d_query = (d_query_t.T * scale_by).astype(BF)
    d_cross_query_ref[0] = d_query
    grad = grad + dot_nt(d_query, cross_ref[0])
    state_grad_ref[0] = grad
    kept = keep * grad
    d_gate2 = row_sums(kept * branch2_ref[0].astype(F32))
    mods_ref[0] = jnp.concatenate(
        [jnp.zeros((2, hat.shape[1]), F32), d_gate2, d_shift, d_scale, d_gate5, jnp.zeros((2, hat.shape[1]), F32)],
        axis=0,
    )
    d_branch = (kept * mod[2:3]).astype(BF)
    kept1_ref[0] = d_branch
    d_att_t = dot_nt(attn_ref[3], d_branch)
    n_keys = value_ref.shape[1]
    d_query_t, d_keys, d_values = attend_back(
        lambda head, at: exponent_ref[0, head, at, :],
        lambda pair: query_ref[0, :, pair * LANES : (pair + 1) * LANES],
        lambda head, at: keys_t_ref[0, head * HDIM : (head + 1) * HDIM, at],
        lambda pair, at: value_ref[0, at, pair * LANES : (pair + 1) * LANES],
        d_att_t,
        att_t_ref[0].astype(F32),
        lambda head: inverse_ref[0, head : head + 1, :],
        (n_keys, min(n_keys, 256)),
    )
    d_query = (d_query_t.T * scale_by).astype(BF)
    d_keys, d_values = d_keys.astype(BF), d_values.astype(BF)
    d_query_ref[0] = d_query
    d_key_ref[0] = d_keys
    d_value_ref[0] = d_values
    d_normed = dot_nt(d_keys, attn_ref[1]) + dot_nt(d_values, attn_ref[2])
    own_grad_ref[0] = d_normed[:rows] + dot_nt(d_query, attn_ref[0])
    other_grad_ref[0] = d_normed[rows:].astype(BF)


def space_finish_kernel(n_parts, own_ref, state_grad_ref, own_grad_ref, *rest):
    parts, (mod_ref, out_ref, mods_ref) = rest[:n_parts], rest[n_parts:]
    d_normed = own_grad_ref[0]
    for part in parts:
        d_normed = d_normed + part[0].astype(F32)
    hat, inverse = norm_parts(fold(own_ref).astype(F32))
    grad = state_grad_ref[0] + norm_back(d_normed, hat, inverse, mod_ref[1:2, :])
    out_ref[...] = grad.astype(BF).reshape(out_ref.shape)
    mods_ref[0] = jnp.concatenate(
        [row_sums(d_normed), row_sums(d_normed * hat), jnp.zeros((6, hat.shape[1]), F32)], axis=0
    )


def time_kernel(
    counts_ref,
    state_ref,
    cot_ref,
    mod_ref,
    bias_ref,
    attn_ref,
    turned_ref,
    up_ref,
    down_ref,
    out_ref,
    grad_ref,
    normed_ref,
    d_qkv_ref,
    att_ref,
    branch4_ref,
    normed2_ref,
    act_ref,
    d_lifted_ref,
    branch5_ref,
    mods_ref,
    exponent_ref,
):
    scale_by = HDIM ** (-0.5)
    frames, block, width = state_ref.shape
    run_rows = frames * SUB
    runs = block // SUB
    mod = mod_ref[...]

    def load(ref):
        cube = ref[...].astype(F32)
        parts = [cube[:, r * SUB : (r + 1) * SUB].reshape(run_rows, width) for r in range(runs)]
        return jnp.concatenate(parts, axis=0)

    def store(ref, value):
        parts = [value[r * run_rows : (r + 1) * run_rows].reshape(frames, SUB, width) for r in range(runs)]
        ref[...] = jnp.concatenate(parts, axis=1).astype(ref.dtype)

    def run_of(value, r):
        return value[r * run_rows : (r + 1) * run_rows]

    state = load(state_ref)
    rows = state.shape[0]
    frame = (lax.broadcasted_iota(jnp.int32, (rows, 1), 0) // SUB) % frames
    keep = (frame < counts_ref[0]).astype(F32)
    hat1, inverse1 = norm_parts(state)
    normed = (hat1 * (1.0 + mod[1:2]) + mod[0:1]).astype(BF)
    normed_ref[0] = normed
    queries = (dot(normed, attn_ref[0]).astype(BF) * scale_by).astype(BF)
    keys = dot(normed, attn_ref[1]).astype(BF)
    values = dot(normed, attn_ref[2]).astype(BF)
    att_parts, att_t_parts, inverse_parts, keys_t_parts = [], [], [], []
    for r in range(runs):
        normed_run = run_of(normed, r)
        keys_t_parts.append(dot_nt(turned_ref[0], normed_run).astype(BF))
        values_t = dot_nt(turned_ref[1], normed_run).astype(BF)

        def keep_exponent(head, exponent):
            exponent_ref[r, head] = exponent

        att_t, inverses = attend(
            run_of(queries, r), run_of(keys, r), values_t, bias_ref[...], keep_exponent
        )
        att_t_parts.append(att_t)
        inverse_parts.append(inverses)
        att_parts.append(att_t.T.astype(BF))
    att = jnp.concatenate(att_parts, axis=0)
    att_ref[0] = att
    branch2 = dot(att, attn_ref[3])
    state = state + (keep * mod[2:3]) * branch2
    hat2, inverse2 = norm_parts(state)
    normed2 = (hat2 * (1.0 + mod[4:5]) + mod[3:4]).astype(BF)
    normed2_ref[0] = normed2
    act, slope = gelu_parts(dot(normed2, up_ref[...]))
    act = act.astype(BF)
    act_ref[0] = act
    branch5 = dot(act, down_ref[...])
    store(out_ref, state + (keep * mod[5:6]) * branch5)
    grad = load(cot_ref)
    kept = keep * grad
    d_gate5 = row_sums(kept * branch5)
    d_branch = (kept * mod[5:6]).astype(BF)
    branch5_ref[0] = d_branch
    d_act = dot_nt(d_branch, down_ref[...])
    d_lifted = (d_act * slope).astype(BF)
    d_lifted_ref[0] = d_lifted
    d_normed2 = dot_nt(d_lifted, up_ref[...])
    grad = grad + norm_back(d_normed2, hat2, inverse2, mod[4:5])
    kept = keep * grad
    d_gate2 = row_sums(kept * branch2)
    d_branch = (kept * mod[2:3]).astype(BF)
    branch4_ref[0] = d_branch
    d_query_parts, d_key_parts, d_value_parts = [], [], []
    for r in range(runs):
        d_att_t = dot_nt(attn_ref[3], run_of(d_branch, r))
        query_run, value_run = run_of(queries, r), run_of(values, r)
        d_query_t, d_keys, d_values = attend_back(
            lambda head, at: exponent_ref[r, head, at, :],
            lambda pair: pair_of(query_run, pair),
            lambda head, at: head_rows(keys_t_parts[r], head)[:, at],
            lambda pair, at: pair_of(value_run, pair)[at],
            d_att_t,
            att_t_parts[r],
            lambda head: inverse_parts[r][head],
            (run_rows, run_rows),
        )
        d_query_parts.append((d_query_t.T * scale_by).astype(BF))
        d_key_parts.append(d_keys.astype(BF))
        d_value_parts.append(d_values.astype(BF))
    d_qkv = [jnp.concatenate(parts, axis=0) for parts in (d_query_parts, d_key_parts, d_value_parts)]
    d_normed1 = None
    for i in range(3):
        d_qkv_ref[0, :, i * width : (i + 1) * width] = d_qkv[i]
        part = dot_nt(d_qkv[i], attn_ref[i])
        d_normed1 = part if d_normed1 is None else d_normed1 + part
    grad = grad + norm_back(d_normed1, hat1, inverse1, mod[1:2])
    store(grad_ref, grad)
    mods_ref[0] = jnp.concatenate(
        [
            row_sums(d_normed1),
            row_sums(d_normed1 * hat1),
            d_gate2,
            row_sums(d_normed2),
            row_sums(d_normed2 * hat2),
            d_gate5,
            jnp.zeros((2, width), F32),
        ],
        axis=0,
    )


class Reducer:
    def __init__(self, shapes, small_rows, sizes):
        self.width = width = shapes[0][1]
        self.shapes = shapes
        bits = {name: [(name, 1 << i) for i in range(sizes[name].bit_length() - 1)] for name in ("ta", "pa")}
        kinds = [bits["ta"] + bits["pa"], bits["ta"][::-1] + bits["pa"], bits["pa"] + bits["ta"]]
        self.ways = [("dev", 1)] + kinds[0]
        self.loads, row = [], 0
        for i, shape in enumerate(shapes):
            for column in range(shape[1] // width):
                self.loads.append((i, row, column * width, shape[0]))
                row += shape[0]
        self.total = row
        self.parts = next(n for n in PARTS if row % (2 * n * TILE) == 0)
        self.part_rows = row // 2 // self.parts
        self.half_rows = row // 2
        self.orders = [[("dev", 1)] + kinds[PATTERN[p % len(PATTERN)]] for p in range(self.parts)]
        self.steps = len(self.ways)
        self.small_rows = small_rows
        self.counts, self.halves, self.boxes, at = [self.part_rows], [True], [], 0
        for _ in range(1, self.steps):
            halve = (self.counts[-1] // 2) % TILE == 0
            self.halves.append(halve)
            self.counts.append(self.counts[-1] // 2 if halve else self.counts[-1])
        for p in range(self.parts):
            self.boxes.append([])
            for count in self.counts:
                self.boxes[p].append(at)
                at += count
        self.box_rows = at
        self.phases = 2 * self.steps + 1

    def scratch(self):
        shapes = [
            pltpu.VMEM((self.total, self.width), BF),
            pltpu.VMEM((self.total, self.width), BF),
            pltpu.VMEM((self.box_rows, self.width), BF),
            pltpu.SemaphoreType.DMA((len(self.loads),)),
            pltpu.SemaphoreType.DMA((self.parts, 2)),
            pltpu.SemaphoreType.DMA((self.parts, 2 * self.steps)),
            pltpu.SemaphoreType.DMA((self.parts, 2 * self.steps)),
        ]
        if self.small_rows:
            shapes += [
                pltpu.VMEM((self.steps, self.small_rows, self.width), F32),
                pltpu.SemaphoreType.DMA((self.steps,)),
                pltpu.SemaphoreType.DMA((self.steps,)),
            ]
        return shapes

    def bind(self, sources, out, scratch, small_in=None, small_out=None):
        self.sources, self.out = sources, out
        self.work, self.whole, self.inbox, self.in_sem, self.out_sem, self.send_sem, self.recv_sem = scratch[:7]
        self.small_in, self.small_out = small_in, small_out
        if self.small_rows:
            self.small_box, self.small_send, self.small_recv = scratch[7:]

    def bit(self, way):
        return (lax.axis_index(way[0]) // way[1]) % 2

    def peer(self, way):
        return {way[0]: lax.axis_index(way[0]) + way[1] - 2 * way[1] * self.bit(way)}

    def greet(self):
        barrier = pltpu.get_barrier_semaphore()
        for way in self.ways:
            pl.semaphore_signal(barrier, inc=1, device_id=self.peer(way), device_id_type=pl.DeviceIdType.MESH)
        return len(self.ways)

    def base(self, p, step):
        row = self.bit(self.orders[p][0]) * self.half_rows + p * self.part_rows
        for s in range(1, step + 1):
            if self.halves[s]:
                row = row + self.bit(self.orders[p][s]) * self.counts[s]
        return row

    def rows(self, ref, row, count):
        return ref.at[pl.ds(pl.multiple_of(row, TILE), count)]

    def load(self, i):
        source, row, column, rows = self.loads[i]
        view = self.sources[source].at[:, column : column + self.width]
        return pltpu.make_async_copy(view, self.work.at[row : row + rows], self.in_sem.at[i])

    def remote(self, src, dst, p, step, way):
        return pltpu.make_async_remote_copy(
            src_ref=src,
            dst_ref=dst,
            send_sem=self.send_sem.at[p, step],
            recv_sem=self.recv_sem.at[p, step],
            device_id=self.peer(way),
            device_id_type=pl.DeviceIdType.MESH,
        )

    def down(self, p, step):
        way, count = self.orders[p][step], self.counts[step]
        if step == 0:
            row = (1 - self.bit(way)) * self.half_rows + p * self.part_rows
        else:
            row = self.base(p, step - 1)
            if self.halves[step]:
                row = row + (1 - self.bit(way)) * count
        box = self.boxes[p][step]
        return self.remote(self.rows(self.work, row, count), self.inbox.at[box : box + count], p, step, way)

    def end_down(self, p, step):
        self.down(p, step).wait()
        count, base, box = self.counts[step], self.base(p, step), self.boxes[p][step]
        chunk = next(c for c in (96, 64, 48, 32, TILE) if count % c == 0)

        def body(i, carry):
            at = pl.ds(pl.multiple_of(base + i * chunk, TILE), chunk)
            got = self.inbox[pl.ds(pl.multiple_of(box + i * chunk, TILE), chunk), :]
            total = (self.work[at, :].astype(F32) + got.astype(F32)).astype(BF)
            if step == self.steps - 1:
                self.whole[at, :] = total
            else:
                self.work[at, :] = total
            return carry

        lax.fori_loop(0, count // chunk, body, 0)

    def up(self, p, turn):
        step = self.steps - 1 - turn
        if not self.halves[step]:
            return None
        rows = self.rows(self.whole, self.base(p, step), self.counts[step])
        return self.remote(rows, rows, p, self.steps + turn, self.orders[p][step])

    def store(self, p, side):
        rows = pl.ds(side * self.half_rows + p * self.part_rows, self.part_rows)
        return pltpu.make_async_copy(self.whole.at[rows], self.out.at[rows], self.out_sem.at[p, side])

    def small(self, step):
        return pltpu.make_async_remote_copy(
            src_ref=self.small_out,
            dst_ref=self.small_box.at[step],
            send_sem=self.small_send.at[step],
            recv_sem=self.small_recv.at[step],
            device_id=self.peer(self.ways[step]),
            device_id_type=pl.DeviceIdType.MESH,
        )

    def prepare(self):
        for i in range(len(self.loads)):
            self.load(i).start()
        if self.small_rows:
            self.small_out[...] = self.small_in[...]

    def phase(self, k):
        n = self.steps
        if k == 0:
            for i in range(len(self.loads)):
                self.load(i).wait()
        for p in range(self.parts):
            if 1 <= k <= n:
                self.end_down(p, k - 1)
            elif k > n:
                before = self.up(p, k - n - 1)
                if before is not None:
                    before.wait()
            if k < n:
                self.down(p, k).start()
            elif k < 2 * n:
                after = self.up(p, k - n)
                if after is not None:
                    after.start()
            else:
                self.store(p, 0).start()
                self.store(p, 1).start()
        if k == 2 * n:
            for p in range(self.parts):
                self.store(p, 0).wait()
                self.store(p, 1).wait()
        if self.small_rows and k <= n:
            if k > 0:
                self.small(k - 1).wait()
                self.small_out[...] = self.small_out[...] + self.small_box[k - 1]
            if k < n:
                self.small(k).start()

    def unpack(self, reduced):
        results, at = [], 0
        for rows, columns in self.shapes:
            turns = columns // self.width
            blocks = [reduced[at + i * rows : at + (i + 1) * rows] for i in range(turns)]
            at += turns * rows
            results.append((blocks[0] if turns == 1 else jnp.concatenate(blocks, axis=1)).astype(F32))
        return results


def reduce_all(arrays, small, sizes):
    reducer = Reducer([a.shape for a in arrays], small.shape[0], sizes)
    n = len(arrays)

    def kernel(*refs):
        reducer.bind(refs[:n], refs[n + 1], refs[n + 3 :], refs[n], refs[n + 2])
        reducer.prepare()
        pl.semaphore_wait(pltpu.get_barrier_semaphore(), reducer.greet())
        for k in range(reducer.phases):
            reducer.phase(k)

    any_spec, vmem_spec = pl.BlockSpec(memory_space=pl.ANY), pl.BlockSpec(memory_space=pltpu.VMEM)
    reduced, small_sum = pl.pallas_call(
        kernel,
        in_specs=[any_spec] * n + [vmem_spec],
        out_specs=[any_spec, vmem_spec],
        out_shape=[shape_of((reducer.total, reducer.width), BF), shape_of(small.shape, F32)],
        scratch_shapes=reducer.scratch(),
        compiler_params=pltpu.CompilerParams(collective_id=0, has_side_effects=True, vmem_limit_bytes=VMEM_BYTES),
        cost_estimate=pl.CostEstimate(
            flops=8 * reducer.total * reducer.width, bytes_accessed=4 * reducer.total * reducer.width, transcendentals=0
        ),
    )(*arrays, small)
    return reducer.unpack(reduced), small_sum


def whole(array):
    zeros = (0,) * array.ndim
    return pl.BlockSpec(array.shape, lambda *grid: zeros)


def framed(array):
    tail = (0,) * (array.ndim - 1)
    return pl.BlockSpec((1,) + tuple(array.shape[1:]), lambda frame: (frame,) + tail)


SCALARS = pl.BlockSpec(memory_space=pltpu.SMEM)
HBM = pl.BlockSpec(memory_space=pl.ANY)


def shape_of(shape, dtype):
    return jax.ShapeDtypeStruct(shape, dtype)


def call(kernel, grid, inputs, in_specs, outputs, out_specs, flops, scratch=(), collective_id=None):
    moved = sum(math.prod(a.shape) * a.dtype.itemsize for a in (*inputs, *outputs))
    return pl.pallas_call(
        kernel,
        grid=grid,
        in_specs=in_specs,
        out_specs=out_specs,
        out_shape=outputs,
        scratch_shapes=list(scratch),
        compiler_params=pltpu.CompilerParams(
            vmem_limit_bytes=VMEM_BYTES, collective_id=collective_id, has_side_effects=collective_id is not None
        ),
        cost_estimate=pl.CostEstimate(flops=int(flops), bytes_accessed=int(moved), transcendentals=0),
    )(*inputs)


def make_per_device(sizes):
    n_ta, n_pa, n_dev = sizes["ta"], sizes["pa"], sizes["dev"]

    def per_device(
        latents,
        context,
        cotangent,
        timesteps,
        frame_counts,
        text_lengths,
        step_proj,
        mod_table,
        patch_attn,
        cross_attn,
        patch_up,
        patch_down,
        frame_attn,
        frame_up,
        frame_down,
    ):
        lay = Layout(sizes, latents.shape)
        clips_dev, frames, patches, width = latents.shape
        clips, run, group, near, halves = lay.clips, lay.run, lay.group, lay.near, lay.halves
        space_rows, other_rows, key_rows = lay.space_rows, lay.other_rows, lay.key_rows
        time_patches, all_frames = lay.time_patches, lay.all_frames
        ta, pa, dev = (lax.axis_index(name) for name in ("ta", "pa", "dev"))
        clip, member = lay.clip(lay.here()), lay.member(lay.here())

        def place(clip_id, member_id):
            return (clip_id * run + member_id % run) * n_dev + member_id // run

        def space_pairs(step):
            pairs = []
            for p in range(n_pa):
                for d in range(n_dev):
                    k = d * clips_dev + (p + step) % clips_dev
                    pairs.append((p * n_dev + d, place(k, p // near)))
            return pairs

        def time_pairs(step):
            u, w = step % halves, step // halves
            pairs = []
            for t in range(n_ta):
                for p in range(n_pa):
                    for d in range(n_dev):
                        s = (t % halves + u) % halves
                        j = (t // halves + w) % clips_dev
                        k = d * clips_dev + j
                        pairs.append(
                            (
                                (t * n_pa + p) * n_dev + d,
                                ((p % near) * halves + s) * n_pa * n_dev + place(k, p // near),
                            )
                        )
            return pairs

        def back(pairs):
            return [(b, a) for a, b in pairs]

        def group_pairs(step):
            return [
                (place(k, g), place(k, (g + step) % group)) for k in range(clips) for g in range(group)
            ]

        def ta_pairs(step):
            return [(t, t ^ step) for t in range(n_ta)]

        whole_axes = ("ta", "pa", "dev")
        pair_axes = ("pa", "dev")

        def of_clip(local):
            both = lax.all_gather(local, "dev", axis=0, tiled=True)
            return lax.dynamic_index_in_dim(both, clip, 0, keepdims=False)

        def sinusoid(steps):
            half = step_proj.shape[0] // 2
            frequency = jnp.exp(-math.log(10000.0) * jnp.arange(half, dtype=F32) / half)
            angles = steps.astype(F32)[:, None] * frequency[None, :]
            return jnp.concatenate([jnp.cos(angles), jnp.sin(angles)], axis=1)

        numbers = lax.all_gather(jnp.stack([timesteps, frame_counts, text_lengths], axis=1), "dev", axis=0, tiled=True)
        own_numbers = lax.dynamic_index_in_dim(numbers, clip, 0, keepdims=False)
        embeddings = sinusoid(numbers[:, 0])
        embedding = lax.dynamic_index_in_dim(embeddings, clip, 0, keepdims=True)
        timing = jnp.dot(embedding, step_proj.astype(F32), precision=HIGHEST).reshape(6, width)
        table = mod_table.astype(F32)
        pad = jnp.zeros((2, width), F32)
        space_mod = jnp.concatenate([timing + table[0], pad])
        frame_mod = jnp.concatenate([timing + table[1], pad])
        counts = jnp.stack([own_numbers[1], own_numbers[2], ta * frames, 0]).astype(jnp.int32)
        text = of_clip(context)
        text_count = text.shape[0]
        text_rows = -(-text_count // LANES) * LANES
        text_wide = jnp.pad(text, ((0, text_rows - text_count), (0, 0)))
        text_keys = dot(text_wide, cross_attn[1]).astype(BF)
        text_values = dot(text_wide, cross_attn[2]).astype(BF)
        cross_ends = jnp.stack([cross_attn[0], cross_attn[3]])
        patch_turned = jnp.swapaxes(patch_attn[1:3], 1, 2)
        frame_turned = jnp.swapaxes(frame_attn[1:3], 1, 2)

        def out(*shape, dtype=BF):
            return shape_of((frames,) + shape, dtype)

        def moved_tokens():
            return shape_of((all_frames, time_patches, width), BF)

        hidden = patch_up.shape[1]
        inputs = (
            counts, latents, cotangent, space_mod, patch_attn, patch_turned, cross_ends, text_keys, text_values.T,
            patch_up, patch_down,
        )
        outputs = (
            moved_tokens(),
            moved_tokens(),
            out(space_rows, width),
            out(key_rows, width),
            out(space_rows, width),
            out(width, key_rows),
            out(key_rows, width),
            out(HEADS, key_rows, space_rows),
            out(width, space_rows),
            out(space_rows, width),
            out(8, space_rows, dtype=F32),
            out(space_rows, width),
            out(space_rows, width),
            out(HEADS, text_rows, space_rows),
            out(width, space_rows),
            out(space_rows, width),
            out(8, space_rows, dtype=F32),
            out(space_rows, width, dtype=F32),
            out(space_rows, width),
            out(space_rows, hidden),
            out(space_rows, hidden),
            out(space_rows, width),
            out(space_rows, width),
        )
        dense = 2 * frames * space_rows * width * (6 * width + 2 * hidden) + 8 * frames * key_rows * width * width
        dma = pltpu.SemaphoreType.DMA
        state, cot, *saved = call(
            lambda *refs: space_forward_kernel(lay, *refs),
            (frames,),
            inputs,
            [SCALARS, HBM, HBM] + [whole(a) for a in inputs[3:]],
            outputs,
            [HBM, HBM] + [framed(a) for a in outputs[2:]],
            dense + 16 * frames * space_rows * key_rows * width,
            [
                pltpu.VMEM((frames, near, patches, width), BF),
                pltpu.VMEM((frames, group - 1, near, patches, width), BF),
                pltpu.VMEM((frames, space_rows, width), BF),
                dma((clips_dev, frames)),
                dma((frames, near)),
                dma((group - 1, frames)),
                dma((group - 1, frames)),
                dma((n_ta, frames)),
                dma((n_ta, frames)),
                dma((clips_dev, halves)),
                dma((n_ta,)),
            ],
            collective_id=1,
        )

        def space_backward(frame_ids, grad, saved):
            count = len(frame_ids)

            def out(*shape, dtype=BF):
                return shape_of((count,) + shape, dtype)

            (_, _, query, keys_t, value, exponent, att_t, _, inverse, _, cross_query, cross_exponent, cross_att_t, _,
             cross_inverse, middle, _, _, slope, branch2, branch5) = saved
            start = frame_ids[0]

            def framed_from(array):
                tail = (0,) * (array.ndim - 1)
                return pl.BlockSpec((1,) + tuple(array.shape[1:]), lambda frame: (frame + start,) + tail)

            inputs = (
                counts, grad, space_mod, patch_attn, cross_ends, text_keys.T, text_values, patch_up, patch_down,
                query, keys_t, value, exponent, att_t, inverse, cross_query, cross_exponent, cross_att_t,
                cross_inverse, middle, slope, branch2, branch5,
            )
            hidden = patch_up.shape[1]
            outputs = (
                out(space_rows, width, dtype=F32),
                out(space_rows, width, dtype=F32),
                out(other_rows, width),
                out(space_rows, width),
                out(space_rows, hidden),
                out(space_rows, width),
                out(space_rows, width),
                out(space_rows, width),
                out(space_rows, width),
                out(key_rows, width),
                out(key_rows, width),
                out(text_rows, width, dtype=F32),
                out(text_rows, width, dtype=F32),
                out(8, width, dtype=F32),
            )
            grad_spec = pl.BlockSpec((n_ta, 1, time_patches, width), lambda frame: (0, frame, 0, 0))
            dense = 2 * count * space_rows * width * (6 * width + 2 * hidden) + 8 * count * key_rows * width * width
            return call(
                lambda *refs: space_backward_kernel(frame_ids[0], *refs),
                (count,),
                inputs,
                [SCALARS, grad_spec] + [whole(a) for a in inputs[2:9]] + [framed_from(a) for a in inputs[9:]],
                outputs,
                [framed(a) for a in outputs],
                dense + 32 * count * space_rows * key_rows * width,
            )

        def space_finish(own, state_grad, own_grad, parts):
            count = own.shape[0]
            inputs = (own, state_grad, own_grad, *parts, space_mod)
            outputs = (
                shape_of((count, near, patches, width), BF),
                shape_of((count, 8, width), F32),
            )
            return call(
                lambda *refs: space_finish_kernel(len(parts), *refs),
                (count,),
                inputs,
                [framed(a) for a in inputs[:-1]] + [whole(space_mod)],
                outputs,
                [framed(a) for a in outputs],
                count * space_rows * width * 30,
            )

        frame_groups = [ids for ids in (tuple(range(min(2, frames))), tuple(range(min(2, frames), frames))) if ids]
        slot = ta % halves
        n_steps = halves * clips_dev

        def exchange(pieces):
            got = [lax.dynamic_index_in_dim(pieces, ta, 0, keepdims=False)]
            for step in range(1, n_ta):
                sent = lax.dynamic_index_in_dim(pieces, ta ^ step, 0, keepdims=False)
                got.append(lax.ppermute(sent, "ta", ta_pairs(step)))
            stacked = jnp.stack(got)
            return jnp.stack(
                [lax.dynamic_index_in_dim(stacked, ta ^ t, 0, keepdims=False) for t in range(n_ta)]
            )

        block_rows = all_frames * BLOCK
        run_rows = all_frames * SUB
        ids = jnp.arange(run_rows, dtype=jnp.int32)
        same = (ids[:, None] % SUB == ids[None, :] % SUB) & (ids[:, None] // SUB < counts[0])
        bias = jnp.where(same, 0.0, MASKED_SCORE).astype(F32)
        hidden = frame_up.shape[1]
        n_blocks = time_patches // BLOCK

        def tokens(features):
            return shape_of((n_blocks, block_rows, features), BF)

        time_inputs = (counts, state, cot, frame_mod, bias, frame_attn, frame_turned, frame_up, frame_down)
        time_outputs = (
            shape_of((all_frames, time_patches, width), BF),
            shape_of((all_frames, time_patches, width), BF),
            tokens(width),
            tokens(3 * width),
            tokens(width),
            tokens(width),
            tokens(width),
            tokens(hidden),
            tokens(hidden),
            tokens(width),
            shape_of((n_blocks, 8, width), F32),
        )

        def blocked(array):
            return pl.BlockSpec((all_frames, BLOCK, array.shape[2]), lambda at: (0, at, 0))

        (out_t, grad_t, normed_t, d_qkv_t, att_tt, branch4, normed4, act4, d_lifted4, branch5, frame_six) = call(
            time_kernel,
            (n_blocks,),
            time_inputs,
            [SCALARS, blocked(state), blocked(cot)] + [whole(a) for a in time_inputs[3:]],
            time_outputs,
            [blocked(a) for a in time_outputs[:2]] + [framed(a) for a in time_outputs[2:]],
            all_frames * time_patches * width * (24 * width + 12 * hidden),
            [pltpu.VMEM((BLOCK // SUB, HEADS, run_rows, run_rows), BF)],
        )

        grad_s = exchange(grad_t.reshape(n_ta, frames, time_patches, width))

        out_t, grad_s = lax.optimization_barrier((out_t, grad_s))
        out_pieces = out_t.reshape(n_ta, frames, time_patches, width)
        out_parts = []
        for step in range(n_steps):
            u, w = step % halves, step // halves
            source = (slot - u) % halves + halves * ((clip % clips_dev - w) % clips_dev)
            sent = lax.dynamic_index_in_dim(out_pieces, source, 0, keepdims=False)
            out_parts.append(lax.ppermute(sent, whole_axes, back(time_pairs(step))))
        out_stack = jnp.stack(out_parts)
        rows = []
        for j in range(clips_dev):
            runs = []
            for s in range(halves):
                step = ((j - ta // halves) % clips_dev) * halves + (s - ta % halves) % halves
                runs.append(lax.dynamic_index_in_dim(out_stack, step, 0, keepdims=False))
            rows.append(jnp.concatenate(runs, axis=1))
        output = jnp.stack(rows)

        def weight_grad(left, right):
            left, right = left.reshape(-1, left.shape[-1]), right.reshape(-1, right.shape[-1])
            return lax.dot_general(left, right, (((0,), (0,)), ((), ())), preferred_element_type=F32).astype(BF)

        d_frame_qkv = weight_grad(normed_t, d_qkv_t)
        d_frame_proj = weight_grad(att_tt, branch4)
        d_frame_up = weight_grad(normed4, d_lifted4)
        d_frame_down = weight_grad(act4, branch5)

        pieces, backs, finish_six = [], [], []
        for i, frame_ids in enumerate(frame_groups):
            own = saved[0][frame_ids[0] : frame_ids[-1] + 1]
            grad = grad_s[:, frame_ids[0] : frame_ids[-1] + 1]
            if i == 1:
                grad, output = lax.optimization_barrier((grad, output))
            backed = space_backward(frame_ids, grad, saved)
            backs.append(backed)
            other_grad = backed[2]
            parts = []
            for step in range(1, group):
                sent = other_grad[:, (step - 1) * space_rows : step * space_rows]
                parts.append(lax.ppermute(sent, pair_axes, back(group_pairs(step))))
            done, mods = space_finish(own, backed[0], backed[1], parts)
            finish_six.append(mods)
            got = []
            for step in range(clips_dev):
                b = (clip - step) % clips_dev
                sent = lax.dynamic_index_in_dim(done, b, 1, keepdims=False)
                got.append(lax.ppermute(sent, pair_axes, back(space_pairs(step))))
            stacked = jnp.stack(got)
            pieces.append(
                jnp.stack(
                    [
                        lax.dynamic_index_in_dim(stacked, (j - pa) % clips_dev, 0, keepdims=False)
                        for j in range(clips_dev)
                    ]
                )
            )
        latents_grad = jnp.concatenate(pieces, axis=1).astype(F32)

        def over_frames(lists, index):
            picked = [entry[index] for entry in lists]
            return picked[0] if len(picked) == 1 else jnp.concatenate(picked)

        def grad_over(lists, index, others, other_index):
            total = None
            for ids, two in zip(frame_groups, others):
                left, right = lists[index][ids[0] : ids[-1] + 1], two[other_index]
                left, right = left.reshape(-1, left.shape[-1]), right.reshape(-1, right.shape[-1])
                part = lax.dot_general(left, right, (((0,), (0,)), ((), ())), preferred_element_type=F32)
                total = part if total is None else total + part
            return total.astype(BF)

        d_patch_up = grad_over(saved, 16, backs, 4)
        d_patch_down = grad_over(saved, 17, backs, 3)
        d_cross_proj = grad_over(saved, 13, backs, 5)
        d_cross_q = grad_over(saved, 9, backs, 6)
        text_t = text.astype(F32).T
        d_tk, d_tv = (over_frames(backs, i) for i in (11, 12))
        d_cross_k = jnp.dot(text_t, jnp.sum(d_tk, axis=0)[:text_count], precision=HIGHEST).astype(BF)
        d_cross_v = jnp.dot(text_t, jnp.sum(d_tv, axis=0)[:text_count], precision=HIGHEST).astype(BF)
        d_patch_proj = grad_over(saved, 7, backs, 7)
        d_patch_q = grad_over([saved[1][:, :space_rows]], 0, backs, 8)
        d_patch_k = grad_over(saved, 1, backs, 9)
        d_patch_v = grad_over(saved, 1, backs, 10)
        six = jnp.sum(over_frames(backs, 13), axis=0) + jnp.sum(jnp.concatenate(finish_six), axis=0)
        mine = jnp.stack([six, jnp.sum(frame_six, axis=0)])
        spread = jnp.where(jnp.arange(clips)[:, None, None, None] == clip, mine[None], 0.0)
        arrays = [
            d_patch_q, d_patch_k, d_patch_v, d_patch_proj, d_cross_q, d_cross_k, d_cross_v, d_cross_proj,
            d_patch_up, d_patch_down, d_frame_qkv, d_frame_proj, d_frame_up, d_frame_down,
        ]
        results, by_clip = reduce_all(arrays, spread.reshape(-1, width), sizes)
        by_clip = by_clip.reshape(clips, 2, 8, width)[:, :, :6]
        d_patch_attn = jnp.stack(results[0:4])
        d_cross = jnp.stack(results[4:8])
        d_patch_up, d_patch_down = results[8:10]
        d_frame_qkv = results[10].reshape(width, 3, width).swapaxes(0, 1)
        d_frame_attn = jnp.concatenate([d_frame_qkv, results[11][None]])
        d_frame_up, d_frame_down = results[12:14]
        d_table = jnp.sum(by_clip, axis=0)
        d_step = lax.dot_general(
            embeddings,
            jnp.sum(by_clip, axis=1).reshape(clips, -1),
            (((0,), (0,)), ((), ())),
            precision=HIGHEST,
        )
        return (
            output,
            latents_grad,
            d_step,
            d_table,
            d_patch_attn,
            d_cross,
            d_patch_up,
            d_patch_down,
            d_frame_attn,
            d_frame_up,
            d_frame_down,
        )

    return per_device


def solution(mesh):
    sizes = dict(mesh.shape)
    tokens = P("dev", "ta", "pa", None)
    in_specs = (tokens, P("dev", None, None), tokens, P("dev"), P("dev"), P("dev")) + (P(),) * 9
    out_specs = (tokens, tokens) + (P(),) * 9
    return jax.shard_map(
        make_per_device(sizes),
        mesh=mesh,
        in_specs=in_specs,
        out_specs=out_specs,
        check_vma=False,
    )
```

```python
import math

import jax
import jax.numpy as jnp
from jax import lax
from jax.experimental import pallas as pl
from jax.experimental.pallas import tpu as pltpu
from jax.sharding import PartitionSpec as P

HEADS = 6
HDIM = 64
PAIRS = HEADS // 2
LANES = 2 * HDIM
EPSILON = 1e-06
MASKED_SCORE = -1e30
HIGHEST = lax.Precision.HIGHEST
F32 = jnp.float32
BF = jnp.bfloat16
VMEM_BYTES = 60 * 2**20
SUM_ROWS = 16
BLOCK = 32
STREAM_RUNS = 2
TIME_LAG = 1
SUB = 8
TILE = 16
TIME_STAGE = 8
SPACE_STAGE = 1
BACK_STAGE = 1
CROSS_AHEAD = 2
SPAN = 512
KEY_CHUNK = 256
PARTS = (7, 5, 4, 3, 2, 1)
PATTERN = (0, 1, 2, 0, 1, 0, 1)


def dot(a, b):
    return jnp.dot(a, b, preferred_element_type=F32)


def dot_nt(a, b):
    return lax.dot_general(a, b, (((1,), (1,)), ((), ())), preferred_element_type=F32)


def norm_parts(values):
    centred = values - jnp.mean(values, axis=-1, keepdims=True)
    inverse = lax.rsqrt(jnp.mean(centred * centred, axis=-1, keepdims=True) + EPSILON)
    return centred * inverse, inverse


def norm_back(d_normed, hat, inverse, scale_by):
    d_hat = d_normed * (1.0 + scale_by)
    mean_d = jnp.mean(d_hat, axis=-1, keepdims=True)
    mean_dh = jnp.mean(d_hat * hat, axis=-1, keepdims=True)
    return inverse * (d_hat - mean_d - hat * mean_dh)


GELU_A = math.sqrt(2.0 / math.pi)
GELU_B = 0.044715


def gelu_parts(values):
    square = values * values
    bent = jnp.tanh(GELU_A * values * (1.0 + GELU_B * square))
    half = 0.5 * (1.0 + bent)
    slope = half + (0.5 * GELU_A) * values * (1.0 - bent * bent) * (1.0 + 3.0 * GELU_B * square)
    return values * half, slope


def row_sums(values):
    return jnp.sum(values, axis=0, keepdims=True)


def head_lanes(values, head):
    lane = lax.broadcasted_iota(jnp.int32, values.shape, 1)
    return jnp.where((lane >= HDIM) == (head % 2 == 1), values, jnp.zeros_like(values))


def pair_of(values, pair):
    return values[:, pair * LANES : (pair + 1) * LANES]


def head_rows(values, head):
    return values[head * HDIM : (head + 1) * HDIM, :]


def lone_rows(values, head):
    rows = head_rows(values, head)
    blank = jnp.zeros_like(rows)
    return jnp.concatenate([rows, blank] if head % 2 == 0 else [blank, rows], axis=0)


def spans(count, size):
    return [slice(at, min(at + size, count)) for at in range(0, count, size)]


def attend(jobs, ahead, keep_exponent):
    units = [
        (i, head, span) for i, job in enumerate(jobs) for head in range(HEADS) for span in spans(job[0].shape[0], SPAN)
    ]
    scores, tops, sums, inverses = {}, {}, {}, {}

    def score(unit, keys_span):
        i, head, span = unit
        queries, keys, _, bias = jobs[i]
        lone = head_lanes(pair_of(queries, head // 2)[span], head)
        value = dot_nt(pair_of(keys, head // 2)[keys_span], lone)
        if bias is not None:
            value = value + bias[keys_span, span]
        scores.setdefault((i, head, span.start), []).append(value)
        top = jnp.max(value, axis=0, keepdims=True)
        old = tops.get((i, head, span.start))
        tops[i, head, span.start] = top if old is None else jnp.maximum(old, top)

    def weigh(unit, index, keys_span):
        i, head, span = unit
        name = (i, head, span.start)
        exponent = jnp.exp(scores[name][index] - tops[name]).astype(BF)
        scores[name][index] = None
        keep_exponent(i, head, keys_span, span, exponent)
        values_t = jobs[i][2]
        count = keys_span.stop - keys_span.start
        lifted = jnp.concatenate([head_rows(values_t, head)[:, keys_span], jnp.ones((SUM_ROWS, count), BF)], axis=0)
        part = dot(lifted, exponent)
        sums[name] = part if name not in sums else sums[name] + part

    def finish(unit):
        i, head, span = unit
        name = (i, head, span.start)
        total = sums[name]
        inverse = 1.0 / total[HDIM : HDIM + 1, :]
        sums[name] = total[:HDIM, :] * inverse
        inverses[name] = inverse

    for turn in range(len(units) + ahead):
        later = units[turn] if turn < len(units) else None
        now = units[turn - ahead] if turn >= ahead else None
        later_spans = spans(jobs[later[0]][1].shape[0], SPAN) if later else []
        now_spans = spans(jobs[now[0]][1].shape[0], SPAN) if now else []
        for index in range(max(len(later_spans), len(now_spans))):
            if index < len(later_spans):
                score(later, later_spans[index])
            if index < len(now_spans):
                weigh(now, index, now_spans[index])
        if now:
            finish(now)

    def joined(parts, i, head):
        starts = [span.start for span in spans(jobs[i][0].shape[0], SPAN)]
        return jnp.concatenate([parts[i, head, start] for start in starts], axis=1)

    return (
        [jnp.concatenate([joined(sums, i, head) for head in range(HEADS)], axis=0) for i in range(len(jobs))],
        [[joined(inverses, i, head) for head in range(HEADS)] for i in range(len(jobs))],
    )


def added(total, part):
    return part if total is None else total + part


def attend_back(jobs, ahead, chunk):
    scaled, centres = {}, {}
    for i, (_, _, _, _, d_att_t, att_t, inverse_of, _) in enumerate(jobs):
        for head in range(HEADS):
            inverse = inverse_of(head)
            d_att_head = head_rows(d_att_t, head)
            centres[i, head] = row_sums(d_att_head * head_rows(att_t, head)) * inverse
            part = (d_att_head * inverse).astype(BF)
            blank = jnp.zeros_like(part)
            scaled[i, head] = jnp.concatenate([part, blank] if head % 2 == 0 else [blank, part], axis=0)
    units = [
        (i, head, rows) for i, job in enumerate(jobs) for head in range(HEADS) for rows in spans(job[7], chunk)
    ]
    d_queries, d_keys, d_values, chances = {}, {}, {}, {}
    for turn in range(len(units) + ahead):
        if turn < len(units):
            i, head, rows = units[turn]
            chances[turn] = dot(jobs[i][3](head // 2, rows), scaled[i, head])
        if turn < ahead:
            continue
        i, head, rows = units[turn - ahead]
        key = (i, head // 2, rows.start)
        exponent = jobs[i][0](head, rows)
        chance = chances.pop(turn - ahead)
        d_values[key] = added(d_values.get(key), dot_nt(exponent, scaled[i, head]))
        score = (exponent.astype(F32) * (chance - centres[i, head])).astype(BF)
        d_keys[key] = added(d_keys.get(key), dot(score, head_lanes(jobs[i][1](head // 2), head)))
        d_queries[i, head] = added(d_queries.get((i, head)), dot(jobs[i][2](head, rows), score))
    results = []
    for i, job in enumerate(jobs):
        starts = [rows.start for rows in spans(job[7], chunk)]
        joined = [
            jnp.concatenate(
                [jnp.concatenate([parts[i, pair, at] for at in starts], axis=0) for pair in range(PAIRS)], axis=1
            )
            for parts in (d_keys, d_values)
        ]
        results.append((jnp.concatenate([d_queries[i, head] for head in range(HEADS)], axis=0), *joined))
    return results


def fold(ref):
    value = ref[...]
    return value.reshape(-1, value.shape[-1])


class Layout:
    def __init__(self, sizes, latents_shape):
        self.clips_dev, self.frames, self.patches, self.width = latents_shape
        self.n_ta, self.n_pa, self.n_dev = sizes["ta"], sizes["pa"], sizes["dev"]
        self.clips = self.clips_dev * self.n_dev
        self.run = self.n_pa // self.clips
        self.group = self.run * self.n_dev
        self.near = self.n_pa // self.group
        self.halves = self.n_ta // self.near
        self.space_rows = self.near * self.patches
        self.time_patches = self.space_rows // self.n_ta
        self.other_rows = (self.group - 1) * self.space_rows
        self.key_rows = self.group * self.space_rows
        self.all_frames = self.n_ta * self.frames

    def here(self):
        return {name: lax.axis_index(name) for name in ("ta", "pa", "dev")}

    def clip(self, me):
        return me["pa"] // self.run

    def member(self, me):
        return me["dev"] * self.run + me["pa"] % self.run

    def space_place(self, ta, clip, member):
        return {"ta": ta, "pa": clip * self.run + member % self.run, "dev": member // self.run}

    def space_target(self, me, j):
        return self.space_place(me["ta"], me["dev"] * self.clips_dev + j, me["pa"] // self.near)

    def owner(self, me, ta, slot):
        return {"ta": ta, "pa": self.near * self.member(me) + slot, "dev": self.clip(me) // self.clips_dev}

    def time_target(self, me, j, s):
        place = self.space_target(me, j)
        return {**place, "ta": (me["pa"] % self.near) * self.halves + s}

    def fellow(self, me, step):
        return self.space_place(me["ta"], self.clip(me), (self.member(me) + step) % self.group)

    def across(self, me, step):
        return {**me, "ta": (me["ta"] + step) % self.n_ta}


def is_me(me, place):
    same = None
    for name, index in place.items():
        if index is not me[name]:
            equal = index == me[name]
            same = equal if same is None else same & equal
    return same


def greet(me, place):
    @pl.when(jnp.logical_not(is_me(me, place)))
    def _():
        pl.semaphore_signal(
            pltpu.get_barrier_semaphore(), inc=1, device_id=place, device_id_type=pl.DeviceIdType.MESH
        )


def await_greetings(me, places):
    amount = jnp.int32(0)
    for place in places:
        amount = amount + jnp.logical_not(is_me(me, place)).astype(jnp.int32)
    pl.semaphore_wait(pltpu.get_barrier_semaphore(), amount)


def push(src, dst, send_sem, recv_sem, place):
    return pltpu.make_async_remote_copy(
        src_ref=src,
        dst_ref=dst,
        send_sem=send_sem,
        recv_sem=recv_sem,
        device_id=place,
        device_id_type=pl.DeviceIdType.MESH,
    )


def start_push(me, src, dst, send_sem, recv_sem, place):
    same = is_me(me, place)

    @pl.when(same)
    def _():
        pltpu.make_async_copy(src, dst, recv_sem).start()

    @pl.when(jnp.logical_not(same))
    def _():
        push(src, dst, send_sem, recv_sem, place).start()


def end_push(me, src, dst, send_sem, recv_sem, place):
    @pl.when(jnp.logical_not(is_me(me, place)))
    def _():
        push(src, dst, send_sem, recv_sem, place).wait_send()


def arrived(dst, recv_sem):
    pltpu.make_async_copy(dst, dst, recv_sem).wait()


def space_forward_kernel(
    lay,
    counts_ref,
    latents_ref,
    cot_ref,
    mod_ref,
    attn_ref,
    turned_ref,
    cross_ref,
    text_keys_ref,
    text_values_t_ref,
    up_ref,
    down_ref,
    state_ref,
    moved_ref,
    own_ref,
    normed_ref,
    query_ref,
    keys_t_ref,
    value_ref,
    exponent_ref,
    att_t_ref,
    att_ref,
    inverse_ref,
    cross_in_ref,
    cross_query_ref,
    cross_exponent_ref,
    cross_att_t_ref,
    cross_att_ref,
    cross_inverse_ref,
    middle_ref,
    normed2_ref,
    act_ref,
    slope_ref,
    branch2_ref,
    branch5_ref,
    own_buf,
    other_buf,
    sent_buf,
    lat_send,
    lat_recv,
    fellow_send,
    fellow_recv,
    state_send,
    state_recv,
    cot_send,
    cot_recv,
):
    scale_by = HDIM ** (-0.5)
    me = lay.here()
    step = pl.program_id(0)
    frames, near = lay.frames, lay.near
    last = step == frames - 1

    def latent_copy(j, f):
        slot = me["pa"] % near
        return (
            latents_ref.at[j, f], own_buf.at[f, slot], lat_send.at[j, f], lat_recv.at[f, slot], lay.space_target(me, j),
        )

    def fellow_copy(turn, f):
        return (
            own_buf.at[f], other_buf.at[f, turn - 1], fellow_send.at[turn - 1, f], fellow_recv.at[turn - 1, f],
            lay.fellow(me, turn),
        )

    def state_copy(turn, f):
        place = lay.across(me, turn)
        row = pl.multiple_of(place["ta"] * lay.time_patches, TILE)
        return (
            sent_buf.at[f, pl.ds(row, lay.time_patches)], state_ref.at[me["ta"] * frames + f], state_send.at[turn, f],
            state_recv.at[turn, f], place,
        )

    def cot_copy(j, s):
        return (
            cot_ref.at[j, :, pl.ds(s * lay.time_patches, lay.time_patches)],
            moved_ref.at[pl.ds(me["ta"] * frames, frames)],
            cot_send.at[j, s], cot_recv.at[me["ta"]], lay.time_target(me, j, s),
        )

    def start_latents(f):
        for j in range(lay.clips_dev):
            start_push(me, *latent_copy(j, f))

    def pass_on(f):
        for slot in range(near):
            arrived(own_buf.at[f, slot], lat_recv.at[f, slot])
        for turn in range(1, lay.group):
            push(*fellow_copy(turn, f)).start()

    @pl.when(step == 0)
    def _():
        for slot in range(near):
            greet(me, lay.owner(me, me["ta"], slot))
        for t in range(lay.n_ta):
            greet(me, lay.owner(me, t, me["ta"] // lay.halves))
        friends = [lay.fellow(me, turn) for turn in range(1, lay.group)]
        friends += [lay.across(me, turn) for turn in range(1, lay.n_ta)]
        for friend in friends:
            greet(me, friend)
        targets = [lay.space_target(me, j) for j in range(lay.clips_dev)]
        targets += [lay.time_target(me, j, s) for j in range(lay.clips_dev) for s in range(lay.halves)]
        await_greetings(me, targets + friends)
        for f in range(frames):
            start_latents(f)
        pass_on(0)

    @pl.when(step == min(2, frames - 1))
    def _():
        for j in range(lay.clips_dev):
            for s in range(lay.halves):
                start_push(me, *cot_copy(j, s))

    for turn in range(1, lay.group):
        arrived(other_buf.at[step, turn - 1], fellow_recv.at[turn - 1, step])
    frame = counts_ref[2] + step
    keep = (frame < counts_ref[0]).astype(F32)
    mod = mod_ref[...]
    own_low = own_buf[step].reshape(lay.space_rows, lay.width)
    own_ref[0] = own_low
    own = own_low.astype(F32)
    rows = lay.space_rows
    normed_own = (norm_parts(own)[0] * (1.0 + mod[1:2]) + mod[0:1]).astype(BF)
    other = other_buf[step].reshape(lay.other_rows, lay.width).astype(F32)
    normed_other = (norm_parts(other)[0] * (1.0 + mod[1:2]) + mod[0:1]).astype(BF)
    normed = jnp.concatenate([normed_own, normed_other], axis=0)
    normed_ref[0] = normed
    queries = (dot(normed_own, attn_ref[0]).astype(BF) * scale_by).astype(BF)
    keys = dot(normed, attn_ref[1]).astype(BF)
    values = dot(normed, attn_ref[2]).astype(BF)
    query_ref[0] = queries
    value_ref[0] = values
    keys_t_ref[0] = dot_nt(turned_ref[0], normed).astype(BF)
    values_t = dot_nt(turned_ref[1], normed).astype(BF)

    def keep_exponent(_, head, keys_span, span, exponent):
        exponent_ref[0, head, keys_span, span] = exponent

    (att_t,), (inverses,) = attend([(queries, keys, values_t, None)], SPACE_STAGE, keep_exponent)
    for head in range(HEADS):
        inverse_ref[0, head : head + 1, :] = inverses[head]
    att_t_ref[0] = att_t.astype(BF)
    att = att_t.T.astype(BF)
    att_ref[0] = att

    @pl.when(jnp.logical_not(last))
    def _():
        pass_on(step + 1)

    branch = dot(att_ref[0], attn_ref[3])
    branch2_ref[0] = branch.astype(BF)
    state = own_ref[0].astype(F32) + (keep * mod[2:3]) * branch
    cross_in = state.astype(BF)
    cross_in_ref[0] = cross_in
    cross_queries = (dot(cross_in, cross_ref[0]).astype(BF) * scale_by).astype(BF)
    cross_query_ref[0] = cross_queries
    text_id = lax.broadcasted_iota(jnp.int32, (text_keys_ref.shape[0], rows), 0)
    bias = jnp.where(text_id < counts_ref[1], 0.0, MASKED_SCORE)

    def keep_cross(_, head, keys_span, span, exponent):
        cross_exponent_ref[0, head, keys_span, span] = exponent

    (cross_t,), (inverses,) = attend(
        [(cross_queries, text_keys_ref[...], text_values_t_ref[...], bias)], CROSS_AHEAD, keep_cross
    )
    for head in range(HEADS):
        cross_inverse_ref[0, head : head + 1, :] = inverses[head]
    cross_att_t_ref[0] = cross_t.astype(BF)
    cross_att = cross_t.T.astype(BF)
    cross_att_ref[0] = cross_att
    state = state + keep * dot(cross_att, cross_ref[1])
    middle_ref[0] = state
    normed2 = (norm_parts(state)[0] * (1.0 + mod[4:5]) + mod[3:4]).astype(BF)
    normed2_ref[0] = normed2
    act, slope = gelu_parts(dot(normed2, up_ref[...]))
    act = act.astype(BF)
    act_ref[0] = act
    slope_ref[0] = slope.astype(BF)
    branch = dot(act, down_ref[...])
    branch5_ref[0] = branch.astype(BF)
    state = state + (keep * mod[5:6]) * branch
    sent_buf[step] = state.astype(BF)
    src, dst, _, sem, _ = state_copy(0, step)
    pltpu.make_async_copy(src, dst, sem).start()
    for turn in range(1, lay.n_ta):
        push(*state_copy(turn, step)).start()

    @pl.when(last)
    def _():
        for f in range(frames):
            for j in range(lay.clips_dev):
                end_push(me, *latent_copy(j, f))
            for turn in range(1, lay.group):
                push(*fellow_copy(turn, f)).wait_send()
            for turn in range(1, lay.n_ta):
                push(*state_copy(turn, f)).wait_send()
            for turn in range(lay.n_ta):
                src, dst, _, sem, _ = state_copy(turn, f)
                arrived(dst, sem)
        for j in range(lay.clips_dev):
            for s in range(lay.halves):
                end_push(me, *cot_copy(j, s))
        for t in range(lay.n_ta):
            arrived(moved_ref.at[pl.ds(t * frames, frames)], cot_recv.at[t])


def space_backward_kernel(
    first_frame,
    counts_ref,
    grad_ref,
    mod_ref,
    attn_ref,
    cross_ref,
    text_keys_t_ref,
    text_values_ref,
    up_ref,
    down_ref,
    query_ref,
    keys_t_ref,
    value_ref,
    exponent_ref,
    att_t_ref,
    inverse_ref,
    cross_query_ref,
    cross_exponent_ref,
    cross_att_t_ref,
    cross_inverse_ref,
    middle_ref,
    slope_ref,
    branch2_ref,
    branch5_ref,
    state_grad_ref,
    own_grad_ref,
    other_grad_ref,
    kept3_ref,
    d_lifted_ref,
    kept2_ref,
    d_cross_query_ref,
    kept1_ref,
    d_query_ref,
    d_key_ref,
    d_value_ref,
    d_text_keys_ref,
    d_text_values_ref,
    mods_ref,
):
    scale_by = HDIM ** (-0.5)
    frame = counts_ref[2] + first_frame + pl.program_id(0)
    keep = (frame < counts_ref[0]).astype(F32)
    mod = mod_ref[...]
    grad = fold(grad_ref).astype(F32)
    rows = grad.shape[0]
    kept = keep * grad
    d_gate5 = row_sums(kept * branch5_ref[0].astype(F32))
    d_branch = (kept * mod[5:6]).astype(BF)
    kept3_ref[0] = d_branch
    d_act = dot_nt(d_branch, down_ref[...])
    d_lifted = (d_act * slope_ref[0].astype(F32)).astype(BF)
    d_lifted_ref[0] = d_lifted
    d_normed = dot_nt(d_lifted, up_ref[...])
    hat, inverse = norm_parts(middle_ref[0])
    grad = grad + norm_back(d_normed, hat, inverse, mod[4:5])
    d_shift, d_scale = row_sums(d_normed), row_sums(d_normed * hat)
    kept = (keep * grad).astype(BF)
    kept2_ref[0] = kept
    d_att_t = dot_nt(cross_ref[1], kept)
    job = (
        lambda head, at: cross_exponent_ref[0, head, at, :],
        lambda pair: cross_query_ref[0, :, pair * LANES : (pair + 1) * LANES],
        lambda head, at: text_keys_t_ref[head * HDIM : (head + 1) * HDIM, at],
        lambda pair, at: text_values_ref[at, pair * LANES : (pair + 1) * LANES],
        d_att_t,
        cross_att_t_ref[0].astype(F32),
        lambda head: cross_inverse_ref[0, head : head + 1, :],
        text_values_ref.shape[0],
    )
    ((d_query_t, d_keys, d_values),) = attend_back([job], CROSS_AHEAD, KEY_CHUNK)
    d_text_keys_ref[0] = d_keys
    d_text_values_ref[0] = d_values
    d_query = (d_query_t.T * scale_by).astype(BF)
    d_cross_query_ref[0] = d_query
    grad = grad + dot_nt(d_query, cross_ref[0])
    state_grad_ref[0] = grad
    kept = keep * grad
    d_gate2 = row_sums(kept * branch2_ref[0].astype(F32))
    mods_ref[0] = jnp.concatenate(
        [jnp.zeros((2, hat.shape[1]), F32), d_gate2, d_shift, d_scale, d_gate5, jnp.zeros((2, hat.shape[1]), F32)],
        axis=0,
    )
    d_branch = (kept * mod[2:3]).astype(BF)
    kept1_ref[0] = d_branch
    d_att_t = dot_nt(attn_ref[3], d_branch)
    job = (
        lambda head, at: exponent_ref[0, head, at, :],
        lambda pair: query_ref[0, :, pair * LANES : (pair + 1) * LANES],
        lambda head, at: keys_t_ref[0, head * HDIM : (head + 1) * HDIM, at],
        lambda pair, at: value_ref[0, at, pair * LANES : (pair + 1) * LANES],
        d_att_t,
        att_t_ref[0].astype(F32),
        lambda head: inverse_ref[0, head : head + 1, :],
        value_ref.shape[1],
    )
    ((d_query_t, d_keys, d_values),) = attend_back([job], BACK_STAGE, KEY_CHUNK)
    d_query = (d_query_t.T * scale_by).astype(BF)
    d_keys, d_values = d_keys.astype(BF), d_values.astype(BF)
    d_query_ref[0] = d_query
    d_key_ref[0] = d_keys
    d_value_ref[0] = d_values
    d_normed = dot_nt(d_keys, attn_ref[1]) + dot_nt(d_values, attn_ref[2])
    own_grad_ref[0] = d_normed[:rows] + dot_nt(d_query, attn_ref[0])
    other_grad_ref[0] = d_normed[rows:].astype(BF)


def space_finish_kernel(n_parts, own_ref, state_grad_ref, own_grad_ref, *rest):
    parts, (mod_ref, out_ref, mods_ref) = rest[:n_parts], rest[n_parts:]
    d_normed = own_grad_ref[0]
    for part in parts:
        d_normed = d_normed + part[0].astype(F32)
    hat, inverse = norm_parts(fold(own_ref).astype(F32))
    grad = state_grad_ref[0] + norm_back(d_normed, hat, inverse, mod_ref[1:2, :])
    out_ref[...] = grad.astype(BF).reshape(out_ref.shape)
    mods_ref[0] = jnp.concatenate(
        [row_sums(d_normed), row_sums(d_normed * hat), jnp.zeros((6, hat.shape[1]), F32)], axis=0
    )


def interleave(streams, lag):
    live, turn = list(enumerate(streams)), 0
    while live:
        left = []
        for i, stream in live:
            if turn < i * lag or next(stream, DONE) is not DONE:
                left.append((i, stream))
        live, turn = left, turn + 1


DONE = object()


def time_kernel(
    counts_ref,
    state_ref,
    cot_ref,
    mod_ref,
    bias_ref,
    qkv_ref,
    proj_ref,
    up_ref,
    down_ref,
    out_ref,
    grad_ref,
    normed_ref,
    d_qkv_ref,
    att_ref,
    branch4_ref,
    normed2_ref,
    act_ref,
    d_lifted_ref,
    branch5_ref,
    mods_ref,
    exponent_ref,
):
    scale_by = HDIM ** (-0.5)
    frames, block, width = state_ref.shape
    run_rows = frames * SUB
    runs = min(STREAM_RUNS, block // SUB)
    mod = mod_ref[...]
    totals = []

    def stream(first_run):
        patches = slice(first_run * SUB, (first_run + runs) * SUB)
        mine = slice(first_run * run_rows, (first_run + runs) * run_rows)

        def load(ref):
            cube = ref[:, patches, :].astype(F32)
            parts = [cube[:, r * SUB : (r + 1) * SUB].reshape(run_rows, width) for r in range(runs)]
            return jnp.concatenate(parts, axis=0)

        def store(ref, value):
            parts = [value[r * run_rows : (r + 1) * run_rows].reshape(frames, SUB, width) for r in range(runs)]
            ref[:, patches, :] = jnp.concatenate(parts, axis=1).astype(ref.dtype)

        def run_of(value, r):
            return value[r * run_rows : (r + 1) * run_rows]

        state = load(state_ref)
        frame = (lax.broadcasted_iota(jnp.int32, (runs * run_rows, 1), 0) // SUB) % frames
        keep = (frame < counts_ref[0]).astype(F32)
        hat1, inverse1 = norm_parts(state)
        normed = (hat1 * (1.0 + mod[1:2]) + mod[0:1]).astype(BF)
        normed_ref[0, mine] = normed
        yield
        qkv = dot(normed, qkv_ref[...])
        queries = (qkv[:, :width].astype(BF) * scale_by).astype(BF)
        keys = qkv[:, width : 2 * width].astype(BF)
        values = qkv[:, 2 * width :].astype(BF)
        yield
        keys_t_runs, jobs = [], []
        for r in range(runs):
            keys_t_runs.append(run_of(keys, r).T)
            jobs.append((run_of(queries, r), run_of(keys, r), run_of(values, r).T, bias_ref[...]))

        def keep_exponent(r, head, keys_span, span, exponent):
            exponent_ref[first_run + r, head, keys_span, span] = exponent

        att_t_runs, inverse_runs = attend(jobs, TIME_STAGE, keep_exponent)
        yield
        att = jnp.concatenate([att_t.T.astype(BF) for att_t in att_t_runs], axis=0)
        att_ref[0, mine] = att
        branch2 = dot(att, proj_ref[...])
        yield
        state = state + (keep * mod[2:3]) * branch2
        hat2, inverse2 = norm_parts(state)
        normed2 = (hat2 * (1.0 + mod[4:5]) + mod[3:4]).astype(BF)
        normed2_ref[0, mine] = normed2
        yield
        lifted = dot(normed2, up_ref[...])
        yield
        act, slope = gelu_parts(lifted)
        act = act.astype(BF)
        act_ref[0, mine] = act
        grad = load(cot_ref)
        kept = keep * grad
        d_branch = (kept * mod[5:6]).astype(BF)
        branch5_ref[0, mine] = d_branch
        yield
        d_act = dot_nt(d_branch, down_ref[...])
        yield
        d_lifted = (d_act * slope).astype(BF)
        d_lifted_ref[0, mine] = d_lifted
        branch5 = dot(act, down_ref[...])
        yield
        store(out_ref, state + (keep * mod[5:6]) * branch5)
        d_gate5 = row_sums(kept * branch5)
        d_normed2 = dot_nt(d_lifted, up_ref[...])
        yield
        grad = grad + norm_back(d_normed2, hat2, inverse2, mod[4:5])
        kept = keep * grad
        d_gate2 = row_sums(kept * branch2)
        d_branch = (kept * mod[2:3]).astype(BF)
        branch4_ref[0, mine] = d_branch
        yield
        d_att_t_runs = [dot_nt(proj_ref[...], run_of(d_branch, r)) for r in range(runs)]
        yield

        def job(r):
            query_run, value_run = run_of(queries, r), run_of(values, r)
            return (
                lambda head, at: exponent_ref[first_run + r, head, at, :],
                lambda pair: pair_of(query_run, pair),
                lambda head, at: head_rows(keys_t_runs[r], head)[:, at],
                lambda pair, at: pair_of(value_run, pair)[at],
                d_att_t_runs[r],
                att_t_runs[r],
                lambda head: inverse_runs[r][head],
                run_rows,
            )

        backs = attend_back([job(r) for r in range(runs)], TIME_STAGE, run_rows)
        yield
        d_qkv = jnp.concatenate(
            [
                jnp.concatenate([(d_query_t.T * scale_by).astype(BF) for d_query_t, _, _ in backs], axis=0),
                jnp.concatenate([d_keys.astype(BF) for _, d_keys, _ in backs], axis=0),
                jnp.concatenate([d_values.astype(BF) for _, _, d_values in backs], axis=0),
            ],
            axis=1,
        )
        d_qkv_ref[0, mine] = d_qkv
        d_normed1 = dot_nt(d_qkv, qkv_ref[...])
        yield
        grad = grad + norm_back(d_normed1, hat1, inverse1, mod[1:2])
        store(grad_ref, grad)
        totals.append(
            jnp.concatenate(
                [
                    row_sums(d_normed1),
                    row_sums(d_normed1 * hat1),
                    d_gate2,
                    row_sums(d_normed2),
                    row_sums(d_normed2 * hat2),
                    d_gate5,
                    jnp.zeros((2, width), F32),
                ],
                axis=0,
            )
        )

    interleave([stream(first) for first in range(0, block // SUB, runs)], TIME_LAG)
    mods_ref[0] = sum(totals[1:], totals[0])


class Reducer:
    def __init__(self, shapes, small_rows, sizes):
        self.width = width = shapes[0][1]
        self.shapes = shapes
        bits = {name: [(name, 1 << i) for i in range(sizes[name].bit_length() - 1)] for name in ("ta", "pa")}
        kinds = [bits["ta"] + bits["pa"], bits["ta"][::-1] + bits["pa"], bits["pa"] + bits["ta"]]
        self.ways = [("dev", 1)] + kinds[0]
        self.loads, row = [], 0
        for i, shape in enumerate(shapes):
            for column in range(shape[1] // width):
                self.loads.append((i, row, column * width, shape[0]))
                row += shape[0]
        self.total = row
        self.parts = next(n for n in PARTS if row % (2 * n * TILE) == 0)
        self.part_rows = row // 2 // self.parts
        self.half_rows = row // 2
        self.orders = [[("dev", 1)] + kinds[PATTERN[p % len(PATTERN)]] for p in range(self.parts)]
        self.steps = len(self.ways)
        self.small_rows = small_rows
        self.counts, self.halves, self.boxes, at = [self.part_rows], [True], [], 0
        for _ in range(1, self.steps):
            halve = (self.counts[-1] // 2) % TILE == 0
            self.halves.append(halve)
            self.counts.append(self.counts[-1] // 2 if halve else self.counts[-1])
        for p in range(self.parts):
            self.boxes.append([])
            for count in self.counts:
                self.boxes[p].append(at)
                at += count
        self.box_rows = at
        self.phases = 2 * self.steps + 1

    def scratch(self):
        shapes = [
            pltpu.VMEM((self.total, self.width), BF),
            pltpu.VMEM((self.total, self.width), BF),
            pltpu.VMEM((self.box_rows, self.width), BF),
            pltpu.SemaphoreType.DMA((len(self.loads),)),
            pltpu.SemaphoreType.DMA((self.parts, 2)),
            pltpu.SemaphoreType.DMA((self.parts, 2 * self.steps)),
            pltpu.SemaphoreType.DMA((self.parts, 2 * self.steps)),
        ]
        if self.small_rows:
            shapes += [
                pltpu.VMEM((self.steps, self.small_rows, self.width), F32),
                pltpu.SemaphoreType.DMA((self.steps,)),
                pltpu.SemaphoreType.DMA((self.steps,)),
            ]
        return shapes

    def bind(self, sources, out, scratch, small_in=None, small_out=None):
        self.sources, self.out = sources, out
        self.work, self.whole, self.inbox, self.in_sem, self.out_sem, self.send_sem, self.recv_sem = scratch[:7]
        self.small_in, self.small_out = small_in, small_out
        if self.small_rows:
            self.small_box, self.small_send, self.small_recv = scratch[7:]

    def bit(self, way):
        return (lax.axis_index(way[0]) // way[1]) % 2

    def peer(self, way):
        return {way[0]: lax.axis_index(way[0]) + way[1] - 2 * way[1] * self.bit(way)}

    def greet(self):
        barrier = pltpu.get_barrier_semaphore()
        for way in self.ways:
            pl.semaphore_signal(barrier, inc=1, device_id=self.peer(way), device_id_type=pl.DeviceIdType.MESH)
        return len(self.ways)

    def base(self, p, step):
        row = self.bit(self.orders[p][0]) * self.half_rows + p * self.part_rows
        for s in range(1, step + 1):
            if self.halves[s]:
                row = row + self.bit(self.orders[p][s]) * self.counts[s]
        return row

    def rows(self, ref, row, count):
        return ref.at[pl.ds(pl.multiple_of(row, TILE), count)]

    def load(self, i):
        source, row, column, rows = self.loads[i]
        view = self.sources[source].at[:, column : column + self.width]
        return pltpu.make_async_copy(view, self.work.at[row : row + rows], self.in_sem.at[i])

    def remote(self, src, dst, p, step, way):
        return pltpu.make_async_remote_copy(
            src_ref=src,
            dst_ref=dst,
            send_sem=self.send_sem.at[p, step],
            recv_sem=self.recv_sem.at[p, step],
            device_id=self.peer(way),
            device_id_type=pl.DeviceIdType.MESH,
        )

    def down(self, p, step):
        way, count = self.orders[p][step], self.counts[step]
        if step == 0:
            row = (1 - self.bit(way)) * self.half_rows + p * self.part_rows
        else:
            row = self.base(p, step - 1)
            if self.halves[step]:
                row = row + (1 - self.bit(way)) * count
        box = self.boxes[p][step]
        return self.remote(self.rows(self.work, row, count), self.inbox.at[box : box + count], p, step, way)

    def end_down(self, p, step):
        self.down(p, step).wait()
        count, base, box = self.counts[step], self.base(p, step), self.boxes[p][step]
        chunk = next(c for c in (96, 64, 48, 32, TILE) if count % c == 0)

        def body(i, carry):
            at = pl.ds(pl.multiple_of(base + i * chunk, TILE), chunk)
            got = self.inbox[pl.ds(pl.multiple_of(box + i * chunk, TILE), chunk), :]
            total = (self.work[at, :].astype(F32) + got.astype(F32)).astype(BF)
            if step == self.steps - 1:
                self.whole[at, :] = total
            else:
                self.work[at, :] = total
            return carry

        lax.fori_loop(0, count // chunk, body, 0)

    def up(self, p, turn):
        step = self.steps - 1 - turn
        if not self.halves[step]:
            return None
        rows = self.rows(self.whole, self.base(p, step), self.counts[step])
        return self.remote(rows, rows, p, self.steps + turn, self.orders[p][step])

    def store(self, p, side):
        rows = pl.ds(side * self.half_rows + p * self.part_rows, self.part_rows)
        return pltpu.make_async_copy(self.whole.at[rows], self.out.at[rows], self.out_sem.at[p, side])

    def small(self, step):
        return pltpu.make_async_remote_copy(
            src_ref=self.small_out,
            dst_ref=self.small_box.at[step],
            send_sem=self.small_send.at[step],
            recv_sem=self.small_recv.at[step],
            device_id=self.peer(self.ways[step]),
            device_id_type=pl.DeviceIdType.MESH,
        )

    def prepare(self):
        for i in range(len(self.loads)):
            self.load(i).start()
        if self.small_rows:
            self.small_out[...] = self.small_in[...]

    def phase(self, k):
        n = self.steps
        if k == 0:
            for i in range(len(self.loads)):
                self.load(i).wait()
        for p in range(self.parts):
            if 1 <= k <= n:
                self.end_down(p, k - 1)
            elif k > n:
                before = self.up(p, k - n - 1)
                if before is not None:
                    before.wait()
            if k < n:
                self.down(p, k).start()
            elif k < 2 * n:
                after = self.up(p, k - n)
                if after is not None:
                    after.start()
            else:
                self.store(p, 0).start()
                self.store(p, 1).start()
        if k == 2 * n:
            for p in range(self.parts):
                self.store(p, 0).wait()
                self.store(p, 1).wait()
        if self.small_rows and k <= n:
            if k > 0:
                self.small(k - 1).wait()
                self.small_out[...] = self.small_out[...] + self.small_box[k - 1]
            if k < n:
                self.small(k).start()

    def unpack(self, reduced):
        results, at = [], 0
        for rows, columns in self.shapes:
            turns = columns // self.width
            blocks = [reduced[at + i * rows : at + (i + 1) * rows] for i in range(turns)]
            at += turns * rows
            results.append((blocks[0] if turns == 1 else jnp.concatenate(blocks, axis=1)).astype(F32))
        return results


def reduce_all(arrays, small, sizes):
    reducer = Reducer([a.shape for a in arrays], small.shape[0], sizes)
    n = len(arrays)

    def kernel(*refs):
        reducer.bind(refs[:n], refs[n + 1], refs[n + 3 :], refs[n], refs[n + 2])
        reducer.prepare()
        pl.semaphore_wait(pltpu.get_barrier_semaphore(), reducer.greet())
        for k in range(reducer.phases):
            reducer.phase(k)

    any_spec, vmem_spec = pl.BlockSpec(memory_space=pl.ANY), pl.BlockSpec(memory_space=pltpu.VMEM)
    reduced, small_sum = pl.pallas_call(
        kernel,
        in_specs=[any_spec] * n + [vmem_spec],
        out_specs=[any_spec, vmem_spec],
        out_shape=[shape_of((reducer.total, reducer.width), BF), shape_of(small.shape, F32)],
        scratch_shapes=reducer.scratch(),
        compiler_params=pltpu.CompilerParams(collective_id=0, has_side_effects=True, vmem_limit_bytes=VMEM_BYTES),
        cost_estimate=pl.CostEstimate(
            flops=8 * reducer.total * reducer.width, bytes_accessed=4 * reducer.total * reducer.width, transcendentals=0
        ),
    )(*arrays, small)
    return reducer.unpack(reduced), small_sum


def whole(array):
    zeros = (0,) * array.ndim
    return pl.BlockSpec(array.shape, lambda *grid: zeros)


def framed(array):
    tail = (0,) * (array.ndim - 1)
    return pl.BlockSpec((1,) + tuple(array.shape[1:]), lambda frame: (frame,) + tail)


SCALARS = pl.BlockSpec(memory_space=pltpu.SMEM)
HBM = pl.BlockSpec(memory_space=pl.ANY)


def shape_of(shape, dtype):
    return jax.ShapeDtypeStruct(shape, dtype)


def call(kernel, grid, inputs, in_specs, outputs, out_specs, flops, scratch=(), collective_id=None):
    moved = sum(math.prod(a.shape) * a.dtype.itemsize for a in (*inputs, *outputs))
    return pl.pallas_call(
        kernel,
        grid=grid,
        in_specs=in_specs,
        out_specs=out_specs,
        out_shape=outputs,
        scratch_shapes=list(scratch),
        compiler_params=pltpu.CompilerParams(
            vmem_limit_bytes=VMEM_BYTES, collective_id=collective_id, has_side_effects=collective_id is not None
        ),
        cost_estimate=pl.CostEstimate(flops=int(flops), bytes_accessed=int(moved), transcendentals=0),
    )(*inputs)


def make_per_device(sizes):
    n_ta, n_pa, n_dev = sizes["ta"], sizes["pa"], sizes["dev"]

    def per_device(
        latents,
        context,
        cotangent,
        timesteps,
        frame_counts,
        text_lengths,
        step_proj,
        mod_table,
        patch_attn,
        cross_attn,
        patch_up,
        patch_down,
        frame_attn,
        frame_up,
        frame_down,
    ):
        lay = Layout(sizes, latents.shape)
        clips_dev, frames, patches, width = latents.shape
        clips, run, group, near, halves = lay.clips, lay.run, lay.group, lay.near, lay.halves
        space_rows, other_rows, key_rows = lay.space_rows, lay.other_rows, lay.key_rows
        time_patches, all_frames = lay.time_patches, lay.all_frames
        ta, pa, dev = (lax.axis_index(name) for name in ("ta", "pa", "dev"))
        clip, member = lay.clip(lay.here()), lay.member(lay.here())

        def place(clip_id, member_id):
            return (clip_id * run + member_id % run) * n_dev + member_id // run

        def space_pairs(step):
            pairs = []
            for p in range(n_pa):
                for d in range(n_dev):
                    k = d * clips_dev + (p + step) % clips_dev
                    pairs.append((p * n_dev + d, place(k, p // near)))
            return pairs

        def time_pairs(step):
            u, w = step % halves, step // halves
            pairs = []
            for t in range(n_ta):
                for p in range(n_pa):
                    for d in range(n_dev):
                        s = (t % halves + u) % halves
                        j = (t // halves + w) % clips_dev
                        k = d * clips_dev + j
                        pairs.append(
                            (
                                (t * n_pa + p) * n_dev + d,
                                ((p % near) * halves + s) * n_pa * n_dev + place(k, p // near),
                            )
                        )
            return pairs

        def back(pairs):
            return [(b, a) for a, b in pairs]

        def group_pairs(step):
            return [
                (place(k, g), place(k, (g + step) % group)) for k in range(clips) for g in range(group)
            ]

        def ta_pairs(step):
            return [(t, t ^ step) for t in range(n_ta)]

        whole_axes = ("ta", "pa", "dev")
        pair_axes = ("pa", "dev")

        def of_clip(local):
            both = lax.all_gather(local, "dev", axis=0, tiled=True)
            return lax.dynamic_index_in_dim(both, clip, 0, keepdims=False)

        def sinusoid(steps):
            half = step_proj.shape[0] // 2
            frequency = jnp.exp(-math.log(10000.0) * jnp.arange(half, dtype=F32) / half)
            angles = steps.astype(F32)[:, None] * frequency[None, :]
            return jnp.concatenate([jnp.cos(angles), jnp.sin(angles)], axis=1)

        numbers = lax.all_gather(jnp.stack([timesteps, frame_counts, text_lengths], axis=1), "dev", axis=0, tiled=True)
        own_numbers = lax.dynamic_index_in_dim(numbers, clip, 0, keepdims=False)
        embeddings = sinusoid(numbers[:, 0])
        embedding = lax.dynamic_index_in_dim(embeddings, clip, 0, keepdims=True)
        timing = jnp.dot(embedding, step_proj.astype(F32), precision=HIGHEST).reshape(6, width)
        table = mod_table.astype(F32)
        pad = jnp.zeros((2, width), F32)
        space_mod = jnp.concatenate([timing + table[0], pad])
        frame_mod = jnp.concatenate([timing + table[1], pad])
        counts = jnp.stack([own_numbers[1], own_numbers[2], ta * frames, 0]).astype(jnp.int32)
        text = of_clip(context)
        text_count = text.shape[0]
        text_rows = -(-text_count // LANES) * LANES
        text_wide = jnp.pad(text, ((0, text_rows - text_count), (0, 0)))
        text_keys = dot(text_wide, cross_attn[1]).astype(BF)
        text_values = dot(text_wide, cross_attn[2]).astype(BF)
        cross_ends = jnp.stack([cross_attn[0], cross_attn[3]])
        patch_turned = jnp.swapaxes(patch_attn[1:3], 1, 2)

        def out(*shape, dtype=BF):
            return shape_of((frames,) + shape, dtype)

        def moved_tokens():
            return shape_of((all_frames, time_patches, width), BF)

        hidden = patch_up.shape[1]
        inputs = (
            counts, latents, cotangent, space_mod, patch_attn, patch_turned, cross_ends, text_keys, text_values.T,
            patch_up, patch_down,
        )
        outputs = (
            moved_tokens(),
            moved_tokens(),
            out(space_rows, width),
            out(key_rows, width),
            out(space_rows, width),
            out(width, key_rows),
            out(key_rows, width),
            out(HEADS, key_rows, space_rows),
            out(width, space_rows),
            out(space_rows, width),
            out(8, space_rows, dtype=F32),
            out(space_rows, width),
            out(space_rows, width),
            out(HEADS, text_rows, space_rows),
            out(width, space_rows),
            out(space_rows, width),
            out(8, space_rows, dtype=F32),
            out(space_rows, width, dtype=F32),
            out(space_rows, width),
            out(space_rows, hidden),
            out(space_rows, hidden),
            out(space_rows, width),
            out(space_rows, width),
        )
        dense = 2 * frames * space_rows * width * (6 * width + 2 * hidden) + 8 * frames * key_rows * width * width
        dma = pltpu.SemaphoreType.DMA
        state, cot, *saved = call(
            lambda *refs: space_forward_kernel(lay, *refs),
            (frames,),
            inputs,
            [SCALARS, HBM, HBM] + [whole(a) for a in inputs[3:]],
            outputs,
            [HBM, HBM] + [framed(a) for a in outputs[2:]],
            dense + 16 * frames * space_rows * key_rows * width,
            [
                pltpu.VMEM((frames, near, patches, width), BF),
                pltpu.VMEM((frames, group - 1, near, patches, width), BF),
                pltpu.VMEM((frames, space_rows, width), BF),
                dma((clips_dev, frames)),
                dma((frames, near)),
                dma((group - 1, frames)),
                dma((group - 1, frames)),
                dma((n_ta, frames)),
                dma((n_ta, frames)),
                dma((clips_dev, halves)),
                dma((n_ta,)),
            ],
            collective_id=1,
        )

        def space_backward(frame_ids, grad, saved):
            count = len(frame_ids)

            def out(*shape, dtype=BF):
                return shape_of((count,) + shape, dtype)

            (_, _, query, keys_t, value, exponent, att_t, _, inverse, _, cross_query, cross_exponent, cross_att_t, _,
             cross_inverse, middle, _, _, slope, branch2, branch5) = saved
            start = frame_ids[0]

            def framed_from(array):
                tail = (0,) * (array.ndim - 1)
                return pl.BlockSpec((1,) + tuple(array.shape[1:]), lambda frame: (frame + start,) + tail)

            inputs = (
                counts, grad, space_mod, patch_attn, cross_ends, text_keys.T, text_values, patch_up, patch_down,
                query, keys_t, value, exponent, att_t, inverse, cross_query, cross_exponent, cross_att_t,
                cross_inverse, middle, slope, branch2, branch5,
            )
            hidden = patch_up.shape[1]
            outputs = (
                out(space_rows, width, dtype=F32),
                out(space_rows, width, dtype=F32),
                out(other_rows, width),
                out(space_rows, width),
                out(space_rows, hidden),
                out(space_rows, width),
                out(space_rows, width),
                out(space_rows, width),
                out(space_rows, width),
                out(key_rows, width),
                out(key_rows, width),
                out(text_rows, width, dtype=F32),
                out(text_rows, width, dtype=F32),
                out(8, width, dtype=F32),
            )
            grad_spec = pl.BlockSpec((n_ta, 1, time_patches, width), lambda frame: (0, frame, 0, 0))
            dense = 2 * count * space_rows * width * (6 * width + 2 * hidden) + 8 * count * key_rows * width * width
            return call(
                lambda *refs: space_backward_kernel(frame_ids[0], *refs),
                (count,),
                inputs,
                [SCALARS, grad_spec] + [whole(a) for a in inputs[2:9]] + [framed_from(a) for a in inputs[9:]],
                outputs,
                [framed(a) for a in outputs],
                dense + 32 * count * space_rows * key_rows * width,
            )

        def space_finish(own, state_grad, own_grad, parts):
            count = own.shape[0]
            inputs = (own, state_grad, own_grad, *parts, space_mod)
            outputs = (
                shape_of((count, near, patches, width), BF),
                shape_of((count, 8, width), F32),
            )
            return call(
                lambda *refs: space_finish_kernel(len(parts), *refs),
                (count,),
                inputs,
                [framed(a) for a in inputs[:-1]] + [whole(space_mod)],
                outputs,
                [framed(a) for a in outputs],
                count * space_rows * width * 30,
            )

        frame_groups = [ids for ids in (tuple(range(min(2, frames))), tuple(range(min(2, frames), frames))) if ids]
        slot = ta % halves
        n_steps = halves * clips_dev

        def exchange(pieces):
            got = [lax.dynamic_index_in_dim(pieces, ta, 0, keepdims=False)]
            for step in range(1, n_ta):
                sent = lax.dynamic_index_in_dim(pieces, ta ^ step, 0, keepdims=False)
                got.append(lax.ppermute(sent, "ta", ta_pairs(step)))
            stacked = jnp.stack(got)
            return jnp.stack(
                [lax.dynamic_index_in_dim(stacked, ta ^ t, 0, keepdims=False) for t in range(n_ta)]
            )

        block_rows = all_frames * BLOCK
        run_rows = all_frames * SUB
        ids = jnp.arange(run_rows, dtype=jnp.int32)
        same = (ids[:, None] % SUB == ids[None, :] % SUB) & (ids[:, None] // SUB < counts[0])
        bias = jnp.where(same, 0.0, MASKED_SCORE).astype(F32)
        hidden = frame_up.shape[1]
        n_blocks = time_patches // BLOCK

        def tokens(features):
            return shape_of((n_blocks, block_rows, features), BF)

        frame_wide = frame_attn[:3].swapaxes(0, 1).reshape(width, 3 * width)
        time_inputs = (counts, state, cot, frame_mod, bias, frame_wide, frame_attn[3], frame_up, frame_down)
        time_outputs = (
            shape_of((all_frames, time_patches, width), BF),
            shape_of((all_frames, time_patches, width), BF),
            tokens(width),
            tokens(3 * width),
            tokens(width),
            tokens(width),
            tokens(width),
            tokens(hidden),
            tokens(hidden),
            tokens(width),
            shape_of((n_blocks, 8, width), F32),
        )

        def blocked(array):
            return pl.BlockSpec((all_frames, BLOCK, array.shape[2]), lambda at: (0, at, 0))

        (out_t, grad_t, normed_t, d_qkv_t, att_tt, branch4, normed4, act4, d_lifted4, branch5, frame_six) = call(
            time_kernel,
            (n_blocks,),
            time_inputs,
            [SCALARS, blocked(state), blocked(cot)] + [whole(a) for a in time_inputs[3:]],
            time_outputs,
            [blocked(a) for a in time_outputs[:2]] + [framed(a) for a in time_outputs[2:]],
            all_frames * time_patches * width * (24 * width + 12 * hidden),
            [pltpu.VMEM((BLOCK // SUB, HEADS, run_rows, run_rows), BF)],
        )

        grad_s = exchange(grad_t.reshape(n_ta, frames, time_patches, width))

        out_t, grad_s = lax.optimization_barrier((out_t, grad_s))
        out_pieces = out_t.reshape(n_ta, frames, time_patches, width)
        out_parts = []
        for step in range(n_steps):
            u, w = step % halves, step // halves
            source = (slot - u) % halves + halves * ((clip % clips_dev - w) % clips_dev)
            sent = lax.dynamic_index_in_dim(out_pieces, source, 0, keepdims=False)
            out_parts.append(lax.ppermute(sent, whole_axes, back(time_pairs(step))))
        out_stack = jnp.stack(out_parts)
        rows = []
        for j in range(clips_dev):
            runs = []
            for s in range(halves):
                step = ((j - ta // halves) % clips_dev) * halves + (s - ta % halves) % halves
                runs.append(lax.dynamic_index_in_dim(out_stack, step, 0, keepdims=False))
            rows.append(jnp.concatenate(runs, axis=1))
        output = jnp.stack(rows)

        def weight_grad(left, right):
            left, right = left.reshape(-1, left.shape[-1]), right.reshape(-1, right.shape[-1])
            return lax.dot_general(left, right, (((0,), (0,)), ((), ())), preferred_element_type=F32).astype(BF)

        d_frame_qkv = weight_grad(normed_t, d_qkv_t)
        d_frame_proj = weight_grad(att_tt, branch4)
        d_frame_up = weight_grad(normed4, d_lifted4)
        d_frame_down = weight_grad(act4, branch5)

        pieces, backs, finish_six = [], [], []
        for i, frame_ids in enumerate(frame_groups):
            own = saved[0][frame_ids[0] : frame_ids[-1] + 1]
            grad = grad_s[:, frame_ids[0] : frame_ids[-1] + 1]
            if i == 1:
                grad, output = lax.optimization_barrier((grad, output))
            backed = space_backward(frame_ids, grad, saved)
            backs.append(backed)
            other_grad = backed[2]
            parts = []
            for step in range(1, group):
                sent = other_grad[:, (step - 1) * space_rows : step * space_rows]
                parts.append(lax.ppermute(sent, pair_axes, back(group_pairs(step))))
            done, mods = space_finish(own, backed[0], backed[1], parts)
            finish_six.append(mods)
            got = []
            for step in range(clips_dev):
                b = (clip - step) % clips_dev
                sent = lax.dynamic_index_in_dim(done, b, 1, keepdims=False)
                got.append(lax.ppermute(sent, pair_axes, back(space_pairs(step))))
            stacked = jnp.stack(got)
            pieces.append(
                jnp.stack(
                    [
                        lax.dynamic_index_in_dim(stacked, (j - pa) % clips_dev, 0, keepdims=False)
                        for j in range(clips_dev)
                    ]
                )
            )
        latents_grad = jnp.concatenate(pieces, axis=1).astype(F32)

        def over_frames(lists, index):
            picked = [entry[index] for entry in lists]
            return picked[0] if len(picked) == 1 else jnp.concatenate(picked)

        def grad_over(lists, index, others, other_index):
            total = None
            for ids, two in zip(frame_groups, others):
                left, right = lists[index][ids[0] : ids[-1] + 1], two[other_index]
                left, right = left.reshape(-1, left.shape[-1]), right.reshape(-1, right.shape[-1])
                part = lax.dot_general(left, right, (((0,), (0,)), ((), ())), preferred_element_type=F32)
                total = part if total is None else total + part
            return total.astype(BF)

        d_patch_up = grad_over(saved, 16, backs, 4)
        d_patch_down = grad_over(saved, 17, backs, 3)
        d_cross_proj = grad_over(saved, 13, backs, 5)
        d_cross_q = grad_over(saved, 9, backs, 6)
        text_t = text.astype(F32).T
        d_tk, d_tv = (over_frames(backs, i) for i in (11, 12))
        d_cross_k = jnp.dot(text_t, jnp.sum(d_tk, axis=0)[:text_count], precision=HIGHEST).astype(BF)
        d_cross_v = jnp.dot(text_t, jnp.sum(d_tv, axis=0)[:text_count], precision=HIGHEST).astype(BF)
        d_patch_proj = grad_over(saved, 7, backs, 7)
        d_patch_q = grad_over([saved[1][:, :space_rows]], 0, backs, 8)
        d_patch_k = grad_over(saved, 1, backs, 9)
        d_patch_v = grad_over(saved, 1, backs, 10)
        six = jnp.sum(over_frames(backs, 13), axis=0) + jnp.sum(jnp.concatenate(finish_six), axis=0)
        mine = jnp.stack([six, jnp.sum(frame_six, axis=0)])
        spread = jnp.where(jnp.arange(clips)[:, None, None, None] == clip, mine[None], 0.0)
        arrays = [
            d_patch_q, d_patch_k, d_patch_v, d_patch_proj, d_cross_q, d_cross_k, d_cross_v, d_cross_proj,
            d_patch_up, d_patch_down, d_frame_qkv, d_frame_proj, d_frame_up, d_frame_down,
        ]
        results, by_clip = reduce_all(arrays, spread.reshape(-1, width), sizes)
        by_clip = by_clip.reshape(clips, 2, 8, width)[:, :, :6]
        d_patch_attn = jnp.stack(results[0:4])
        d_cross = jnp.stack(results[4:8])
        d_patch_up, d_patch_down = results[8:10]
        d_frame_qkv = results[10].reshape(width, 3, width).swapaxes(0, 1)
        d_frame_attn = jnp.concatenate([d_frame_qkv, results[11][None]])
        d_frame_up, d_frame_down = results[12:14]
        d_table = jnp.sum(by_clip, axis=0)
        d_step = lax.dot_general(
            embeddings,
            jnp.sum(by_clip, axis=1).reshape(clips, -1),
            (((0,), (0,)), ((), ())),
            precision=HIGHEST,
        )
        return (
            output,
            latents_grad,
            d_step,
            d_table,
            d_patch_attn,
            d_cross,
            d_patch_up,
            d_patch_down,
            d_frame_attn,
            d_frame_up,
            d_frame_down,
        )

    return per_device


def solution(mesh):
    sizes = dict(mesh.shape)
    tokens = P("dev", "ta", "pa", None)
    in_specs = (tokens, P("dev", None, None), tokens, P("dev"), P("dev"), P("dev")) + (P(),) * 9
    out_specs = (tokens, tokens) + (P(),) * 9
    return jax.shard_map(
        make_per_device(sizes),
        mesh=mesh,
        in_specs=in_specs,
        out_specs=out_specs,
        check_vma=False,
    )
```

```python
import math

import jax
import jax.numpy as jnp
from jax import lax
from jax.experimental import pallas as pl
from jax.experimental.pallas import tpu as pltpu
from jax.sharding import PartitionSpec as P

HEADS = 6
HDIM = 64
PAIRS = HEADS // 2
LANES = 2 * HDIM
EPSILON = 1e-06
MASKED_SCORE = -1e30
HIGHEST = lax.Precision.HIGHEST
F32 = jnp.float32
BF = jnp.bfloat16
VMEM_BYTES = 60 * 2**20
SUM_ROWS = 16
BLOCK = 32
STREAM_RUNS = 2
TIME_LAG = 1
SUB = 8
TILE = 16
TIME_STAGE = 8
SPACE_STAGE = 1
BACK_STAGE = 1
CROSS_AHEAD = 2
SPAN = 512
KEY_CHUNK = 256
PARTS = (7, 6, 5, 4, 3, 2)
HIDDEN_PARTS = (3, 2)
PATTERN = (0, 1, 2, 0, 1, 0, 1)


def dot(a, b):
    return jnp.dot(a, b, preferred_element_type=F32)


def dot_nt(a, b):
    return lax.dot_general(a, b, (((1,), (1,)), ((), ())), preferred_element_type=F32)


def dot_tn(a, b):
    return lax.dot_general(a, b, (((0,), (0,)), ((), ())), preferred_element_type=F32)


def norm_parts(values):
    centred = values - jnp.mean(values, axis=-1, keepdims=True)
    inverse = lax.rsqrt(jnp.mean(centred * centred, axis=-1, keepdims=True) + EPSILON)
    return centred * inverse, inverse


def norm_back(d_normed, hat, inverse, scale_by):
    d_hat = d_normed * (1.0 + scale_by)
    mean_d = jnp.mean(d_hat, axis=-1, keepdims=True)
    mean_dh = jnp.mean(d_hat * hat, axis=-1, keepdims=True)
    return inverse * (d_hat - mean_d - hat * mean_dh)


GELU_A = math.sqrt(2.0 / math.pi)
GELU_B = 0.044715


def gelu_parts(values):
    square = values * values
    bent = jnp.tanh(GELU_A * values * (1.0 + GELU_B * square))
    half = 0.5 * (1.0 + bent)
    slope = half + (0.5 * GELU_A) * values * (1.0 - bent * bent) * (1.0 + 3.0 * GELU_B * square)
    return values * half, slope


def row_sums(values):
    return jnp.sum(values, axis=0, keepdims=True)


def head_lanes(values, head):
    lane = lax.broadcasted_iota(jnp.int32, values.shape, 1)
    return jnp.where((lane >= HDIM) == (head % 2 == 1), values, jnp.zeros_like(values))


def pair_of(values, pair):
    return values[:, pair * LANES : (pair + 1) * LANES]


def head_rows(values, head):
    return values[head * HDIM : (head + 1) * HDIM, :]


def lone_rows(values, head):
    rows = head_rows(values, head)
    blank = jnp.zeros_like(rows)
    return jnp.concatenate([rows, blank] if head % 2 == 0 else [blank, rows], axis=0)


def spans(count, size):
    return [slice(at, min(at + size, count)) for at in range(0, count, size)]


def attend(jobs, ahead, keep_exponent):
    units = [
        (i, head, span) for i, job in enumerate(jobs) for head in range(HEADS) for span in spans(job[0].shape[0], SPAN)
    ]
    scores, tops, sums, inverses = {}, {}, {}, {}

    def score(unit, keys_span):
        i, head, span = unit
        queries, keys, _, bias = jobs[i]
        lone = head_lanes(pair_of(queries, head // 2)[span], head)
        value = dot_nt(pair_of(keys, head // 2)[keys_span], lone)
        if bias is not None:
            value = value + bias[keys_span, span]
        scores.setdefault((i, head, span.start), []).append(value)
        top = jnp.max(value, axis=0, keepdims=True)
        old = tops.get((i, head, span.start))
        tops[i, head, span.start] = top if old is None else jnp.maximum(old, top)

    def weigh(unit, index, keys_span):
        i, head, span = unit
        name = (i, head, span.start)
        exponent = jnp.exp(scores[name][index] - tops[name]).astype(BF)
        scores[name][index] = None
        keep_exponent(i, head, keys_span, span, exponent)
        values_t = jobs[i][2]
        count = keys_span.stop - keys_span.start
        lifted = jnp.concatenate([head_rows(values_t, head)[:, keys_span], jnp.ones((SUM_ROWS, count), BF)], axis=0)
        part = dot(lifted, exponent)
        sums[name] = part if name not in sums else sums[name] + part

    def finish(unit):
        i, head, span = unit
        name = (i, head, span.start)
        total = sums[name]
        inverse = 1.0 / total[HDIM : HDIM + 1, :]
        sums[name] = total[:HDIM, :] * inverse
        inverses[name] = inverse

    for turn in range(len(units) + ahead):
        later = units[turn] if turn < len(units) else None
        now = units[turn - ahead] if turn >= ahead else None
        later_spans = spans(jobs[later[0]][1].shape[0], SPAN) if later else []
        now_spans = spans(jobs[now[0]][1].shape[0], SPAN) if now else []
        for index in range(max(len(later_spans), len(now_spans))):
            if index < len(later_spans):
                score(later, later_spans[index])
            if index < len(now_spans):
                weigh(now, index, now_spans[index])
        if now:
            finish(now)

    def joined(parts, i, head):
        starts = [span.start for span in spans(jobs[i][0].shape[0], SPAN)]
        return jnp.concatenate([parts[i, head, start] for start in starts], axis=1)

    return (
        [jnp.concatenate([joined(sums, i, head) for head in range(HEADS)], axis=0) for i in range(len(jobs))],
        [[joined(inverses, i, head) for head in range(HEADS)] for i in range(len(jobs))],
    )


def added(total, part):
    return part if total is None else total + part


def attend_back(jobs, ahead, chunk):
    scaled, centres = {}, {}
    for i, (_, _, _, _, d_att_t, att_t, inverse_of, _, _) in enumerate(jobs):
        for head in range(HEADS):
            inverse = inverse_of(head)
            d_att_head = head_rows(d_att_t, head)
            centres[i, head] = row_sums(d_att_head * head_rows(att_t, head)) * inverse
            part = (d_att_head * inverse).astype(BF)
            blank = jnp.zeros_like(part)
            scaled[i, head] = jnp.concatenate([part, blank] if head % 2 == 0 else [blank, part], axis=0)
    units = [
        (i, head, rows) for i, job in enumerate(jobs) for head in range(HEADS) for rows in spans(job[7], chunk)
    ]
    d_queries, d_keys, d_values, chances = {}, {}, {}, {}
    for turn in range(len(units) + ahead):
        if turn < len(units):
            i, head, rows = units[turn]
            chances[turn] = dot(jobs[i][3](head // 2, rows), scaled[i, head])
        if turn < ahead:
            continue
        i, head, rows = units[turn - ahead]
        key = (i, head // 2, rows.start)
        exponent = jobs[i][0](head, rows)
        chance = chances.pop(turn - ahead)
        d_values[key] = added(d_values.get(key), dot_nt(exponent, scaled[i, head]))
        score = (exponent.astype(F32) * (chance - centres[i, head])).astype(BF)
        d_keys[key] = added(d_keys.get(key), dot(score, head_lanes(jobs[i][1](head // 2), head)))
        d_queries[i, head] = added(d_queries.get((i, head)), dot(jobs[i][2](head, rows), score))
        if rows.stop == jobs[i][7] and jobs[i][8] is not None:
            jobs[i][8](head)
    results = []
    for i, job in enumerate(jobs):
        starts = [rows.start for rows in spans(job[7], chunk)]
        joined = [
            jnp.concatenate(
                [jnp.concatenate([parts[i, pair, at] for at in starts], axis=0) for pair in range(PAIRS)], axis=1
            )
            for parts in (d_keys, d_values)
        ]
        results.append((jnp.concatenate([d_queries[i, head] for head in range(HEADS)], axis=0), *joined))
    return results


def fold(ref):
    value = ref[...]
    return value.reshape(-1, value.shape[-1])


class Layout:
    def __init__(self, sizes, latents_shape):
        self.clips_dev, self.frames, self.patches, self.width = latents_shape
        self.n_ta, self.n_pa, self.n_dev = sizes["ta"], sizes["pa"], sizes["dev"]
        self.clips = self.clips_dev * self.n_dev
        self.run = self.n_pa // self.clips
        self.group = self.run * self.n_dev
        self.near = self.n_pa // self.group
        self.halves = self.n_ta // self.near
        self.space_rows = self.near * self.patches
        self.time_patches = self.space_rows // self.n_ta
        self.other_rows = (self.group - 1) * self.space_rows
        self.key_rows = self.group * self.space_rows
        self.all_frames = self.n_ta * self.frames

    def here(self):
        return {name: lax.axis_index(name) for name in ("ta", "pa", "dev")}

    def clip(self, me):
        return me["pa"] // self.run

    def member(self, me):
        return me["dev"] * self.run + me["pa"] % self.run

    def space_place(self, ta, clip, member):
        return {"ta": ta, "pa": clip * self.run + member % self.run, "dev": member // self.run}

    def space_target(self, me, j):
        return self.space_place(me["ta"], me["dev"] * self.clips_dev + j, me["pa"] // self.near)

    def owner(self, me, ta, slot):
        return {"ta": ta, "pa": self.near * self.member(me) + slot, "dev": self.clip(me) // self.clips_dev}

    def time_target(self, me, j, s):
        place = self.space_target(me, j)
        return {**place, "ta": (me["pa"] % self.near) * self.halves + s}

    def fellow(self, me, step):
        return self.space_place(me["ta"], self.clip(me), (self.member(me) + step) % self.group)

    def across(self, me, step):
        return {**me, "ta": (me["ta"] + step) % self.n_ta}


def is_me(me, place):
    same = None
    for name, index in place.items():
        if index is not me[name]:
            equal = index == me[name]
            same = equal if same is None else same & equal
    return same


def greet(me, place):
    @pl.when(jnp.logical_not(is_me(me, place)))
    def _():
        pl.semaphore_signal(
            pltpu.get_barrier_semaphore(), inc=1, device_id=place, device_id_type=pl.DeviceIdType.MESH
        )


def await_greetings(me, places, amount=0):
    amount = jnp.int32(amount)
    for place in places:
        amount = amount + jnp.logical_not(is_me(me, place)).astype(jnp.int32)
    pl.semaphore_wait(pltpu.get_barrier_semaphore(), amount)


def push(src, dst, send_sem, recv_sem, place):
    return pltpu.make_async_remote_copy(
        src_ref=src,
        dst_ref=dst,
        send_sem=send_sem,
        recv_sem=recv_sem,
        device_id=place,
        device_id_type=pl.DeviceIdType.MESH,
    )


def start_push(me, src, dst, send_sem, recv_sem, place):
    same = is_me(me, place)

    @pl.when(same)
    def _():
        pltpu.make_async_copy(src, dst, recv_sem).start()

    @pl.when(jnp.logical_not(same))
    def _():
        push(src, dst, send_sem, recv_sem, place).start()


def end_push(me, src, dst, send_sem, recv_sem, place):
    @pl.when(jnp.logical_not(is_me(me, place)))
    def _():
        push(src, dst, send_sem, recv_sem, place).wait_send()


def arrived(dst, recv_sem):
    pltpu.make_async_copy(dst, dst, recv_sem).wait()


def space_forward_kernel(
    lay,
    counts_ref,
    latents_ref,
    cot_ref,
    mod_ref,
    attn_ref,
    turned_ref,
    cross_ref,
    text_keys_ref,
    text_values_t_ref,
    up_ref,
    down_ref,
    state_ref,
    moved_ref,
    own_ref,
    normed_ref,
    query_ref,
    keys_t_ref,
    value_ref,
    exponent_ref,
    att_t_ref,
    att_ref,
    inverse_ref,
    cross_in_ref,
    cross_query_ref,
    cross_exponent_ref,
    cross_att_t_ref,
    cross_att_ref,
    cross_inverse_ref,
    middle_ref,
    normed2_ref,
    act_ref,
    slope_ref,
    branch2_ref,
    branch5_ref,
    own_buf,
    other_buf,
    sent_buf,
    lat_send,
    lat_recv,
    fellow_send,
    fellow_recv,
    state_send,
    state_recv,
    cot_send,
    cot_recv,
):
    scale_by = HDIM ** (-0.5)
    me = lay.here()
    step = pl.program_id(0)
    frames, near = lay.frames, lay.near
    last = step == frames - 1

    def latent_copy(j, f):
        slot = me["pa"] % near
        return (
            latents_ref.at[j, f], own_buf.at[f, slot], lat_send.at[j, f], lat_recv.at[f, slot], lay.space_target(me, j),
        )

    def fellow_copy(turn, f):
        return (
            own_buf.at[f], other_buf.at[f, turn - 1], fellow_send.at[turn - 1, f], fellow_recv.at[turn - 1, f],
            lay.fellow(me, turn),
        )

    def state_copy(turn, f):
        place = lay.across(me, turn)
        row = pl.multiple_of(place["ta"] * lay.time_patches, TILE)
        return (
            sent_buf.at[f, pl.ds(row, lay.time_patches)], state_ref.at[me["ta"] * frames + f], state_send.at[turn, f],
            state_recv.at[turn, f], place,
        )

    def cot_copy(j, s):
        return (
            cot_ref.at[j, :, pl.ds(s * lay.time_patches, lay.time_patches)],
            moved_ref.at[pl.ds(me["ta"] * frames, frames)],
            cot_send.at[j, s], cot_recv.at[me["ta"]], lay.time_target(me, j, s),
        )

    def start_latents(f):
        for j in range(lay.clips_dev):
            start_push(me, *latent_copy(j, f))

    def pass_on(f):
        for slot in range(near):
            arrived(own_buf.at[f, slot], lat_recv.at[f, slot])
        for turn in range(1, lay.group):
            push(*fellow_copy(turn, f)).start()

    @pl.when(step == 0)
    def _():
        for slot in range(near):
            greet(me, lay.owner(me, me["ta"], slot))
        for t in range(lay.n_ta):
            greet(me, lay.owner(me, t, me["ta"] // lay.halves))
        friends = [lay.fellow(me, turn) for turn in range(1, lay.group)]
        friends += [lay.across(me, turn) for turn in range(1, lay.n_ta)]
        for friend in friends:
            greet(me, friend)
        targets = [lay.space_target(me, j) for j in range(lay.clips_dev)]
        targets += [lay.time_target(me, j, s) for j in range(lay.clips_dev) for s in range(lay.halves)]
        await_greetings(me, targets + friends)
        for f in range(frames):
            start_latents(f)
        pass_on(0)

    @pl.when(step == min(2, frames - 1))
    def _():
        for j in range(lay.clips_dev):
            for s in range(lay.halves):
                start_push(me, *cot_copy(j, s))

    for turn in range(1, lay.group):
        arrived(other_buf.at[step, turn - 1], fellow_recv.at[turn - 1, step])
    frame = counts_ref[2] + step
    keep = (frame < counts_ref[0]).astype(F32)
    mod = mod_ref[...]
    own_low = own_buf[step].reshape(lay.space_rows, lay.width)
    own_ref[0] = own_low
    own = own_low.astype(F32)
    rows = lay.space_rows
    normed_own = (norm_parts(own)[0] * (1.0 + mod[1:2]) + mod[0:1]).astype(BF)
    other = other_buf[step].reshape(lay.other_rows, lay.width).astype(F32)
    normed_other = (norm_parts(other)[0] * (1.0 + mod[1:2]) + mod[0:1]).astype(BF)
    normed = jnp.concatenate([normed_own, normed_other], axis=0)
    normed_ref[0] = normed
    queries = (dot(normed_own, attn_ref[0]).astype(BF) * scale_by).astype(BF)
    keys = dot(normed, attn_ref[1]).astype(BF)
    values = dot(normed, attn_ref[2]).astype(BF)
    query_ref[0] = queries
    value_ref[0] = values
    keys_t_ref[0] = dot_nt(turned_ref[0], normed).astype(BF)
    values_t = dot_nt(turned_ref[1], normed).astype(BF)

    def keep_exponent(_, head, keys_span, span, exponent):
        exponent_ref[0, head, keys_span, span] = exponent

    (att_t,), (inverses,) = attend([(queries, keys, values_t, None)], SPACE_STAGE, keep_exponent)
    for head in range(HEADS):
        inverse_ref[0, head : head + 1, :] = inverses[head]
    att_t_ref[0] = att_t.astype(BF)
    att = att_t.T.astype(BF)
    att_ref[0] = att

    @pl.when(jnp.logical_not(last))
    def _():
        pass_on(step + 1)

    branch = dot(att_ref[0], attn_ref[3])
    branch2_ref[0] = branch.astype(BF)
    state = own_ref[0].astype(F32) + (keep * mod[2:3]) * branch
    cross_in = state.astype(BF)
    cross_in_ref[0] = cross_in
    cross_queries = (dot(cross_in, cross_ref[0]).astype(BF) * scale_by).astype(BF)
    cross_query_ref[0] = cross_queries
    text_id = lax.broadcasted_iota(jnp.int32, (text_keys_ref.shape[0], rows), 0)
    bias = jnp.where(text_id < counts_ref[1], 0.0, MASKED_SCORE)

    def keep_cross(_, head, keys_span, span, exponent):
        cross_exponent_ref[0, head, keys_span, span] = exponent

    (cross_t,), (inverses,) = attend(
        [(cross_queries, text_keys_ref[...], text_values_t_ref[...], bias)], CROSS_AHEAD, keep_cross
    )
    for head in range(HEADS):
        cross_inverse_ref[0, head : head + 1, :] = inverses[head]
    cross_att_t_ref[0] = cross_t.astype(BF)
    cross_att = cross_t.T.astype(BF)
    cross_att_ref[0] = cross_att
    state = state + keep * dot(cross_att, cross_ref[1])
    middle_ref[0] = state
    normed2 = (norm_parts(state)[0] * (1.0 + mod[4:5]) + mod[3:4]).astype(BF)
    normed2_ref[0] = normed2
    act, slope = gelu_parts(dot(normed2, up_ref[...]))
    act = act.astype(BF)
    act_ref[0] = act
    slope_ref[0] = slope.astype(BF)
    branch = dot(act, down_ref[...])
    branch5_ref[0] = branch.astype(BF)
    state = state + (keep * mod[5:6]) * branch
    sent_buf[step] = state.astype(BF)
    src, dst, _, sem, _ = state_copy(0, step)
    pltpu.make_async_copy(src, dst, sem).start()
    for turn in range(1, lay.n_ta):
        push(*state_copy(turn, step)).start()

    @pl.when(last)
    def _():
        for f in range(frames):
            for j in range(lay.clips_dev):
                end_push(me, *latent_copy(j, f))
            for turn in range(1, lay.group):
                push(*fellow_copy(turn, f)).wait_send()
            for turn in range(1, lay.n_ta):
                push(*state_copy(turn, f)).wait_send()
            for turn in range(lay.n_ta):
                src, dst, _, sem, _ = state_copy(turn, f)
                arrived(dst, sem)
        for j in range(lay.clips_dev):
            for s in range(lay.halves):
                end_push(me, *cot_copy(j, s))
        for t in range(lay.n_ta):
            arrived(moved_ref.at[pl.ds(t * frames, frames)], cot_recv.at[t])


def space_backward_kernel(
    lay,
    reducer,
    counts_ref,
    grad_ref,
    out_t_ref,
    exponent_ref,
    *refs,
):
    n_sources = len(reducer.shapes)
    sources, refs = refs[:n_sources], refs[n_sources:]
    (mod_ref, attn_ref, cross_ref, text_keys_t_ref, text_values_ref, up_ref, down_ref, own_ref, query_ref, keys_t_ref,
     value_ref, att_t_ref, inverse_ref, cross_query_ref, cross_exponent_ref, cross_att_t_ref, cross_inverse_ref,
     middle_ref, slope_ref, branch2_ref, branch5_ref) = refs[:21]
    (output_ref, lat_grad_ref, reduced_ref, kept3_ref, d_lifted_ref, kept2_ref, d_cross_query_ref, kept1_ref,
     d_query_ref, d_key_ref, d_value_ref, d_text_keys_ref, d_text_values_ref, mods_ref) = refs[21:35]
    (exponent_buf, other_buf, fellow_buf, state_buf, own_buf, done_buf, exponent_sem, fellow_send, fellow_recv,
     out_send, out_recv, grad_send, grad_recv) = refs[35:48]
    reducer.bind(sources, reduced_ref, refs[48:])
    scale_by = HDIM ** (-0.5)
    me = lay.here()
    step = pl.program_id(0)
    frames = lay.frames
    rows = lay.space_rows
    mod = mod_ref[...]

    def hook(number):
        for f in range(frames):
            places = frames * 3 - 1
            due = [k for k in range(reducer.phases) if 1 + k * places // reducer.phases == f * 3 + number]
            if f == 0 and number == 0:
                due = [-1]
            if due:

                @pl.when(step == f)
                def _():
                    for k in due:
                        reducer.phase(k) if k >= 0 else reducer.prepare()

    def exponent_copy(head, f):
        return pltpu.make_async_copy(exponent_ref.at[f, head], exponent_buf.at[head], exponent_sem.at[head])

    def fellow_copy(turn, f):
        return (
            other_buf.at[f % 2, turn - 1], fellow_buf.at[f, turn - 1], fellow_send.at[turn - 1, f],
            fellow_recv.at[turn - 1, f], lay.fellow(me, -turn),
        )

    def out_copy(t):
        part, j = me["ta"] % lay.halves, lay.clip(me) % lay.clips_dev
        return (
            out_t_ref.at[pl.ds(t * frames, frames)], output_ref.at[j, :, part], out_send.at[t],
            out_recv.at[j, part], lay.owner(me, t, me["ta"] // lay.halves),
        )

    def grad_copy(slot, f):
        j = lay.clip(me) % lay.clips_dev
        return (
            done_buf.at[f, slot], lat_grad_ref.at[j, f], grad_send.at[slot, f], grad_recv.at[j, f],
            lay.owner(me, me["ta"], slot),
        )

    @pl.when(step == 0)
    def _():
        for head in range(HEADS):
            exponent_copy(head, 0).start()
        fellows = [lay.fellow(me, turn) for turn in range(1, lay.group)]
        senders = [lay.space_target(me, j) for j in range(lay.clips_dev)]
        senders += [lay.time_target(me, j, s) for j in range(lay.clips_dev) for s in range(lay.halves)]
        for place in fellows + senders:
            greet(me, place)
        takers = [lay.owner(me, me["ta"], slot) for slot in range(lay.near)]
        takers += [lay.owner(me, t, me["ta"] // lay.halves) for t in range(lay.n_ta)]
        await_greetings(me, fellows + takers, reducer.greet())
        for t in range(lay.n_ta):
            start_push(me, *out_copy(t))

    mods_ref[0] = jnp.zeros(mods_ref.shape[1:], F32)

    @pl.when(step < frames)
    def _():
        hook(0)
        keep = (counts_ref[2] + step < counts_ref[0]).astype(F32)
        grad = grad_ref[0].astype(F32)
        kept = keep * grad
        d_gate5 = row_sums(kept * branch5_ref[0].astype(F32))
        d_branch = (kept * mod[5:6]).astype(BF)
        kept3_ref[0] = d_branch
        d_act = dot_nt(d_branch, down_ref[...])
        d_lifted = (d_act * slope_ref[0].astype(F32)).astype(BF)
        d_lifted_ref[0] = d_lifted
        d_normed = dot_nt(d_lifted, up_ref[...])
        hat, inverse = norm_parts(middle_ref[0])
        grad = grad + norm_back(d_normed, hat, inverse, mod[4:5])
        d_shift, d_scale = row_sums(d_normed), row_sums(d_normed * hat)
        kept = (keep * grad).astype(BF)
        kept2_ref[0] = kept
        d_att_t = dot_nt(cross_ref[1], kept)
        job = (
            lambda head, at: cross_exponent_ref[0, head, at, :],
            lambda pair: cross_query_ref[0, :, pair * LANES : (pair + 1) * LANES],
            lambda head, at: text_keys_t_ref[head * HDIM : (head + 1) * HDIM, at],
            lambda pair, at: text_values_ref[at, pair * LANES : (pair + 1) * LANES],
            d_att_t,
            cross_att_t_ref[0].astype(F32),
            lambda head: cross_inverse_ref[0, head : head + 1, :],
            text_values_ref.shape[0],
            None,
        )
        ((d_query_t, d_keys, d_values),) = attend_back([job], CROSS_AHEAD, KEY_CHUNK)
        d_text_keys_ref[0] = d_keys
        d_text_values_ref[0] = d_values
        d_query = (d_query_t.T * scale_by).astype(BF)
        d_cross_query_ref[0] = d_query
        grad = grad + dot_nt(d_query, cross_ref[0])
        state_buf[step % 2] = grad
        kept = keep * grad
        d_gate2 = row_sums(kept * branch2_ref[0].astype(F32))
        mods_ref[0, 2:6, :] = jnp.concatenate([d_gate2, d_shift, d_scale, d_gate5], axis=0)
        d_branch = (kept * mod[2:3]).astype(BF)
        kept1_ref[0] = d_branch
        hook(1)
        d_att_t = dot_nt(attn_ref[3], kept1_ref[0])
        later = jnp.minimum(step + 1, frames - 1)

        def exponent_of(head, at):
            if at.start == 0:
                exponent_copy(head, step).wait()
            return exponent_buf[head, at, :]

        job = (
            exponent_of,
            lambda pair: query_ref[0, :, pair * LANES : (pair + 1) * LANES],
            lambda head, at: keys_t_ref[0, head * HDIM : (head + 1) * HDIM, at],
            lambda pair, at: value_ref[0, at, pair * LANES : (pair + 1) * LANES],
            d_att_t,
            att_t_ref[0].astype(F32),
            lambda head: inverse_ref[0, head : head + 1, :],
            value_ref.shape[1],
            lambda head: exponent_copy(head, later).start(),
        )
        ((d_query_t, d_keys, d_values),) = attend_back([job], BACK_STAGE, KEY_CHUNK)
        d_query = (d_query_t.T * scale_by).astype(BF)
        d_keys, d_values = d_keys.astype(BF), d_values.astype(BF)
        d_query_ref[0] = d_query
        d_key_ref[0] = d_keys
        d_value_ref[0] = d_values
        d_normed = dot_nt(d_keys, attn_ref[1]) + dot_nt(d_values, attn_ref[2])
        own_buf[step % 2] = d_normed[:rows] + dot_nt(d_query, attn_ref[0])

        @pl.when(step > 1)
        def _():
            for turn in range(1, lay.group):
                push(*fellow_copy(turn, step - 2)).wait_send()

        for turn in range(1, lay.group):
            other_buf[step % 2, turn - 1] = d_normed[turn * rows : (turn + 1) * rows].astype(BF)
            push(*fellow_copy(turn, step)).start()
        hook(2)

    @pl.when(step > 0)
    def _():
        f = step - 1
        d_normed = own_buf[f % 2]
        for turn in range(1, lay.group):
            arrived(fellow_buf.at[f, turn - 1], fellow_recv.at[turn - 1, f])
            d_normed = d_normed + fellow_buf[f, turn - 1].astype(F32)
        hat, inverse = norm_parts(own_ref[0].astype(F32))
        grad = state_buf[f % 2] + norm_back(d_normed, hat, inverse, mod[1:2])
        done_buf[f] = grad.astype(BF).reshape(done_buf.shape[1:])
        mods_ref[0, 0:2, :] = jnp.concatenate([row_sums(d_normed), row_sums(d_normed * hat)], axis=0)
        for slot in range(lay.near):
            start_push(me, *grad_copy(slot, f))

    @pl.when(step == frames)
    def _():
        for head in range(HEADS):
            exponent_copy(head, frames - 1).wait()
        for turn in range(1, lay.group):
            for f in range(max(frames - 2, 0), frames):
                push(*fellow_copy(turn, f)).wait_send()
        for t in range(lay.n_ta):
            end_push(me, *out_copy(t))
        for f in range(frames):
            for slot in range(lay.near):
                end_push(me, *grad_copy(slot, f))
        for j in range(lay.clips_dev):
            for s in range(lay.halves):
                arrived(output_ref.at[j, :, s], out_recv.at[j, s])
            for f in range(frames):
                arrived(lat_grad_ref.at[j, f], grad_recv.at[j, f])


def interleave(streams, lag):
    live, turn = list(enumerate(streams)), 0
    while live:
        left = []
        for i, stream in live:
            if turn < i * lag or next(stream, DONE) is not DONE:
                left.append((i, stream))
        live, turn = left, turn + 1


DONE = object()


def time_kernel(
    lay,
    counts_ref,
    state_ref,
    cot_ref,
    mod_ref,
    bias_ref,
    qkv_ref,
    proj_ref,
    up_ref,
    down_ref,
    grad_s_ref,
    early_ref,
    late_ref,
    d_qkv_sum_ref,
    d_proj_sum_ref,
    d_up_sum_ref,
    d_down_sum_ref,
    mods_ref,
    exponent_ref,
    sent_buf,
    out_buf,
    d_qkv_sum,
    d_proj_sum,
    d_up_sum,
    d_down_sum,
    normed_ref,
    d_qkv_ref,
    att_ref,
    branch4_ref,
    normed2_ref,
    act_ref,
    d_lifted_ref,
    branch5_ref,
    grad_send,
    grad_recv,
    out_send,
    out_recv,
):
    frames, block, width = state_ref.shape
    me = lay.here()
    step = pl.program_id(0)
    last = pl.num_programs(0) - 1

    def grad_copy(turn, i):
        place = lay.across(me, turn)
        row = pl.multiple_of(me["ta"] * lay.time_patches + i * block, TILE)
        return (
            sent_buf.at[i, pl.ds(place["ta"] * lay.frames, lay.frames)], grad_s_ref.at[:, pl.ds(row, block)],
            grad_send.at[turn, i], grad_recv.at[turn, i], place,
        )

    def out_copy(t, i):
        part, j = me["ta"] % lay.halves, lay.clip(me) % lay.clips_dev
        return (
            out_buf.at[i, pl.ds(t * lay.frames, lay.frames)], early_ref.at[j, :, part, pl.ds(i * block, block)],
            out_send.at[t, i], out_recv.at[j, part, i], lay.owner(me, t, me["ta"] // lay.halves),
        )

    early = lay.time_patches // block - 1

    @pl.when(step == 0)
    def _():
        friends = [lay.across(me, turn) for turn in range(1, lay.n_ta)]
        senders, takers = [], []
        if early:
            senders = [lay.time_target(me, j, s) for j in range(lay.clips_dev) for s in range(lay.halves)]
            takers = [lay.owner(me, t, me["ta"] // lay.halves) for t in range(lay.n_ta)]
        for place in friends + senders:
            greet(me, place)
        await_greetings(me, friends + takers)
        for total in (d_qkv_sum, d_proj_sum, d_up_sum, d_down_sum):
            total[...] = jnp.zeros_like(total)

    @pl.when(step > 0)
    def _():
        for t in range(lay.n_ta):
            start_push(me, *out_copy(t, step - 1))

    scale_by = HDIM ** (-0.5)
    run_rows = frames * SUB
    runs = min(STREAM_RUNS, block // SUB)
    mod = mod_ref[...]
    totals = []

    def stream(first_run):
        patches = slice(first_run * SUB, (first_run + runs) * SUB)
        mine = slice(first_run * run_rows, (first_run + runs) * run_rows)

        def load(ref):
            cube = ref[:, patches, :].astype(F32)
            parts = [cube[:, r * SUB : (r + 1) * SUB].reshape(run_rows, width) for r in range(runs)]
            return jnp.concatenate(parts, axis=0)

        def stored(value):
            parts = [value[r * run_rows : (r + 1) * run_rows].reshape(frames, SUB, width) for r in range(runs)]
            return jnp.concatenate(parts, axis=1).astype(BF)

        def run_of(value, r):
            return value[r * run_rows : (r + 1) * run_rows]

        state = load(state_ref)
        frame = (lax.broadcasted_iota(jnp.int32, (runs * run_rows, 1), 0) // SUB) % frames
        keep = (frame < counts_ref[0]).astype(F32)
        hat1, inverse1 = norm_parts(state)
        normed = (hat1 * (1.0 + mod[1:2]) + mod[0:1]).astype(BF)
        normed_ref[mine] = normed
        yield
        qkv = dot(normed, qkv_ref[...])
        queries = (qkv[:, :width].astype(BF) * scale_by).astype(BF)
        keys = qkv[:, width : 2 * width].astype(BF)
        values = qkv[:, 2 * width :].astype(BF)
        yield
        keys_t_runs, jobs = [], []
        for r in range(runs):
            keys_t_runs.append(run_of(keys, r).T)
            jobs.append((run_of(queries, r), run_of(keys, r), run_of(values, r).T, bias_ref[...]))

        def keep_exponent(r, head, keys_span, span, exponent):
            exponent_ref[first_run + r, head, keys_span, span] = exponent

        att_t_runs, inverse_runs = attend(jobs, TIME_STAGE, keep_exponent)
        yield
        att = jnp.concatenate([att_t.T.astype(BF) for att_t in att_t_runs], axis=0)
        att_ref[mine] = att
        branch2 = dot(att, proj_ref[...])
        yield
        state = state + (keep * mod[2:3]) * branch2
        hat2, inverse2 = norm_parts(state)
        normed2 = (hat2 * (1.0 + mod[4:5]) + mod[3:4]).astype(BF)
        normed2_ref[mine] = normed2
        yield
        lifted = dot(normed2, up_ref[...])
        yield
        act, slope = gelu_parts(lifted)
        act = act.astype(BF)
        act_ref[mine] = act
        grad = load(cot_ref)
        kept = keep * grad
        d_branch = (kept * mod[5:6]).astype(BF)
        branch5_ref[mine] = d_branch
        yield
        d_act = dot_nt(d_branch, down_ref[...])
        yield
        d_lifted = (d_act * slope).astype(BF)
        d_lifted_ref[mine] = d_lifted
        branch5 = dot(act, down_ref[...])
        yield
        final = stored(state + (keep * mod[5:6]) * branch5)
        out_buf[step, :, patches, :] = final
        late_ref[:, patches, :] = final
        d_gate5 = row_sums(kept * branch5)
        d_normed2 = dot_nt(d_lifted, up_ref[...])
        yield
        grad = grad + norm_back(d_normed2, hat2, inverse2, mod[4:5])
        kept = keep * grad
        d_gate2 = row_sums(kept * branch2)
        d_branch = (kept * mod[2:3]).astype(BF)
        branch4_ref[mine] = d_branch
        yield
        d_att_t_runs = [dot_nt(proj_ref[...], run_of(d_branch, r)) for r in range(runs)]
        yield

        def job(r):
            query_run, value_run = run_of(queries, r), run_of(values, r)
            return (
                lambda head, at: exponent_ref[first_run + r, head, at, :],
                lambda pair: pair_of(query_run, pair),
                lambda head, at: head_rows(keys_t_runs[r], head)[:, at],
                lambda pair, at: pair_of(value_run, pair)[at],
                d_att_t_runs[r],
                att_t_runs[r],
                lambda head: inverse_runs[r][head],
                run_rows,
                None,
            )

        backs = attend_back([job(r) for r in range(runs)], TIME_STAGE, run_rows)
        yield
        d_qkv = jnp.concatenate(
            [
                jnp.concatenate([(d_query_t.T * scale_by).astype(BF) for d_query_t, _, _ in backs], axis=0),
                jnp.concatenate([d_keys.astype(BF) for _, d_keys, _ in backs], axis=0),
                jnp.concatenate([d_values.astype(BF) for _, _, d_values in backs], axis=0),
            ],
            axis=1,
        )
        d_qkv_ref[mine] = d_qkv
        d_normed1 = dot_nt(d_qkv, qkv_ref[...])
        yield
        grad = grad + norm_back(d_normed1, hat1, inverse1, mod[1:2])
        sent_buf[step, :, patches, :] = stored(grad)
        totals.append(
            jnp.concatenate(
                [
                    row_sums(d_normed1),
                    row_sums(d_normed1 * hat1),
                    d_gate2,
                    row_sums(d_normed2),
                    row_sums(d_normed2 * hat2),
                    d_gate5,
                    jnp.zeros((2, width), F32),
                ],
                axis=0,
            )
        )

    interleave([stream(first) for first in range(0, block // SUB, runs)], TIME_LAG)
    mods_ref[0] = sum(totals[1:], totals[0])
    src, dst, _, sem, _ = grad_copy(0, step)
    pltpu.make_async_copy(src, dst, sem).start()
    for turn in range(1, lay.n_ta):
        push(*grad_copy(turn, step)).start()

    d_qkv_sum[...] += dot_tn(normed_ref[...], d_qkv_ref[...])
    d_proj_sum[...] += dot_tn(att_ref[...], branch4_ref[...])
    d_up_sum[...] += dot_tn(normed2_ref[...], d_lifted_ref[...])
    d_down_sum[...] += dot_tn(branch5_ref[...], act_ref[...])

    @pl.when(step == last)
    def _():
        d_qkv_sum_ref[...] = d_qkv_sum[...].astype(BF)
        d_proj_sum_ref[...] = d_proj_sum[...].astype(BF)
        d_up_sum_ref[...] = d_up_sum[...].astype(BF)
        d_down_sum_ref[...] = d_down_sum[...].astype(BF)
        for i in range(early):
            for t in range(lay.n_ta):
                end_push(me, *out_copy(t, i))
            for j in range(lay.clips_dev):
                for s in range(lay.halves):
                    arrived(early_ref.at[j, :, s, i * block : (i + 1) * block], out_recv.at[j, s, i])
        for i in range(lay.time_patches // block):
            for turn in range(lay.n_ta):
                src, dst, _, sem, place = grad_copy(turn, i)
                if turn:
                    push(*grad_copy(turn, i)).wait_send()
                arrived(dst, sem)


class Reducer:
    def __init__(self, shapes, small_rows, sizes, parts):
        self.width = width = shapes[0][1]
        self.shapes = shapes
        bits = {name: [(name, 1 << i) for i in range(sizes[name].bit_length() - 1)] for name in ("ta", "pa")}
        kinds = [bits["ta"] + bits["pa"], bits["ta"][::-1] + bits["pa"], bits["pa"] + bits["ta"]]
        self.ways = [("dev", 1)] + kinds[0]
        self.loads, row = [], 0
        for i, shape in enumerate(shapes):
            for column in range(shape[1] // width):
                self.loads.append((i, row, column * width, shape[0]))
                row += shape[0]
        self.total = row
        cut = TILE << sum(len(ways) for ways in bits.values())
        self.parts = next((n for n in parts if row % (2 * n * cut) == 0), 1)
        self.part_rows = row // 2 // self.parts
        self.half_rows = row // 2
        self.orders = [[("dev", 1)] + kinds[PATTERN[p % len(PATTERN)]] for p in range(self.parts)]
        self.steps = len(self.ways)
        self.small_rows = small_rows
        self.counts, self.halves, self.boxes, at = [self.part_rows], [True], [], 0
        for _ in range(1, self.steps):
            halve = (self.counts[-1] // 2) % TILE == 0
            self.halves.append(halve)
            self.counts.append(self.counts[-1] // 2 if halve else self.counts[-1])
        for p in range(self.parts):
            self.boxes.append([])
            for count in self.counts:
                self.boxes[p].append(at)
                at += count
        self.box_rows = at
        self.phases = 2 * self.steps + 1

    def scratch(self):
        shapes = [
            pltpu.VMEM((self.total, self.width), BF),
            pltpu.VMEM((self.total, self.width), BF),
            pltpu.VMEM((self.box_rows, self.width), BF),
            pltpu.SemaphoreType.DMA((len(self.loads),)),
            pltpu.SemaphoreType.DMA((self.parts, 2)),
            pltpu.SemaphoreType.DMA((self.parts, 2 * self.steps)),
            pltpu.SemaphoreType.DMA((self.parts, 2 * self.steps)),
        ]
        if self.small_rows:
            shapes += [
                pltpu.VMEM((self.steps, self.small_rows, self.width), F32),
                pltpu.SemaphoreType.DMA((self.steps,)),
                pltpu.SemaphoreType.DMA((self.steps,)),
            ]
        return shapes

    def bind(self, sources, out, scratch, small_in=None, small_out=None):
        self.sources, self.out = sources, out
        self.work, self.whole, self.inbox, self.in_sem, self.out_sem, self.send_sem, self.recv_sem = scratch[:7]
        self.small_in, self.small_out = small_in, small_out
        if self.small_rows:
            self.small_box, self.small_send, self.small_recv = scratch[7:]

    def bit(self, way):
        return (lax.axis_index(way[0]) // way[1]) % 2

    def peer(self, way):
        return {way[0]: lax.axis_index(way[0]) + way[1] - 2 * way[1] * self.bit(way)}

    def greet(self):
        barrier = pltpu.get_barrier_semaphore()
        for way in self.ways:
            pl.semaphore_signal(barrier, inc=1, device_id=self.peer(way), device_id_type=pl.DeviceIdType.MESH)
        return len(self.ways)

    def base(self, p, step):
        row = self.bit(self.orders[p][0]) * self.half_rows + p * self.part_rows
        for s in range(1, step + 1):
            if self.halves[s]:
                row = row + self.bit(self.orders[p][s]) * self.counts[s]
        return row

    def rows(self, ref, row, count):
        return ref.at[pl.ds(pl.multiple_of(row, TILE), count)]

    def load(self, i):
        source, row, column, rows = self.loads[i]
        view = self.sources[source].at[:, column : column + self.width]
        return pltpu.make_async_copy(view, self.work.at[row : row + rows], self.in_sem.at[i])

    def remote(self, src, dst, p, step, way):
        return pltpu.make_async_remote_copy(
            src_ref=src,
            dst_ref=dst,
            send_sem=self.send_sem.at[p, step],
            recv_sem=self.recv_sem.at[p, step],
            device_id=self.peer(way),
            device_id_type=pl.DeviceIdType.MESH,
        )

    def down(self, p, step):
        way, count = self.orders[p][step], self.counts[step]
        if step == 0:
            row = (1 - self.bit(way)) * self.half_rows + p * self.part_rows
        else:
            row = self.base(p, step - 1)
            if self.halves[step]:
                row = row + (1 - self.bit(way)) * count
        box = self.boxes[p][step]
        return self.remote(self.rows(self.work, row, count), self.inbox.at[box : box + count], p, step, way)

    def end_down(self, p, step):
        self.down(p, step).wait()
        count, base, box = self.counts[step], self.base(p, step), self.boxes[p][step]
        chunk = next(c for c in (96, 64, 48, 32, TILE) if count % c == 0)

        def body(i, carry):
            at = pl.ds(pl.multiple_of(base + i * chunk, TILE), chunk)
            got = self.inbox[pl.ds(pl.multiple_of(box + i * chunk, TILE), chunk), :]
            total = (self.work[at, :].astype(F32) + got.astype(F32)).astype(BF)
            if step == self.steps - 1:
                self.whole[at, :] = total
            else:
                self.work[at, :] = total
            return carry

        lax.fori_loop(0, count // chunk, body, 0)

    def up(self, p, turn):
        step = self.steps - 1 - turn
        if not self.halves[step]:
            return None
        rows = self.rows(self.whole, self.base(p, step), self.counts[step])
        return self.remote(rows, rows, p, self.steps + turn, self.orders[p][step])

    def store(self, p, side):
        rows = pl.ds(side * self.half_rows + p * self.part_rows, self.part_rows)
        return pltpu.make_async_copy(self.whole.at[rows], self.out.at[rows], self.out_sem.at[p, side])

    def small(self, step):
        return pltpu.make_async_remote_copy(
            src_ref=self.small_out,
            dst_ref=self.small_box.at[step],
            send_sem=self.small_send.at[step],
            recv_sem=self.small_recv.at[step],
            device_id=self.peer(self.ways[step]),
            device_id_type=pl.DeviceIdType.MESH,
        )

    def prepare(self):
        for i in range(len(self.loads)):
            self.load(i).start()
        if self.small_rows:
            self.small_out[...] = self.small_in[...]

    def phase(self, k):
        n = self.steps
        if k == 0:
            for i in range(len(self.loads)):
                self.load(i).wait()
        for p in range(self.parts):
            if 1 <= k <= n:
                self.end_down(p, k - 1)
            elif k > n:
                before = self.up(p, k - n - 1)
                if before is not None:
                    before.wait()
            if k < n:
                self.down(p, k).start()
            elif k < 2 * n:
                after = self.up(p, k - n)
                if after is not None:
                    after.start()
            else:
                self.store(p, 0).start()
                self.store(p, 1).start()
        if k == 2 * n:
            for p in range(self.parts):
                self.store(p, 0).wait()
                self.store(p, 1).wait()
        if self.small_rows and k <= n:
            if k > 0:
                self.small(k - 1).wait()
                self.small_out[...] = self.small_out[...] + self.small_box[k - 1]
            if k < n:
                self.small(k).start()

    def unpack(self, reduced):
        results, at = [], 0
        for rows, columns in self.shapes:
            turns = columns // self.width
            blocks = [reduced[at + i * rows : at + (i + 1) * rows] for i in range(turns)]
            at += turns * rows
            results.append((blocks[0] if turns == 1 else jnp.concatenate(blocks, axis=1)).astype(F32))
        return results


def reduce_all(arrays, small, sizes):
    reducer = Reducer([a.shape for a in arrays], small.shape[0], sizes, PARTS)
    n = len(arrays)

    def kernel(*refs):
        reducer.bind(refs[:n], refs[n + 1], refs[n + 3 :], refs[n], refs[n + 2])
        reducer.prepare()
        pl.semaphore_wait(pltpu.get_barrier_semaphore(), reducer.greet())
        for k in range(reducer.phases):
            reducer.phase(k)

    any_spec, vmem_spec = pl.BlockSpec(memory_space=pl.ANY), pl.BlockSpec(memory_space=pltpu.VMEM)
    reduced, small_sum = pl.pallas_call(
        kernel,
        in_specs=[any_spec] * n + [vmem_spec],
        out_specs=[any_spec, vmem_spec],
        out_shape=[shape_of((reducer.total, reducer.width), BF), shape_of(small.shape, F32)],
        scratch_shapes=reducer.scratch(),
        compiler_params=pltpu.CompilerParams(collective_id=0, has_side_effects=True, vmem_limit_bytes=VMEM_BYTES),
        cost_estimate=pl.CostEstimate(
            flops=8 * reducer.total * reducer.width, bytes_accessed=4 * reducer.total * reducer.width, transcendentals=0
        ),
    )(*arrays, small)
    return reducer.unpack(reduced), small_sum


def whole(array):
    zeros = (0,) * array.ndim
    return pl.BlockSpec(array.shape, lambda *grid: zeros)


def framed(array):
    tail = (0,) * (array.ndim - 1)
    return pl.BlockSpec((1,) + tuple(array.shape[1:]), lambda frame: (frame,) + tail)


SCALARS = pl.BlockSpec(memory_space=pltpu.SMEM)
HBM = pl.BlockSpec(memory_space=pl.ANY)


def shape_of(shape, dtype):
    return jax.ShapeDtypeStruct(shape, dtype)


def call(kernel, grid, inputs, in_specs, outputs, out_specs, flops, scratch=(), collective_id=None):
    moved = sum(math.prod(a.shape) * a.dtype.itemsize for a in (*inputs, *outputs))
    return pl.pallas_call(
        kernel,
        grid=grid,
        in_specs=in_specs,
        out_specs=out_specs,
        out_shape=outputs,
        scratch_shapes=list(scratch),
        compiler_params=pltpu.CompilerParams(
            vmem_limit_bytes=VMEM_BYTES, collective_id=collective_id, has_side_effects=collective_id is not None
        ),
        cost_estimate=pl.CostEstimate(flops=int(flops), bytes_accessed=int(moved), transcendentals=0),
    )(*inputs)


def make_per_device(sizes):
    n_ta, n_pa, n_dev = sizes["ta"], sizes["pa"], sizes["dev"]

    def per_device(
        latents,
        context,
        cotangent,
        timesteps,
        frame_counts,
        text_lengths,
        step_proj,
        mod_table,
        patch_attn,
        cross_attn,
        patch_up,
        patch_down,
        frame_attn,
        frame_up,
        frame_down,
    ):
        lay = Layout(sizes, latents.shape)
        clips_dev, frames, patches, width = latents.shape
        clips, run, group, near, halves = lay.clips, lay.run, lay.group, lay.near, lay.halves
        space_rows, other_rows, key_rows = lay.space_rows, lay.other_rows, lay.key_rows
        time_patches, all_frames = lay.time_patches, lay.all_frames
        ta, pa, dev = (lax.axis_index(name) for name in ("ta", "pa", "dev"))
        clip, member = lay.clip(lay.here()), lay.member(lay.here())

        def place(clip_id, member_id):
            return (clip_id * run + member_id % run) * n_dev + member_id // run

        def space_pairs(step):
            pairs = []
            for p in range(n_pa):
                for d in range(n_dev):
                    k = d * clips_dev + (p + step) % clips_dev
                    pairs.append((p * n_dev + d, place(k, p // near)))
            return pairs

        def time_pairs(step):
            u, w = step % halves, step // halves
            pairs = []
            for t in range(n_ta):
                for p in range(n_pa):
                    for d in range(n_dev):
                        s = (t % halves + u) % halves
                        j = (t // halves + w) % clips_dev
                        k = d * clips_dev + j
                        pairs.append(
                            (
                                (t * n_pa + p) * n_dev + d,
                                ((p % near) * halves + s) * n_pa * n_dev + place(k, p // near),
                            )
                        )
            return pairs

        def back(pairs):
            return [(b, a) for a, b in pairs]

        def group_pairs(step):
            return [
                (place(k, g), place(k, (g + step) % group)) for k in range(clips) for g in range(group)
            ]

        def ta_pairs(step):
            return [(t, t ^ step) for t in range(n_ta)]

        whole_axes = ("ta", "pa", "dev")
        pair_axes = ("pa", "dev")

        def of_clip(local):
            both = lax.all_gather(local, "dev", axis=0, tiled=True)
            return lax.dynamic_index_in_dim(both, clip, 0, keepdims=False)

        def sinusoid(steps):
            half = step_proj.shape[0] // 2
            frequency = jnp.exp(-math.log(10000.0) * jnp.arange(half, dtype=F32) / half)
            angles = steps.astype(F32)[:, None] * frequency[None, :]
            return jnp.concatenate([jnp.cos(angles), jnp.sin(angles)], axis=1)

        numbers = lax.all_gather(jnp.stack([timesteps, frame_counts, text_lengths], axis=1), "dev", axis=0, tiled=True)
        own_numbers = lax.dynamic_index_in_dim(numbers, clip, 0, keepdims=False)
        embeddings = sinusoid(numbers[:, 0])
        embedding = lax.dynamic_index_in_dim(embeddings, clip, 0, keepdims=True)
        timing = jnp.dot(embedding, step_proj.astype(F32), precision=HIGHEST).reshape(6, width)
        table = mod_table.astype(F32)
        pad = jnp.zeros((2, width), F32)
        space_mod = jnp.concatenate([timing + table[0], pad])
        frame_mod = jnp.concatenate([timing + table[1], pad])
        counts = jnp.stack([own_numbers[1], own_numbers[2], ta * frames, 0]).astype(jnp.int32)
        text = of_clip(context)
        text_count = text.shape[0]
        text_rows = -(-text_count // LANES) * LANES
        text_wide = jnp.pad(text, ((0, text_rows - text_count), (0, 0)))
        text_keys = dot(text_wide, cross_attn[1]).astype(BF)
        text_values = dot(text_wide, cross_attn[2]).astype(BF)
        cross_ends = jnp.stack([cross_attn[0], cross_attn[3]])
        patch_turned = jnp.swapaxes(patch_attn[1:3], 1, 2)

        def out(*shape, dtype=BF):
            return shape_of((frames,) + shape, dtype)

        def moved_tokens():
            return shape_of((all_frames, time_patches, width), BF)

        hidden = patch_up.shape[1]
        inputs = (
            counts, latents, cotangent, space_mod, patch_attn, patch_turned, cross_ends, text_keys, text_values.T,
            patch_up, patch_down,
        )
        outputs = (
            moved_tokens(),
            moved_tokens(),
            out(space_rows, width),
            out(key_rows, width),
            out(space_rows, width),
            out(width, key_rows),
            out(key_rows, width),
            out(HEADS, key_rows, space_rows),
            out(width, space_rows),
            out(space_rows, width),
            out(8, space_rows, dtype=F32),
            out(space_rows, width),
            out(space_rows, width),
            out(HEADS, text_rows, space_rows),
            out(width, space_rows),
            out(space_rows, width),
            out(8, space_rows, dtype=F32),
            out(space_rows, width, dtype=F32),
            out(space_rows, width),
            out(space_rows, hidden),
            out(space_rows, hidden),
            out(space_rows, width),
            out(space_rows, width),
        )
        dense = 2 * frames * space_rows * width * (6 * width + 2 * hidden) + 8 * frames * key_rows * width * width
        dma = pltpu.SemaphoreType.DMA
        state, cot, *saved = call(
            lambda *refs: space_forward_kernel(lay, *refs),
            (frames,),
            inputs,
            [SCALARS, HBM, HBM] + [whole(a) for a in inputs[3:]],
            outputs,
            [HBM, HBM] + [framed(a) for a in outputs[2:]],
            dense + 16 * frames * space_rows * key_rows * width,
            [
                pltpu.VMEM((frames, near, patches, width), BF),
                pltpu.VMEM((frames, group - 1, near, patches, width), BF),
                pltpu.VMEM((frames, space_rows, width), BF),
                dma((clips_dev, frames)),
                dma((frames, near)),
                dma((group - 1, frames)),
                dma((group - 1, frames)),
                dma((n_ta, frames)),
                dma((n_ta, frames)),
                dma((clips_dev, halves)),
                dma((n_ta,)),
            ],
            collective_id=1,
        )

        block_rows = all_frames * BLOCK
        run_rows = all_frames * SUB
        ids = jnp.arange(run_rows, dtype=jnp.int32)
        same = (ids[:, None] % SUB == ids[None, :] % SUB) & (ids[:, None] // SUB < counts[0])
        bias = jnp.where(same, 0.0, MASKED_SCORE).astype(F32)
        hidden = frame_up.shape[1]
        n_blocks = time_patches // BLOCK

        early = max(n_blocks - 1, 1) * BLOCK
        frame_wide = frame_attn[:3].swapaxes(0, 1).reshape(width, 3 * width)
        time_inputs = (counts, state, cot, frame_mod, bias, frame_wide, frame_attn[3], frame_up, frame_down)
        time_outputs = (
            out(space_rows, width),
            shape_of((clips_dev, frames, halves, early, width), BF),
            shape_of((all_frames, BLOCK, width), BF),
            shape_of((width, 3 * width), BF),
            shape_of((width, width), BF),
            shape_of((width, hidden), BF),
            shape_of((width, hidden), BF),
            shape_of((n_blocks, 8, width), F32),
        )

        def blocked(array):
            return pl.BlockSpec((all_frames, BLOCK, array.shape[2]), lambda at: (0, at, 0))

        def vmem(*shape, dtype=BF):
            return pltpu.VMEM(shape, dtype)

        (grad_s, early_out, late_out, d_frame_qkv, d_frame_proj, d_frame_up, d_frame_down, frame_six) = call(
            lambda *refs: time_kernel(lay, *refs),
            (n_blocks,),
            time_inputs,
            [SCALARS, blocked(state), blocked(cot)] + [whole(a) for a in time_inputs[3:]],
            time_outputs,
            [HBM, HBM] + [whole(a) for a in time_outputs[2:-1]] + [framed(time_outputs[-1])],
            all_frames * time_patches * width * (32 * width + 20 * hidden),
            [
                vmem(BLOCK // SUB, HEADS, run_rows, run_rows),
                vmem(n_blocks, all_frames, BLOCK, width),
                vmem(n_blocks, all_frames, BLOCK, width),
                vmem(width, 3 * width, dtype=F32),
                vmem(width, width, dtype=F32),
                vmem(width, hidden, dtype=F32),
                vmem(width, hidden, dtype=F32),
                vmem(block_rows, width),
                vmem(block_rows, 3 * width),
                vmem(block_rows, width),
                vmem(block_rows, width),
                vmem(block_rows, width),
                vmem(block_rows, hidden),
                vmem(block_rows, hidden),
                vmem(block_rows, width),
                dma((n_ta, n_blocks)),
                dma((n_ta, n_blocks)),
                dma((n_ta, n_blocks)),
                dma((clips_dev, halves, n_blocks)),
            ],
            collective_id=2,
        )

        def weight_grad(left, right):
            left, right = left.reshape(-1, left.shape[-1]), right.reshape(-1, right.shape[-1])
            return lax.dot_general(left, right, (((0,), (0,)), ((), ())), preferred_element_type=F32).astype(BF)

        (own, _, query, keys_t, value, exponent, att_t, _, inverse, _, cross_query, cross_exponent, cross_att_t, _,
         cross_inverse, middle, _, _, slope, branch2, branch5) = saved
        frame_grads = [d_frame_proj, d_frame_qkv, d_frame_up, d_frame_down]
        reducer = Reducer([a.shape for a in frame_grads], 0, sizes, HIDDEN_PARTS)
        fixed = (space_mod, patch_attn, cross_ends, text_keys.T, text_values, patch_up, patch_down)
        by_frame = (
            query, keys_t, value, att_t, inverse, cross_query, cross_exponent, cross_att_t, cross_inverse, middle,
            slope, branch2, branch5,
        )
        back_outputs = (
            shape_of((clips_dev, frames, halves, BLOCK, width), BF),
            shape_of(latents.shape, BF),
            shape_of((reducer.total, width), BF),
            out(space_rows, width),
            out(space_rows, hidden),
            out(space_rows, width),
            out(space_rows, width),
            out(space_rows, width),
            out(space_rows, width),
            out(key_rows, width),
            out(key_rows, width),
            out(text_rows, width, dtype=F32),
            out(text_rows, width, dtype=F32),
            shape_of((frames + 1, 8, width), F32),
        )

        def now(array):
            tail = (0,) * (array.ndim - 1)
            return pl.BlockSpec((1,) + tuple(array.shape[1:]), lambda at: (jnp.minimum(at, frames - 1),) + tail)

        def before(array):
            tail = (0,) * (array.ndim - 1)
            return pl.BlockSpec((1,) + tuple(array.shape[1:]), lambda at: (jnp.maximum(at, 1) - 1,) + tail)

        dense = 2 * frames * space_rows * width * (6 * width + 2 * hidden) + 8 * frames * key_rows * width * width
        output, lat_grad, frame_sums, *backs = call(
            lambda *refs: space_backward_kernel(lay, reducer, *refs),
            (frames + 1,),
            (counts, grad_s, late_out, exponent, *frame_grads, *fixed, own, *by_frame),
            [SCALARS, now(grad_s), HBM, HBM] + [HBM] * len(frame_grads) + [whole(a) for a in fixed] + [before(own)]
            + [now(a) for a in by_frame],
            back_outputs,
            [HBM, HBM, HBM] + [now(a) for a in back_outputs[3:-1]] + [framed(back_outputs[-1])],
            dense + 32 * frames * space_rows * key_rows * width,
            [
                pltpu.VMEM((HEADS, key_rows, space_rows), BF),
                pltpu.VMEM((2, group - 1, space_rows, width), BF),
                pltpu.VMEM((frames, group - 1, space_rows, width), BF),
                pltpu.VMEM((2, space_rows, width), F32),
                pltpu.VMEM((2, space_rows, width), F32),
                pltpu.VMEM((frames, near, patches, width), BF),
                dma((HEADS,)),
                dma((group - 1, frames)),
                dma((group - 1, frames)),
                dma((n_ta,)),
                dma((clips_dev, halves)),
                dma((near, frames)),
                dma((clips_dev, frames)),
                *reducer.scratch(),
            ],
            collective_id=3,
        )
        latents_grad = lat_grad.astype(F32)
        if n_blocks > 1:
            output = jnp.concatenate([early_out, output], axis=3)
        output = output.reshape(latents.shape)

        kept3, d_lifted2, kept2, d_cross_query, kept1, d_query, d_key, d_value, d_tk, d_tv, space_six = backs
        d_patch_up = weight_grad(saved[16], d_lifted2)
        d_patch_down = weight_grad(saved[17], kept3)
        d_cross_proj = weight_grad(saved[13], kept2)
        d_cross_q = weight_grad(saved[9], d_cross_query)
        text_t = text.astype(F32).T
        d_cross_k = jnp.dot(text_t, jnp.sum(d_tk, axis=0)[:text_count], precision=HIGHEST).astype(BF)
        d_cross_v = jnp.dot(text_t, jnp.sum(d_tv, axis=0)[:text_count], precision=HIGHEST).astype(BF)
        d_patch_proj = weight_grad(saved[7], kept1)
        d_patch_q = weight_grad(saved[1][:, :space_rows], d_query)
        d_patch_k = weight_grad(saved[1], d_key)
        d_patch_v = weight_grad(saved[1], d_value)
        six = jnp.sum(space_six, axis=0)
        mine = jnp.stack([six, jnp.sum(frame_six, axis=0)])
        spread = jnp.where(jnp.arange(clips)[:, None, None, None] == clip, mine[None], 0.0)
        arrays = [
            d_patch_q, d_patch_k, d_patch_v, d_patch_proj, d_cross_q, d_cross_k, d_cross_v, d_cross_proj,
            d_patch_up, d_patch_down,
        ]
        results, by_clip = reduce_all(arrays, spread.reshape(-1, width), sizes)
        by_clip = by_clip.reshape(clips, 2, 8, width)[:, :, :6]
        d_patch_attn = jnp.stack(results[0:4])
        d_cross = jnp.stack(results[4:8])
        d_patch_up, d_patch_down = results[8:10]
        d_frame_proj, d_frame_qkv, d_frame_up, d_frame_down = reducer.unpack(frame_sums)
        d_frame_qkv = d_frame_qkv.reshape(width, 3, width).swapaxes(0, 1)
        d_frame_attn = jnp.concatenate([d_frame_qkv, d_frame_proj[None]])
        d_frame_down = d_frame_down.T
        d_table = jnp.sum(by_clip, axis=0)
        d_step = lax.dot_general(
            embeddings,
            jnp.sum(by_clip, axis=1).reshape(clips, -1),
            (((0,), (0,)), ((), ())),
            precision=HIGHEST,
        )
        return (
            output,
            latents_grad,
            d_step,
            d_table,
            d_patch_attn,
            d_cross,
            d_patch_up,
            d_patch_down,
            d_frame_attn,
            d_frame_up,
            d_frame_down,
        )

    return per_device


def solution(mesh):
    sizes = dict(mesh.shape)
    tokens = P("dev", "ta", "pa", None)
    in_specs = (tokens, P("dev", None, None), tokens, P("dev"), P("dev"), P("dev")) + (P(),) * 9
    out_specs = (tokens, tokens) + (P(),) * 9
    return jax.shard_map(
        make_per_device(sizes),
        mesh=mesh,
        in_specs=in_specs,
        out_specs=out_specs,
        check_vma=False,
    )
```

```python
import math

import jax
import jax.numpy as jnp
from jax import lax
from jax.experimental import pallas as pl
from jax.experimental.pallas import tpu as pltpu
from jax.sharding import PartitionSpec as P

HEADS = 6
HDIM = 64
PAIRS = HEADS // 2
LANES = 2 * HDIM
EPSILON = 1e-06
MASKED_SCORE = -1e30
HIGHEST = lax.Precision.HIGHEST
F32 = jnp.float32
BF = jnp.bfloat16
VMEM_BYTES = 60 * 2**20
SUM_ROWS = 16
BLOCK = 32
STREAM_RUNS = 2
LATE_COT = 2
TIME_LAG = 1
SUB = 8
TILE = 16
TIME_STAGE = 8
SPACE_STAGE = 1
BACK_STAGE = 1
CROSS_AHEAD = 2
SPAN = 512
KEY_CHUNK = 256
PARTS = (12, 7, 6, 5, 4, 3, 2)
HIDDEN_PARTS = (3, 2)
PATTERN = (0, 1, 2, 0, 1, 0, 1)


def dot(a, b):
    return jnp.dot(a, b, preferred_element_type=F32)


def dot_nt(a, b):
    return lax.dot_general(a, b, (((1,), (1,)), ((), ())), preferred_element_type=F32)


def dot_tn(a, b):
    return lax.dot_general(a, b, (((0,), (0,)), ((), ())), preferred_element_type=F32)


def norm_parts(values):
    centred = values - jnp.mean(values, axis=-1, keepdims=True)
    inverse = lax.rsqrt(jnp.mean(centred * centred, axis=-1, keepdims=True) + EPSILON)
    return centred * inverse, inverse


def norm_back(d_normed, hat, inverse, scale_by):
    d_hat = d_normed * (1.0 + scale_by)
    mean_d = jnp.mean(d_hat, axis=-1, keepdims=True)
    mean_dh = jnp.mean(d_hat * hat, axis=-1, keepdims=True)
    return inverse * (d_hat - mean_d - hat * mean_dh)


GELU_A = math.sqrt(2.0 / math.pi)
GELU_B = 0.044715


def gelu_parts(values):
    square = values * values
    bent = jnp.tanh(GELU_A * values * (1.0 + GELU_B * square))
    half = 0.5 * (1.0 + bent)
    slope = half + (0.5 * GELU_A) * values * (1.0 - bent * bent) * (1.0 + 3.0 * GELU_B * square)
    return values * half, slope


def row_sums(values):
    return jnp.sum(values, axis=0, keepdims=True)


def head_lanes(values, head):
    lane = lax.broadcasted_iota(jnp.int32, values.shape, 1)
    return jnp.where((lane >= HDIM) == (head % 2 == 1), values, jnp.zeros_like(values))


def pair_of(values, pair):
    return values[:, pair * LANES : (pair + 1) * LANES]


def head_rows(values, head):
    return values[head * HDIM : (head + 1) * HDIM, :]


def lone_rows(values, head):
    rows = head_rows(values, head)
    blank = jnp.zeros_like(rows)
    return jnp.concatenate([rows, blank] if head % 2 == 0 else [blank, rows], axis=0)


def spans(count, size):
    return [slice(at, min(at + size, count)) for at in range(0, count, size)]


def attend(jobs, ahead, keep_exponent):
    units = [
        (i, head, span) for i, job in enumerate(jobs) for head in range(HEADS) for span in spans(job[0].shape[0], SPAN)
    ]
    scores, tops, sums, inverses = {}, {}, {}, {}

    def score(unit, keys_span):
        i, head, span = unit
        queries, keys, _, bias = jobs[i]
        lone = head_lanes(pair_of(queries, head // 2)[span], head)
        value = dot_nt(pair_of(keys, head // 2)[keys_span], lone)
        if bias is not None:
            value = value + bias[keys_span, span]
        scores.setdefault((i, head, span.start), []).append(value)
        top = jnp.max(value, axis=0, keepdims=True)
        old = tops.get((i, head, span.start))
        tops[i, head, span.start] = top if old is None else jnp.maximum(old, top)

    def weigh(unit, index, keys_span):
        i, head, span = unit
        name = (i, head, span.start)
        exponent = jnp.exp(scores[name][index] - tops[name]).astype(BF)
        scores[name][index] = None
        keep_exponent(i, head, keys_span, span, exponent)
        values_t = jobs[i][2]
        count = keys_span.stop - keys_span.start
        lifted = jnp.concatenate([head_rows(values_t, head)[:, keys_span], jnp.ones((SUM_ROWS, count), BF)], axis=0)
        part = dot(lifted, exponent)
        sums[name] = part if name not in sums else sums[name] + part

    def finish(unit):
        i, head, span = unit
        name = (i, head, span.start)
        total = sums[name]
        inverse = 1.0 / total[HDIM : HDIM + 1, :]
        sums[name] = total[:HDIM, :] * inverse
        inverses[name] = inverse

    for turn in range(len(units) + ahead):
        later = units[turn] if turn < len(units) else None
        now = units[turn - ahead] if turn >= ahead else None
        later_spans = spans(jobs[later[0]][1].shape[0], SPAN) if later else []
        now_spans = spans(jobs[now[0]][1].shape[0], SPAN) if now else []
        for index in range(max(len(later_spans), len(now_spans))):
            if index < len(later_spans):
                score(later, later_spans[index])
            if index < len(now_spans):
                weigh(now, index, now_spans[index])
        if now:
            finish(now)

    def joined(parts, i, head):
        starts = [span.start for span in spans(jobs[i][0].shape[0], SPAN)]
        return jnp.concatenate([parts[i, head, start] for start in starts], axis=1)

    return (
        [jnp.concatenate([joined(sums, i, head) for head in range(HEADS)], axis=0) for i in range(len(jobs))],
        [[joined(inverses, i, head) for head in range(HEADS)] for i in range(len(jobs))],
    )


def added(total, part):
    return part if total is None else total + part


def attend_back(jobs, ahead, chunk):
    scaled, centres = {}, {}
    for i, (_, _, _, _, d_att_t, att_t, inverse_of, _, _) in enumerate(jobs):
        for head in range(HEADS):
            inverse = inverse_of(head)
            d_att_head = head_rows(d_att_t, head)
            centres[i, head] = row_sums(d_att_head * head_rows(att_t, head)) * inverse
            part = (d_att_head * inverse).astype(BF)
            blank = jnp.zeros_like(part)
            scaled[i, head] = jnp.concatenate([part, blank] if head % 2 == 0 else [blank, part], axis=0)
    units = [
        (i, head, rows) for i, job in enumerate(jobs) for head in range(HEADS) for rows in spans(job[7], chunk)
    ]
    d_queries, d_keys, d_values, chances = {}, {}, {}, {}
    for turn in range(len(units) + ahead):
        if turn < len(units):
            i, head, rows = units[turn]
            chances[turn] = dot(jobs[i][3](head // 2, rows), scaled[i, head])
        if turn < ahead:
            continue
        i, head, rows = units[turn - ahead]
        key = (i, head // 2, rows.start)
        exponent = jobs[i][0](head, rows)
        chance = chances.pop(turn - ahead)
        d_values[key] = added(d_values.get(key), dot_nt(exponent, scaled[i, head]))
        score = (exponent.astype(F32) * (chance - centres[i, head])).astype(BF)
        d_keys[key] = added(d_keys.get(key), dot(score, head_lanes(jobs[i][1](head // 2), head)))
        d_queries[i, head] = added(d_queries.get((i, head)), dot(jobs[i][2](head, rows), score))
        if rows.stop == jobs[i][7] and jobs[i][8] is not None:
            jobs[i][8](head)
    results = []
    for i, job in enumerate(jobs):
        starts = [rows.start for rows in spans(job[7], chunk)]
        joined = [
            jnp.concatenate(
                [jnp.concatenate([parts[i, pair, at] for at in starts], axis=0) for pair in range(PAIRS)], axis=1
            )
            for parts in (d_keys, d_values)
        ]
        results.append((jnp.concatenate([d_queries[i, head] for head in range(HEADS)], axis=0), *joined))
    return results


def fold(ref):
    value = ref[...]
    return value.reshape(-1, value.shape[-1])


class Layout:
    def __init__(self, sizes, latents_shape):
        self.clips_dev, self.frames, self.patches, self.width = latents_shape
        self.n_ta, self.n_pa, self.n_dev = sizes["ta"], sizes["pa"], sizes["dev"]
        self.clips = self.clips_dev * self.n_dev
        self.run = self.n_pa // self.clips
        self.group = self.run * self.n_dev
        self.near = self.n_pa // self.group
        self.halves = self.n_ta // self.near
        self.space_rows = self.near * self.patches
        self.time_patches = self.space_rows // self.n_ta
        self.other_rows = (self.group - 1) * self.space_rows
        self.key_rows = self.group * self.space_rows
        self.all_frames = self.n_ta * self.frames
        self.blocks = self.time_patches // BLOCK
        self.early_cot = max(self.blocks - LATE_COT, 1)

    def here(self):
        return {name: lax.axis_index(name) for name in ("ta", "pa", "dev")}

    def clip(self, me):
        return me["pa"] // self.run

    def member(self, me):
        return me["dev"] * self.run + me["pa"] % self.run

    def space_place(self, ta, clip, member):
        return {"ta": ta, "pa": clip * self.run + member % self.run, "dev": member // self.run}

    def space_target(self, me, j):
        return self.space_place(me["ta"], me["dev"] * self.clips_dev + j, me["pa"] // self.near)

    def owner(self, me, ta, slot):
        return {"ta": ta, "pa": self.near * self.member(me) + slot, "dev": self.clip(me) // self.clips_dev}

    def time_target(self, me, j, s):
        place = self.space_target(me, j)
        return {**place, "ta": (me["pa"] % self.near) * self.halves + s}

    def fellow(self, me, step):
        return self.space_place(me["ta"], self.clip(me), (self.member(me) + step) % self.group)

    def across(self, me, step):
        return {**me, "ta": (me["ta"] + step) % self.n_ta}


def is_me(me, place):
    same = None
    for name, index in place.items():
        if index is not me[name]:
            equal = index == me[name]
            same = equal if same is None else same & equal
    return same


def greet(me, place):
    @pl.when(jnp.logical_not(is_me(me, place)))
    def _():
        pl.semaphore_signal(
            pltpu.get_barrier_semaphore(), inc=1, device_id=place, device_id_type=pl.DeviceIdType.MESH
        )


def await_greetings(me, places, amount=0):
    amount = jnp.int32(amount)
    for place in places:
        amount = amount + jnp.logical_not(is_me(me, place)).astype(jnp.int32)
    pl.semaphore_wait(pltpu.get_barrier_semaphore(), amount)


def push(src, dst, send_sem, recv_sem, place):
    return pltpu.make_async_remote_copy(
        src_ref=src,
        dst_ref=dst,
        send_sem=send_sem,
        recv_sem=recv_sem,
        device_id=place,
        device_id_type=pl.DeviceIdType.MESH,
    )


def start_push(me, src, dst, send_sem, recv_sem, place):
    same = is_me(me, place)

    @pl.when(same)
    def _():
        pltpu.make_async_copy(src, dst, recv_sem).start()

    @pl.when(jnp.logical_not(same))
    def _():
        push(src, dst, send_sem, recv_sem, place).start()


def end_push(me, src, dst, send_sem, recv_sem, place):
    @pl.when(jnp.logical_not(is_me(me, place)))
    def _():
        push(src, dst, send_sem, recv_sem, place).wait_send()


def arrived(dst, recv_sem):
    pltpu.make_async_copy(dst, dst, recv_sem).wait()


def space_forward_kernel(
    lay,
    counts_ref,
    latents_ref,
    cot_ref,
    mod_ref,
    attn_ref,
    turned_ref,
    cross_ref,
    text_keys_ref,
    text_values_t_ref,
    up_ref,
    down_ref,
    state_ref,
    moved_ref,
    own_ref,
    normed_ref,
    query_ref,
    keys_t_ref,
    value_ref,
    exponent_ref,
    att_t_ref,
    att_ref,
    inverse_ref,
    cross_in_ref,
    cross_query_ref,
    cross_exponent_ref,
    cross_att_t_ref,
    cross_att_ref,
    cross_inverse_ref,
    middle_ref,
    normed2_ref,
    act_ref,
    slope_ref,
    branch2_ref,
    branch5_ref,
    own_buf,
    other_buf,
    sent_buf,
    lat_send,
    lat_recv,
    fellow_send,
    fellow_recv,
    state_send,
    state_recv,
    cot_send,
    cot_recv,
):
    scale_by = HDIM ** (-0.5)
    me = lay.here()
    step = pl.program_id(0)
    frames, near = lay.frames, lay.near
    last = step == frames - 1

    def latent_copy(j, f):
        slot = me["pa"] % near
        return (
            latents_ref.at[j, f], own_buf.at[f, slot], lat_send.at[j, f], lat_recv.at[f, slot], lay.space_target(me, j),
        )

    def fellow_copy(turn, f):
        return (
            own_buf.at[f], other_buf.at[f, turn - 1], fellow_send.at[turn - 1, f], fellow_recv.at[turn - 1, f],
            lay.fellow(me, turn),
        )

    def state_copy(turn, f):
        place = lay.across(me, turn)
        row = pl.multiple_of(place["ta"] * lay.time_patches, TILE)
        return (
            sent_buf.at[f, pl.ds(row, lay.time_patches)], state_ref.at[me["ta"] * frames + f], state_send.at[turn, f],
            state_recv.at[turn, f], place,
        )

    def cot_copy(j, s):
        return (
            cot_ref.at[j, :, pl.ds(s * lay.time_patches, lay.early_cot * BLOCK)],
            moved_ref.at[pl.ds(me["ta"] * frames, frames)],
            cot_send.at[j, s], cot_recv.at[me["ta"]], lay.time_target(me, j, s),
        )

    def start_latents(f):
        for j in range(lay.clips_dev):
            start_push(me, *latent_copy(j, f))

    def pass_on(f):
        for slot in range(near):
            arrived(own_buf.at[f, slot], lat_recv.at[f, slot])
        for turn in range(1, lay.group):
            push(*fellow_copy(turn, f)).start()

    @pl.when(step == 0)
    def _():
        for slot in range(near):
            greet(me, lay.owner(me, me["ta"], slot))
        for t in range(lay.n_ta):
            greet(me, lay.owner(me, t, me["ta"] // lay.halves))
        friends = [lay.fellow(me, turn) for turn in range(1, lay.group)]
        friends += [lay.across(me, turn) for turn in range(1, lay.n_ta)]
        for friend in friends:
            greet(me, friend)
        targets = [lay.space_target(me, j) for j in range(lay.clips_dev)]
        targets += [lay.time_target(me, j, s) for j in range(lay.clips_dev) for s in range(lay.halves)]
        await_greetings(me, targets + friends)
        for f in range(frames):
            start_latents(f)
        pass_on(0)

    @pl.when(step == min(2, frames - 1))
    def _():
        for j in range(lay.clips_dev):
            for s in range(lay.halves):
                start_push(me, *cot_copy(j, s))

    for turn in range(1, lay.group):
        arrived(other_buf.at[step, turn - 1], fellow_recv.at[turn - 1, step])
    frame = counts_ref[2] + step
    keep = (frame < counts_ref[0]).astype(F32)
    mod = mod_ref[...]
    own_low = own_buf[step].reshape(lay.space_rows, lay.width)
    own_ref[0] = own_low
    own = own_low.astype(F32)
    rows = lay.space_rows
    normed_own = (norm_parts(own)[0] * (1.0 + mod[1:2]) + mod[0:1]).astype(BF)
    other = other_buf[step].reshape(lay.other_rows, lay.width).astype(F32)
    normed_other = (norm_parts(other)[0] * (1.0 + mod[1:2]) + mod[0:1]).astype(BF)
    normed = jnp.concatenate([normed_own, normed_other], axis=0)
    normed_ref[0] = normed
    queries = (dot(normed_own, attn_ref[0]).astype(BF) * scale_by).astype(BF)
    keys = dot(normed, attn_ref[1]).astype(BF)
    values = dot(normed, attn_ref[2]).astype(BF)
    query_ref[0] = queries
    value_ref[0] = values
    keys_t_ref[0] = dot_nt(turned_ref[0], normed).astype(BF)
    values_t = dot_nt(turned_ref[1], normed).astype(BF)

    def keep_exponent(_, head, keys_span, span, exponent):
        exponent_ref[0, head, keys_span, span] = exponent

    (att_t,), (inverses,) = attend([(queries, keys, values_t, None)], SPACE_STAGE, keep_exponent)
    for head in range(HEADS):
        inverse_ref[0, head : head + 1, :] = inverses[head]
    att_t_ref[0] = att_t.astype(BF)
    att = att_t.T.astype(BF)
    att_ref[0] = att

    @pl.when(jnp.logical_not(last))
    def _():
        pass_on(step + 1)

    branch = dot(att_ref[0], attn_ref[3])
    branch2_ref[0] = branch.astype(BF)
    state = own_ref[0].astype(F32) + (keep * mod[2:3]) * branch
    cross_in = state.astype(BF)
    cross_in_ref[0] = cross_in
    cross_queries = (dot(cross_in, cross_ref[0]).astype(BF) * scale_by).astype(BF)
    cross_query_ref[0] = cross_queries
    text_id = lax.broadcasted_iota(jnp.int32, (text_keys_ref.shape[0], rows), 0)
    bias = jnp.where(text_id < counts_ref[1], 0.0, MASKED_SCORE)

    def keep_cross(_, head, keys_span, span, exponent):
        cross_exponent_ref[0, head, keys_span, span] = exponent

    (cross_t,), (inverses,) = attend(
        [(cross_queries, text_keys_ref[...], text_values_t_ref[...], bias)], CROSS_AHEAD, keep_cross
    )
    for head in range(HEADS):
        cross_inverse_ref[0, head : head + 1, :] = inverses[head]
    cross_att_t_ref[0] = cross_t.astype(BF)
    cross_att = cross_t.T.astype(BF)
    cross_att_ref[0] = cross_att
    state = state + keep * dot(cross_att, cross_ref[1])
    middle_ref[0] = state
    normed2 = (norm_parts(state)[0] * (1.0 + mod[4:5]) + mod[3:4]).astype(BF)
    normed2_ref[0] = normed2
    act, slope = gelu_parts(dot(normed2, up_ref[...]))
    act = act.astype(BF)
    act_ref[0] = act
    slope_ref[0] = slope.astype(BF)
    branch = dot(act, down_ref[...])
    branch5_ref[0] = branch.astype(BF)
    state = state + (keep * mod[5:6]) * branch
    sent_buf[step] = state.astype(BF)
    src, dst, _, sem, _ = state_copy(0, step)
    pltpu.make_async_copy(src, dst, sem).start()
    for turn in range(1, lay.n_ta):
        push(*state_copy(turn, step)).start()

    @pl.when(last)
    def _():
        for f in range(frames):
            for j in range(lay.clips_dev):
                end_push(me, *latent_copy(j, f))
            for turn in range(1, lay.group):
                push(*fellow_copy(turn, f)).wait_send()
            for turn in range(1, lay.n_ta):
                push(*state_copy(turn, f)).wait_send()
            for turn in range(lay.n_ta):
                src, dst, _, sem, _ = state_copy(turn, f)
                arrived(dst, sem)
        for j in range(lay.clips_dev):
            for s in range(lay.halves):
                end_push(me, *cot_copy(j, s))
        for t in range(lay.n_ta):
            arrived(moved_ref.at[pl.ds(t * frames, frames)], cot_recv.at[t])


def space_backward_kernel(
    lay,
    reducer,
    counts_ref,
    grad_ref,
    out_t_ref,
    exponent_ref,
    *refs,
):
    n_sources = len(reducer.shapes)
    sources, refs = refs[:n_sources], refs[n_sources:]
    (mod_ref, attn_ref, cross_ref, text_keys_t_ref, text_values_ref, up_ref, down_ref, own_ref, query_ref, keys_t_ref,
     value_ref, att_t_ref, inverse_ref, cross_query_ref, cross_exponent_ref, cross_att_t_ref, cross_inverse_ref,
     middle_ref, slope_ref, branch2_ref, branch5_ref) = refs[:21]
    (output_ref, lat_grad_ref, reduced_ref, kept3_ref, d_lifted_ref, kept2_ref, d_cross_query_ref, kept1_ref,
     d_query_ref, d_pair_ref, d_text_keys_ref, d_text_values_ref, mods_ref) = refs[21:34]
    (exponent_buf, other_buf, fellow_buf, state_buf, own_buf, done_buf, exponent_sem, fellow_send, fellow_recv,
     out_send, out_recv, grad_send, grad_recv) = refs[34:47]
    reducer.bind(sources, reduced_ref, refs[47:])
    scale_by = HDIM ** (-0.5)
    me = lay.here()
    step = pl.program_id(0)
    frames = lay.frames
    rows = lay.space_rows
    mod = mod_ref[...]

    slots = frames * 3
    lengths = [0, 1] + [2] * 2 + [1] * (reducer.phases - 8) + [1, 2, 2]
    due_at, at = [], 0
    for length in lengths:
        at += length
        due_at.append(at)
    scale = min(1.0, (slots - 1) / at)
    due_at = [int(when * scale) for when in due_at]

    def hook(number):
        for f in range(frames):
            due = [k for k, when in enumerate(due_at) if when == f * 3 + number]
            if due:

                @pl.when(step == f)
                def _():
                    for k in due:
                        if k == 0:
                            reducer.prepare()
                        reducer.phase(k)

    def exponent_copy(head, f):
        return pltpu.make_async_copy(exponent_ref.at[f, head], exponent_buf.at[head], exponent_sem.at[head])

    def fellow_copy(turn, f):
        return (
            other_buf.at[f % 2, turn - 1], fellow_buf.at[f, turn - 1], fellow_send.at[turn - 1, f],
            fellow_recv.at[turn - 1, f], lay.fellow(me, -turn),
        )

    def out_copy(t):
        part, j = me["ta"] % lay.halves, lay.clip(me) % lay.clips_dev
        return (
            out_t_ref.at[pl.ds(t * frames, frames)], output_ref.at[j, :, part], out_send.at[t],
            out_recv.at[j, part], lay.owner(me, t, me["ta"] // lay.halves),
        )

    def grad_copy(slot, f):
        j = lay.clip(me) % lay.clips_dev
        return (
            done_buf.at[f, slot], lat_grad_ref.at[j, f], grad_send.at[slot, f], grad_recv.at[j, f],
            lay.owner(me, me["ta"], slot),
        )

    @pl.when(step == 0)
    def _():
        for head in range(HEADS):
            exponent_copy(head, 0).start()
        fellows = [lay.fellow(me, turn) for turn in range(1, lay.group)]
        senders = [lay.space_target(me, j) for j in range(lay.clips_dev)]
        senders += [lay.time_target(me, j, s) for j in range(lay.clips_dev) for s in range(lay.halves)]
        for place in fellows + senders:
            greet(me, place)
        takers = [lay.owner(me, me["ta"], slot) for slot in range(lay.near)]
        takers += [lay.owner(me, t, me["ta"] // lay.halves) for t in range(lay.n_ta)]
        await_greetings(me, fellows + takers, reducer.greet())
        for t in range(lay.n_ta):
            start_push(me, *out_copy(t))

    mods_ref[0] = jnp.zeros(mods_ref.shape[1:], F32)

    @pl.when(step < frames)
    def _():
        hook(0)
        keep = (counts_ref[2] + step < counts_ref[0]).astype(F32)
        grad = grad_ref[0].astype(F32)
        kept = keep * grad
        d_gate5 = row_sums(kept * branch5_ref[0].astype(F32))
        d_branch = (kept * mod[5:6]).astype(BF)
        kept3_ref[0] = d_branch
        d_act = dot_nt(d_branch, down_ref[...])
        d_lifted = (d_act * slope_ref[0].astype(F32)).astype(BF)
        d_lifted_ref[0] = d_lifted
        d_normed = dot_nt(d_lifted, up_ref[...])
        hat, inverse = norm_parts(middle_ref[0])
        grad = grad + norm_back(d_normed, hat, inverse, mod[4:5])
        d_shift, d_scale = row_sums(d_normed), row_sums(d_normed * hat)
        kept = (keep * grad).astype(BF)
        kept2_ref[0] = kept
        d_att_t = dot_nt(cross_ref[1], kept)
        job = (
            lambda head, at: cross_exponent_ref[0, head, at, :],
            lambda pair: cross_query_ref[0, :, pair * LANES : (pair + 1) * LANES],
            lambda head, at: text_keys_t_ref[head * HDIM : (head + 1) * HDIM, at],
            lambda pair, at: text_values_ref[at, pair * LANES : (pair + 1) * LANES],
            d_att_t,
            cross_att_t_ref[0].astype(F32),
            lambda head: cross_inverse_ref[0, head : head + 1, :],
            text_values_ref.shape[0],
            None,
        )
        ((d_query_t, d_keys, d_values),) = attend_back([job], CROSS_AHEAD, KEY_CHUNK)
        d_text_keys_ref[0] = d_keys
        d_text_values_ref[0] = d_values
        d_query = (d_query_t.T * scale_by).astype(BF)
        d_cross_query_ref[0] = d_query
        grad = grad + dot_nt(d_query, cross_ref[0])
        state_buf[step % 2] = grad
        kept = keep * grad
        d_gate2 = row_sums(kept * branch2_ref[0].astype(F32))
        mods_ref[0, 2:6, :] = jnp.concatenate([d_gate2, d_shift, d_scale, d_gate5], axis=0)
        d_branch = (kept * mod[2:3]).astype(BF)
        kept1_ref[0] = d_branch
        hook(1)
        d_att_t = dot_nt(attn_ref[3], kept1_ref[0])
        later = jnp.minimum(step + 1, frames - 1)

        def end_head(head):
            exponent_copy(head, later).start()
            if head == HEADS // 2 - 1:
                hook(2)

        def exponent_of(head, at):
            if at.start == 0:
                exponent_copy(head, step).wait()
            return exponent_buf[head, at, :]

        job = (
            exponent_of,
            lambda pair: query_ref[0, :, pair * LANES : (pair + 1) * LANES],
            lambda head, at: keys_t_ref[0, head * HDIM : (head + 1) * HDIM, at],
            lambda pair, at: value_ref[0, at, pair * LANES : (pair + 1) * LANES],
            d_att_t,
            att_t_ref[0].astype(F32),
            lambda head: inverse_ref[0, head : head + 1, :],
            value_ref.shape[1],
            end_head,
        )
        ((d_query_t, d_keys, d_values),) = attend_back([job], BACK_STAGE, KEY_CHUNK)
        d_query = (d_query_t.T * scale_by).astype(BF)
        d_keys, d_values = d_keys.astype(BF), d_values.astype(BF)
        d_query_ref[0] = d_query
        d_pair_ref[0, :, : lay.width] = d_keys
        d_pair_ref[0, :, lay.width :] = d_values
        d_normed = dot_nt(d_keys, attn_ref[1]) + dot_nt(d_values, attn_ref[2])
        own_buf[step % 2] = d_normed[:rows] + dot_nt(d_query, attn_ref[0])

        @pl.when(step > 1)
        def _():
            for turn in range(1, lay.group):
                push(*fellow_copy(turn, step - 2)).wait_send()

        for turn in range(1, lay.group):
            other_buf[step % 2, turn - 1] = d_normed[turn * rows : (turn + 1) * rows].astype(BF)
            push(*fellow_copy(turn, step)).start()

    @pl.when(step > 0)
    def _():
        f = step - 1
        d_normed = own_buf[f % 2]
        for turn in range(1, lay.group):
            arrived(fellow_buf.at[f, turn - 1], fellow_recv.at[turn - 1, f])
            d_normed = d_normed + fellow_buf[f, turn - 1].astype(F32)
        hat, inverse = norm_parts(own_ref[0].astype(F32))
        grad = state_buf[f % 2] + norm_back(d_normed, hat, inverse, mod[1:2])
        done_buf[f] = grad.astype(BF).reshape(done_buf.shape[1:])
        mods_ref[0, 0:2, :] = jnp.concatenate([row_sums(d_normed), row_sums(d_normed * hat)], axis=0)
        for slot in range(lay.near):
            start_push(me, *grad_copy(slot, f))

    @pl.when(step == frames)
    def _():
        for k in range(len(due_at), reducer.phases):
            reducer.phase(k)
        for head in range(HEADS):
            exponent_copy(head, frames - 1).wait()
        for turn in range(1, lay.group):
            for f in range(max(frames - 2, 0), frames):
                push(*fellow_copy(turn, f)).wait_send()
        for t in range(lay.n_ta):
            end_push(me, *out_copy(t))
        for f in range(frames):
            for slot in range(lay.near):
                end_push(me, *grad_copy(slot, f))
        for j in range(lay.clips_dev):
            for s in range(lay.halves):
                arrived(output_ref.at[j, :, s], out_recv.at[j, s])
            for f in range(frames):
                arrived(lat_grad_ref.at[j, f], grad_recv.at[j, f])


def interleave(streams, lag):
    live, turn = list(enumerate(streams)), 0
    while live:
        left = []
        for i, stream in live:
            if turn < i * lag or next(stream, DONE) is not DONE:
                left.append((i, stream))
        live, turn = left, turn + 1


DONE = object()


def time_kernel(
    lay,
    counts_ref,
    state_ref,
    early_cot_ref,
    cotangent_ref,
    mod_ref,
    bias_ref,
    qkv_ref,
    proj_ref,
    up_ref,
    down_ref,
    grad_s_ref,
    early_ref,
    late_ref,
    d_qkv_sum_ref,
    d_proj_sum_ref,
    d_up_sum_ref,
    d_down_sum_ref,
    mods_ref,
    exponent_ref,
    sent_buf,
    out_buf,
    d_qkv_sum,
    d_proj_sum,
    d_up_sum,
    d_down_sum,
    normed_ref,
    d_qkv_ref,
    att_ref,
    branch4_ref,
    normed2_ref,
    act_ref,
    d_lifted_ref,
    branch5_ref,
    grad_send,
    grad_recv,
    out_send,
    out_recv,
    cot_buf,
    cot_load,
    cot_send,
    cot_recv,
):
    frames, block, width = state_ref.shape
    me = lay.here()
    step = pl.program_id(0)
    last = pl.num_programs(0) - 1

    def grad_copy(turn, i):
        place = lay.across(me, turn)
        row = pl.multiple_of(me["ta"] * lay.time_patches + i * block, TILE)
        return (
            sent_buf.at[i, pl.ds(place["ta"] * lay.frames, lay.frames)], grad_s_ref.at[:, pl.ds(row, block)],
            grad_send.at[turn, i], grad_recv.at[turn, i], place,
        )

    def out_copy(t, i):
        part, j = me["ta"] % lay.halves, lay.clip(me) % lay.clips_dev
        return (
            out_buf.at[i, pl.ds(t * lay.frames, lay.frames)], early_ref.at[j, :, part, pl.ds(i * block, block)],
            out_send.at[t, i], out_recv.at[j, part, i], lay.owner(me, t, me["ta"] // lay.halves),
        )

    def cot_copy(j, s, b):
        row = s * lay.time_patches + (lay.early_cot + b) * block
        return (
            cotangent_ref.at[j, :, row : row + block], cot_buf.at[lay.early_cot + b, pl.ds(me["ta"] * lay.frames, lay.frames)],
            cot_send.at[j, s, b], cot_recv.at[me["ta"], b], lay.time_target(me, j, s),
        )

    def cot_here(i):
        return pltpu.make_async_copy(early_cot_ref.at[:, pl.ds(i * block, block)], cot_buf.at[i], cot_load.at[i])

    late_cot = lay.blocks - lay.early_cot
    early = lay.blocks - 1

    @pl.when(step == 0)
    def _():
        friends = [lay.across(me, turn) for turn in range(1, lay.n_ta)]
        for i in range(lay.early_cot):
            cot_here(i).start()
        parts = [(j, s) for j in range(lay.clips_dev) for s in range(lay.halves)]
        homes = [lay.owner(me, t, me["ta"] // lay.halves) for t in range(lay.n_ta)]
        places = [lay.time_target(me, j, s) for j, s in parts]
        senders = (places if early else []) + (homes if late_cot else [])
        takers = (homes if early else []) + (places if late_cot else [])
        for place in friends + senders:
            greet(me, place)
        await_greetings(me, friends + takers)
        for b in range(late_cot):
            for j, s in parts:
                start_push(me, *cot_copy(j, s, b))
        for total in (d_qkv_sum, d_proj_sum, d_up_sum, d_down_sum):
            total[...] = jnp.zeros_like(total)

    @pl.when(step > 0)
    def _():
        for t in range(lay.n_ta):
            start_push(me, *out_copy(t, step - 1))

    @pl.when(step < lay.early_cot)
    def _():
        cot_here(step).wait()

    if late_cot:

        @pl.when(step >= lay.early_cot)
        def _():
            for t in range(lay.n_ta):
                arrived(cot_buf.at[step, pl.ds(t * lay.frames, lay.frames)], cot_recv.at[t, step - lay.early_cot])

    scale_by = HDIM ** (-0.5)
    run_rows = frames * SUB
    runs = min(STREAM_RUNS, block // SUB)
    mod = mod_ref[...]
    totals = []

    def stream(first_run):
        patches = slice(first_run * SUB, (first_run + runs) * SUB)
        mine = slice(first_run * run_rows, (first_run + runs) * run_rows)

        def load(cube):
            cube = cube.astype(F32)
            parts = [cube[:, r * SUB : (r + 1) * SUB].reshape(run_rows, width) for r in range(runs)]
            return jnp.concatenate(parts, axis=0)

        def stored(value):
            parts = [value[r * run_rows : (r + 1) * run_rows].reshape(frames, SUB, width) for r in range(runs)]
            return jnp.concatenate(parts, axis=1).astype(BF)

        def run_of(value, r):
            return value[r * run_rows : (r + 1) * run_rows]

        state = load(state_ref[:, patches, :])
        frame = (lax.broadcasted_iota(jnp.int32, (runs * run_rows, 1), 0) // SUB) % frames
        keep = (frame < counts_ref[0]).astype(F32)
        hat1, inverse1 = norm_parts(state)
        normed = (hat1 * (1.0 + mod[1:2]) + mod[0:1]).astype(BF)
        normed_ref[mine] = normed
        yield
        qkv = dot(normed, qkv_ref[...])
        queries = (qkv[:, :width].astype(BF) * scale_by).astype(BF)
        keys = qkv[:, width : 2 * width].astype(BF)
        values = qkv[:, 2 * width :].astype(BF)
        yield
        keys_t_runs, jobs = [], []
        for r in range(runs):
            keys_t_runs.append(run_of(keys, r).T)
            jobs.append((run_of(queries, r), run_of(keys, r), run_of(values, r).T, bias_ref[...]))

        def keep_exponent(r, head, keys_span, span, exponent):
            exponent_ref[first_run + r, head, keys_span, span] = exponent

        att_t_runs, inverse_runs = attend(jobs, TIME_STAGE, keep_exponent)
        yield
        att = jnp.concatenate([att_t.T.astype(BF) for att_t in att_t_runs], axis=0)
        att_ref[mine] = att
        branch2 = dot(att, proj_ref[...])
        yield
        state = state + (keep * mod[2:3]) * branch2
        hat2, inverse2 = norm_parts(state)
        normed2 = (hat2 * (1.0 + mod[4:5]) + mod[3:4]).astype(BF)
        normed2_ref[mine] = normed2
        yield
        lifted = dot(normed2, up_ref[...])
        yield
        act, slope = gelu_parts(lifted)
        act = act.astype(BF)
        act_ref[mine] = act
        grad = load(cot_buf[step, :, patches, :])
        kept = keep * grad
        d_branch = (kept * mod[5:6]).astype(BF)
        branch5_ref[mine] = d_branch
        yield
        d_act = dot_nt(d_branch, down_ref[...])
        yield
        d_lifted = (d_act * slope).astype(BF)
        d_lifted_ref[mine] = d_lifted
        branch5 = dot(act, down_ref[...])
        yield
        final = stored(state + (keep * mod[5:6]) * branch5)
        out_buf[step, :, patches, :] = final
        late_ref[:, patches, :] = final
        d_gate5 = row_sums(kept * branch5)
        d_normed2 = dot_nt(d_lifted, up_ref[...])
        yield
        grad = grad + norm_back(d_normed2, hat2, inverse2, mod[4:5])
        kept = keep * grad
        d_gate2 = row_sums(kept * branch2)
        d_branch = (kept * mod[2:3]).astype(BF)
        branch4_ref[mine] = d_branch
        yield
        d_att_t_runs = [dot_nt(proj_ref[...], run_of(d_branch, r)) for r in range(runs)]
        yield

        def job(r):
            query_run, value_run = run_of(queries, r), run_of(values, r)
            return (
                lambda head, at: exponent_ref[first_run + r, head, at, :],
                lambda pair: pair_of(query_run, pair),
                lambda head, at: head_rows(keys_t_runs[r], head)[:, at],
                lambda pair, at: pair_of(value_run, pair)[at],
                d_att_t_runs[r],
                att_t_runs[r],
                lambda head: inverse_runs[r][head],
                run_rows,
                None,
            )

        backs = attend_back([job(r) for r in range(runs)], TIME_STAGE, run_rows)
        yield
        d_qkv = jnp.concatenate(
            [
                jnp.concatenate([(d_query_t.T * scale_by).astype(BF) for d_query_t, _, _ in backs], axis=0),
                jnp.concatenate([d_keys.astype(BF) for _, d_keys, _ in backs], axis=0),
                jnp.concatenate([d_values.astype(BF) for _, _, d_values in backs], axis=0),
            ],
            axis=1,
        )
        d_qkv_ref[mine] = d_qkv
        d_normed1 = dot_nt(d_qkv, qkv_ref[...])
        yield
        grad = grad + norm_back(d_normed1, hat1, inverse1, mod[1:2])
        sent_buf[step, :, patches, :] = stored(grad)
        totals.append(
            jnp.concatenate(
                [
                    row_sums(d_normed1),
                    row_sums(d_normed1 * hat1),
                    d_gate2,
                    row_sums(d_normed2),
                    row_sums(d_normed2 * hat2),
                    d_gate5,
                    jnp.zeros((2, width), F32),
                ],
                axis=0,
            )
        )

    interleave([stream(first) for first in range(0, block // SUB, runs)], TIME_LAG)
    mods_ref[0] = sum(totals[1:], totals[0])
    src, dst, _, sem, _ = grad_copy(0, step)
    pltpu.make_async_copy(src, dst, sem).start()
    for turn in range(1, lay.n_ta):
        push(*grad_copy(turn, step)).start()

    d_qkv_sum[...] += dot_tn(normed_ref[...], d_qkv_ref[...])
    d_proj_sum[...] += dot_tn(att_ref[...], branch4_ref[...])
    d_up_sum[...] += dot_tn(normed2_ref[...], d_lifted_ref[...])
    d_down_sum[...] += dot_tn(branch5_ref[...], act_ref[...])

    @pl.when(step == last)
    def _():
        d_qkv_sum_ref[...] = d_qkv_sum[...].astype(BF)
        d_proj_sum_ref[...] = d_proj_sum[...].astype(BF)
        d_up_sum_ref[...] = d_up_sum[...].astype(BF)
        d_down_sum_ref[...] = d_down_sum[...].astype(BF)
        for b in range(late_cot):
            for j in range(lay.clips_dev):
                for s in range(lay.halves):
                    end_push(me, *cot_copy(j, s, b))
        for i in range(early):
            for t in range(lay.n_ta):
                end_push(me, *out_copy(t, i))
            for j in range(lay.clips_dev):
                for s in range(lay.halves):
                    arrived(early_ref.at[j, :, s, i * block : (i + 1) * block], out_recv.at[j, s, i])
        for i in range(lay.time_patches // block):
            for turn in range(lay.n_ta):
                src, dst, _, sem, place = grad_copy(turn, i)
                if turn:
                    push(*grad_copy(turn, i)).wait_send()
                arrived(dst, sem)


class Reducer:
    def __init__(self, shapes, small_rows, sizes, parts, direct=False):
        self.direct = direct
        self.width = width = shapes[0][1]
        self.shapes = shapes
        bits = {name: [(name, 1 << i) for i in range(sizes[name].bit_length() - 1)] for name in ("ta", "pa")}
        kinds = [bits["ta"] + bits["pa"], bits["ta"][::-1] + bits["pa"], bits["pa"] + bits["ta"]]
        self.ways = [("dev", 1)] + kinds[0]
        self.loads, row = [], 0
        for i, shape in enumerate(shapes):
            for column in range(shape[1] // width):
                self.loads.append((i, row, column * width, shape[0]))
                row += shape[0]
        self.total = row
        cut = TILE << sum(len(ways) for ways in bits.values())
        self.parts = next((n for n in parts if row % (2 * n * cut) == 0), 1)
        self.part_rows = row // 2 // self.parts
        self.half_rows = row // 2
        self.orders = [[("dev", 1)] + kinds[PATTERN[p % len(PATTERN)]] for p in range(self.parts)]
        self.steps = len(self.ways)
        self.small_rows = small_rows
        self.counts, self.halves, self.boxes, at = [self.part_rows], [True], [], 0
        for _ in range(1, self.steps):
            halve = (self.counts[-1] // 2) % TILE == 0
            self.halves.append(halve)
            self.counts.append(self.counts[-1] // 2 if halve else self.counts[-1])
        for p in range(self.parts):
            self.boxes.append([])
            for count in self.counts:
                self.boxes[p].append(at)
                at += count
        self.box_rows = at
        self.phases = 2 * self.steps + 1

    def scratch(self):
        shapes = [
            pltpu.VMEM((self.total, self.width), BF),
            pltpu.VMEM((self.total, self.width), BF),
            pltpu.VMEM((self.box_rows, self.width), BF),
            pltpu.SemaphoreType.DMA((len(self.loads),)),
            pltpu.SemaphoreType.DMA((self.parts, 2)),
            pltpu.SemaphoreType.DMA((self.parts, 2 * self.steps)),
            pltpu.SemaphoreType.DMA((self.parts, 2 * self.steps)),
        ]
        if self.small_rows:
            shapes += [
                pltpu.VMEM((self.steps, self.small_rows, self.width), F32),
                pltpu.SemaphoreType.DMA((self.steps,)),
                pltpu.SemaphoreType.DMA((self.steps,)),
            ]
        return shapes

    def bind(self, sources, out, scratch, small_in=None, small_out=None):
        self.sources, self.out = sources, out
        self.work, self.whole, self.inbox, self.in_sem, self.out_sem, self.send_sem, self.recv_sem = scratch[:7]
        self.small_in, self.small_out = small_in, small_out
        if self.small_rows:
            self.small_box, self.small_send, self.small_recv = scratch[7:]

    def bit(self, way):
        return (lax.axis_index(way[0]) // way[1]) % 2

    def peer(self, way):
        return {way[0]: lax.axis_index(way[0]) + way[1] - 2 * way[1] * self.bit(way)}

    def greet(self):
        barrier = pltpu.get_barrier_semaphore()
        for way in self.ways:
            pl.semaphore_signal(barrier, inc=1, device_id=self.peer(way), device_id_type=pl.DeviceIdType.MESH)
        return len(self.ways)

    def base(self, p, step):
        row = self.bit(self.orders[p][0]) * self.half_rows + p * self.part_rows
        for s in range(1, step + 1):
            if self.halves[s]:
                row = row + self.bit(self.orders[p][s]) * self.counts[s]
        return row

    def rows(self, ref, row, count):
        return ref.at[pl.ds(pl.multiple_of(row, TILE), count)]

    def load(self, i):
        source, row, column, rows = self.loads[i]
        view = self.sources[source].at[:, column : column + self.width]
        return pltpu.make_async_copy(view, self.work.at[row : row + rows], self.in_sem.at[i])

    def remote(self, src, dst, p, step, way):
        return pltpu.make_async_remote_copy(
            src_ref=src,
            dst_ref=dst,
            send_sem=self.send_sem.at[p, step],
            recv_sem=self.recv_sem.at[p, step],
            device_id=self.peer(way),
            device_id_type=pl.DeviceIdType.MESH,
        )

    def down(self, p, step):
        way, count = self.orders[p][step], self.counts[step]
        if step == 0:
            row = (1 - self.bit(way)) * self.half_rows + p * self.part_rows
        else:
            row = self.base(p, step - 1)
            if self.halves[step]:
                row = row + (1 - self.bit(way)) * count
        box = self.boxes[p][step]
        return self.remote(self.rows(self.work, row, count), self.inbox.at[box : box + count], p, step, way)

    def end_down(self, p, step):
        self.down(p, step).wait()
        count, base, box = self.counts[step], self.base(p, step), self.boxes[p][step]
        chunk = next(c for c in (96, 64, 48, 32, TILE) if count % c == 0)

        def body(i, carry):
            at = pl.ds(pl.multiple_of(base + i * chunk, TILE), chunk)
            got = self.inbox[pl.ds(pl.multiple_of(box + i * chunk, TILE), chunk), :]
            total = (self.work[at, :].astype(F32) + got.astype(F32)).astype(BF)
            if step == self.steps - 1:
                self.whole[at, :] = total
            else:
                self.work[at, :] = total
            return carry

        lax.fori_loop(0, count // chunk, body, 0)

    def up(self, p, turn):
        step = self.steps - 1 - turn
        if not self.halves[step]:
            return None
        rows = self.rows(self.whole, self.base(p, step), self.counts[step])
        return self.remote(rows, rows, p, self.steps + turn, self.orders[p][step])

    def store(self, p, side):
        rows = pl.ds(side * self.half_rows + p * self.part_rows, self.part_rows)
        return pltpu.make_async_copy(self.whole.at[rows], self.out.at[rows], self.out_sem.at[p, side])

    def small(self, step):
        return pltpu.make_async_remote_copy(
            src_ref=self.small_out,
            dst_ref=self.small_box.at[step],
            send_sem=self.small_send.at[step],
            recv_sem=self.small_recv.at[step],
            device_id=self.peer(self.ways[step]),
            device_id_type=pl.DeviceIdType.MESH,
        )

    def prepare(self):
        for i, (source, row, column, rows) in enumerate(self.loads):
            if self.direct:
                self.work[row : row + rows, :] = self.sources[source][:, column : column + self.width].astype(BF)
            else:
                self.load(i).start()
        if self.small_rows:
            self.small_out[...] = self.small_in[...]

    def phase(self, k):
        n = self.steps
        if k == 0 and not self.direct:
            for i in range(len(self.loads)):
                self.load(i).wait()
        for p in range(self.parts):
            if 1 <= k <= n:
                self.end_down(p, k - 1)
            elif k > n:
                before = self.up(p, k - n - 1)
                if before is not None:
                    before.wait()
            if k < n:
                self.down(p, k).start()
            elif k < 2 * n:
                after = self.up(p, k - n)
                if after is not None:
                    after.start()
            else:
                self.store(p, 0).start()
                self.store(p, 1).start()
        if k == 2 * n:
            for p in range(self.parts):
                self.store(p, 0).wait()
                self.store(p, 1).wait()
        if self.small_rows and k <= n:
            if k > 0:
                self.small(k - 1).wait()
                self.small_out[...] = self.small_out[...] + self.small_box[k - 1]
            if k < n:
                self.small(k).start()

    def unpack(self, reduced):
        results, at = [], 0
        for rows, columns in self.shapes:
            turns = columns // self.width
            blocks = [reduced[at + i * rows : at + (i + 1) * rows] for i in range(turns)]
            at += turns * rows
            results.append((blocks[0] if turns == 1 else jnp.concatenate(blocks, axis=1)).astype(F32))
        return results


def weights_kernel(
    reducer,
    counts_ref,
    small_ref,
    text_ref,
    normed_ref,
    d_query_ref,
    d_pair_ref,
    att_ref,
    branch2_ref,
    cross_in_ref,
    d_cross_query_ref,
    cross_att_ref,
    cross_branch_ref,
    normed2_ref,
    d_lifted_ref,
    branch5_ref,
    act_ref,
    d_text_keys_ref,
    d_text_values_ref,
    reduced_ref,
    small_out_ref,
    q_sum,
    pair_sum,
    proj_sum,
    cross_q_sum,
    cross_k_sum,
    cross_v_sum,
    cross_proj_sum,
    up_sum,
    down_sum,
    text_k_sum,
    text_v_sum,
    *scratch,
):
    step = pl.program_id(0)
    sums = (q_sum, pair_sum, proj_sum, cross_q_sum, cross_proj_sum, up_sum, down_sum, text_k_sum, text_v_sum)
    grads = [q_sum, pair_sum, proj_sum, cross_q_sum, cross_k_sum, cross_v_sum, cross_proj_sum, up_sum, down_sum]
    reducer.bind(grads, reduced_ref, scratch, small_ref, small_out_ref)

    @pl.when(step == 0)
    def _():
        reducer.greet()
        for total in sums:
            total[...] = jnp.zeros_like(total)

    rows = d_query_ref.shape[1]
    q_sum[...] += dot_tn(normed_ref[0, :rows, :], d_query_ref[0])
    pair_sum[...] += dot_tn(normed_ref[0], d_pair_ref[0])
    proj_sum[...] += dot_tn(att_ref[0], branch2_ref[0])
    cross_q_sum[...] += dot_tn(cross_in_ref[0], d_cross_query_ref[0])
    cross_proj_sum[...] += dot_tn(cross_att_ref[0], cross_branch_ref[0])
    up_sum[...] += dot_tn(normed2_ref[0], d_lifted_ref[0])
    down_sum[...] += dot_tn(branch5_ref[0], act_ref[0])
    text_k_sum[...] += d_text_keys_ref[0]
    text_v_sum[...] += d_text_values_ref[0]

    @pl.when(step == pl.num_programs(0) - 1)
    def _():
        for total, result in ((text_k_sum, cross_k_sum), (text_v_sum, cross_v_sum)):
            value = total[...]
            head = value.astype(BF)
            rest = (value - head.astype(F32)).astype(BF)
            result[...] = dot_tn(text_ref[...], head) + dot_tn(text_ref[...], rest)
        reducer.prepare()
        pl.semaphore_wait(pltpu.get_barrier_semaphore(), len(reducer.ways))
        for k in range(reducer.phases):
            reducer.phase(k)


def whole(array):
    zeros = (0,) * array.ndim
    return pl.BlockSpec(array.shape, lambda *grid: zeros)


def framed(array):
    tail = (0,) * (array.ndim - 1)
    return pl.BlockSpec((1,) + tuple(array.shape[1:]), lambda frame: (frame,) + tail)


SCALARS = pl.BlockSpec(memory_space=pltpu.SMEM)
HBM = pl.BlockSpec(memory_space=pl.ANY)


def shape_of(shape, dtype):
    return jax.ShapeDtypeStruct(shape, dtype)


def call(kernel, grid, inputs, in_specs, outputs, out_specs, flops, scratch=(), collective_id=None):
    moved = sum(math.prod(a.shape) * a.dtype.itemsize for a in (*inputs, *outputs))
    return pl.pallas_call(
        kernel,
        grid=grid,
        in_specs=in_specs,
        out_specs=out_specs,
        out_shape=outputs,
        scratch_shapes=list(scratch),
        compiler_params=pltpu.CompilerParams(
            vmem_limit_bytes=VMEM_BYTES, collective_id=collective_id, has_side_effects=collective_id is not None
        ),
        cost_estimate=pl.CostEstimate(flops=int(flops), bytes_accessed=int(moved), transcendentals=0),
    )(*inputs)


def make_per_device(sizes):
    n_ta, n_pa, n_dev = sizes["ta"], sizes["pa"], sizes["dev"]

    def per_device(
        latents,
        context,
        cotangent,
        timesteps,
        frame_counts,
        text_lengths,
        step_proj,
        mod_table,
        patch_attn,
        cross_attn,
        patch_up,
        patch_down,
        frame_attn,
        frame_up,
        frame_down,
    ):
        lay = Layout(sizes, latents.shape)
        clips_dev, frames, patches, width = latents.shape
        clips, run, group, near, halves = lay.clips, lay.run, lay.group, lay.near, lay.halves
        space_rows, other_rows, key_rows = lay.space_rows, lay.other_rows, lay.key_rows
        time_patches, all_frames = lay.time_patches, lay.all_frames
        ta, pa, dev = (lax.axis_index(name) for name in ("ta", "pa", "dev"))
        clip, member = lay.clip(lay.here()), lay.member(lay.here())

        def place(clip_id, member_id):
            return (clip_id * run + member_id % run) * n_dev + member_id // run

        def space_pairs(step):
            pairs = []
            for p in range(n_pa):
                for d in range(n_dev):
                    k = d * clips_dev + (p + step) % clips_dev
                    pairs.append((p * n_dev + d, place(k, p // near)))
            return pairs

        def time_pairs(step):
            u, w = step % halves, step // halves
            pairs = []
            for t in range(n_ta):
                for p in range(n_pa):
                    for d in range(n_dev):
                        s = (t % halves + u) % halves
                        j = (t // halves + w) % clips_dev
                        k = d * clips_dev + j
                        pairs.append(
                            (
                                (t * n_pa + p) * n_dev + d,
                                ((p % near) * halves + s) * n_pa * n_dev + place(k, p // near),
                            )
                        )
            return pairs

        def back(pairs):
            return [(b, a) for a, b in pairs]

        def group_pairs(step):
            return [
                (place(k, g), place(k, (g + step) % group)) for k in range(clips) for g in range(group)
            ]

        def ta_pairs(step):
            return [(t, t ^ step) for t in range(n_ta)]

        whole_axes = ("ta", "pa", "dev")
        pair_axes = ("pa", "dev")

        def of_clip(local):
            both = lax.all_gather(local, "dev", axis=0, tiled=True)
            return lax.dynamic_index_in_dim(both, clip, 0, keepdims=False)

        def sinusoid(steps):
            half = step_proj.shape[0] // 2
            frequency = jnp.exp(-math.log(10000.0) * jnp.arange(half, dtype=F32) / half)
            angles = steps.astype(F32)[:, None] * frequency[None, :]
            return jnp.concatenate([jnp.cos(angles), jnp.sin(angles)], axis=1)

        numbers = lax.all_gather(jnp.stack([timesteps, frame_counts, text_lengths], axis=1), "dev", axis=0, tiled=True)
        own_numbers = lax.dynamic_index_in_dim(numbers, clip, 0, keepdims=False)
        embeddings = sinusoid(numbers[:, 0])
        embedding = lax.dynamic_index_in_dim(embeddings, clip, 0, keepdims=True)
        timing = jnp.dot(embedding, step_proj.astype(F32), precision=HIGHEST).reshape(6, width)
        table = mod_table.astype(F32)
        pad = jnp.zeros((2, width), F32)
        space_mod = jnp.concatenate([timing + table[0], pad])
        frame_mod = jnp.concatenate([timing + table[1], pad])
        counts = jnp.stack([own_numbers[1], own_numbers[2], ta * frames, 0]).astype(jnp.int32)
        text = of_clip(context)
        text_count = text.shape[0]
        text_rows = -(-text_count // LANES) * LANES
        text_wide = jnp.pad(text, ((0, text_rows - text_count), (0, 0)))
        text_keys = dot(text_wide, cross_attn[1]).astype(BF)
        text_values = dot(text_wide, cross_attn[2]).astype(BF)
        cross_ends = jnp.stack([cross_attn[0], cross_attn[3]])
        patch_turned = jnp.swapaxes(patch_attn[1:3], 1, 2)

        def out(*shape, dtype=BF):
            return shape_of((frames,) + shape, dtype)

        def moved_tokens():
            return shape_of((all_frames, time_patches, width), BF)

        hidden = patch_up.shape[1]
        inputs = (
            counts, latents, cotangent, space_mod, patch_attn, patch_turned, cross_ends, text_keys, text_values.T,
            patch_up, patch_down,
        )
        outputs = (
            moved_tokens(),
            shape_of((all_frames, lay.early_cot * BLOCK, width), BF),
            out(space_rows, width),
            out(key_rows, width),
            out(space_rows, width),
            out(width, key_rows),
            out(key_rows, width),
            out(HEADS, key_rows, space_rows),
            out(width, space_rows),
            out(space_rows, width),
            out(8, space_rows, dtype=F32),
            out(space_rows, width),
            out(space_rows, width),
            out(HEADS, text_rows, space_rows),
            out(width, space_rows),
            out(space_rows, width),
            out(8, space_rows, dtype=F32),
            out(space_rows, width, dtype=F32),
            out(space_rows, width),
            out(space_rows, hidden),
            out(space_rows, hidden),
            out(space_rows, width),
            out(space_rows, width),
        )
        dense = 2 * frames * space_rows * width * (6 * width + 2 * hidden) + 8 * frames * key_rows * width * width
        dma = pltpu.SemaphoreType.DMA
        state, cot, *saved = call(
            lambda *refs: space_forward_kernel(lay, *refs),
            (frames,),
            inputs,
            [SCALARS, HBM, HBM] + [whole(a) for a in inputs[3:]],
            outputs,
            [HBM, HBM] + [framed(a) for a in outputs[2:]],
            dense + 16 * frames * space_rows * key_rows * width,
            [
                pltpu.VMEM((frames, near, patches, width), BF),
                pltpu.VMEM((frames, group - 1, near, patches, width), BF),
                pltpu.VMEM((frames, space_rows, width), BF),
                dma((clips_dev, frames)),
                dma((frames, near)),
                dma((group - 1, frames)),
                dma((group - 1, frames)),
                dma((n_ta, frames)),
                dma((n_ta, frames)),
                dma((clips_dev, halves)),
                dma((n_ta,)),
            ],
            collective_id=1,
        )

        block_rows = all_frames * BLOCK
        run_rows = all_frames * SUB
        ids = jnp.arange(run_rows, dtype=jnp.int32)
        same = (ids[:, None] % SUB == ids[None, :] % SUB) & (ids[:, None] // SUB < counts[0])
        bias = jnp.where(same, 0.0, MASKED_SCORE).astype(F32)
        hidden = frame_up.shape[1]
        n_blocks = time_patches // BLOCK

        early = max(n_blocks - 1, 1) * BLOCK
        frame_wide = frame_attn[:3].swapaxes(0, 1).reshape(width, 3 * width)
        time_inputs = (counts, state, cot, cotangent, frame_mod, bias, frame_wide, frame_attn[3], frame_up, frame_down)
        time_outputs = (
            out(space_rows, width),
            shape_of((clips_dev, frames, halves, early, width), BF),
            shape_of((all_frames, BLOCK, width), BF),
            shape_of((width, 3 * width), BF),
            shape_of((width, width), BF),
            shape_of((width, hidden), BF),
            shape_of((width, hidden), BF),
            shape_of((n_blocks, 8, width), F32),
        )

        def blocked(array):
            return pl.BlockSpec((all_frames, BLOCK, array.shape[2]), lambda at: (0, at, 0))

        def vmem(*shape, dtype=BF):
            return pltpu.VMEM(shape, dtype)

        (grad_s, early_out, late_out, d_frame_qkv, d_frame_proj, d_frame_up, d_frame_down, frame_six) = call(
            lambda *refs: time_kernel(lay, *refs),
            (n_blocks,),
            time_inputs,
            [SCALARS, blocked(state), HBM, HBM] + [whole(a) for a in time_inputs[4:]],
            time_outputs,
            [HBM, HBM] + [whole(a) for a in time_outputs[2:-1]] + [framed(time_outputs[-1])],
            all_frames * time_patches * width * (32 * width + 20 * hidden),
            [
                vmem(BLOCK // SUB, HEADS, run_rows, run_rows),
                vmem(n_blocks, all_frames, BLOCK, width),
                vmem(n_blocks, all_frames, BLOCK, width),
                vmem(width, 3 * width, dtype=F32),
                vmem(width, width, dtype=F32),
                vmem(width, hidden, dtype=F32),
                vmem(width, hidden, dtype=F32),
                vmem(block_rows, width),
                vmem(block_rows, 3 * width),
                vmem(block_rows, width),
                vmem(block_rows, width),
                vmem(block_rows, width),
                vmem(block_rows, hidden),
                vmem(block_rows, hidden),
                vmem(block_rows, width),
                dma((n_ta, n_blocks)),
                dma((n_ta, n_blocks)),
                dma((n_ta, n_blocks)),
                dma((clips_dev, halves, n_blocks)),
                vmem(n_blocks, all_frames, BLOCK, width),
                dma((n_blocks,)),
                dma((clips_dev, halves, n_blocks)),
                dma((n_ta, n_blocks)),
            ],
            collective_id=2,
        )

        (own, _, query, keys_t, value, exponent, att_t, _, inverse, _, cross_query, cross_exponent, cross_att_t, _,
         cross_inverse, middle, _, _, slope, branch2, branch5) = saved
        frame_grads = [d_frame_proj, d_frame_qkv, d_frame_up, d_frame_down]
        reducer = Reducer([a.shape for a in frame_grads], 0, sizes, HIDDEN_PARTS)
        fixed = (space_mod, patch_attn, cross_ends, text_keys.T, text_values, patch_up, patch_down)
        by_frame = (
            query, keys_t, value, att_t, inverse, cross_query, cross_exponent, cross_att_t, cross_inverse, middle,
            slope, branch2, branch5,
        )
        back_outputs = (
            shape_of((clips_dev, frames, halves, BLOCK, width), BF),
            shape_of(latents.shape, BF),
            shape_of((reducer.total, width), BF),
            out(space_rows, width),
            out(space_rows, hidden),
            out(space_rows, width),
            out(space_rows, width),
            out(space_rows, width),
            out(space_rows, width),
            out(key_rows, 2 * width),
            out(text_rows, width, dtype=F32),
            out(text_rows, width, dtype=F32),
            shape_of((frames + 1, 8, width), F32),
        )

        def now(array):
            tail = (0,) * (array.ndim - 1)
            return pl.BlockSpec((1,) + tuple(array.shape[1:]), lambda at: (jnp.minimum(at, frames - 1),) + tail)

        def before(array):
            tail = (0,) * (array.ndim - 1)
            return pl.BlockSpec((1,) + tuple(array.shape[1:]), lambda at: (jnp.maximum(at, 1) - 1,) + tail)

        dense = 2 * frames * space_rows * width * (6 * width + 2 * hidden) + 8 * frames * key_rows * width * width
        output, lat_grad, frame_sums, *backs = call(
            lambda *refs: space_backward_kernel(lay, reducer, *refs),
            (frames + 1,),
            (counts, grad_s, late_out, exponent, *frame_grads, *fixed, own, *by_frame),
            [SCALARS, now(grad_s), HBM, HBM] + [HBM] * len(frame_grads) + [whole(a) for a in fixed] + [before(own)]
            + [now(a) for a in by_frame],
            back_outputs,
            [HBM, HBM, HBM] + [now(a) for a in back_outputs[3:-1]] + [framed(back_outputs[-1])],
            dense + 32 * frames * space_rows * key_rows * width,
            [
                pltpu.VMEM((HEADS, key_rows, space_rows), BF),
                pltpu.VMEM((2, group - 1, space_rows, width), BF),
                pltpu.VMEM((frames, group - 1, space_rows, width), BF),
                pltpu.VMEM((2, space_rows, width), F32),
                pltpu.VMEM((2, space_rows, width), F32),
                pltpu.VMEM((frames, near, patches, width), BF),
                dma((HEADS,)),
                dma((group - 1, frames)),
                dma((group - 1, frames)),
                dma((n_ta,)),
                dma((clips_dev, halves)),
                dma((near, frames)),
                dma((clips_dev, frames)),
                *reducer.scratch(),
            ],
            collective_id=3,
        )
        latents_grad = lat_grad.astype(F32)
        if n_blocks > 1:
            output = jnp.concatenate([early_out, output], axis=3)
        output = output.reshape(latents.shape)

        kept3, d_lifted2, kept2, d_cross_query, kept1, d_query, d_pair, d_tk, d_tv, space_six = backs
        mine = jnp.stack([jnp.sum(space_six, axis=0), jnp.sum(frame_six, axis=0)])
        spread = jnp.where(jnp.arange(clips)[:, None, None, None] == clip, mine[None], 0.0).reshape(-1, width)
        square, pair, lifted = (width, width), (width, 2 * width), (width, hidden)
        shapes = [square, pair, square, square, square, square, square, lifted, lifted]
        tail = Reducer(shapes, spread.shape[0], sizes, PARTS, direct=True)
        by_frame = (
            saved[1], d_query, d_pair, saved[7], kept1, saved[9], d_cross_query, saved[13], kept2, saved[16], d_lifted2,
            kept3, saved[17], d_tk, d_tv,
        )
        tail_outputs = (shape_of((tail.total, width), BF), shape_of(spread.shape, F32))
        reduced, by_clip = call(
            lambda *refs: weights_kernel(tail, *refs),
            (frames,),
            (counts, spread, text_wide, *by_frame),
            [SCALARS, whole(spread), whole(text_wide)] + [framed(a) for a in by_frame],
            tail_outputs,
            [HBM, whole(spread)],
            2 * frames * space_rows * width * (4 * width + 2 * hidden) + 4 * frames * key_rows * width * width,
            [vmem(*shape, dtype=F32) for shape in shapes]
            + [vmem(text_rows, width, dtype=F32)] * 2
            + tail.scratch(),
            collective_id=0,
        )
        d_patch_q, d_patch_pair, d_patch_proj, *d_cross, d_patch_up, d_patch_down = tail.unpack(reduced)
        d_patch_attn = jnp.stack([d_patch_q, d_patch_pair[:, :width], d_patch_pair[:, width:], d_patch_proj])
        d_cross = jnp.stack(d_cross)
        d_patch_down = d_patch_down.T
        by_clip = by_clip.reshape(clips, 2, 8, width)[:, :, :6]
        d_frame_proj, d_frame_qkv, d_frame_up, d_frame_down = reducer.unpack(frame_sums)
        d_frame_qkv = d_frame_qkv.reshape(width, 3, width).swapaxes(0, 1)
        d_frame_attn = jnp.concatenate([d_frame_qkv, d_frame_proj[None]])
        d_frame_down = d_frame_down.T
        d_table = jnp.sum(by_clip, axis=0)
        d_step = lax.dot_general(
            embeddings,
            jnp.sum(by_clip, axis=1).reshape(clips, -1),
            (((0,), (0,)), ((), ())),
            precision=HIGHEST,
        )
        return (
            output,
            latents_grad,
            d_step,
            d_table,
            d_patch_attn,
            d_cross,
            d_patch_up,
            d_patch_down,
            d_frame_attn,
            d_frame_up,
            d_frame_down,
        )

    return per_device


def solution(mesh):
    sizes = dict(mesh.shape)
    tokens = P("dev", "ta", "pa", None)
    in_specs = (tokens, P("dev", None, None), tokens, P("dev"), P("dev"), P("dev")) + (P(),) * 9
    out_specs = (tokens, tokens) + (P(),) * 9
    return jax.shard_map(
        make_per_device(sizes),
        mesh=mesh,
        in_specs=in_specs,
        out_specs=out_specs,
        check_vma=False,
    )
```

```python
import math

import jax
import jax.numpy as jnp
from jax import lax
from jax.experimental import pallas as pl
from jax.experimental.pallas import tpu as pltpu
from jax.sharding import PartitionSpec as P

HEADS = 6
HDIM = 64
PAIRS = HEADS // 2
LANES = 2 * HDIM
EPSILON = 1e-06
MASKED_SCORE = -1e30
HIGHEST = lax.Precision.HIGHEST
F32 = jnp.float32
BF = jnp.bfloat16
VMEM_BYTES = 60 * 2**20
SUM_ROWS = 16
BLOCK = 32
STREAM_RUNS = 2
LATE_COT = 2
TIME_LAG = 1
SUB = 8
TILE = 16
TIME_STAGE = 8
SPACE_STAGE = 1
BACK_STAGE = 1
CROSS_AHEAD = 2
SPAN = 512
KEY_CHUNK = 256
PARTS = (12, 7, 6, 5, 4, 3, 2)
HIDDEN_PARTS = (3, 2)
PATTERN = (0, 1, 2)


def dot(a, b):
    return jnp.dot(a, b, preferred_element_type=F32)


def dot_nt(a, b):
    return lax.dot_general(a, b, (((1,), (1,)), ((), ())), preferred_element_type=F32)


def dot_tn(a, b):
    return lax.dot_general(a, b, (((0,), (0,)), ((), ())), preferred_element_type=F32)


def norm_parts(values):
    centred = values - jnp.mean(values, axis=-1, keepdims=True)
    inverse = lax.rsqrt(jnp.mean(centred * centred, axis=-1, keepdims=True) + EPSILON)
    return centred * inverse, inverse


def norm_back(d_normed, hat, inverse, scale_by):
    d_hat = d_normed * (1.0 + scale_by)
    mean_d = jnp.mean(d_hat, axis=-1, keepdims=True)
    mean_dh = jnp.mean(d_hat * hat, axis=-1, keepdims=True)
    return inverse * (d_hat - mean_d - hat * mean_dh)


GELU_A = math.sqrt(2.0 / math.pi)
GELU_B = 0.044715


def gelu_parts(values):
    square = values * values
    bent = jnp.tanh(GELU_A * values * (1.0 + GELU_B * square))
    half = 0.5 * (1.0 + bent)
    slope = half + (0.5 * GELU_A) * values * (1.0 - bent * bent) * (1.0 + 3.0 * GELU_B * square)
    return values * half, slope


def row_sums(values):
    return jnp.sum(values, axis=0, keepdims=True)


def head_lanes(values, head):
    lane = lax.broadcasted_iota(jnp.int32, values.shape, 1)
    return jnp.where((lane >= HDIM) == (head % 2 == 1), values, jnp.zeros_like(values))


def pair_of(values, pair):
    return values[:, pair * LANES : (pair + 1) * LANES]


def head_rows(values, head):
    return values[head * HDIM : (head + 1) * HDIM, :]


def lone_rows(values, head):
    rows = head_rows(values, head)
    blank = jnp.zeros_like(rows)
    return jnp.concatenate([rows, blank] if head % 2 == 0 else [blank, rows], axis=0)


def spans(count, size):
    return [slice(at, min(at + size, count)) for at in range(0, count, size)]


def attend(jobs, ahead, keep_exponent):
    units = [
        (i, head, span) for i, job in enumerate(jobs) for head in range(HEADS) for span in spans(job[0].shape[0], SPAN)
    ]
    scores, tops, sums, inverses = {}, {}, {}, {}

    def score(unit, keys_span):
        i, head, span = unit
        queries, keys, _, bias = jobs[i]
        lone = head_lanes(pair_of(queries, head // 2)[span], head)
        value = dot_nt(pair_of(keys, head // 2)[keys_span], lone)
        if bias is not None:
            value = value + bias[keys_span, span]
        scores.setdefault((i, head, span.start), []).append(value)
        top = jnp.max(value, axis=0, keepdims=True)
        old = tops.get((i, head, span.start))
        tops[i, head, span.start] = top if old is None else jnp.maximum(old, top)

    def weigh(unit, index, keys_span):
        i, head, span = unit
        name = (i, head, span.start)
        exponent = jnp.exp(scores[name][index] - tops[name]).astype(BF)
        scores[name][index] = None
        keep_exponent(i, head, keys_span, span, exponent)
        values_t = jobs[i][2]
        count = keys_span.stop - keys_span.start
        lifted = jnp.concatenate([head_rows(values_t, head)[:, keys_span], jnp.ones((SUM_ROWS, count), BF)], axis=0)
        part = dot(lifted, exponent)
        sums[name] = part if name not in sums else sums[name] + part

    def finish(unit):
        i, head, span = unit
        name = (i, head, span.start)
        total = sums[name]
        inverse = 1.0 / total[HDIM : HDIM + 1, :]
        sums[name] = total[:HDIM, :] * inverse
        inverses[name] = inverse

    for turn in range(len(units) + ahead):
        later = units[turn] if turn < len(units) else None
        now = units[turn - ahead] if turn >= ahead else None
        later_spans = spans(jobs[later[0]][1].shape[0], SPAN) if later else []
        now_spans = spans(jobs[now[0]][1].shape[0], SPAN) if now else []
        for index in range(max(len(later_spans), len(now_spans))):
            if index < len(later_spans):
                score(later, later_spans[index])
            if index < len(now_spans):
                weigh(now, index, now_spans[index])
        if now:
            finish(now)

    def joined(parts, i, head):
        starts = [span.start for span in spans(jobs[i][0].shape[0], SPAN)]
        return jnp.concatenate([parts[i, head, start] for start in starts], axis=1)

    return (
        [jnp.concatenate([joined(sums, i, head) for head in range(HEADS)], axis=0) for i in range(len(jobs))],
        [[joined(inverses, i, head) for head in range(HEADS)] for i in range(len(jobs))],
    )


def added(total, part):
    return part if total is None else total + part


def attend_back(jobs, ahead, chunk):
    scaled, centres = {}, {}
    for i, (_, _, _, _, d_att_t, att_t, inverse_of, _, _) in enumerate(jobs):
        for head in range(HEADS):
            inverse = inverse_of(head)
            d_att_head = head_rows(d_att_t, head)
            centres[i, head] = row_sums(d_att_head * head_rows(att_t, head)) * inverse
            part = (d_att_head * inverse).astype(BF)
            blank = jnp.zeros_like(part)
            scaled[i, head] = jnp.concatenate([part, blank] if head % 2 == 0 else [blank, part], axis=0)
    units = [
        (i, head, rows) for i, job in enumerate(jobs) for head in range(HEADS) for rows in spans(job[7], chunk)
    ]
    d_queries, d_keys, d_values, chances = {}, {}, {}, {}
    for turn in range(len(units) + ahead):
        if turn < len(units):
            i, head, rows = units[turn]
            chances[turn] = dot(jobs[i][3](head // 2, rows), scaled[i, head])
        if turn < ahead:
            continue
        i, head, rows = units[turn - ahead]
        key = (i, head // 2, rows.start)
        exponent = jobs[i][0](head, rows)
        chance = chances.pop(turn - ahead)
        d_values[key] = added(d_values.get(key), dot_nt(exponent, scaled[i, head]))
        score = (exponent.astype(F32) * (chance - centres[i, head])).astype(BF)
        d_keys[key] = added(d_keys.get(key), dot(score, head_lanes(jobs[i][1](head // 2), head)))
        d_queries[i, head] = added(d_queries.get((i, head)), dot(jobs[i][2](head, rows), score))
        if rows.stop == jobs[i][7] and jobs[i][8] is not None:
            jobs[i][8](head)
    results = []
    for i, job in enumerate(jobs):
        starts = [rows.start for rows in spans(job[7], chunk)]
        joined = [
            jnp.concatenate(
                [jnp.concatenate([parts[i, pair, at] for at in starts], axis=0) for pair in range(PAIRS)], axis=1
            )
            for parts in (d_keys, d_values)
        ]
        results.append((jnp.concatenate([d_queries[i, head] for head in range(HEADS)], axis=0), *joined))
    return results


def fold(ref):
    value = ref[...]
    return value.reshape(-1, value.shape[-1])


class Layout:
    def __init__(self, sizes, latents_shape):
        self.clips_dev, self.frames, self.patches, self.width = latents_shape
        self.n_ta, self.n_pa, self.n_dev = sizes["ta"], sizes["pa"], sizes["dev"]
        self.clips = self.clips_dev * self.n_dev
        self.run = self.n_pa // self.clips
        self.group = self.run * self.n_dev
        self.near = self.n_pa // self.group
        self.halves = self.n_ta // self.near
        self.space_rows = self.near * self.patches
        self.time_patches = self.space_rows // self.n_ta
        self.other_rows = (self.group - 1) * self.space_rows
        self.key_rows = self.group * self.space_rows
        self.all_frames = self.n_ta * self.frames
        self.blocks = self.time_patches // BLOCK
        self.early_cot = max(self.blocks - LATE_COT, 1)

    def here(self):
        return {name: lax.axis_index(name) for name in ("ta", "pa", "dev")}

    def clip(self, me):
        return me["pa"] // self.run

    def member(self, me):
        return me["dev"] * self.run + me["pa"] % self.run

    def space_place(self, ta, clip, member):
        return {"ta": ta, "pa": clip * self.run + member % self.run, "dev": member // self.run}

    def space_target(self, me, j):
        return self.space_place(me["ta"], me["dev"] * self.clips_dev + j, me["pa"] // self.near)

    def owner(self, me, ta, slot):
        return {"ta": ta, "pa": self.near * self.member(me) + slot, "dev": self.clip(me) // self.clips_dev}

    def time_target(self, me, j, s):
        place = self.space_target(me, j)
        return {**place, "ta": (me["pa"] % self.near) * self.halves + s}

    def fellow(self, me, step):
        return self.space_place(me["ta"], self.clip(me), (self.member(me) + step) % self.group)

    def across(self, me, step):
        return {**me, "ta": (me["ta"] + step) % self.n_ta}


def is_me(me, place):
    same = None
    for name, index in place.items():
        if index is not me[name]:
            equal = index == me[name]
            same = equal if same is None else same & equal
    return same


def greet(me, place):
    @pl.when(jnp.logical_not(is_me(me, place)))
    def _():
        pl.semaphore_signal(
            pltpu.get_barrier_semaphore(), inc=1, device_id=place, device_id_type=pl.DeviceIdType.MESH
        )


def await_greetings(me, places, amount=0):
    amount = jnp.int32(amount)
    for place in places:
        amount = amount + jnp.logical_not(is_me(me, place)).astype(jnp.int32)
    pl.semaphore_wait(pltpu.get_barrier_semaphore(), amount)


def push(src, dst, send_sem, recv_sem, place):
    return pltpu.make_async_remote_copy(
        src_ref=src,
        dst_ref=dst,
        send_sem=send_sem,
        recv_sem=recv_sem,
        device_id=place,
        device_id_type=pl.DeviceIdType.MESH,
    )


def start_push(me, src, dst, send_sem, recv_sem, place):
    same = is_me(me, place)

    @pl.when(same)
    def _():
        pltpu.make_async_copy(src, dst, recv_sem).start()

    @pl.when(jnp.logical_not(same))
    def _():
        push(src, dst, send_sem, recv_sem, place).start()


def end_push(me, src, dst, send_sem, recv_sem, place):
    @pl.when(jnp.logical_not(is_me(me, place)))
    def _():
        push(src, dst, send_sem, recv_sem, place).wait_send()


def arrived(dst, recv_sem):
    pltpu.make_async_copy(dst, dst, recv_sem).wait()


def space_forward_kernel(
    lay,
    counts_ref,
    latents_ref,
    cot_ref,
    mod_ref,
    attn_ref,
    cross_ref,
    text_keys_ref,
    text_values_t_ref,
    up_ref,
    down_ref,
    state_ref,
    moved_ref,
    own_ref,
    normed_ref,
    query_ref,
    keys_t_ref,
    value_ref,
    exponent_ref,
    att_t_ref,
    att_ref,
    inverse_ref,
    cross_in_ref,
    cross_query_ref,
    cross_exponent_ref,
    cross_att_t_ref,
    cross_att_ref,
    cross_inverse_ref,
    middle_ref,
    normed2_ref,
    act_ref,
    slope_ref,
    branch2_ref,
    branch5_ref,
    own_buf,
    other_buf,
    sent_buf,
    lat_send,
    lat_recv,
    fellow_send,
    fellow_recv,
    state_send,
    state_recv,
    cot_send,
    cot_recv,
):
    scale_by = HDIM ** (-0.5)
    me = lay.here()
    step = pl.program_id(0)
    frames, near = lay.frames, lay.near
    last = step == frames - 1

    def latent_copy(j, f):
        slot = me["pa"] % near
        return (
            latents_ref.at[j, f], own_buf.at[f, slot], lat_send.at[j, f], lat_recv.at[f, slot], lay.space_target(me, j),
        )

    def fellow_copy(turn, f):
        return (
            own_buf.at[f], other_buf.at[f, turn - 1], fellow_send.at[turn - 1, f], fellow_recv.at[turn - 1, f],
            lay.fellow(me, turn),
        )

    def state_copy(turn, f):
        place = lay.across(me, turn)
        row = pl.multiple_of(place["ta"] * lay.time_patches, TILE)
        return (
            sent_buf.at[f, pl.ds(row, lay.time_patches)], state_ref.at[me["ta"] * frames + f], state_send.at[turn, f],
            state_recv.at[turn, f], place,
        )

    def cot_copy(j, s):
        return (
            cot_ref.at[j, :, pl.ds(s * lay.time_patches, lay.early_cot * BLOCK)],
            moved_ref.at[pl.ds(me["ta"] * frames, frames)],
            cot_send.at[j, s], cot_recv.at[me["ta"]], lay.time_target(me, j, s),
        )

    def start_latents(f):
        for j in range(lay.clips_dev):
            start_push(me, *latent_copy(j, f))

    def pass_on(f):
        for slot in range(near):
            arrived(own_buf.at[f, slot], lat_recv.at[f, slot])
        for turn in range(1, lay.group):
            push(*fellow_copy(turn, f)).start()

    @pl.when(step == 0)
    def _():
        for slot in range(near):
            greet(me, lay.owner(me, me["ta"], slot))
        for t in range(lay.n_ta):
            greet(me, lay.owner(me, t, me["ta"] // lay.halves))
        friends = [lay.fellow(me, turn) for turn in range(1, lay.group)]
        friends += [lay.across(me, turn) for turn in range(1, lay.n_ta)]
        for friend in friends:
            greet(me, friend)
        targets = [lay.space_target(me, j) for j in range(lay.clips_dev)]
        targets += [lay.time_target(me, j, s) for j in range(lay.clips_dev) for s in range(lay.halves)]
        await_greetings(me, targets + friends)
        for f in range(frames):
            start_latents(f)
        pass_on(0)

    @pl.when(step == min(2, frames - 1))
    def _():
        for j in range(lay.clips_dev):
            for s in range(lay.halves):
                start_push(me, *cot_copy(j, s))

    for turn in range(1, lay.group):
        arrived(other_buf.at[step, turn - 1], fellow_recv.at[turn - 1, step])
    frame = counts_ref[2] + step
    keep = (frame < counts_ref[0]).astype(F32)
    mod = mod_ref[...]
    own_low = own_buf[step].reshape(lay.space_rows, lay.width)
    own_ref[0] = own_low
    own = own_low.astype(F32)
    rows = lay.space_rows
    normed_own = (norm_parts(own)[0] * (1.0 + mod[1:2]) + mod[0:1]).astype(BF)
    other = other_buf[step].reshape(lay.other_rows, lay.width).astype(F32)
    normed_other = (norm_parts(other)[0] * (1.0 + mod[1:2]) + mod[0:1]).astype(BF)
    normed = jnp.concatenate([normed_own, normed_other], axis=0)
    normed_ref[0] = normed
    queries = (dot(normed_own, attn_ref[0]).astype(BF) * scale_by).astype(BF)
    keys = dot(normed, attn_ref[1]).astype(BF)
    values = dot(normed, attn_ref[2]).astype(BF)
    query_ref[0] = queries
    value_ref[0] = values
    keys_t_ref[0] = keys.T
    values_t = values.T

    def keep_exponent(_, head, keys_span, span, exponent):
        exponent_ref[0, head, keys_span, span] = exponent

    (att_t,), (inverses,) = attend([(queries, keys, values_t, None)], SPACE_STAGE, keep_exponent)
    for head in range(HEADS):
        inverse_ref[0, head : head + 1, :] = inverses[head]
    att_t_ref[0] = att_t.astype(BF)
    att = att_t.T.astype(BF)
    att_ref[0] = att

    @pl.when(jnp.logical_not(last))
    def _():
        pass_on(step + 1)

    branch = dot(att_ref[0], attn_ref[3])
    branch2_ref[0] = branch.astype(BF)
    state = own_ref[0].astype(F32) + (keep * mod[2:3]) * branch
    cross_in = state.astype(BF)
    cross_in_ref[0] = cross_in
    cross_queries = (dot(cross_in, cross_ref[0]).astype(BF) * scale_by).astype(BF)
    cross_query_ref[0] = cross_queries
    text_id = lax.broadcasted_iota(jnp.int32, (text_keys_ref.shape[0], rows), 0)
    bias = jnp.where(text_id < counts_ref[1], 0.0, MASKED_SCORE)

    def keep_cross(_, head, keys_span, span, exponent):
        cross_exponent_ref[0, head, keys_span, span] = exponent

    (cross_t,), (inverses,) = attend(
        [(cross_queries, text_keys_ref[...], text_values_t_ref[...], bias)], CROSS_AHEAD, keep_cross
    )
    for head in range(HEADS):
        cross_inverse_ref[0, head : head + 1, :] = inverses[head]
    cross_att_t_ref[0] = cross_t.astype(BF)
    cross_att = cross_t.T.astype(BF)
    cross_att_ref[0] = cross_att
    state = state + keep * dot(cross_att, cross_ref[1])
    middle_ref[0] = state
    normed2 = (norm_parts(state)[0] * (1.0 + mod[4:5]) + mod[3:4]).astype(BF)
    normed2_ref[0] = normed2
    act, slope = gelu_parts(dot(normed2, up_ref[...]))
    act = act.astype(BF)
    act_ref[0] = act
    slope_ref[0] = slope.astype(BF)
    branch = dot(act, down_ref[...])
    branch5_ref[0] = branch.astype(BF)
    state = state + (keep * mod[5:6]) * branch
    sent_buf[step] = state.astype(BF)
    src, dst, _, sem, _ = state_copy(0, step)
    pltpu.make_async_copy(src, dst, sem).start()
    for turn in range(1, lay.n_ta):
        push(*state_copy(turn, step)).start()

    @pl.when(last)
    def _():
        for f in range(frames):
            for j in range(lay.clips_dev):
                end_push(me, *latent_copy(j, f))
            for turn in range(1, lay.group):
                push(*fellow_copy(turn, f)).wait_send()
            for turn in range(1, lay.n_ta):
                push(*state_copy(turn, f)).wait_send()
            for turn in range(lay.n_ta):
                src, dst, _, sem, _ = state_copy(turn, f)
                arrived(dst, sem)
        for j in range(lay.clips_dev):
            for s in range(lay.halves):
                end_push(me, *cot_copy(j, s))
        for t in range(lay.n_ta):
            arrived(moved_ref.at[pl.ds(t * frames, frames)], cot_recv.at[t])


def space_backward_kernel(
    lay,
    reducer,
    counts_ref,
    grad_ref,
    out_t_ref,
    exponent_ref,
    *refs,
):
    n_sources = len(reducer.shapes)
    sources, refs = refs[:n_sources], refs[n_sources:]
    (mod_ref, attn_ref, cross_ref, text_keys_t_ref, text_values_ref, up_ref, down_ref, own_ref, query_ref, keys_t_ref,
     value_ref, att_t_ref, inverse_ref, cross_query_ref, cross_exponent_ref, cross_att_t_ref, cross_inverse_ref,
     middle_ref, slope_ref, branch2_ref, branch5_ref) = refs[:21]
    (output_ref, lat_grad_ref, last_done_ref, reduced_ref, kept3_ref, d_lifted_ref, kept2_ref, d_cross_query_ref, kept1_ref,
     d_query_ref, d_pair_ref, d_text_keys_ref, d_text_values_ref, mods_ref) = refs[21:35]
    (exponent_buf, other_buf, fellow_buf, state_buf, own_buf, done_buf, exponent_sem, fellow_send, fellow_recv,
     out_send, out_recv, grad_send, grad_recv) = refs[35:48]
    reducer.bind(sources, reduced_ref, refs[48:])
    scale_by = HDIM ** (-0.5)
    me = lay.here()
    step = pl.program_id(0)
    frames = lay.frames
    rows = lay.space_rows
    mod = mod_ref[...]

    slots = frames * 3
    lengths = [0, 1] + [2] * 2 + [1] * (reducer.phases - 8) + [1, 2, 2]
    due_at, at = [], 0
    for length in lengths:
        at += length
        due_at.append(at)
    scale = min(1.0, (slots - 1) / at)
    due_at = [int(when * scale) for when in due_at]

    def hook(number):
        for f in range(frames):
            due = [k for k, when in enumerate(due_at) if when == f * 3 + number]
            if due:

                @pl.when(step == f)
                def _():
                    for k in due:
                        if k == 0:
                            reducer.prepare()
                        reducer.phase(k)

    def exponent_copy(head, f):
        return pltpu.make_async_copy(exponent_ref.at[f, head], exponent_buf.at[head], exponent_sem.at[head])

    def fellow_copy(turn, f):
        return (
            other_buf.at[f % 2, turn - 1], fellow_buf.at[f, turn - 1], fellow_send.at[turn - 1, f],
            fellow_recv.at[turn - 1, f], lay.fellow(me, -turn),
        )

    def out_copy(t):
        part, j = me["ta"] % lay.halves, lay.clip(me) % lay.clips_dev
        return (
            out_t_ref.at[pl.ds(t * frames, frames)], output_ref.at[j, :, part], out_send.at[t],
            out_recv.at[j, part], lay.owner(me, t, me["ta"] // lay.halves),
        )

    def grad_copy(slot, f):
        j = lay.clip(me) % lay.clips_dev
        return (
            done_buf.at[f, slot], lat_grad_ref.at[j, f], grad_send.at[slot, f], grad_recv.at[j, f],
            lay.owner(me, me["ta"], slot),
        )

    @pl.when(step == 0)
    def _():
        for head in range(HEADS):
            exponent_copy(head, 0).start()
        fellows = [lay.fellow(me, turn) for turn in range(1, lay.group)]
        senders = [lay.space_target(me, j) for j in range(lay.clips_dev)]
        senders += [lay.time_target(me, j, s) for j in range(lay.clips_dev) for s in range(lay.halves)]
        for place in fellows + senders:
            greet(me, place)
        takers = [lay.owner(me, me["ta"], slot) for slot in range(lay.near)]
        takers += [lay.owner(me, t, me["ta"] // lay.halves) for t in range(lay.n_ta)]
        await_greetings(me, fellows + takers, reducer.greet())
        for t in range(lay.n_ta):
            start_push(me, *out_copy(t))

    mods_ref[0] = jnp.zeros(mods_ref.shape[1:], F32)

    @pl.when(step < frames)
    def _():
        hook(0)
        keep = (counts_ref[2] + step < counts_ref[0]).astype(F32)
        grad = grad_ref[0].astype(F32)
        kept = keep * grad
        d_gate5 = row_sums(kept * branch5_ref[0].astype(F32))
        d_branch = (kept * mod[5:6]).astype(BF)
        kept3_ref[0] = d_branch
        d_act = dot_nt(d_branch, down_ref[...])
        d_lifted = (d_act * slope_ref[0].astype(F32)).astype(BF)
        d_lifted_ref[0] = d_lifted
        d_normed = dot_nt(d_lifted, up_ref[...])
        hat, inverse = norm_parts(middle_ref[0])
        grad = grad + norm_back(d_normed, hat, inverse, mod[4:5])
        d_shift, d_scale = row_sums(d_normed), row_sums(d_normed * hat)
        kept = (keep * grad).astype(BF)
        kept2_ref[0] = kept
        d_att_t = dot_nt(cross_ref[1], kept)
        job = (
            lambda head, at: cross_exponent_ref[0, head, at, :],
            lambda pair: cross_query_ref[0, :, pair * LANES : (pair + 1) * LANES],
            lambda head, at: text_keys_t_ref[head * HDIM : (head + 1) * HDIM, at],
            lambda pair, at: text_values_ref[at, pair * LANES : (pair + 1) * LANES],
            d_att_t,
            cross_att_t_ref[0].astype(F32),
            lambda head: cross_inverse_ref[0, head : head + 1, :],
            text_values_ref.shape[0],
            None,
        )
        ((d_query_t, d_keys, d_values),) = attend_back([job], CROSS_AHEAD, KEY_CHUNK)
        d_text_keys_ref[0] = d_keys
        d_text_values_ref[0] = d_values
        d_query = (d_query_t.T * scale_by).astype(BF)
        d_cross_query_ref[0] = d_query
        grad = grad + dot_nt(d_query, cross_ref[0])
        state_buf[step % 2] = grad
        kept = keep * grad
        d_gate2 = row_sums(kept * branch2_ref[0].astype(F32))
        mods_ref[0, 2:6, :] = jnp.concatenate([d_gate2, d_shift, d_scale, d_gate5], axis=0)
        d_branch = (kept * mod[2:3]).astype(BF)
        kept1_ref[0] = d_branch
        hook(1)
        d_att_t = dot_nt(attn_ref[3], kept1_ref[0])
        later = jnp.minimum(step + 1, frames - 1)

        def end_head(head):
            exponent_copy(head, later).start()
            if head == HEADS // 2 - 1:
                hook(2)

        def exponent_of(head, at):
            if at.start == 0:
                exponent_copy(head, step).wait()
            return exponent_buf[head, at, :]

        job = (
            exponent_of,
            lambda pair: query_ref[0, :, pair * LANES : (pair + 1) * LANES],
            lambda head, at: keys_t_ref[0, head * HDIM : (head + 1) * HDIM, at],
            lambda pair, at: value_ref[0, at, pair * LANES : (pair + 1) * LANES],
            d_att_t,
            att_t_ref[0].astype(F32),
            lambda head: inverse_ref[0, head : head + 1, :],
            value_ref.shape[1],
            end_head,
        )
        ((d_query_t, d_keys, d_values),) = attend_back([job], BACK_STAGE, KEY_CHUNK)
        d_query = (d_query_t.T * scale_by).astype(BF)
        d_keys, d_values = d_keys.astype(BF), d_values.astype(BF)
        d_query_ref[0] = d_query
        d_pair_ref[0, :, : lay.width] = d_keys
        d_pair_ref[0, :, lay.width :] = d_values
        d_normed = dot_nt(d_keys, attn_ref[1]) + dot_nt(d_values, attn_ref[2])
        own_buf[step % 2] = d_normed[:rows] + dot_nt(d_query, attn_ref[0])

        @pl.when(step > 1)
        def _():
            for turn in range(1, lay.group):
                push(*fellow_copy(turn, step - 2)).wait_send()

        for turn in range(1, lay.group):
            other_buf[step % 2, turn - 1] = d_normed[turn * rows : (turn + 1) * rows].astype(BF)
            push(*fellow_copy(turn, step)).start()

    @pl.when(step > 0)
    def _():
        f = step - 1
        d_normed = own_buf[f % 2]
        for turn in range(1, lay.group):
            arrived(fellow_buf.at[f, turn - 1], fellow_recv.at[turn - 1, f])
            d_normed = d_normed + fellow_buf[f, turn - 1].astype(F32)
        hat, inverse = norm_parts(own_ref[0].astype(F32))
        grad = state_buf[f % 2] + norm_back(d_normed, hat, inverse, mod[1:2])
        done = grad.astype(BF).reshape(done_buf.shape[1:])
        done_buf[f] = done
        last_done_ref[...] = done
        mods_ref[0, 0:2, :] = jnp.concatenate([row_sums(d_normed), row_sums(d_normed * hat)], axis=0)

    @pl.when((step > 0) & (step < frames))
    def _():
        for slot in range(lay.near):
            start_push(me, *grad_copy(slot, step - 1))

    @pl.when(step == frames)
    def _():
        for k in range(len(due_at), reducer.phases):
            reducer.phase(k)
        for head in range(HEADS):
            exponent_copy(head, frames - 1).wait()
        for turn in range(1, lay.group):
            for f in range(max(frames - 2, 0), frames):
                push(*fellow_copy(turn, f)).wait_send()
        for t in range(lay.n_ta):
            end_push(me, *out_copy(t))
        for f in range(frames - 1):
            for slot in range(lay.near):
                end_push(me, *grad_copy(slot, f))
        for j in range(lay.clips_dev):
            for s in range(lay.halves):
                arrived(output_ref.at[j, :, s], out_recv.at[j, s])
            for f in range(frames - 1):
                arrived(lat_grad_ref.at[j, f], grad_recv.at[j, f])


def interleave(streams, lag):
    live, turn = list(enumerate(streams)), 0
    while live:
        left = []
        for i, stream in live:
            if turn < i * lag or next(stream, DONE) is not DONE:
                left.append((i, stream))
        live, turn = left, turn + 1


DONE = object()


def time_kernel(
    lay,
    counts_ref,
    state_ref,
    early_cot_ref,
    cotangent_ref,
    mod_ref,
    bias_ref,
    attn_ref,
    up_ref,
    down_ref,
    grad_s_ref,
    early_ref,
    late_ref,
    d_qkv_sum_ref,
    d_proj_sum_ref,
    d_up_sum_ref,
    d_down_sum_ref,
    mods_ref,
    exponent_ref,
    sent_buf,
    out_buf,
    d_qkv_sum,
    d_proj_sum,
    d_up_sum,
    d_down_sum,
    normed_ref,
    d_qkv_ref,
    att_ref,
    branch4_ref,
    normed2_ref,
    act_ref,
    d_lifted_ref,
    branch5_ref,
    grad_send,
    grad_recv,
    out_send,
    out_recv,
    cot_buf,
    cot_load,
    cot_send,
    cot_recv,
):
    frames, block, width = state_ref.shape
    me = lay.here()
    step = pl.program_id(0)
    last = pl.num_programs(0) - 1

    def grad_copy(turn, i):
        place = lay.across(me, turn)
        row = pl.multiple_of(me["ta"] * lay.time_patches + i * block, TILE)
        return (
            sent_buf.at[i, pl.ds(place["ta"] * lay.frames, lay.frames)], grad_s_ref.at[:, pl.ds(row, block)],
            grad_send.at[turn, i], grad_recv.at[turn, i], place,
        )

    def out_copy(t, i):
        part, j = me["ta"] % lay.halves, lay.clip(me) % lay.clips_dev
        return (
            out_buf.at[i, pl.ds(t * lay.frames, lay.frames)], early_ref.at[j, :, part, pl.ds(i * block, block)],
            out_send.at[t, i], out_recv.at[j, part, i], lay.owner(me, t, me["ta"] // lay.halves),
        )

    def cot_copy(j, s, b):
        row = s * lay.time_patches + (lay.early_cot + b) * block
        return (
            cotangent_ref.at[j, :, row : row + block], cot_buf.at[lay.early_cot + b, pl.ds(me["ta"] * lay.frames, lay.frames)],
            cot_send.at[j, s, b], cot_recv.at[me["ta"], b], lay.time_target(me, j, s),
        )

    def cot_here(i):
        return pltpu.make_async_copy(early_cot_ref.at[:, pl.ds(i * block, block)], cot_buf.at[i], cot_load.at[i])

    late_cot = lay.blocks - lay.early_cot
    early = lay.blocks - 1

    @pl.when(step == 0)
    def _():
        friends = [lay.across(me, turn) for turn in range(1, lay.n_ta)]
        for i in range(lay.early_cot):
            cot_here(i).start()
        parts = [(j, s) for j in range(lay.clips_dev) for s in range(lay.halves)]
        homes = [lay.owner(me, t, me["ta"] // lay.halves) for t in range(lay.n_ta)]
        places = [lay.time_target(me, j, s) for j, s in parts]
        senders = (places if early else []) + (homes if late_cot else [])
        takers = (homes if early else []) + (places if late_cot else [])
        for place in friends + senders:
            greet(me, place)
        await_greetings(me, friends + takers)
        for b in range(late_cot):
            for j, s in parts:
                start_push(me, *cot_copy(j, s, b))
        for total in (d_qkv_sum, d_proj_sum, d_up_sum, d_down_sum):
            total[...] = jnp.zeros_like(total)

    @pl.when(step > 0)
    def _():
        for t in range(lay.n_ta):
            start_push(me, *out_copy(t, step - 1))

    @pl.when(step < lay.early_cot)
    def _():
        cot_here(step).wait()

    if late_cot:

        @pl.when(step >= lay.early_cot)
        def _():
            for t in range(lay.n_ta):
                arrived(cot_buf.at[step, pl.ds(t * lay.frames, lay.frames)], cot_recv.at[t, step - lay.early_cot])

    scale_by = HDIM ** (-0.5)
    run_rows = frames * SUB
    runs = min(STREAM_RUNS, block // SUB)
    mod = mod_ref[...]
    totals = []

    def stream(first_run):
        patches = slice(first_run * SUB, (first_run + runs) * SUB)
        mine = slice(first_run * run_rows, (first_run + runs) * run_rows)

        def load(cube):
            cube = cube.astype(F32)
            parts = [cube[:, r * SUB : (r + 1) * SUB].reshape(run_rows, width) for r in range(runs)]
            return jnp.concatenate(parts, axis=0)

        def stored(value):
            parts = [value[r * run_rows : (r + 1) * run_rows].reshape(frames, SUB, width) for r in range(runs)]
            return jnp.concatenate(parts, axis=1).astype(BF)

        def run_of(value, r):
            return value[r * run_rows : (r + 1) * run_rows]

        state = load(state_ref[:, patches, :])
        frame = (lax.broadcasted_iota(jnp.int32, (runs * run_rows, 1), 0) // SUB) % frames
        keep = (frame < counts_ref[0]).astype(F32)
        hat1, inverse1 = norm_parts(state)
        normed = (hat1 * (1.0 + mod[1:2]) + mod[0:1]).astype(BF)
        normed_ref[mine] = normed
        yield
        queries = (dot(normed, attn_ref[0]).astype(BF) * scale_by).astype(BF)
        keys = dot(normed, attn_ref[1]).astype(BF)
        values = dot(normed, attn_ref[2]).astype(BF)
        yield
        keys_t_runs, jobs = [], []
        for r in range(runs):
            keys_t_runs.append(run_of(keys, r).T)
            jobs.append((run_of(queries, r), run_of(keys, r), run_of(values, r).T, bias_ref[...]))

        def keep_exponent(r, head, keys_span, span, exponent):
            exponent_ref[first_run + r, head, keys_span, span] = exponent

        att_t_runs, inverse_runs = attend(jobs, TIME_STAGE, keep_exponent)
        yield
        att = jnp.concatenate([att_t.T.astype(BF) for att_t in att_t_runs], axis=0)
        att_ref[mine] = att
        branch2 = dot(att, attn_ref[3])
        yield
        state = state + (keep * mod[2:3]) * branch2
        hat2, inverse2 = norm_parts(state)
        normed2 = (hat2 * (1.0 + mod[4:5]) + mod[3:4]).astype(BF)
        normed2_ref[mine] = normed2
        yield
        lifted = dot(normed2, up_ref[...])
        yield
        act, slope = gelu_parts(lifted)
        act = act.astype(BF)
        act_ref[mine] = act
        grad = load(cot_buf[step, :, patches, :])
        kept = keep * grad
        d_branch = (kept * mod[5:6]).astype(BF)
        branch5_ref[mine] = d_branch
        yield
        d_act = dot_nt(d_branch, down_ref[...])
        yield
        d_lifted = (d_act * slope).astype(BF)
        d_lifted_ref[mine] = d_lifted
        branch5 = dot(act, down_ref[...])
        yield
        final = stored(state + (keep * mod[5:6]) * branch5)
        out_buf[step, :, patches, :] = final
        late_ref[:, patches, :] = final
        d_gate5 = row_sums(kept * branch5)
        d_normed2 = dot_nt(d_lifted, up_ref[...])
        yield
        grad = grad + norm_back(d_normed2, hat2, inverse2, mod[4:5])
        kept = keep * grad
        d_gate2 = row_sums(kept * branch2)
        d_branch = (kept * mod[2:3]).astype(BF)
        branch4_ref[mine] = d_branch
        yield
        d_att_t_runs = [dot_nt(attn_ref[3], run_of(d_branch, r)) for r in range(runs)]
        yield

        def job(r):
            query_run, value_run = run_of(queries, r), run_of(values, r)
            return (
                lambda head, at: exponent_ref[first_run + r, head, at, :],
                lambda pair: pair_of(query_run, pair),
                lambda head, at: head_rows(keys_t_runs[r], head)[:, at],
                lambda pair, at: pair_of(value_run, pair)[at],
                d_att_t_runs[r],
                att_t_runs[r],
                lambda head: inverse_runs[r][head],
                run_rows,
                None,
            )

        backs = attend_back([job(r) for r in range(runs)], TIME_STAGE, run_rows)
        yield
        d_qkv = jnp.concatenate(
            [
                jnp.concatenate([(d_query_t.T * scale_by).astype(BF) for d_query_t, _, _ in backs], axis=0),
                jnp.concatenate([d_keys.astype(BF) for _, d_keys, _ in backs], axis=0),
                jnp.concatenate([d_values.astype(BF) for _, _, d_values in backs], axis=0),
            ],
            axis=1,
        )
        d_qkv_ref[mine] = d_qkv
        d_normed1 = sum(dot_nt(d_qkv[:, i * width : (i + 1) * width], attn_ref[i]) for i in range(3))
        yield
        grad = grad + norm_back(d_normed1, hat1, inverse1, mod[1:2])
        sent_buf[step, :, patches, :] = stored(grad)
        totals.append(
            jnp.concatenate(
                [
                    row_sums(d_normed1),
                    row_sums(d_normed1 * hat1),
                    d_gate2,
                    row_sums(d_normed2),
                    row_sums(d_normed2 * hat2),
                    d_gate5,
                    jnp.zeros((2, width), F32),
                ],
                axis=0,
            )
        )

    interleave([stream(first) for first in range(0, block // SUB, runs)], TIME_LAG)
    mods_ref[0] = sum(totals[1:], totals[0])
    src, dst, _, sem, _ = grad_copy(0, step)
    pltpu.make_async_copy(src, dst, sem).start()
    for turn in range(1, lay.n_ta):
        push(*grad_copy(turn, step)).start()

    d_qkv_sum[...] += dot_tn(normed_ref[...], d_qkv_ref[...])
    d_proj_sum[...] += dot_tn(att_ref[...], branch4_ref[...])
    d_up_sum[...] += dot_tn(normed2_ref[...], d_lifted_ref[...])
    d_down_sum[...] += dot_tn(branch5_ref[...], act_ref[...])

    @pl.when(step == last)
    def _():
        d_qkv_sum_ref[...] = d_qkv_sum[...].astype(BF)
        d_proj_sum_ref[...] = d_proj_sum[...].astype(BF)
        d_up_sum_ref[...] = d_up_sum[...].astype(BF)
        d_down_sum_ref[...] = d_down_sum[...].astype(BF)
        for b in range(late_cot):
            for j in range(lay.clips_dev):
                for s in range(lay.halves):
                    end_push(me, *cot_copy(j, s, b))
        for i in range(early):
            for t in range(lay.n_ta):
                end_push(me, *out_copy(t, i))
            for j in range(lay.clips_dev):
                for s in range(lay.halves):
                    arrived(early_ref.at[j, :, s, i * block : (i + 1) * block], out_recv.at[j, s, i])
        for i in range(lay.time_patches // block):
            for turn in range(lay.n_ta):
                src, dst, _, sem, place = grad_copy(turn, i)
                if turn:
                    push(*grad_copy(turn, i)).wait_send()
                arrived(dst, sem)


class Reducer:
    def __init__(self, shapes, small_rows, sizes, parts, direct=False):
        self.direct = direct
        self.width = width = shapes[0][1]
        self.shapes = shapes
        bits = {name: [(name, 1 << i) for i in range(sizes[name].bit_length() - 1)] for name in ("ta", "pa")}
        kinds = [bits["ta"] + bits["pa"], bits["ta"][::-1] + bits["pa"], bits["pa"] + bits["ta"]]
        self.ways = [("dev", 1)] + kinds[0]
        self.loads, row = [], 0
        for i, shape in enumerate(shapes):
            for column in range(shape[1] // width):
                self.loads.append((i, row, column * width, shape[0]))
                row += shape[0]
        self.total = row
        cut = TILE << sum(len(ways) for ways in bits.values())
        self.parts = next((n for n in parts if row % (2 * n * cut) == 0), 1)
        self.part_rows = row // 2 // self.parts
        self.half_rows = row // 2
        self.orders = [[("dev", 1)] + kinds[PATTERN[p % len(PATTERN)]] for p in range(self.parts)]
        self.steps = len(self.ways)
        self.small_rows = small_rows
        self.counts, self.halves, self.boxes, at = [self.part_rows], [True], [], 0
        for _ in range(1, self.steps):
            halve = (self.counts[-1] // 2) % TILE == 0
            self.halves.append(halve)
            self.counts.append(self.counts[-1] // 2 if halve else self.counts[-1])
        for p in range(self.parts):
            self.boxes.append([])
            for count in self.counts:
                self.boxes[p].append(at)
                at += count
        self.box_rows = at
        self.phases = 2 * self.steps + 1

    def scratch(self):
        shapes = [
            pltpu.VMEM((self.total, self.width), BF),
            pltpu.VMEM((self.total, self.width), BF),
            pltpu.VMEM((self.box_rows, self.width), BF),
            pltpu.SemaphoreType.DMA((len(self.loads),)),
            pltpu.SemaphoreType.DMA((self.parts, 2)),
            pltpu.SemaphoreType.DMA((self.parts, 2 * self.steps)),
            pltpu.SemaphoreType.DMA((self.parts, 2 * self.steps)),
        ]
        if self.small_rows:
            shapes += [
                pltpu.VMEM((self.steps, self.small_rows, self.width), F32),
                pltpu.SemaphoreType.DMA((self.steps,)),
                pltpu.SemaphoreType.DMA((self.steps,)),
            ]
        return shapes

    def bind(self, sources, out, scratch, small_in=None, small_out=None):
        self.sources, self.out = sources, out
        self.work, self.whole, self.inbox, self.in_sem, self.out_sem, self.send_sem, self.recv_sem = scratch[:7]
        self.small_in, self.small_out = small_in, small_out
        if self.small_rows:
            self.small_box, self.small_send, self.small_recv = scratch[7:]

    def bit(self, way):
        return (lax.axis_index(way[0]) // way[1]) % 2

    def peer(self, way):
        return {way[0]: lax.axis_index(way[0]) + way[1] - 2 * way[1] * self.bit(way)}

    def greet(self):
        barrier = pltpu.get_barrier_semaphore()
        for way in self.ways:
            pl.semaphore_signal(barrier, inc=1, device_id=self.peer(way), device_id_type=pl.DeviceIdType.MESH)
        return len(self.ways)

    def base(self, p, step):
        row = self.bit(self.orders[p][0]) * self.half_rows + p * self.part_rows
        for s in range(1, step + 1):
            if self.halves[s]:
                row = row + self.bit(self.orders[p][s]) * self.counts[s]
        return row

    def rows(self, ref, row, count):
        return ref.at[pl.ds(pl.multiple_of(row, TILE), count)]

    def load(self, i):
        source, row, column, rows = self.loads[i]
        view = self.sources[source].at[:, column : column + self.width]
        return pltpu.make_async_copy(view, self.work.at[row : row + rows], self.in_sem.at[i])

    def remote(self, src, dst, p, step, way):
        return pltpu.make_async_remote_copy(
            src_ref=src,
            dst_ref=dst,
            send_sem=self.send_sem.at[p, step],
            recv_sem=self.recv_sem.at[p, step],
            device_id=self.peer(way),
            device_id_type=pl.DeviceIdType.MESH,
        )

    def down(self, p, step):
        way, count = self.orders[p][step], self.counts[step]
        if step == 0:
            row = (1 - self.bit(way)) * self.half_rows + p * self.part_rows
        else:
            row = self.base(p, step - 1)
            if self.halves[step]:
                row = row + (1 - self.bit(way)) * count
        box = self.boxes[p][step]
        return self.remote(self.rows(self.work, row, count), self.inbox.at[box : box + count], p, step, way)

    def end_down(self, p, step):
        self.down(p, step).wait()
        count, base, box = self.counts[step], self.base(p, step), self.boxes[p][step]
        chunk = next(c for c in (96, 64, 48, 32, TILE) if count % c == 0)

        def body(i, carry):
            at = pl.ds(pl.multiple_of(base + i * chunk, TILE), chunk)
            got = self.inbox[pl.ds(pl.multiple_of(box + i * chunk, TILE), chunk), :]
            total = (self.work[at, :].astype(F32) + got.astype(F32)).astype(BF)
            if step == self.steps - 1:
                self.whole[at, :] = total
            else:
                self.work[at, :] = total
            return carry

        lax.fori_loop(0, count // chunk, body, 0)

    def up(self, p, turn):
        step = self.steps - 1 - turn
        if not self.halves[step]:
            return None
        rows = self.rows(self.whole, self.base(p, step), self.counts[step])
        return self.remote(rows, rows, p, self.steps + turn, self.orders[p][step])

    def store(self, p, side):
        rows = pl.ds(side * self.half_rows + p * self.part_rows, self.part_rows)
        return pltpu.make_async_copy(self.whole.at[rows], self.out.at[rows], self.out_sem.at[p, side])

    def small(self, step):
        return pltpu.make_async_remote_copy(
            src_ref=self.small_out,
            dst_ref=self.small_box.at[step],
            send_sem=self.small_send.at[step],
            recv_sem=self.small_recv.at[step],
            device_id=self.peer(self.ways[step]),
            device_id_type=pl.DeviceIdType.MESH,
        )

    def prepare(self):
        for i, (source, row, column, rows) in enumerate(self.loads):
            if self.direct:
                self.work[row : row + rows, :] = self.sources[source][:, column : column + self.width].astype(BF)
            else:
                self.load(i).start()
        if self.small_rows:
            self.small_out[...] = self.small_in[...]

    def phase(self, k):
        n = self.steps
        if k == 0 and not self.direct:
            for i in range(len(self.loads)):
                self.load(i).wait()
        for p in range(self.parts):
            if 1 <= k <= n:
                self.end_down(p, k - 1)
            elif k > n:
                before = self.up(p, k - n - 1)
                if before is not None:
                    before.wait()
            if k < n:
                self.down(p, k).start()
            elif k < 2 * n:
                after = self.up(p, k - n)
                if after is not None:
                    after.start()
            else:
                self.store(p, 0).start()
                self.store(p, 1).start()
        if k == 2 * n:
            for p in range(self.parts):
                self.store(p, 0).wait()
                self.store(p, 1).wait()
        if self.small_rows and k <= n:
            if k > 0:
                self.small(k - 1).wait()
                self.small_out[...] = self.small_out[...] + self.small_box[k - 1]
            if k < n:
                self.small(k).start()

    def unpack(self, reduced):
        results, at = [], 0
        for rows, columns in self.shapes:
            turns = columns // self.width
            blocks = [reduced[at + i * rows : at + (i + 1) * rows] for i in range(turns)]
            at += turns * rows
            results.append((blocks[0] if turns == 1 else jnp.concatenate(blocks, axis=1)).astype(F32))
        return results


def weights_kernel(
    lay,
    reducer,
    counts_ref,
    last_done_ref,
    small_ref,
    text_ref,
    normed_ref,
    d_query_ref,
    d_pair_ref,
    att_ref,
    branch2_ref,
    cross_in_ref,
    d_cross_query_ref,
    cross_att_ref,
    cross_branch_ref,
    normed2_ref,
    d_lifted_ref,
    branch5_ref,
    act_ref,
    d_text_keys_ref,
    d_text_values_ref,
    reduced_ref,
    lat_last_ref,
    small_out_ref,
    q_sum,
    pair_sum,
    proj_sum,
    cross_q_sum,
    cross_k_sum,
    cross_v_sum,
    cross_proj_sum,
    up_sum,
    down_sum,
    text_k_sum,
    text_v_sum,
    grad_send,
    grad_recv,
    *scratch,
):
    step = pl.program_id(0)
    sums = (q_sum, pair_sum, proj_sum, cross_q_sum, cross_proj_sum, up_sum, down_sum, text_k_sum, text_v_sum)
    grads = [q_sum, pair_sum, proj_sum, cross_q_sum, cross_k_sum, cross_v_sum, cross_proj_sum, up_sum, down_sum]
    reducer.bind(grads, reduced_ref, scratch, small_ref, small_out_ref)

    me = lay.here()

    def grad_copy(slot):
        j = lay.clip(me) % lay.clips_dev
        return last_done_ref.at[slot], lat_last_ref.at[j], grad_send.at[slot], grad_recv.at[j], lay.owner(me, me["ta"], slot)

    @pl.when(step == 0)
    def _():
        for j in range(lay.clips_dev):
            greet(me, lay.space_target(me, j))
        amount = reducer.greet()
        await_greetings(me, [lay.owner(me, me["ta"], slot) for slot in range(lay.near)], amount)
        for slot in range(lay.near):
            start_push(me, *grad_copy(slot))
        for total in sums:
            total[...] = jnp.zeros_like(total)

    rows = d_query_ref.shape[1]
    q_sum[...] += dot_tn(normed_ref[0, :rows, :], d_query_ref[0])
    pair_sum[...] += dot_tn(normed_ref[0], d_pair_ref[0])
    proj_sum[...] += dot_tn(att_ref[0], branch2_ref[0])
    cross_q_sum[...] += dot_tn(cross_in_ref[0], d_cross_query_ref[0])
    cross_proj_sum[...] += dot_tn(cross_att_ref[0], cross_branch_ref[0])
    up_sum[...] += dot_tn(normed2_ref[0], d_lifted_ref[0])
    down_sum[...] += dot_tn(branch5_ref[0], act_ref[0])
    text_k_sum[...] += d_text_keys_ref[0]
    text_v_sum[...] += d_text_values_ref[0]

    @pl.when(step == pl.num_programs(0) - 1)
    def _():
        for total, result in ((text_k_sum, cross_k_sum), (text_v_sum, cross_v_sum)):
            value = total[...]
            head = value.astype(BF)
            rest = (value - head.astype(F32)).astype(BF)
            result[...] = dot_tn(text_ref[...], head) + dot_tn(text_ref[...], rest)
        reducer.prepare()
        for k in range(reducer.phases):
            reducer.phase(k)
        for slot in range(lay.near):
            end_push(me, *grad_copy(slot))
        for j in range(lay.clips_dev):
            arrived(lat_last_ref.at[j], grad_recv.at[j])


def whole(array):
    zeros = (0,) * array.ndim
    return pl.BlockSpec(array.shape, lambda *grid: zeros)


def framed(array):
    tail = (0,) * (array.ndim - 1)
    return pl.BlockSpec((1,) + tuple(array.shape[1:]), lambda frame: (frame,) + tail)


SCALARS = pl.BlockSpec(memory_space=pltpu.SMEM)
HBM = pl.BlockSpec(memory_space=pl.ANY)


def shape_of(shape, dtype):
    return jax.ShapeDtypeStruct(shape, dtype)


def call(kernel, grid, inputs, in_specs, outputs, out_specs, flops, scratch=(), collective_id=None):
    moved = sum(math.prod(a.shape) * a.dtype.itemsize for a in (*inputs, *outputs))
    return pl.pallas_call(
        kernel,
        grid=grid,
        in_specs=in_specs,
        out_specs=out_specs,
        out_shape=outputs,
        scratch_shapes=list(scratch),
        compiler_params=pltpu.CompilerParams(
            vmem_limit_bytes=VMEM_BYTES, collective_id=collective_id, has_side_effects=collective_id is not None
        ),
        cost_estimate=pl.CostEstimate(flops=int(flops), bytes_accessed=int(moved), transcendentals=0),
    )(*inputs)


def make_per_device(sizes):
    n_ta, n_pa, n_dev = sizes["ta"], sizes["pa"], sizes["dev"]

    def per_device(
        latents,
        context,
        cotangent,
        timesteps,
        frame_counts,
        text_lengths,
        step_proj,
        mod_table,
        patch_attn,
        cross_attn,
        patch_up,
        patch_down,
        frame_attn,
        frame_up,
        frame_down,
    ):
        lay = Layout(sizes, latents.shape)
        clips_dev, frames, patches, width = latents.shape
        clips, run, group, near, halves = lay.clips, lay.run, lay.group, lay.near, lay.halves
        space_rows, other_rows, key_rows = lay.space_rows, lay.other_rows, lay.key_rows
        time_patches, all_frames = lay.time_patches, lay.all_frames
        ta, pa, dev = (lax.axis_index(name) for name in ("ta", "pa", "dev"))
        clip, member = lay.clip(lay.here()), lay.member(lay.here())

        def place(clip_id, member_id):
            return (clip_id * run + member_id % run) * n_dev + member_id // run

        def space_pairs(step):
            pairs = []
            for p in range(n_pa):
                for d in range(n_dev):
                    k = d * clips_dev + (p + step) % clips_dev
                    pairs.append((p * n_dev + d, place(k, p // near)))
            return pairs

        def time_pairs(step):
            u, w = step % halves, step // halves
            pairs = []
            for t in range(n_ta):
                for p in range(n_pa):
                    for d in range(n_dev):
                        s = (t % halves + u) % halves
                        j = (t // halves + w) % clips_dev
                        k = d * clips_dev + j
                        pairs.append(
                            (
                                (t * n_pa + p) * n_dev + d,
                                ((p % near) * halves + s) * n_pa * n_dev + place(k, p // near),
                            )
                        )
            return pairs

        def back(pairs):
            return [(b, a) for a, b in pairs]

        def group_pairs(step):
            return [
                (place(k, g), place(k, (g + step) % group)) for k in range(clips) for g in range(group)
            ]

        def ta_pairs(step):
            return [(t, t ^ step) for t in range(n_ta)]

        whole_axes = ("ta", "pa", "dev")
        pair_axes = ("pa", "dev")

        def of_clip(local):
            both = lax.all_gather(local, "dev", axis=0, tiled=True)
            return lax.dynamic_index_in_dim(both, clip, 0, keepdims=False)

        def sinusoid(steps):
            half = step_proj.shape[0] // 2
            frequency = jnp.exp(-math.log(10000.0) * jnp.arange(half, dtype=F32) / half)
            angles = steps.astype(F32)[:, None] * frequency[None, :]
            return jnp.concatenate([jnp.cos(angles), jnp.sin(angles)], axis=1)

        numbers = lax.all_gather(jnp.stack([timesteps, frame_counts, text_lengths], axis=1), "dev", axis=0, tiled=True)
        own_numbers = lax.dynamic_index_in_dim(numbers, clip, 0, keepdims=False)
        embeddings = sinusoid(numbers[:, 0])
        embedding = lax.dynamic_index_in_dim(embeddings, clip, 0, keepdims=True)
        timing = jnp.dot(embedding, step_proj.astype(F32), precision=HIGHEST).reshape(6, width)
        table = mod_table.astype(F32)
        pad = jnp.zeros((2, width), F32)
        space_mod = jnp.concatenate([timing + table[0], pad])
        frame_mod = jnp.concatenate([timing + table[1], pad])
        counts = jnp.stack([own_numbers[1], own_numbers[2], ta * frames, 0]).astype(jnp.int32)
        text = of_clip(context)
        text_count = text.shape[0]
        text_rows = -(-text_count // LANES) * LANES
        text_wide = jnp.pad(text, ((0, text_rows - text_count), (0, 0)))
        text_keys = dot(text_wide, cross_attn[1]).astype(BF)
        text_values = dot(text_wide, cross_attn[2]).astype(BF)
        cross_ends = jnp.stack([cross_attn[0], cross_attn[3]])

        def out(*shape, dtype=BF):
            return shape_of((frames,) + shape, dtype)

        def moved_tokens():
            return shape_of((all_frames, time_patches, width), BF)

        hidden = patch_up.shape[1]
        inputs = (
            counts, latents, cotangent, space_mod, patch_attn, cross_ends, text_keys, text_values.T,
            patch_up, patch_down,
        )
        outputs = (
            moved_tokens(),
            shape_of((all_frames, lay.early_cot * BLOCK, width), BF),
            out(space_rows, width),
            out(key_rows, width),
            out(space_rows, width),
            out(width, key_rows),
            out(key_rows, width),
            out(HEADS, key_rows, space_rows),
            out(width, space_rows),
            out(space_rows, width),
            out(8, space_rows, dtype=F32),
            out(space_rows, width),
            out(space_rows, width),
            out(HEADS, text_rows, space_rows),
            out(width, space_rows),
            out(space_rows, width),
            out(8, space_rows, dtype=F32),
            out(space_rows, width, dtype=F32),
            out(space_rows, width),
            out(space_rows, hidden),
            out(space_rows, hidden),
            out(space_rows, width),
            out(space_rows, width),
        )
        dense = 2 * frames * space_rows * width * (6 * width + 2 * hidden) + 8 * frames * key_rows * width * width
        dma = pltpu.SemaphoreType.DMA
        state, cot, *saved = call(
            lambda *refs: space_forward_kernel(lay, *refs),
            (frames,),
            inputs,
            [SCALARS, HBM, HBM] + [whole(a) for a in inputs[3:]],
            outputs,
            [HBM, HBM] + [framed(a) for a in outputs[2:]],
            dense + 16 * frames * space_rows * key_rows * width,
            [
                pltpu.VMEM((frames, near, patches, width), BF),
                pltpu.VMEM((frames, group - 1, near, patches, width), BF),
                pltpu.VMEM((frames, space_rows, width), BF),
                dma((clips_dev, frames)),
                dma((frames, near)),
                dma((group - 1, frames)),
                dma((group - 1, frames)),
                dma((n_ta, frames)),
                dma((n_ta, frames)),
                dma((clips_dev, halves)),
                dma((n_ta,)),
            ],
            collective_id=1,
        )

        block_rows = all_frames * BLOCK
        run_rows = all_frames * SUB
        ids = jnp.arange(run_rows, dtype=jnp.int32)
        same = (ids[:, None] % SUB == ids[None, :] % SUB) & (ids[:, None] // SUB < counts[0])
        bias = jnp.where(same, 0.0, MASKED_SCORE).astype(F32)
        hidden = frame_up.shape[1]
        n_blocks = time_patches // BLOCK

        early = max(n_blocks - 1, 1) * BLOCK
        time_inputs = (counts, state, cot, cotangent, frame_mod, bias, frame_attn, frame_up, frame_down)
        time_outputs = (
            out(space_rows, width),
            shape_of((clips_dev, frames, halves, early, width), BF),
            shape_of((all_frames, BLOCK, width), BF),
            shape_of((width, 3 * width), BF),
            shape_of((width, width), BF),
            shape_of((width, hidden), BF),
            shape_of((width, hidden), BF),
            shape_of((n_blocks, 8, width), F32),
        )

        def blocked(array):
            return pl.BlockSpec((all_frames, BLOCK, array.shape[2]), lambda at: (0, at, 0))

        def vmem(*shape, dtype=BF):
            return pltpu.VMEM(shape, dtype)

        (grad_s, early_out, late_out, d_frame_qkv, d_frame_proj, d_frame_up, d_frame_down, frame_six) = call(
            lambda *refs: time_kernel(lay, *refs),
            (n_blocks,),
            time_inputs,
            [SCALARS, blocked(state), HBM, HBM] + [whole(a) for a in time_inputs[4:]],
            time_outputs,
            [HBM, HBM] + [whole(a) for a in time_outputs[2:-1]] + [framed(time_outputs[-1])],
            all_frames * time_patches * width * (32 * width + 20 * hidden),
            [
                vmem(BLOCK // SUB, HEADS, run_rows, run_rows),
                vmem(n_blocks, all_frames, BLOCK, width),
                vmem(n_blocks, all_frames, BLOCK, width),
                vmem(width, 3 * width, dtype=F32),
                vmem(width, width, dtype=F32),
                vmem(width, hidden, dtype=F32),
                vmem(width, hidden, dtype=F32),
                vmem(block_rows, width),
                vmem(block_rows, 3 * width),
                vmem(block_rows, width),
                vmem(block_rows, width),
                vmem(block_rows, width),
                vmem(block_rows, hidden),
                vmem(block_rows, hidden),
                vmem(block_rows, width),
                dma((n_ta, n_blocks)),
                dma((n_ta, n_blocks)),
                dma((n_ta, n_blocks)),
                dma((clips_dev, halves, n_blocks)),
                vmem(n_blocks, all_frames, BLOCK, width),
                dma((n_blocks,)),
                dma((clips_dev, halves, n_blocks)),
                dma((n_ta, n_blocks)),
            ],
            collective_id=2,
        )

        (own, _, query, keys_t, value, exponent, att_t, _, inverse, _, cross_query, cross_exponent, cross_att_t, _,
         cross_inverse, middle, _, _, slope, branch2, branch5) = saved
        frame_grads = [d_frame_proj, d_frame_qkv, d_frame_up, d_frame_down]
        reducer = Reducer([a.shape for a in frame_grads], 0, sizes, HIDDEN_PARTS)
        fixed = (space_mod, patch_attn, cross_ends, text_keys.T, text_values, patch_up, patch_down)
        by_frame = (
            query, keys_t, value, att_t, inverse, cross_query, cross_exponent, cross_att_t, cross_inverse, middle,
            slope, branch2, branch5,
        )
        back_outputs = (
            shape_of((clips_dev, frames, halves, BLOCK, width), BF),
            shape_of((clips_dev, max(frames - 1, 1), patches, width), BF),
            shape_of((near, patches, width), BF),
            shape_of((reducer.total, width), BF),
            out(space_rows, width),
            out(space_rows, hidden),
            out(space_rows, width),
            out(space_rows, width),
            out(space_rows, width),
            out(space_rows, width),
            out(key_rows, 2 * width),
            out(text_rows, width, dtype=F32),
            out(text_rows, width, dtype=F32),
            shape_of((frames + 1, 8, width), F32),
        )

        def now(array):
            tail = (0,) * (array.ndim - 1)
            return pl.BlockSpec((1,) + tuple(array.shape[1:]), lambda at: (jnp.minimum(at, frames - 1),) + tail)

        def before(array):
            tail = (0,) * (array.ndim - 1)
            return pl.BlockSpec((1,) + tuple(array.shape[1:]), lambda at: (jnp.maximum(at, 1) - 1,) + tail)

        dense = 2 * frames * space_rows * width * (6 * width + 2 * hidden) + 8 * frames * key_rows * width * width
        output, lat_grad, last_done, frame_sums, *backs = call(
            lambda *refs: space_backward_kernel(lay, reducer, *refs),
            (frames + 1,),
            (counts, grad_s, late_out, exponent, *frame_grads, *fixed, own, *by_frame),
            [SCALARS, now(grad_s), HBM, HBM] + [HBM] * len(frame_grads) + [whole(a) for a in fixed] + [before(own)]
            + [now(a) for a in by_frame],
            back_outputs,
            [HBM, HBM, whole(back_outputs[2]), HBM] + [now(a) for a in back_outputs[4:-1]] + [framed(back_outputs[-1])],
            dense + 32 * frames * space_rows * key_rows * width,
            [
                pltpu.VMEM((HEADS, key_rows, space_rows), BF),
                pltpu.VMEM((2, group - 1, space_rows, width), BF),
                pltpu.VMEM((frames, group - 1, space_rows, width), BF),
                pltpu.VMEM((2, space_rows, width), F32),
                pltpu.VMEM((2, space_rows, width), F32),
                pltpu.VMEM((frames, near, patches, width), BF),
                dma((HEADS,)),
                dma((group - 1, frames)),
                dma((group - 1, frames)),
                dma((n_ta,)),
                dma((clips_dev, halves)),
                dma((near, frames)),
                dma((clips_dev, frames)),
                *reducer.scratch(),
            ],
            collective_id=3,
        )
        if n_blocks > 1:
            output = jnp.concatenate([early_out, output], axis=3)
        output = output.reshape(latents.shape)

        kept3, d_lifted2, kept2, d_cross_query, kept1, d_query, d_pair, d_tk, d_tv, space_six = backs
        mine = jnp.stack([jnp.sum(space_six, axis=0), jnp.sum(frame_six, axis=0)])
        spread = jnp.where(jnp.arange(clips)[:, None, None, None] == clip, mine[None], 0.0).reshape(-1, width)
        square, pair, lifted = (width, width), (width, 2 * width), (width, hidden)
        shapes = [square, pair, square, square, square, square, square, lifted, lifted]
        tail = Reducer(shapes, spread.shape[0], sizes, PARTS, direct=True)
        by_frame = (
            saved[1], d_query, d_pair, saved[7], kept1, saved[9], d_cross_query, saved[13], kept2, saved[16], d_lifted2,
            kept3, saved[17], d_tk, d_tv,
        )
        tail_outputs = (
            shape_of((tail.total, width), BF),
            shape_of((clips_dev, patches, width), BF),
            shape_of(spread.shape, F32),
        )
        reduced, lat_last, by_clip = call(
            lambda *refs: weights_kernel(lay, tail, *refs),
            (frames,),
            (counts, last_done, spread, text_wide, *by_frame),
            [SCALARS, HBM, whole(spread), whole(text_wide)] + [framed(a) for a in by_frame],
            tail_outputs,
            [HBM, HBM, whole(spread)],
            2 * frames * space_rows * width * (4 * width + 2 * hidden) + 4 * frames * key_rows * width * width,
            [vmem(*shape, dtype=F32) for shape in shapes]
            + [vmem(text_rows, width, dtype=F32)] * 2
            + [dma((near,)), dma((clips_dev,))]
            + tail.scratch(),
            collective_id=0,
        )
        d_patch_q, d_patch_pair, d_patch_proj, *d_cross, d_patch_up, d_patch_down = tail.unpack(reduced)
        d_patch_attn = jnp.stack([d_patch_q, d_patch_pair[:, :width], d_patch_pair[:, width:], d_patch_proj])
        d_cross = jnp.stack(d_cross)
        d_patch_down = d_patch_down.T
        lat_last = lat_last[:, None]
        latents_grad = jnp.concatenate([lat_grad, lat_last], axis=1) if frames > 1 else lat_last
        latents_grad = latents_grad.astype(F32)
        by_clip = by_clip.reshape(clips, 2, 8, width)[:, :, :6]
        d_frame_proj, d_frame_qkv, d_frame_up, d_frame_down = reducer.unpack(frame_sums)
        d_frame_qkv = d_frame_qkv.reshape(width, 3, width).swapaxes(0, 1)
        d_frame_attn = jnp.concatenate([d_frame_qkv, d_frame_proj[None]])
        d_frame_down = d_frame_down.T
        d_table = jnp.sum(by_clip, axis=0)
        d_step = lax.dot_general(
            embeddings,
            jnp.sum(by_clip, axis=1).reshape(clips, -1),
            (((0,), (0,)), ((), ())),
            precision=HIGHEST,
        )
        return (
            output,
            latents_grad,
            d_step,
            d_table,
            d_patch_attn,
            d_cross,
            d_patch_up,
            d_patch_down,
            d_frame_attn,
            d_frame_up,
            d_frame_down,
        )

    return per_device


def solution(mesh):
    sizes = dict(mesh.shape)
    tokens = P("dev", "ta", "pa", None)
    in_specs = (tokens, P("dev", None, None), tokens, P("dev"), P("dev"), P("dev")) + (P(),) * 9
    out_specs = (tokens, tokens) + (P(),) * 9
    return jax.shard_map(
        make_per_device(sizes),
        mesh=mesh,
        in_specs=in_specs,
        out_specs=out_specs,
        check_vma=False,
    )
```

```python
import math

import jax
import jax.numpy as jnp
from jax import lax
from jax.experimental import pallas as pl
from jax.experimental.pallas import tpu as pltpu
from jax.sharding import PartitionSpec as P

HEADS = 6
HDIM = 64
PAIRS = HEADS // 2
LANES = 2 * HDIM
EPSILON = 1e-06
MASKED_SCORE = -1e30
HIGHEST = lax.Precision.HIGHEST
F32 = jnp.float32
BF = jnp.bfloat16
VMEM_BYTES = 60 * 2**20
SUM_ROWS = 16
BLOCK = 32
STREAM_RUNS = 2
LATE_COT = 2
TIME_LAG = 1
SUB = 8
TILE = 16
TIME_STAGE = 8
SPACE_STAGE = 1
BACK_STAGE = 1
CROSS_AHEAD = 2
SPAN = 512
KEY_CHUNK = 256
PARTS = (12, 7, 6, 5, 4, 3, 2)
HIDDEN_PARTS = (3, 2)
PATTERN = (0, 1, 2)


def dot(a, b):
    return jnp.dot(a, b, preferred_element_type=F32)


def dot_nt(a, b):
    return lax.dot_general(a, b, (((1,), (1,)), ((), ())), preferred_element_type=F32)


def dot_tn(a, b):
    return lax.dot_general(a, b, (((0,), (0,)), ((), ())), preferred_element_type=F32)


def norm_parts(values):
    centred = values - jnp.mean(values, axis=-1, keepdims=True)
    inverse = lax.rsqrt(jnp.mean(centred * centred, axis=-1, keepdims=True) + EPSILON)
    return centred * inverse, inverse


def norm_back(d_normed, hat, inverse, scale_by):
    d_hat = d_normed * (1.0 + scale_by)
    mean_d = jnp.mean(d_hat, axis=-1, keepdims=True)
    mean_dh = jnp.mean(d_hat * hat, axis=-1, keepdims=True)
    return inverse * (d_hat - mean_d - hat * mean_dh)


GELU_A = math.sqrt(2.0 / math.pi)
GELU_B = 0.044715


def gelu_parts(values):
    square = values * values
    bent = jnp.tanh(GELU_A * values * (1.0 + GELU_B * square))
    half = 0.5 * (1.0 + bent)
    slope = half + (0.5 * GELU_A) * values * (1.0 - bent * bent) * (1.0 + 3.0 * GELU_B * square)
    return values * half, slope


def row_sums(values):
    return jnp.sum(values, axis=0, keepdims=True)


def head_lanes(values, head):
    lane = lax.broadcasted_iota(jnp.int32, values.shape, 1)
    return jnp.where((lane >= HDIM) == (head % 2 == 1), values, jnp.zeros_like(values))


def pair_of(values, pair):
    return values[:, pair * LANES : (pair + 1) * LANES]


def head_rows(values, head):
    return values[head * HDIM : (head + 1) * HDIM, :]


def lone_rows(values, head):
    rows = head_rows(values, head)
    blank = jnp.zeros_like(rows)
    return jnp.concatenate([rows, blank] if head % 2 == 0 else [blank, rows], axis=0)


def spans(count, size):
    return [slice(at, min(at + size, count)) for at in range(0, count, size)]


def attend(jobs, ahead, keep_exponent):
    units = [
        (i, head, span) for i, job in enumerate(jobs) for head in range(HEADS) for span in spans(job[0].shape[0], SPAN)
    ]
    scores, tops, sums, inverses = {}, {}, {}, {}

    def score(unit, keys_span):
        i, head, span = unit
        queries, keys, _, bias = jobs[i]
        lone = head_lanes(pair_of(queries, head // 2)[span], head)
        value = dot_nt(pair_of(keys, head // 2)[keys_span], lone)
        if bias is not None:
            value = value + bias[keys_span, span]
        scores.setdefault((i, head, span.start), []).append(value)
        top = jnp.max(value, axis=0, keepdims=True)
        old = tops.get((i, head, span.start))
        tops[i, head, span.start] = top if old is None else jnp.maximum(old, top)

    def weigh(unit, index, keys_span):
        i, head, span = unit
        name = (i, head, span.start)
        exponent = jnp.exp(scores[name][index] - tops[name]).astype(BF)
        scores[name][index] = None
        keep_exponent(i, head, keys_span, span, exponent)
        values_t = jobs[i][2]
        count = keys_span.stop - keys_span.start
        lifted = jnp.concatenate([head_rows(values_t, head)[:, keys_span], jnp.ones((SUM_ROWS, count), BF)], axis=0)
        part = dot(lifted, exponent)
        sums[name] = part if name not in sums else sums[name] + part

    def finish(unit):
        i, head, span = unit
        name = (i, head, span.start)
        total = sums[name]
        inverse = 1.0 / total[HDIM : HDIM + 1, :]
        sums[name] = total[:HDIM, :] * inverse
        inverses[name] = inverse

    for turn in range(len(units) + ahead):
        later = units[turn] if turn < len(units) else None
        now = units[turn - ahead] if turn >= ahead else None
        later_spans = spans(jobs[later[0]][1].shape[0], SPAN) if later else []
        now_spans = spans(jobs[now[0]][1].shape[0], SPAN) if now else []
        for index in range(max(len(later_spans), len(now_spans))):
            if index < len(later_spans):
                score(later, later_spans[index])
            if index < len(now_spans):
                weigh(now, index, now_spans[index])
        if now:
            finish(now)

    def joined(parts, i, head):
        starts = [span.start for span in spans(jobs[i][0].shape[0], SPAN)]
        return jnp.concatenate([parts[i, head, start] for start in starts], axis=1)

    return (
        [jnp.concatenate([joined(sums, i, head) for head in range(HEADS)], axis=0) for i in range(len(jobs))],
        [[joined(inverses, i, head) for head in range(HEADS)] for i in range(len(jobs))],
    )


def added(total, part):
    return part if total is None else total + part


def attend_back(jobs, ahead, chunk):
    scaled, centres = {}, {}
    for i, (_, _, _, _, d_att_t, att_t, inverse_of, _, _) in enumerate(jobs):
        for head in range(HEADS):
            inverse = inverse_of(head)
            d_att_head = head_rows(d_att_t, head)
            centres[i, head] = row_sums(d_att_head * head_rows(att_t, head)) * inverse
            part = (d_att_head * inverse).astype(BF)
            blank = jnp.zeros_like(part)
            scaled[i, head] = jnp.concatenate([part, blank] if head % 2 == 0 else [blank, part], axis=0)
    units = [
        (i, head, rows) for i, job in enumerate(jobs) for head in range(HEADS) for rows in spans(job[7], chunk)
    ]
    d_queries, d_keys, d_values, chances = {}, {}, {}, {}
    for turn in range(len(units) + ahead):
        if turn < len(units):
            i, head, rows = units[turn]
            chances[turn] = dot(jobs[i][3](head // 2, rows), scaled[i, head])
        if turn < ahead:
            continue
        i, head, rows = units[turn - ahead]
        key = (i, head // 2, rows.start)
        exponent = jobs[i][0](head, rows)
        chance = chances.pop(turn - ahead)
        d_values[key] = added(d_values.get(key), dot_nt(exponent, scaled[i, head]))
        score = (exponent.astype(F32) * (chance - centres[i, head])).astype(BF)
        d_keys[key] = added(d_keys.get(key), dot(score, head_lanes(jobs[i][1](head // 2), head)))
        d_queries[i, head] = added(d_queries.get((i, head)), dot(jobs[i][2](head, rows), score))
        if rows.stop == jobs[i][7] and jobs[i][8] is not None:
            jobs[i][8](head)
    results = []
    for i, job in enumerate(jobs):
        starts = [rows.start for rows in spans(job[7], chunk)]
        joined = [
            jnp.concatenate(
                [jnp.concatenate([parts[i, pair, at] for at in starts], axis=0) for pair in range(PAIRS)], axis=1
            )
            for parts in (d_keys, d_values)
        ]
        results.append((jnp.concatenate([d_queries[i, head] for head in range(HEADS)], axis=0), *joined))
    return results


def fold(ref):
    value = ref[...]
    return value.reshape(-1, value.shape[-1])


class Layout:
    def __init__(self, sizes, latents_shape):
        self.clips_dev, self.frames, self.patches, self.width = latents_shape
        self.n_ta, self.n_pa, self.n_dev = sizes["ta"], sizes["pa"], sizes["dev"]
        self.clips = self.clips_dev * self.n_dev
        self.run = self.n_pa // self.clips
        self.group = self.run * self.n_dev
        self.near = self.n_pa // self.group
        self.halves = self.n_ta // self.near
        self.space_rows = self.near * self.patches
        self.time_patches = self.space_rows // self.n_ta
        self.other_rows = (self.group - 1) * self.space_rows
        self.key_rows = self.group * self.space_rows
        self.all_frames = self.n_ta * self.frames
        self.blocks = self.time_patches // BLOCK
        self.early_cot = max(self.blocks - LATE_COT, 1)

    def here(self):
        return {name: lax.axis_index(name) for name in ("ta", "pa", "dev")}

    def clip(self, me):
        return me["pa"] // self.run

    def member(self, me):
        return me["dev"] * self.run + me["pa"] % self.run

    def space_place(self, ta, clip, member):
        return {"ta": ta, "pa": clip * self.run + member % self.run, "dev": member // self.run}

    def space_target(self, me, j):
        return self.space_place(me["ta"], me["dev"] * self.clips_dev + j, me["pa"] // self.near)

    def owner(self, me, ta, slot):
        return {"ta": ta, "pa": self.near * self.member(me) + slot, "dev": self.clip(me) // self.clips_dev}

    def chunk(self, ta, clip):
        return (ta + self.halves * (clip % self.near)) % self.n_ta

    def own_chunk(self, me):
        return self.chunk(me["ta"], self.clip(me))

    def home(self, me, ta):
        return self.owner(me, ta, self.own_chunk(me) // self.halves)

    def time_target(self, me, j, s):
        clip = me["dev"] * self.clips_dev + j
        chunk = (me["pa"] % self.near) * self.halves + s
        return {**self.space_target(me, j), "ta": (chunk + self.n_ta - self.halves * (clip % self.near)) % self.n_ta}

    def fellow(self, me, step):
        return self.space_place(me["ta"], self.clip(me), (self.member(me) + step) % self.group)

    def across(self, me, step):
        return {**me, "ta": (me["ta"] + step) % self.n_ta}


def is_me(me, place):
    same = None
    for name, index in place.items():
        if index is not me[name]:
            equal = index == me[name]
            same = equal if same is None else same & equal
    return same


def greet(me, place):
    @pl.when(jnp.logical_not(is_me(me, place)))
    def _():
        pl.semaphore_signal(
            pltpu.get_barrier_semaphore(), inc=1, device_id=place, device_id_type=pl.DeviceIdType.MESH
        )


def await_greetings(me, places, amount=0):
    amount = jnp.int32(amount)
    for place in places:
        amount = amount + jnp.logical_not(is_me(me, place)).astype(jnp.int32)
    pl.semaphore_wait(pltpu.get_barrier_semaphore(), amount)


def push(src, dst, send_sem, recv_sem, place):
    return pltpu.make_async_remote_copy(
        src_ref=src,
        dst_ref=dst,
        send_sem=send_sem,
        recv_sem=recv_sem,
        device_id=place,
        device_id_type=pl.DeviceIdType.MESH,
    )


def start_push(me, src, dst, send_sem, recv_sem, place):
    same = is_me(me, place)

    @pl.when(same)
    def _():
        pltpu.make_async_copy(src, dst, recv_sem).start()

    @pl.when(jnp.logical_not(same))
    def _():
        push(src, dst, send_sem, recv_sem, place).start()


def end_push(me, src, dst, send_sem, recv_sem, place):
    @pl.when(jnp.logical_not(is_me(me, place)))
    def _():
        push(src, dst, send_sem, recv_sem, place).wait_send()


def arrived(dst, recv_sem):
    pltpu.make_async_copy(dst, dst, recv_sem).wait()


def space_forward_kernel(
    lay,
    counts_ref,
    latents_ref,
    cot_ref,
    mod_ref,
    attn_ref,
    cross_ref,
    text_keys_ref,
    text_values_t_ref,
    up_ref,
    down_ref,
    state_ref,
    moved_ref,
    own_ref,
    normed_ref,
    query_ref,
    keys_t_ref,
    value_ref,
    exponent_ref,
    att_t_ref,
    att_ref,
    inverse_ref,
    cross_in_ref,
    cross_query_ref,
    cross_exponent_ref,
    cross_att_t_ref,
    cross_att_ref,
    cross_inverse_ref,
    middle_ref,
    normed2_ref,
    act_ref,
    slope_ref,
    branch2_ref,
    branch5_ref,
    own_buf,
    other_buf,
    sent_buf,
    lat_send,
    lat_recv,
    fellow_send,
    fellow_recv,
    state_send,
    state_recv,
    cot_send,
    cot_recv,
):
    scale_by = HDIM ** (-0.5)
    me = lay.here()
    step = pl.program_id(0)
    frames, near = lay.frames, lay.near
    last = step == frames - 1

    def latent_copy(j, f):
        slot = me["pa"] % near
        return (
            latents_ref.at[j, f], own_buf.at[f, slot], lat_send.at[j, f], lat_recv.at[f, slot], lay.space_target(me, j),
        )

    def fellow_copy(turn, f):
        return (
            own_buf.at[f], other_buf.at[f, turn - 1], fellow_send.at[turn - 1, f], fellow_recv.at[turn - 1, f],
            lay.fellow(me, turn),
        )

    def state_copy(turn, f):
        place = lay.across(me, turn)
        row = pl.multiple_of(lay.chunk(place["ta"], lay.clip(me)) * lay.time_patches, TILE)
        return (
            sent_buf.at[f, pl.ds(row, lay.time_patches)], state_ref.at[me["ta"] * frames + f], state_send.at[turn, f],
            state_recv.at[turn, f], place,
        )

    def cot_copy(j, s):
        return (
            cot_ref.at[j, :, pl.ds(s * lay.time_patches, lay.early_cot * BLOCK)],
            moved_ref.at[pl.ds(me["ta"] * frames, frames)],
            cot_send.at[j, s], cot_recv.at[me["ta"]], lay.time_target(me, j, s),
        )

    def start_latents(f):
        for j in range(lay.clips_dev):
            start_push(me, *latent_copy(j, f))

    def pass_on(f):
        for slot in range(near):
            arrived(own_buf.at[f, slot], lat_recv.at[f, slot])
        for turn in range(1, lay.group):
            push(*fellow_copy(turn, f)).start()

    @pl.when(step == 0)
    def _():
        for slot in range(near):
            greet(me, lay.owner(me, me["ta"], slot))
        for t in range(lay.n_ta):
            greet(me, lay.home(me, t))
        friends = [lay.fellow(me, turn) for turn in range(1, lay.group)]
        friends += [lay.across(me, turn) for turn in range(1, lay.n_ta)]
        for friend in friends:
            greet(me, friend)
        targets = [lay.space_target(me, j) for j in range(lay.clips_dev)]
        targets += [lay.time_target(me, j, s) for j in range(lay.clips_dev) for s in range(lay.halves)]
        await_greetings(me, targets + friends)
        for f in range(frames):
            start_latents(f)
        pass_on(0)

    @pl.when(step == min(2, frames - 1))
    def _():
        for j in range(lay.clips_dev):
            for s in range(lay.halves):
                start_push(me, *cot_copy(j, s))

    for turn in range(1, lay.group):
        arrived(other_buf.at[step, turn - 1], fellow_recv.at[turn - 1, step])
    frame = counts_ref[2] + step
    keep = (frame < counts_ref[0]).astype(F32)
    mod = mod_ref[...]
    own_low = own_buf[step].reshape(lay.space_rows, lay.width)
    own_ref[0] = own_low
    own = own_low.astype(F32)
    rows = lay.space_rows
    normed_own = (norm_parts(own)[0] * (1.0 + mod[1:2]) + mod[0:1]).astype(BF)
    other = other_buf[step].reshape(lay.other_rows, lay.width).astype(F32)
    normed_other = (norm_parts(other)[0] * (1.0 + mod[1:2]) + mod[0:1]).astype(BF)
    normed = jnp.concatenate([normed_own, normed_other], axis=0)
    normed_ref[0] = normed
    queries = (dot(normed_own, attn_ref[0]).astype(BF) * scale_by).astype(BF)
    keys = dot(normed, attn_ref[1]).astype(BF)
    values = dot(normed, attn_ref[2]).astype(BF)
    query_ref[0] = queries
    value_ref[0] = values
    keys_t_ref[0] = keys.T
    values_t = values.T

    def keep_exponent(_, head, keys_span, span, exponent):
        exponent_ref[0, head, keys_span, span] = exponent

    (att_t,), (inverses,) = attend([(queries, keys, values_t, None)], SPACE_STAGE, keep_exponent)
    for head in range(HEADS):
        inverse_ref[0, head : head + 1, :] = inverses[head]
    att_t_ref[0] = att_t.astype(BF)
    att = att_t.T.astype(BF)
    att_ref[0] = att

    @pl.when(jnp.logical_not(last))
    def _():
        pass_on(step + 1)

    branch = dot(att_ref[0], attn_ref[3])
    branch2_ref[0] = branch.astype(BF)
    state = own_ref[0].astype(F32) + (keep * mod[2:3]) * branch
    cross_in = state.astype(BF)
    cross_in_ref[0] = cross_in
    cross_queries = (dot(cross_in, cross_ref[0]).astype(BF) * scale_by).astype(BF)
    cross_query_ref[0] = cross_queries
    text_id = lax.broadcasted_iota(jnp.int32, (text_keys_ref.shape[0], rows), 0)
    bias = jnp.where(text_id < counts_ref[1], 0.0, MASKED_SCORE)

    def keep_cross(_, head, keys_span, span, exponent):
        cross_exponent_ref[0, head, keys_span, span] = exponent

    (cross_t,), (inverses,) = attend(
        [(cross_queries, text_keys_ref[...], text_values_t_ref[...], bias)], CROSS_AHEAD, keep_cross
    )
    for head in range(HEADS):
        cross_inverse_ref[0, head : head + 1, :] = inverses[head]
    cross_att_t_ref[0] = cross_t.astype(BF)
    cross_att = cross_t.T.astype(BF)
    cross_att_ref[0] = cross_att
    state = state + keep * dot(cross_att, cross_ref[1])
    middle_ref[0] = state
    normed2 = (norm_parts(state)[0] * (1.0 + mod[4:5]) + mod[3:4]).astype(BF)
    normed2_ref[0] = normed2
    act, slope = gelu_parts(dot(normed2, up_ref[...]))
    act = act.astype(BF)
    act_ref[0] = act
    slope_ref[0] = slope.astype(BF)
    branch = dot(act, down_ref[...])
    branch5_ref[0] = branch.astype(BF)
    state = state + (keep * mod[5:6]) * branch
    sent_buf[step] = state.astype(BF)
    src, dst, _, sem, _ = state_copy(0, step)
    pltpu.make_async_copy(src, dst, sem).start()
    for turn in range(1, lay.n_ta):
        push(*state_copy(turn, step)).start()

    @pl.when(last)
    def _():
        for f in range(frames):
            for j in range(lay.clips_dev):
                end_push(me, *latent_copy(j, f))
            for turn in range(1, lay.group):
                push(*fellow_copy(turn, f)).wait_send()
            for turn in range(1, lay.n_ta):
                push(*state_copy(turn, f)).wait_send()
            for turn in range(lay.n_ta):
                src, dst, _, sem, _ = state_copy(turn, f)
                arrived(dst, sem)
        for j in range(lay.clips_dev):
            for s in range(lay.halves):
                end_push(me, *cot_copy(j, s))
        for t in range(lay.n_ta):
            arrived(moved_ref.at[pl.ds(t * frames, frames)], cot_recv.at[t])


def space_backward_kernel(
    lay,
    reducer,
    counts_ref,
    grad_ref,
    out_t_ref,
    exponent_ref,
    *refs,
):
    n_sources = len(reducer.shapes)
    sources, refs = refs[:n_sources], refs[n_sources:]
    (mod_ref, attn_ref, cross_ref, text_keys_t_ref, text_values_ref, up_ref, down_ref, own_ref, query_ref, keys_t_ref,
     value_ref, att_t_ref, inverse_ref, cross_query_ref, cross_exponent_ref, cross_att_t_ref, cross_inverse_ref,
     middle_ref, slope_ref, branch2_ref, branch5_ref) = refs[:21]
    (output_ref, lat_grad_ref, last_done_ref, reduced_ref, kept3_ref, d_lifted_ref, kept2_ref, d_cross_query_ref, kept1_ref,
     d_query_ref, d_pair_ref, d_text_keys_ref, d_text_values_ref, mods_ref) = refs[21:35]
    (exponent_buf, other_buf, fellow_buf, state_buf, own_buf, done_buf, exponent_sem, fellow_send, fellow_recv,
     out_send, out_recv, grad_send, grad_recv) = refs[35:48]
    reducer.bind(sources, reduced_ref, refs[48:])
    scale_by = HDIM ** (-0.5)
    me = lay.here()
    step = pl.program_id(0)
    frames = lay.frames
    rows = lay.space_rows
    mod = mod_ref[...]

    slots = frames * 3
    lengths = [0, 1] + [2] * 2 + [1] * (reducer.phases - 8) + [1, 2, 2]
    due_at, at = [], 0
    for length in lengths:
        at += length
        due_at.append(at)
    scale = min(1.0, (slots - 1) / at)
    due_at = [int(when * scale) for when in due_at]

    def hook(number):
        for f in range(frames):
            due = [k for k, when in enumerate(due_at) if when == f * 3 + number]
            if due:

                @pl.when(step == f)
                def _():
                    for k in due:
                        if k == 0:
                            reducer.prepare()
                        reducer.phase(k)

    def exponent_copy(head, f):
        return pltpu.make_async_copy(exponent_ref.at[f, head], exponent_buf.at[head], exponent_sem.at[head])

    def fellow_copy(turn, f):
        return (
            other_buf.at[f % 2, turn - 1], fellow_buf.at[f, turn - 1], fellow_send.at[turn - 1, f],
            fellow_recv.at[turn - 1, f], lay.fellow(me, -turn),
        )

    def out_copy(t):
        part, j = lay.own_chunk(me) % lay.halves, lay.clip(me) % lay.clips_dev
        return (
            out_t_ref.at[pl.ds(t * frames, frames)], output_ref.at[j, :, part], out_send.at[t],
            out_recv.at[j, part], lay.home(me, t),
        )

    def grad_copy(slot, f):
        j = lay.clip(me) % lay.clips_dev
        return (
            done_buf.at[f, slot], lat_grad_ref.at[j, f], grad_send.at[slot, f], grad_recv.at[j, f],
            lay.owner(me, me["ta"], slot),
        )

    @pl.when(step == 0)
    def _():
        for head in range(HEADS):
            exponent_copy(head, 0).start()
        fellows = [lay.fellow(me, turn) for turn in range(1, lay.group)]
        senders = [lay.space_target(me, j) for j in range(lay.clips_dev)]
        senders += [lay.time_target(me, j, s) for j in range(lay.clips_dev) for s in range(lay.halves)]
        for place in fellows + senders:
            greet(me, place)
        takers = [lay.owner(me, me["ta"], slot) for slot in range(lay.near)]
        takers += [lay.home(me, t) for t in range(lay.n_ta)]
        await_greetings(me, fellows + takers, reducer.greet())
        for t in range(lay.n_ta):
            start_push(me, *out_copy(t))

    mods_ref[0] = jnp.zeros(mods_ref.shape[1:], F32)

    @pl.when(step < frames)
    def _():
        hook(0)
        keep = (counts_ref[2] + step < counts_ref[0]).astype(F32)
        grad = grad_ref[0].astype(F32)
        kept = keep * grad
        d_gate5 = row_sums(kept * branch5_ref[0].astype(F32))
        d_branch = (kept * mod[5:6]).astype(BF)
        kept3_ref[0] = d_branch
        d_act = dot_nt(d_branch, down_ref[...])
        d_lifted = (d_act * slope_ref[0].astype(F32)).astype(BF)
        d_lifted_ref[0] = d_lifted
        d_normed = dot_nt(d_lifted, up_ref[...])
        hat, inverse = norm_parts(middle_ref[0])
        grad = grad + norm_back(d_normed, hat, inverse, mod[4:5])
        d_shift, d_scale = row_sums(d_normed), row_sums(d_normed * hat)
        kept = (keep * grad).astype(BF)
        kept2_ref[0] = kept
        d_att_t = dot_nt(cross_ref[1], kept)
        job = (
            lambda head, at: cross_exponent_ref[0, head, at, :],
            lambda pair: cross_query_ref[0, :, pair * LANES : (pair + 1) * LANES],
            lambda head, at: text_keys_t_ref[head * HDIM : (head + 1) * HDIM, at],
            lambda pair, at: text_values_ref[at, pair * LANES : (pair + 1) * LANES],
            d_att_t,
            cross_att_t_ref[0].astype(F32),
            lambda head: cross_inverse_ref[0, head : head + 1, :],
            text_values_ref.shape[0],
            None,
        )
        ((d_query_t, d_keys, d_values),) = attend_back([job], CROSS_AHEAD, KEY_CHUNK)
        d_text_keys_ref[0] = d_keys
        d_text_values_ref[0] = d_values
        d_query = (d_query_t.T * scale_by).astype(BF)
        d_cross_query_ref[0] = d_query
        grad = grad + dot_nt(d_query, cross_ref[0])
        state_buf[step % 2] = grad
        kept = keep * grad
        d_gate2 = row_sums(kept * branch2_ref[0].astype(F32))
        mods_ref[0, 2:6, :] = jnp.concatenate([d_gate2, d_shift, d_scale, d_gate5], axis=0)
        d_branch = (kept * mod[2:3]).astype(BF)
        kept1_ref[0] = d_branch
        hook(1)
        d_att_t = dot_nt(attn_ref[3], kept1_ref[0])
        later = jnp.minimum(step + 1, frames - 1)

        def end_head(head):
            exponent_copy(head, later).start()
            if head == HEADS // 2 - 1:
                hook(2)

        def exponent_of(head, at):
            if at.start == 0:
                exponent_copy(head, step).wait()
            return exponent_buf[head, at, :]

        job = (
            exponent_of,
            lambda pair: query_ref[0, :, pair * LANES : (pair + 1) * LANES],
            lambda head, at: keys_t_ref[0, head * HDIM : (head + 1) * HDIM, at],
            lambda pair, at: value_ref[0, at, pair * LANES : (pair + 1) * LANES],
            d_att_t,
            att_t_ref[0].astype(F32),
            lambda head: inverse_ref[0, head : head + 1, :],
            value_ref.shape[1],
            end_head,
        )
        ((d_query_t, d_keys, d_values),) = attend_back([job], BACK_STAGE, KEY_CHUNK)
        d_query = (d_query_t.T * scale_by).astype(BF)
        d_keys, d_values = d_keys.astype(BF), d_values.astype(BF)
        d_query_ref[0] = d_query
        d_pair_ref[0, :, : lay.width] = d_keys
        d_pair_ref[0, :, lay.width :] = d_values
        d_normed = dot_nt(d_keys, attn_ref[1]) + dot_nt(d_values, attn_ref[2])
        own_buf[step % 2] = d_normed[:rows] + dot_nt(d_query, attn_ref[0])

        @pl.when(step > 1)
        def _():
            for turn in range(1, lay.group):
                push(*fellow_copy(turn, step - 2)).wait_send()

        for turn in range(1, lay.group):
            other_buf[step % 2, turn - 1] = d_normed[turn * rows : (turn + 1) * rows].astype(BF)
            push(*fellow_copy(turn, step)).start()

    @pl.when(step > 0)
    def _():
        f = step - 1
        d_normed = own_buf[f % 2]
        for turn in range(1, lay.group):
            arrived(fellow_buf.at[f, turn - 1], fellow_recv.at[turn - 1, f])
            d_normed = d_normed + fellow_buf[f, turn - 1].astype(F32)
        hat, inverse = norm_parts(own_ref[0].astype(F32))
        grad = state_buf[f % 2] + norm_back(d_normed, hat, inverse, mod[1:2])
        done = grad.astype(BF).reshape(done_buf.shape[1:])
        done_buf[f] = done
        last_done_ref[...] = done
        mods_ref[0, 0:2, :] = jnp.concatenate([row_sums(d_normed), row_sums(d_normed * hat)], axis=0)

    @pl.when((step > 0) & (step < frames))
    def _():
        for slot in range(lay.near):
            start_push(me, *grad_copy(slot, step - 1))

    @pl.when(step == frames)
    def _():
        for k in range(len(due_at), reducer.phases):
            reducer.phase(k)
        for head in range(HEADS):
            exponent_copy(head, frames - 1).wait()
        for turn in range(1, lay.group):
            for f in range(max(frames - 2, 0), frames):
                push(*fellow_copy(turn, f)).wait_send()
        for t in range(lay.n_ta):
            end_push(me, *out_copy(t))
        for f in range(frames - 1):
            for slot in range(lay.near):
                end_push(me, *grad_copy(slot, f))
        for j in range(lay.clips_dev):
            for s in range(lay.halves):
                arrived(output_ref.at[j, :, s], out_recv.at[j, s])
            for f in range(frames - 1):
                arrived(lat_grad_ref.at[j, f], grad_recv.at[j, f])


def interleave(streams, lag):
    live, turn = list(enumerate(streams)), 0
    while live:
        left = []
        for i, stream in live:
            if turn < i * lag or next(stream, DONE) is not DONE:
                left.append((i, stream))
        live, turn = left, turn + 1


DONE = object()


def time_kernel(
    lay,
    counts_ref,
    state_ref,
    early_cot_ref,
    cotangent_ref,
    mod_ref,
    bias_ref,
    attn_ref,
    up_ref,
    down_ref,
    grad_s_ref,
    early_ref,
    late_ref,
    d_qkv_sum_ref,
    d_proj_sum_ref,
    d_up_sum_ref,
    d_down_sum_ref,
    mods_ref,
    exponent_ref,
    sent_buf,
    out_buf,
    d_qkv_sum,
    d_proj_sum,
    d_up_sum,
    d_down_sum,
    normed_ref,
    d_qkv_ref,
    att_ref,
    branch4_ref,
    normed2_ref,
    act_ref,
    d_lifted_ref,
    branch5_ref,
    grad_send,
    grad_recv,
    out_send,
    out_recv,
    cot_buf,
    cot_load,
    cot_send,
    cot_recv,
):
    frames, block, width = state_ref.shape
    me = lay.here()
    step = pl.program_id(0)
    last = pl.num_programs(0) - 1

    def grad_copy(turn, i):
        place = lay.across(me, turn)
        row = pl.multiple_of(lay.own_chunk(me) * lay.time_patches + i * block, TILE)
        return (
            sent_buf.at[i, pl.ds(place["ta"] * lay.frames, lay.frames)], grad_s_ref.at[:, pl.ds(row, block)],
            grad_send.at[turn, i], grad_recv.at[turn, i], place,
        )

    def out_copy(t, i):
        part, j = lay.own_chunk(me) % lay.halves, lay.clip(me) % lay.clips_dev
        return (
            out_buf.at[i, pl.ds(t * lay.frames, lay.frames)], early_ref.at[j, :, part, pl.ds(i * block, block)],
            out_send.at[t, i], out_recv.at[j, part, i], lay.home(me, t),
        )

    def cot_copy(j, s, b):
        row = s * lay.time_patches + (lay.early_cot + b) * block
        return (
            cotangent_ref.at[j, :, row : row + block], cot_buf.at[lay.early_cot + b, pl.ds(me["ta"] * lay.frames, lay.frames)],
            cot_send.at[j, s, b], cot_recv.at[me["ta"], b], lay.time_target(me, j, s),
        )

    def cot_here(i):
        return pltpu.make_async_copy(early_cot_ref.at[:, pl.ds(i * block, block)], cot_buf.at[i], cot_load.at[i])

    late_cot = lay.blocks - lay.early_cot
    early = lay.blocks - 1

    @pl.when(step == 0)
    def _():
        friends = [lay.across(me, turn) for turn in range(1, lay.n_ta)]
        for i in range(lay.early_cot):
            cot_here(i).start()
        parts = [(j, s) for j in range(lay.clips_dev) for s in range(lay.halves)]
        homes = [lay.home(me, t) for t in range(lay.n_ta)]
        places = [lay.time_target(me, j, s) for j, s in parts]
        senders = (places if early else []) + (homes if late_cot else [])
        takers = (homes if early else []) + (places if late_cot else [])
        for place in friends + senders:
            greet(me, place)
        await_greetings(me, friends + takers)
        for b in range(late_cot):
            for j, s in parts:
                start_push(me, *cot_copy(j, s, b))
        for total in (d_qkv_sum, d_proj_sum, d_up_sum, d_down_sum):
            total[...] = jnp.zeros_like(total)

    @pl.when(step > 0)
    def _():
        for t in range(lay.n_ta):
            start_push(me, *out_copy(t, step - 1))

    @pl.when(step < lay.early_cot)
    def _():
        cot_here(step).wait()

    if late_cot:

        @pl.when(step >= lay.early_cot)
        def _():
            for t in range(lay.n_ta):
                arrived(cot_buf.at[step, pl.ds(t * lay.frames, lay.frames)], cot_recv.at[t, step - lay.early_cot])

    scale_by = HDIM ** (-0.5)
    run_rows = frames * SUB
    runs = min(STREAM_RUNS, block // SUB)
    mod = mod_ref[...]
    totals = []

    def stream(first_run):
        patches = slice(first_run * SUB, (first_run + runs) * SUB)
        mine = slice(first_run * run_rows, (first_run + runs) * run_rows)

        def load(cube):
            cube = cube.astype(F32)
            parts = [cube[:, r * SUB : (r + 1) * SUB].reshape(run_rows, width) for r in range(runs)]
            return jnp.concatenate(parts, axis=0)

        def stored(value):
            parts = [value[r * run_rows : (r + 1) * run_rows].reshape(frames, SUB, width) for r in range(runs)]
            return jnp.concatenate(parts, axis=1).astype(BF)

        def run_of(value, r):
            return value[r * run_rows : (r + 1) * run_rows]

        state = load(state_ref[:, patches, :])
        frame = (lax.broadcasted_iota(jnp.int32, (runs * run_rows, 1), 0) // SUB) % frames
        keep = (frame < counts_ref[0]).astype(F32)
        hat1, inverse1 = norm_parts(state)
        normed = (hat1 * (1.0 + mod[1:2]) + mod[0:1]).astype(BF)
        normed_ref[mine] = normed
        yield
        queries = (dot(normed, attn_ref[0]).astype(BF) * scale_by).astype(BF)
        keys = dot(normed, attn_ref[1]).astype(BF)
        values = dot(normed, attn_ref[2]).astype(BF)
        yield
        keys_t_runs, jobs = [], []
        for r in range(runs):
            keys_t_runs.append(run_of(keys, r).T)
            jobs.append((run_of(queries, r), run_of(keys, r), run_of(values, r).T, bias_ref[...]))

        def keep_exponent(r, head, keys_span, span, exponent):
            exponent_ref[first_run + r, head, keys_span, span] = exponent

        att_t_runs, inverse_runs = attend(jobs, TIME_STAGE, keep_exponent)
        yield
        att = jnp.concatenate([att_t.T.astype(BF) for att_t in att_t_runs], axis=0)
        att_ref[mine] = att
        branch2 = dot(att, attn_ref[3])
        yield
        state = state + (keep * mod[2:3]) * branch2
        hat2, inverse2 = norm_parts(state)
        normed2 = (hat2 * (1.0 + mod[4:5]) + mod[3:4]).astype(BF)
        normed2_ref[mine] = normed2
        yield
        lifted = dot(normed2, up_ref[...])
        yield
        act, slope = gelu_parts(lifted)
        act = act.astype(BF)
        act_ref[mine] = act
        grad = load(cot_buf[step, :, patches, :])
        kept = keep * grad
        d_branch = (kept * mod[5:6]).astype(BF)
        branch5_ref[mine] = d_branch
        yield
        d_act = dot_nt(d_branch, down_ref[...])
        yield
        d_lifted = (d_act * slope).astype(BF)
        d_lifted_ref[mine] = d_lifted
        branch5 = dot(act, down_ref[...])
        yield
        final = stored(state + (keep * mod[5:6]) * branch5)
        out_buf[step, :, patches, :] = final
        late_ref[:, patches, :] = final
        d_gate5 = row_sums(kept * branch5)
        d_normed2 = dot_nt(d_lifted, up_ref[...])
        yield
        grad = grad + norm_back(d_normed2, hat2, inverse2, mod[4:5])
        kept = keep * grad
        d_gate2 = row_sums(kept * branch2)
        d_branch = (kept * mod[2:3]).astype(BF)
        branch4_ref[mine] = d_branch
        yield
        d_att_t_runs = [dot_nt(attn_ref[3], run_of(d_branch, r)) for r in range(runs)]
        yield

        def job(r):
            query_run, value_run = run_of(queries, r), run_of(values, r)
            return (
                lambda head, at: exponent_ref[first_run + r, head, at, :],
                lambda pair: pair_of(query_run, pair),
                lambda head, at: head_rows(keys_t_runs[r], head)[:, at],
                lambda pair, at: pair_of(value_run, pair)[at],
                d_att_t_runs[r],
                att_t_runs[r],
                lambda head: inverse_runs[r][head],
                run_rows,
                None,
            )

        backs = attend_back([job(r) for r in range(runs)], TIME_STAGE, run_rows)
        yield
        d_qkv = jnp.concatenate(
            [
                jnp.concatenate([(d_query_t.T * scale_by).astype(BF) for d_query_t, _, _ in backs], axis=0),
                jnp.concatenate([d_keys.astype(BF) for _, d_keys, _ in backs], axis=0),
                jnp.concatenate([d_values.astype(BF) for _, _, d_values in backs], axis=0),
            ],
            axis=1,
        )
        d_qkv_ref[mine] = d_qkv
        d_normed1 = sum(dot_nt(d_qkv[:, i * width : (i + 1) * width], attn_ref[i]) for i in range(3))
        yield
        grad = grad + norm_back(d_normed1, hat1, inverse1, mod[1:2])
        sent_buf[step, :, patches, :] = stored(grad)
        totals.append(
            jnp.concatenate(
                [
                    row_sums(d_normed1),
                    row_sums(d_normed1 * hat1),
                    d_gate2,
                    row_sums(d_normed2),
                    row_sums(d_normed2 * hat2),
                    d_gate5,
                    jnp.zeros((2, width), F32),
                ],
                axis=0,
            )
        )

    interleave([stream(first) for first in range(0, block // SUB, runs)], TIME_LAG)
    mods_ref[0] = sum(totals[1:], totals[0])
    src, dst, _, sem, _ = grad_copy(0, step)
    pltpu.make_async_copy(src, dst, sem).start()
    for turn in range(1, lay.n_ta):
        push(*grad_copy(turn, step)).start()

    d_qkv_sum[...] += dot_tn(normed_ref[...], d_qkv_ref[...])
    d_proj_sum[...] += dot_tn(att_ref[...], branch4_ref[...])
    d_up_sum[...] += dot_tn(normed2_ref[...], d_lifted_ref[...])
    d_down_sum[...] += dot_tn(branch5_ref[...], act_ref[...])

    @pl.when(step == last)
    def _():
        d_qkv_sum_ref[...] = d_qkv_sum[...].astype(BF)
        d_proj_sum_ref[...] = d_proj_sum[...].astype(BF)
        d_up_sum_ref[...] = d_up_sum[...].astype(BF)
        d_down_sum_ref[...] = d_down_sum[...].astype(BF)
        for b in range(late_cot):
            for j in range(lay.clips_dev):
                for s in range(lay.halves):
                    end_push(me, *cot_copy(j, s, b))
        for i in range(early):
            for t in range(lay.n_ta):
                end_push(me, *out_copy(t, i))
            for j in range(lay.clips_dev):
                for s in range(lay.halves):
                    arrived(early_ref.at[j, :, s, i * block : (i + 1) * block], out_recv.at[j, s, i])
        for i in range(lay.time_patches // block):
            for turn in range(lay.n_ta):
                src, dst, _, sem, place = grad_copy(turn, i)
                if turn:
                    push(*grad_copy(turn, i)).wait_send()
                arrived(dst, sem)


class Reducer:
    def __init__(self, shapes, small_rows, sizes, parts, direct=False):
        self.direct = direct
        self.width = width = shapes[0][1]
        self.shapes = shapes
        bits = {name: [(name, 1 << i) for i in range(sizes[name].bit_length() - 1)] for name in ("ta", "pa")}
        kinds = [bits["ta"] + bits["pa"], bits["ta"][::-1] + bits["pa"], bits["pa"] + bits["ta"]]
        self.ways = [("dev", 1)] + kinds[0]
        self.loads, row = [], 0
        for i, shape in enumerate(shapes):
            for column in range(shape[1] // width):
                self.loads.append((i, row, column * width, shape[0]))
                row += shape[0]
        self.total = row
        cut = TILE << sum(len(ways) for ways in bits.values())
        self.parts = next((n for n in parts if row % (2 * n * cut) == 0), 1)
        self.part_rows = row // 2 // self.parts
        self.half_rows = row // 2
        self.orders = [[("dev", 1)] + kinds[PATTERN[p % len(PATTERN)]] for p in range(self.parts)]
        self.steps = len(self.ways)
        self.small_rows = small_rows
        self.counts, self.halves, self.boxes, at = [self.part_rows], [True], [], 0
        for _ in range(1, self.steps):
            halve = (self.counts[-1] // 2) % TILE == 0
            self.halves.append(halve)
            self.counts.append(self.counts[-1] // 2 if halve else self.counts[-1])
        for p in range(self.parts):
            self.boxes.append([])
            for count in self.counts:
                self.boxes[p].append(at)
                at += count
        self.box_rows = at
        self.phases = 2 * self.steps + 1

    def scratch(self):
        shapes = [
            pltpu.VMEM((self.total, self.width), BF),
            pltpu.VMEM((self.total, self.width), BF),
            pltpu.VMEM((self.box_rows, self.width), BF),
            pltpu.SemaphoreType.DMA((len(self.loads),)),
            pltpu.SemaphoreType.DMA((self.parts, 2)),
            pltpu.SemaphoreType.DMA((self.parts, 2 * self.steps)),
            pltpu.SemaphoreType.DMA((self.parts, 2 * self.steps)),
        ]
        if self.small_rows:
            shapes += [
                pltpu.VMEM((self.steps, self.small_rows, self.width), F32),
                pltpu.SemaphoreType.DMA((self.steps,)),
                pltpu.SemaphoreType.DMA((self.steps,)),
            ]
        return shapes

    def bind(self, sources, out, scratch, small_in=None, small_out=None):
        self.sources, self.out = sources, out
        self.work, self.whole, self.inbox, self.in_sem, self.out_sem, self.send_sem, self.recv_sem = scratch[:7]
        self.small_in, self.small_out = small_in, small_out
        if self.small_rows:
            self.small_box, self.small_send, self.small_recv = scratch[7:]

    def bit(self, way):
        return (lax.axis_index(way[0]) // way[1]) % 2

    def peer(self, way):
        return {way[0]: lax.axis_index(way[0]) + way[1] - 2 * way[1] * self.bit(way)}

    def greet(self):
        barrier = pltpu.get_barrier_semaphore()
        for way in self.ways:
            pl.semaphore_signal(barrier, inc=1, device_id=self.peer(way), device_id_type=pl.DeviceIdType.MESH)
        return len(self.ways)

    def base(self, p, step):
        row = self.bit(self.orders[p][0]) * self.half_rows + p * self.part_rows
        for s in range(1, step + 1):
            if self.halves[s]:
                row = row + self.bit(self.orders[p][s]) * self.counts[s]
        return row

    def rows(self, ref, row, count):
        return ref.at[pl.ds(pl.multiple_of(row, TILE), count)]

    def load(self, i):
        source, row, column, rows = self.loads[i]
        view = self.sources[source].at[:, column : column + self.width]
        return pltpu.make_async_copy(view, self.work.at[row : row + rows], self.in_sem.at[i])

    def remote(self, src, dst, p, step, way):
        return pltpu.make_async_remote_copy(
            src_ref=src,
            dst_ref=dst,
            send_sem=self.send_sem.at[p, step],
            recv_sem=self.recv_sem.at[p, step],
            device_id=self.peer(way),
            device_id_type=pl.DeviceIdType.MESH,
        )

    def down(self, p, step):
        way, count = self.orders[p][step], self.counts[step]
        if step == 0:
            row = (1 - self.bit(way)) * self.half_rows + p * self.part_rows
        else:
            row = self.base(p, step - 1)
            if self.halves[step]:
                row = row + (1 - self.bit(way)) * count
        box = self.boxes[p][step]
        return self.remote(self.rows(self.work, row, count), self.inbox.at[box : box + count], p, step, way)

    def end_down(self, p, step):
        self.down(p, step).wait()
        count, base, box = self.counts[step], self.base(p, step), self.boxes[p][step]
        chunk = next(c for c in (96, 64, 48, 32, TILE) if count % c == 0)

        def body(i, carry):
            at = pl.ds(pl.multiple_of(base + i * chunk, TILE), chunk)
            got = self.inbox[pl.ds(pl.multiple_of(box + i * chunk, TILE), chunk), :]
            total = (self.work[at, :].astype(F32) + got.astype(F32)).astype(BF)
            if step == self.steps - 1:
                self.whole[at, :] = total
            else:
                self.work[at, :] = total
            return carry

        lax.fori_loop(0, count // chunk, body, 0)

    def up(self, p, turn):
        step = self.steps - 1 - turn
        if not self.halves[step]:
            return None
        rows = self.rows(self.whole, self.base(p, step), self.counts[step])
        return self.remote(rows, rows, p, self.steps + turn, self.orders[p][step])

    def store(self, p, side):
        rows = pl.ds(side * self.half_rows + p * self.part_rows, self.part_rows)
        return pltpu.make_async_copy(self.whole.at[rows], self.out.at[rows], self.out_sem.at[p, side])

    def small(self, step):
        return pltpu.make_async_remote_copy(
            src_ref=self.small_out,
            dst_ref=self.small_box.at[step],
            send_sem=self.small_send.at[step],
            recv_sem=self.small_recv.at[step],
            device_id=self.peer(self.ways[step]),
            device_id_type=pl.DeviceIdType.MESH,
        )

    def prepare(self):
        for i, (source, row, column, rows) in enumerate(self.loads):
            if self.direct:
                self.work[row : row + rows, :] = self.sources[source][:, column : column + self.width].astype(BF)
            else:
                self.load(i).start()
        if self.small_rows:
            self.small_out[...] = self.small_in[...]

    def phase(self, k):
        n = self.steps
        if k == 0 and not self.direct:
            for i in range(len(self.loads)):
                self.load(i).wait()
        for p in range(self.parts):
            if 1 <= k <= n:
                self.end_down(p, k - 1)
            elif k > n:
                before = self.up(p, k - n - 1)
                if before is not None:
                    before.wait()
            if k < n:
                self.down(p, k).start()
            elif k < 2 * n:
                after = self.up(p, k - n)
                if after is not None:
                    after.start()
            else:
                self.store(p, 0).start()
                self.store(p, 1).start()
        if k == 2 * n:
            for p in range(self.parts):
                self.store(p, 0).wait()
                self.store(p, 1).wait()
        if self.small_rows and k <= n:
            if k > 0:
                self.small(k - 1).wait()
                self.small_out[...] = self.small_out[...] + self.small_box[k - 1]
            if k < n:
                self.small(k).start()

    def unpack(self, reduced):
        results, at = [], 0
        for rows, columns in self.shapes:
            turns = columns // self.width
            blocks = [reduced[at + i * rows : at + (i + 1) * rows] for i in range(turns)]
            at += turns * rows
            results.append((blocks[0] if turns == 1 else jnp.concatenate(blocks, axis=1)).astype(F32))
        return results


def weights_kernel(
    lay,
    reducer,
    counts_ref,
    last_done_ref,
    small_ref,
    text_ref,
    normed_ref,
    d_query_ref,
    d_pair_ref,
    att_ref,
    branch2_ref,
    cross_in_ref,
    d_cross_query_ref,
    cross_att_ref,
    cross_branch_ref,
    normed2_ref,
    d_lifted_ref,
    branch5_ref,
    act_ref,
    d_text_keys_ref,
    d_text_values_ref,
    reduced_ref,
    lat_last_ref,
    small_out_ref,
    q_sum,
    pair_sum,
    proj_sum,
    cross_q_sum,
    cross_k_sum,
    cross_v_sum,
    cross_proj_sum,
    up_sum,
    down_sum,
    text_k_sum,
    text_v_sum,
    grad_send,
    grad_recv,
    *scratch,
):
    step = pl.program_id(0)
    sums = (q_sum, pair_sum, proj_sum, cross_q_sum, cross_proj_sum, up_sum, down_sum, text_k_sum, text_v_sum)
    grads = [q_sum, pair_sum, proj_sum, cross_q_sum, cross_k_sum, cross_v_sum, cross_proj_sum, up_sum, down_sum]
    reducer.bind(grads, reduced_ref, scratch, small_ref, small_out_ref)

    me = lay.here()

    def grad_copy(slot):
        j = lay.clip(me) % lay.clips_dev
        return last_done_ref.at[slot], lat_last_ref.at[j], grad_send.at[slot], grad_recv.at[j], lay.owner(me, me["ta"], slot)

    @pl.when(step == 0)
    def _():
        for j in range(lay.clips_dev):
            greet(me, lay.space_target(me, j))
        amount = reducer.greet()
        await_greetings(me, [lay.owner(me, me["ta"], slot) for slot in range(lay.near)], amount)
        for slot in range(lay.near):
            start_push(me, *grad_copy(slot))
        for total in sums:
            total[...] = jnp.zeros_like(total)

    rows = d_query_ref.shape[1]
    q_sum[...] += dot_tn(normed_ref[0, :rows, :], d_query_ref[0])
    pair_sum[...] += dot_tn(normed_ref[0], d_pair_ref[0])
    proj_sum[...] += dot_tn(att_ref[0], branch2_ref[0])
    cross_q_sum[...] += dot_tn(cross_in_ref[0], d_cross_query_ref[0])
    cross_proj_sum[...] += dot_tn(cross_att_ref[0], cross_branch_ref[0])
    up_sum[...] += dot_tn(normed2_ref[0], d_lifted_ref[0])
    down_sum[...] += dot_tn(branch5_ref[0], act_ref[0])
    text_k_sum[...] += d_text_keys_ref[0]
    text_v_sum[...] += d_text_values_ref[0]

    @pl.when(step == pl.num_programs(0) - 1)
    def _():
        for total, result in ((text_k_sum, cross_k_sum), (text_v_sum, cross_v_sum)):
            value = total[...]
            head = value.astype(BF)
            rest = (value - head.astype(F32)).astype(BF)
            result[...] = dot_tn(text_ref[...], head) + dot_tn(text_ref[...], rest)
        reducer.prepare()
        for k in range(reducer.phases):
            reducer.phase(k)
        for slot in range(lay.near):
            end_push(me, *grad_copy(slot))
        for j in range(lay.clips_dev):
            arrived(lat_last_ref.at[j], grad_recv.at[j])


def whole(array):
    zeros = (0,) * array.ndim
    return pl.BlockSpec(array.shape, lambda *grid: zeros)


def framed(array):
    tail = (0,) * (array.ndim - 1)
    return pl.BlockSpec((1,) + tuple(array.shape[1:]), lambda frame: (frame,) + tail)


SCALARS = pl.BlockSpec(memory_space=pltpu.SMEM)
HBM = pl.BlockSpec(memory_space=pl.ANY)


def shape_of(shape, dtype):
    return jax.ShapeDtypeStruct(shape, dtype)


def call(kernel, grid, inputs, in_specs, outputs, out_specs, flops, scratch=(), collective_id=None):
    moved = sum(math.prod(a.shape) * a.dtype.itemsize for a in (*inputs, *outputs))
    return pl.pallas_call(
        kernel,
        grid=grid,
        in_specs=in_specs,
        out_specs=out_specs,
        out_shape=outputs,
        scratch_shapes=list(scratch),
        compiler_params=pltpu.CompilerParams(
            vmem_limit_bytes=VMEM_BYTES, collective_id=collective_id, has_side_effects=collective_id is not None
        ),
        cost_estimate=pl.CostEstimate(flops=int(flops), bytes_accessed=int(moved), transcendentals=0),
    )(*inputs)


def make_per_device(sizes):
    n_ta, n_pa, n_dev = sizes["ta"], sizes["pa"], sizes["dev"]

    def per_device(
        latents,
        context,
        cotangent,
        timesteps,
        frame_counts,
        text_lengths,
        step_proj,
        mod_table,
        patch_attn,
        cross_attn,
        patch_up,
        patch_down,
        frame_attn,
        frame_up,
        frame_down,
    ):
        lay = Layout(sizes, latents.shape)
        clips_dev, frames, patches, width = latents.shape
        clips, run, group, near, halves = lay.clips, lay.run, lay.group, lay.near, lay.halves
        space_rows, other_rows, key_rows = lay.space_rows, lay.other_rows, lay.key_rows
        time_patches, all_frames = lay.time_patches, lay.all_frames
        ta, pa, dev = (lax.axis_index(name) for name in ("ta", "pa", "dev"))
        clip, member = lay.clip(lay.here()), lay.member(lay.here())

        def place(clip_id, member_id):
            return (clip_id * run + member_id % run) * n_dev + member_id // run

        def space_pairs(step):
            pairs = []
            for p in range(n_pa):
                for d in range(n_dev):
                    k = d * clips_dev + (p + step) % clips_dev
                    pairs.append((p * n_dev + d, place(k, p // near)))
            return pairs

        def time_pairs(step):
            u, w = step % halves, step // halves
            pairs = []
            for t in range(n_ta):
                for p in range(n_pa):
                    for d in range(n_dev):
                        s = (t % halves + u) % halves
                        j = (t // halves + w) % clips_dev
                        k = d * clips_dev + j
                        pairs.append(
                            (
                                (t * n_pa + p) * n_dev + d,
                                ((p % near) * halves + s) * n_pa * n_dev + place(k, p // near),
                            )
                        )
            return pairs

        def back(pairs):
            return [(b, a) for a, b in pairs]

        def group_pairs(step):
            return [
                (place(k, g), place(k, (g + step) % group)) for k in range(clips) for g in range(group)
            ]

        def ta_pairs(step):
            return [(t, t ^ step) for t in range(n_ta)]

        whole_axes = ("ta", "pa", "dev")
        pair_axes = ("pa", "dev")

        def of_clip(local):
            both = lax.all_gather(local, "dev", axis=0, tiled=True)
            return lax.dynamic_index_in_dim(both, clip, 0, keepdims=False)

        def sinusoid(steps):
            half = step_proj.shape[0] // 2
            frequency = jnp.exp(-math.log(10000.0) * jnp.arange(half, dtype=F32) / half)
            angles = steps.astype(F32)[:, None] * frequency[None, :]
            return jnp.concatenate([jnp.cos(angles), jnp.sin(angles)], axis=1)

        numbers = lax.all_gather(jnp.stack([timesteps, frame_counts, text_lengths], axis=1), "dev", axis=0, tiled=True)
        own_numbers = lax.dynamic_index_in_dim(numbers, clip, 0, keepdims=False)
        embeddings = sinusoid(numbers[:, 0])
        embedding = lax.dynamic_index_in_dim(embeddings, clip, 0, keepdims=True)
        timing = jnp.dot(embedding, step_proj.astype(F32), precision=HIGHEST).reshape(6, width)
        table = mod_table.astype(F32)
        pad = jnp.zeros((2, width), F32)
        space_mod = jnp.concatenate([timing + table[0], pad])
        frame_mod = jnp.concatenate([timing + table[1], pad])
        counts = jnp.stack([own_numbers[1], own_numbers[2], ta * frames, 0]).astype(jnp.int32)
        text = of_clip(context)
        text_count = text.shape[0]
        text_rows = -(-text_count // LANES) * LANES
        text_wide = jnp.pad(text, ((0, text_rows - text_count), (0, 0)))
        text_keys = dot(text_wide, cross_attn[1]).astype(BF)
        text_values = dot(text_wide, cross_attn[2]).astype(BF)
        cross_ends = jnp.stack([cross_attn[0], cross_attn[3]])

        def out(*shape, dtype=BF):
            return shape_of((frames,) + shape, dtype)

        def moved_tokens():
            return shape_of((all_frames, time_patches, width), BF)

        hidden = patch_up.shape[1]
        inputs = (
            counts, latents, cotangent, space_mod, patch_attn, cross_ends, text_keys, text_values.T,
            patch_up, patch_down,
        )
        outputs = (
            moved_tokens(),
            shape_of((all_frames, lay.early_cot * BLOCK, width), BF),
            out(space_rows, width),
            out(key_rows, width),
            out(space_rows, width),
            out(width, key_rows),
            out(key_rows, width),
            out(HEADS, key_rows, space_rows),
            out(width, space_rows),
            out(space_rows, width),
            out(8, space_rows, dtype=F32),
            out(space_rows, width),
            out(space_rows, width),
            out(HEADS, text_rows, space_rows),
            out(width, space_rows),
            out(space_rows, width),
            out(8, space_rows, dtype=F32),
            out(space_rows, width, dtype=F32),
            out(space_rows, width),
            out(space_rows, hidden),
            out(space_rows, hidden),
            out(space_rows, width),
            out(space_rows, width),
        )
        dense = 2 * frames * space_rows * width * (6 * width + 2 * hidden) + 8 * frames * key_rows * width * width
        dma = pltpu.SemaphoreType.DMA
        state, cot, *saved = call(
            lambda *refs: space_forward_kernel(lay, *refs),
            (frames,),
            inputs,
            [SCALARS, HBM, HBM] + [whole(a) for a in inputs[3:]],
            outputs,
            [HBM, HBM] + [framed(a) for a in outputs[2:]],
            dense + 16 * frames * space_rows * key_rows * width,
            [
                pltpu.VMEM((frames, near, patches, width), BF),
                pltpu.VMEM((frames, group - 1, near, patches, width), BF),
                pltpu.VMEM((frames, space_rows, width), BF),
                dma((clips_dev, frames)),
                dma((frames, near)),
                dma((group - 1, frames)),
                dma((group - 1, frames)),
                dma((n_ta, frames)),
                dma((n_ta, frames)),
                dma((clips_dev, halves)),
                dma((n_ta,)),
            ],
            collective_id=1,
        )

        block_rows = all_frames * BLOCK
        run_rows = all_frames * SUB
        ids = jnp.arange(run_rows, dtype=jnp.int32)
        same = (ids[:, None] % SUB == ids[None, :] % SUB) & (ids[:, None] // SUB < counts[0])
        bias = jnp.where(same, 0.0, MASKED_SCORE).astype(F32)
        hidden = frame_up.shape[1]
        n_blocks = time_patches // BLOCK

        early = max(n_blocks - 1, 1) * BLOCK
        time_inputs = (counts, state, cot, cotangent, frame_mod, bias, frame_attn, frame_up, frame_down)
        time_outputs = (
            out(space_rows, width),
            shape_of((clips_dev, frames, halves, early, width), BF),
            shape_of((all_frames, BLOCK, width), BF),
            shape_of((width, 3 * width), BF),
            shape_of((width, width), BF),
            shape_of((width, hidden), BF),
            shape_of((width, hidden), BF),
            shape_of((n_blocks, 8, width), F32),
        )

        def blocked(array):
            return pl.BlockSpec((all_frames, BLOCK, array.shape[2]), lambda at: (0, at, 0))

        def vmem(*shape, dtype=BF):
            return pltpu.VMEM(shape, dtype)

        (grad_s, early_out, late_out, d_frame_qkv, d_frame_proj, d_frame_up, d_frame_down, frame_six) = call(
            lambda *refs: time_kernel(lay, *refs),
            (n_blocks,),
            time_inputs,
            [SCALARS, blocked(state), HBM, HBM] + [whole(a) for a in time_inputs[4:]],
            time_outputs,
            [HBM, HBM] + [whole(a) for a in time_outputs[2:-1]] + [framed(time_outputs[-1])],
            all_frames * time_patches * width * (32 * width + 20 * hidden),
            [
                vmem(BLOCK // SUB, HEADS, run_rows, run_rows),
                vmem(n_blocks, all_frames, BLOCK, width),
                vmem(n_blocks, all_frames, BLOCK, width),
                vmem(width, 3 * width, dtype=F32),
                vmem(width, width, dtype=F32),
                vmem(width, hidden, dtype=F32),
                vmem(width, hidden, dtype=F32),
                vmem(block_rows, width),
                vmem(block_rows, 3 * width),
                vmem(block_rows, width),
                vmem(block_rows, width),
                vmem(block_rows, width),
                vmem(block_rows, hidden),
                vmem(block_rows, hidden),
                vmem(block_rows, width),
                dma((n_ta, n_blocks)),
                dma((n_ta, n_blocks)),
                dma((n_ta, n_blocks)),
                dma((clips_dev, halves, n_blocks)),
                vmem(n_blocks, all_frames, BLOCK, width),
                dma((n_blocks,)),
                dma((clips_dev, halves, n_blocks)),
                dma((n_ta, n_blocks)),
            ],
            collective_id=2,
        )

        (own, _, query, keys_t, value, exponent, att_t, _, inverse, _, cross_query, cross_exponent, cross_att_t, _,
         cross_inverse, middle, _, _, slope, branch2, branch5) = saved
        frame_grads = [d_frame_proj, d_frame_qkv, d_frame_up, d_frame_down]
        reducer = Reducer([a.shape for a in frame_grads], 0, sizes, HIDDEN_PARTS)
        fixed = (space_mod, patch_attn, cross_ends, text_keys.T, text_values, patch_up, patch_down)
        by_frame = (
            query, keys_t, value, att_t, inverse, cross_query, cross_exponent, cross_att_t, cross_inverse, middle,
            slope, branch2, branch5,
        )
        back_outputs = (
            shape_of((clips_dev, frames, halves, BLOCK, width), BF),
            shape_of((clips_dev, max(frames - 1, 1), patches, width), BF),
            shape_of((near, patches, width), BF),
            shape_of((reducer.total, width), BF),
            out(space_rows, width),
            out(space_rows, hidden),
            out(space_rows, width),
            out(space_rows, width),
            out(space_rows, width),
            out(space_rows, width),
            out(key_rows, 2 * width),
            out(text_rows, width, dtype=F32),
            out(text_rows, width, dtype=F32),
            shape_of((frames + 1, 8, width), F32),
        )

        def now(array):
            tail = (0,) * (array.ndim - 1)
            return pl.BlockSpec((1,) + tuple(array.shape[1:]), lambda at: (jnp.minimum(at, frames - 1),) + tail)

        def before(array):
            tail = (0,) * (array.ndim - 1)
            return pl.BlockSpec((1,) + tuple(array.shape[1:]), lambda at: (jnp.maximum(at, 1) - 1,) + tail)

        dense = 2 * frames * space_rows * width * (6 * width + 2 * hidden) + 8 * frames * key_rows * width * width
        output, lat_grad, last_done, frame_sums, *backs = call(
            lambda *refs: space_backward_kernel(lay, reducer, *refs),
            (frames + 1,),
            (counts, grad_s, late_out, exponent, *frame_grads, *fixed, own, *by_frame),
            [SCALARS, now(grad_s), HBM, HBM] + [HBM] * len(frame_grads) + [whole(a) for a in fixed] + [before(own)]
            + [now(a) for a in by_frame],
            back_outputs,
            [HBM, HBM, whole(back_outputs[2]), HBM] + [now(a) for a in back_outputs[4:-1]] + [framed(back_outputs[-1])],
            dense + 32 * frames * space_rows * key_rows * width,
            [
                pltpu.VMEM((HEADS, key_rows, space_rows), BF),
                pltpu.VMEM((2, group - 1, space_rows, width), BF),
                pltpu.VMEM((frames, group - 1, space_rows, width), BF),
                pltpu.VMEM((2, space_rows, width), F32),
                pltpu.VMEM((2, space_rows, width), F32),
                pltpu.VMEM((frames, near, patches, width), BF),
                dma((HEADS,)),
                dma((group - 1, frames)),
                dma((group - 1, frames)),
                dma((n_ta,)),
                dma((clips_dev, halves)),
                dma((near, frames)),
                dma((clips_dev, frames)),
                *reducer.scratch(),
            ],
            collective_id=3,
        )
        if n_blocks > 1:
            output = jnp.concatenate([early_out, output], axis=3)
        output = output.reshape(latents.shape)

        kept3, d_lifted2, kept2, d_cross_query, kept1, d_query, d_pair, d_tk, d_tv, space_six = backs
        mine = jnp.stack([jnp.sum(space_six, axis=0), jnp.sum(frame_six, axis=0)])
        spread = jnp.where(jnp.arange(clips)[:, None, None, None] == clip, mine[None], 0.0).reshape(-1, width)
        square, pair, lifted = (width, width), (width, 2 * width), (width, hidden)
        shapes = [square, pair, square, square, square, square, square, lifted, lifted]
        tail = Reducer(shapes, spread.shape[0], sizes, PARTS, direct=True)
        by_frame = (
            saved[1], d_query, d_pair, saved[7], kept1, saved[9], d_cross_query, saved[13], kept2, saved[16], d_lifted2,
            kept3, saved[17], d_tk, d_tv,
        )
        tail_outputs = (
            shape_of((tail.total, width), BF),
            shape_of((clips_dev, patches, width), BF),
            shape_of(spread.shape, F32),
        )
        reduced, lat_last, by_clip = call(
            lambda *refs: weights_kernel(lay, tail, *refs),
            (frames,),
            (counts, last_done, spread, text_wide, *by_frame),
            [SCALARS, HBM, whole(spread), whole(text_wide)] + [framed(a) for a in by_frame],
            tail_outputs,
            [HBM, HBM, whole(spread)],
            2 * frames * space_rows * width * (4 * width + 2 * hidden) + 4 * frames * key_rows * width * width,
            [vmem(*shape, dtype=F32) for shape in shapes]
            + [vmem(text_rows, width, dtype=F32)] * 2
            + [dma((near,)), dma((clips_dev,))]
            + tail.scratch(),
            collective_id=0,
        )
        d_patch_q, d_patch_pair, d_patch_proj, *d_cross, d_patch_up, d_patch_down = tail.unpack(reduced)
        d_patch_attn = jnp.stack([d_patch_q, d_patch_pair[:, :width], d_patch_pair[:, width:], d_patch_proj])
        d_cross = jnp.stack(d_cross)
        d_patch_down = d_patch_down.T
        lat_last = lat_last[:, None]
        latents_grad = jnp.concatenate([lat_grad, lat_last], axis=1) if frames > 1 else lat_last
        latents_grad = latents_grad.astype(F32)
        by_clip = by_clip.reshape(clips, 2, 8, width)[:, :, :6]
        d_frame_proj, d_frame_qkv, d_frame_up, d_frame_down = reducer.unpack(frame_sums)
        d_frame_qkv = d_frame_qkv.reshape(width, 3, width).swapaxes(0, 1)
        d_frame_attn = jnp.concatenate([d_frame_qkv, d_frame_proj[None]])
        d_frame_down = d_frame_down.T
        d_table = jnp.sum(by_clip, axis=0)
        d_step = lax.dot_general(
            embeddings,
            jnp.sum(by_clip, axis=1).reshape(clips, -1),
            (((0,), (0,)), ((), ())),
            precision=HIGHEST,
        )
        return (
            output,
            latents_grad,
            d_step,
            d_table,
            d_patch_attn,
            d_cross,
            d_patch_up,
            d_patch_down,
            d_frame_attn,
            d_frame_up,
            d_frame_down,
        )

    return per_device


def solution(mesh):
    sizes = dict(mesh.shape)
    tokens = P("dev", "ta", "pa", None)
    in_specs = (tokens, P("dev", None, None), tokens, P("dev"), P("dev"), P("dev")) + (P(),) * 9
    out_specs = (tokens, tokens) + (P(),) * 9
    return jax.shard_map(
        make_per_device(sizes),
        mesh=mesh,
        in_specs=in_specs,
        out_specs=out_specs,
        check_vma=False,
    )
```

```python
import math

import jax
import jax.numpy as jnp
from jax import lax
from jax.experimental import pallas as pl
from jax.experimental.pallas import tpu as pltpu
from jax.sharding import PartitionSpec as P

HEADS = 6
HDIM = 64
PAIRS = HEADS // 2
LANES = 2 * HDIM
EPSILON = 1e-06
MASKED_SCORE = -1e30
HIGHEST = lax.Precision.HIGHEST
F32 = jnp.float32
BF = jnp.bfloat16
VMEM_BYTES = 60 * 2**20
SUM_ROWS = 16
BLOCK = 32
STREAM_RUNS = 2
LATE_COT = 2
TIME_LAG = 1
SUB = 8
TILE = 16
TIME_STAGE = 8
SPACE_STAGE = 1
BACK_STAGE = 1
CROSS_AHEAD = 2
SPAN = 512
KEY_CHUNK = 256
PARTS = (12, 7, 6, 5, 4, 3, 2)
HIDDEN_PARTS = (3, 2)
PATTERN = (0, 1, 2)


def dot(a, b):
    return jnp.dot(a, b, preferred_element_type=F32)


def dot_nt(a, b):
    return lax.dot_general(a, b, (((1,), (1,)), ((), ())), preferred_element_type=F32)


def dot_tn(a, b):
    return lax.dot_general(a, b, (((0,), (0,)), ((), ())), preferred_element_type=F32)


def norm_parts(values):
    centred = values - jnp.mean(values, axis=-1, keepdims=True)
    inverse = lax.rsqrt(jnp.mean(centred * centred, axis=-1, keepdims=True) + EPSILON)
    return centred * inverse, inverse


def norm_back(d_normed, hat, inverse, scale_by):
    d_hat = d_normed * (1.0 + scale_by)
    mean_d = jnp.mean(d_hat, axis=-1, keepdims=True)
    mean_dh = jnp.mean(d_hat * hat, axis=-1, keepdims=True)
    return inverse * (d_hat - mean_d - hat * mean_dh)


GELU_A = math.sqrt(2.0 / math.pi)
GELU_B = 0.044715


def gelu_parts(values):
    square = values * values
    bent = jnp.tanh(GELU_A * values * (1.0 + GELU_B * square))
    half = 0.5 * (1.0 + bent)
    slope = half + (0.5 * GELU_A) * values * (1.0 - bent * bent) * (1.0 + 3.0 * GELU_B * square)
    return values * half, slope


def row_sums(values):
    return jnp.sum(values, axis=0, keepdims=True)


def head_lanes(values, head):
    lane = lax.broadcasted_iota(jnp.int32, values.shape, 1)
    return jnp.where((lane >= HDIM) == (head % 2 == 1), values, jnp.zeros_like(values))


def pair_of(values, pair):
    return values[:, pair * LANES : (pair + 1) * LANES]


def head_rows(values, head):
    return values[head * HDIM : (head + 1) * HDIM, :]


def lone_rows(values, head):
    rows = head_rows(values, head)
    blank = jnp.zeros_like(rows)
    return jnp.concatenate([rows, blank] if head % 2 == 0 else [blank, rows], axis=0)


def spans(count, size):
    return [slice(at, min(at + size, count)) for at in range(0, count, size)]


def attend(jobs, ahead, keep_exponent):
    units = [
        (i, head, span) for i, job in enumerate(jobs) for head in range(HEADS) for span in spans(job[0].shape[0], SPAN)
    ]
    scores, tops, sums, inverses = {}, {}, {}, {}

    def score(unit, keys_span):
        i, head, span = unit
        queries, keys, _, bias = jobs[i]
        lone = head_lanes(pair_of(queries, head // 2)[span], head)
        value = dot_nt(pair_of(keys, head // 2)[keys_span], lone)
        if bias is not None:
            value = value + bias[keys_span, span]
        scores.setdefault((i, head, span.start), []).append(value)
        top = jnp.max(value, axis=0, keepdims=True)
        old = tops.get((i, head, span.start))
        tops[i, head, span.start] = top if old is None else jnp.maximum(old, top)

    def weigh(unit, index, keys_span):
        i, head, span = unit
        name = (i, head, span.start)
        exponent = jnp.exp(scores[name][index] - tops[name]).astype(BF)
        scores[name][index] = None
        keep_exponent(i, head, keys_span, span, exponent)
        values_t = jobs[i][2]
        count = keys_span.stop - keys_span.start
        lifted = jnp.concatenate([head_rows(values_t, head)[:, keys_span], jnp.ones((SUM_ROWS, count), BF)], axis=0)
        part = dot(lifted, exponent)
        sums[name] = part if name not in sums else sums[name] + part

    def finish(unit):
        i, head, span = unit
        name = (i, head, span.start)
        total = sums[name]
        inverse = 1.0 / total[HDIM : HDIM + 1, :]
        sums[name] = total[:HDIM, :] * inverse
        inverses[name] = inverse

    for turn in range(len(units) + ahead):
        later = units[turn] if turn < len(units) else None
        now = units[turn - ahead] if turn >= ahead else None
        later_spans = spans(jobs[later[0]][1].shape[0], SPAN) if later else []
        now_spans = spans(jobs[now[0]][1].shape[0], SPAN) if now else []
        for index in range(max(len(later_spans), len(now_spans))):
            if index < len(later_spans):
                score(later, later_spans[index])
            if index < len(now_spans):
                weigh(now, index, now_spans[index])
        if now:
            finish(now)

    def joined(parts, i, head):
        starts = [span.start for span in spans(jobs[i][0].shape[0], SPAN)]
        return jnp.concatenate([parts[i, head, start] for start in starts], axis=1)

    return (
        [jnp.concatenate([joined(sums, i, head) for head in range(HEADS)], axis=0) for i in range(len(jobs))],
        [[joined(inverses, i, head) for head in range(HEADS)] for i in range(len(jobs))],
    )


def added(total, part):
    return part if total is None else total + part


def attend_back(jobs, ahead, chunk):
    scaled, centres = {}, {}
    for i, (_, _, _, _, d_att_t, att_t, inverse_of, _, _) in enumerate(jobs):
        for head in range(HEADS):
            inverse = inverse_of(head)
            d_att_head = head_rows(d_att_t, head)
            centres[i, head] = row_sums(d_att_head * head_rows(att_t, head)) * inverse
            part = (d_att_head * inverse).astype(BF)
            blank = jnp.zeros_like(part)
            scaled[i, head] = jnp.concatenate([part, blank] if head % 2 == 0 else [blank, part], axis=0)
    units = [
        (i, head, rows) for i, job in enumerate(jobs) for head in range(HEADS) for rows in spans(job[7], chunk)
    ]
    d_queries, d_keys, d_values, chances = {}, {}, {}, {}
    for turn in range(len(units) + ahead):
        if turn < len(units):
            i, head, rows = units[turn]
            chances[turn] = dot(jobs[i][3](head // 2, rows), scaled[i, head])
        if turn < ahead:
            continue
        i, head, rows = units[turn - ahead]
        key = (i, head // 2, rows.start)
        exponent = jobs[i][0](head, rows)
        chance = chances.pop(turn - ahead)
        d_values[key] = added(d_values.get(key), dot_nt(exponent, scaled[i, head]))
        score = (exponent.astype(F32) * (chance - centres[i, head])).astype(BF)
        d_keys[key] = added(d_keys.get(key), dot(score, head_lanes(jobs[i][1](head // 2), head)))
        d_queries[i, head] = added(d_queries.get((i, head)), dot(jobs[i][2](head, rows), score))
        if rows.stop == jobs[i][7] and jobs[i][8] is not None:
            jobs[i][8](head)
    results = []
    for i, job in enumerate(jobs):
        starts = [rows.start for rows in spans(job[7], chunk)]
        joined = [
            jnp.concatenate(
                [jnp.concatenate([parts[i, pair, at] for at in starts], axis=0) for pair in range(PAIRS)], axis=1
            )
            for parts in (d_keys, d_values)
        ]
        results.append((jnp.concatenate([d_queries[i, head] for head in range(HEADS)], axis=0), *joined))
    return results


def fold(ref):
    value = ref[...]
    return value.reshape(-1, value.shape[-1])


class Layout:
    def __init__(self, sizes, latents_shape):
        self.clips_dev, self.frames, self.patches, self.width = latents_shape
        self.n_ta, self.n_pa, self.n_dev = sizes["ta"], sizes["pa"], sizes["dev"]
        self.clips = self.clips_dev * self.n_dev
        self.run = self.n_pa // self.clips
        self.group = self.run * self.n_dev
        self.near = self.n_pa // self.group
        self.halves = self.n_ta // self.near
        self.space_rows = self.near * self.patches
        self.time_patches = self.space_rows // self.n_ta
        self.other_rows = (self.group - 1) * self.space_rows
        self.key_rows = self.group * self.space_rows
        self.all_frames = self.n_ta * self.frames
        self.blocks = self.time_patches // BLOCK
        self.early_cot = max(self.blocks - LATE_COT, 1)

    def here(self):
        return {name: lax.axis_index(name) for name in ("ta", "pa", "dev")}

    def clip(self, me):
        return me["pa"] // self.run

    def member(self, me):
        return me["dev"] * self.run + me["pa"] % self.run

    def space_place(self, ta, clip, member):
        return {"ta": ta, "pa": clip * self.run + member % self.run, "dev": member // self.run}

    def space_target(self, me, j):
        return self.space_place(me["ta"], me["dev"] * self.clips_dev + j, me["pa"] // self.near)

    def owner(self, me, ta, slot):
        return {"ta": ta, "pa": self.near * self.member(me) + slot, "dev": self.clip(me) // self.clips_dev}

    def chunk(self, ta, clip):
        return (ta + self.halves * (clip % self.near)) % self.n_ta

    def own_chunk(self, me):
        return self.chunk(me["ta"], self.clip(me))

    def home(self, me, ta):
        return self.owner(me, ta, self.own_chunk(me) // self.halves)

    def time_target(self, me, j, s):
        clip = me["dev"] * self.clips_dev + j
        chunk = (me["pa"] % self.near) * self.halves + s
        return {**self.space_target(me, j), "ta": (chunk + self.n_ta - self.halves * (clip % self.near)) % self.n_ta}

    def fellow(self, me, step):
        return self.space_place(me["ta"], self.clip(me), (self.member(me) + step) % self.group)

    def across(self, me, step):
        return {**me, "ta": (me["ta"] + step) % self.n_ta}


def is_me(me, place):
    same = None
    for name, index in place.items():
        if index is not me[name]:
            equal = index == me[name]
            same = equal if same is None else same & equal
    return same


def greet(me, place):
    @pl.when(jnp.logical_not(is_me(me, place)))
    def _():
        pl.semaphore_signal(
            pltpu.get_barrier_semaphore(), inc=1, device_id=place, device_id_type=pl.DeviceIdType.MESH
        )


def await_greetings(me, places, amount=0):
    amount = jnp.int32(amount)
    for place in places:
        amount = amount + jnp.logical_not(is_me(me, place)).astype(jnp.int32)
    pl.semaphore_wait(pltpu.get_barrier_semaphore(), amount)


def push(src, dst, send_sem, recv_sem, place):
    return pltpu.make_async_remote_copy(
        src_ref=src,
        dst_ref=dst,
        send_sem=send_sem,
        recv_sem=recv_sem,
        device_id=place,
        device_id_type=pl.DeviceIdType.MESH,
    )


def start_push(me, src, dst, send_sem, recv_sem, place):
    same = is_me(me, place)

    @pl.when(same)
    def _():
        pltpu.make_async_copy(src, dst, recv_sem).start()

    @pl.when(jnp.logical_not(same))
    def _():
        push(src, dst, send_sem, recv_sem, place).start()


def end_push(me, src, dst, send_sem, recv_sem, place):
    @pl.when(jnp.logical_not(is_me(me, place)))
    def _():
        push(src, dst, send_sem, recv_sem, place).wait_send()


def arrived(dst, recv_sem):
    pltpu.make_async_copy(dst, dst, recv_sem).wait()


def space_forward_kernel(
    lay,
    counts_ref,
    latents_ref,
    cot_ref,
    mod_ref,
    attn_ref,
    cross_ref,
    text_keys_ref,
    text_values_t_ref,
    up_ref,
    down_ref,
    state_ref,
    moved_ref,
    own_ref,
    normed_ref,
    query_ref,
    keys_t_ref,
    value_ref,
    exponent_ref,
    att_t_ref,
    att_ref,
    inverse_ref,
    cross_in_ref,
    cross_query_ref,
    cross_exponent_ref,
    cross_att_t_ref,
    cross_att_ref,
    cross_inverse_ref,
    middle_ref,
    normed2_ref,
    act_ref,
    slope_ref,
    branch2_ref,
    branch5_ref,
    own_buf,
    other_buf,
    sent_buf,
    lat_send,
    lat_recv,
    fellow_send,
    fellow_recv,
    state_send,
    state_recv,
    cot_send,
    cot_recv,
):
    scale_by = HDIM ** (-0.5)
    me = lay.here()
    step = pl.program_id(0)
    frames, near = lay.frames, lay.near
    last = step == frames - 1

    def latent_copy(j, f):
        slot = me["pa"] % near
        return (
            latents_ref.at[j, f], own_buf.at[f, slot], lat_send.at[j, f], lat_recv.at[f, slot], lay.space_target(me, j),
        )

    def fellow_copy(turn, f):
        return (
            own_buf.at[f], other_buf.at[f, turn - 1], fellow_send.at[turn - 1, f], fellow_recv.at[turn - 1, f],
            lay.fellow(me, turn),
        )

    def state_copy(turn, f):
        place = lay.across(me, turn)
        row = pl.multiple_of(lay.chunk(place["ta"], lay.clip(me)) * lay.time_patches, TILE)
        return (
            sent_buf.at[f, pl.ds(row, lay.time_patches)], state_ref.at[me["ta"] * frames + f], state_send.at[turn, f],
            state_recv.at[turn, f], place,
        )

    def cot_copy(j, s):
        return (
            cot_ref.at[j, :, pl.ds(s * lay.time_patches, lay.early_cot * BLOCK)],
            moved_ref.at[pl.ds(me["ta"] * frames, frames)],
            cot_send.at[j, s], cot_recv.at[me["ta"]], lay.time_target(me, j, s),
        )

    def start_latents(f):
        for j in range(lay.clips_dev):
            start_push(me, *latent_copy(j, f))

    def pass_on(f):
        for slot in range(near):
            arrived(own_buf.at[f, slot], lat_recv.at[f, slot])
        for turn in range(1, lay.group):
            push(*fellow_copy(turn, f)).start()

    @pl.when(step == 0)
    def _():
        for slot in range(near):
            greet(me, lay.owner(me, me["ta"], slot))
        for t in range(lay.n_ta):
            greet(me, lay.home(me, t))
        friends = [lay.fellow(me, turn) for turn in range(1, lay.group)]
        friends += [lay.across(me, turn) for turn in range(1, lay.n_ta)]
        for friend in friends:
            greet(me, friend)
        targets = [lay.space_target(me, j) for j in range(lay.clips_dev)]
        targets += [lay.time_target(me, j, s) for j in range(lay.clips_dev) for s in range(lay.halves)]
        await_greetings(me, targets + friends)
        for f in range(frames):
            start_latents(f)
        pass_on(0)

    @pl.when(step == min(2, frames - 1))
    def _():
        for j in range(lay.clips_dev):
            for s in range(lay.halves):
                start_push(me, *cot_copy(j, s))

    for turn in range(1, lay.group):
        arrived(other_buf.at[step, turn - 1], fellow_recv.at[turn - 1, step])
    frame = counts_ref[2] + step
    keep = (frame < counts_ref[0]).astype(F32)
    mod = mod_ref[...]
    own_low = own_buf[step].reshape(lay.space_rows, lay.width)
    own_ref[0] = own_low
    own = own_low.astype(F32)
    rows = lay.space_rows
    normed_own = (norm_parts(own)[0] * (1.0 + mod[1:2]) + mod[0:1]).astype(BF)
    other = other_buf[step].reshape(lay.other_rows, lay.width).astype(F32)
    normed_other = (norm_parts(other)[0] * (1.0 + mod[1:2]) + mod[0:1]).astype(BF)
    normed = jnp.concatenate([normed_own, normed_other], axis=0)
    normed_ref[0] = normed
    queries = (dot(normed_own, attn_ref[0]).astype(BF) * scale_by).astype(BF)
    keys = dot(normed, attn_ref[1]).astype(BF)
    values = dot(normed, attn_ref[2]).astype(BF)
    query_ref[0] = queries
    value_ref[0] = values
    keys_t_ref[0] = keys.T
    values_t = values.T

    def keep_exponent(_, head, keys_span, span, exponent):
        exponent_ref[0, head, keys_span, span] = exponent

    (att_t,), (inverses,) = attend([(queries, keys, values_t, None)], SPACE_STAGE, keep_exponent)
    for head in range(HEADS):
        inverse_ref[0, head : head + 1, :] = inverses[head]
    att_t_ref[0] = att_t.astype(BF)
    att = att_t.T.astype(BF)
    att_ref[0] = att

    @pl.when(jnp.logical_not(last))
    def _():
        pass_on(step + 1)

    branch = dot(att_ref[0], attn_ref[3])
    branch2_ref[0] = branch.astype(BF)
    state = own_ref[0].astype(F32) + (keep * mod[2:3]) * branch
    cross_in = state.astype(BF)
    cross_in_ref[0] = cross_in
    cross_queries = (dot(cross_in, cross_ref[0]).astype(BF) * scale_by).astype(BF)
    cross_query_ref[0] = cross_queries
    text_id = lax.broadcasted_iota(jnp.int32, (text_keys_ref.shape[0], rows), 0)
    bias = jnp.where(text_id < counts_ref[1], 0.0, MASKED_SCORE)

    def keep_cross(_, head, keys_span, span, exponent):
        cross_exponent_ref[0, head, keys_span, span] = exponent

    (cross_t,), (inverses,) = attend(
        [(cross_queries, text_keys_ref[...], text_values_t_ref[...], bias)], CROSS_AHEAD, keep_cross
    )
    for head in range(HEADS):
        cross_inverse_ref[0, head : head + 1, :] = inverses[head]
    cross_att_t_ref[0] = cross_t.astype(BF)
    cross_att = cross_t.T.astype(BF)
    cross_att_ref[0] = cross_att
    state = state + keep * dot(cross_att, cross_ref[1])
    middle_ref[0] = state
    normed2 = (norm_parts(state)[0] * (1.0 + mod[4:5]) + mod[3:4]).astype(BF)
    normed2_ref[0] = normed2
    act, slope = gelu_parts(dot(normed2, up_ref[...]))
    act = act.astype(BF)
    act_ref[0] = act
    slope_ref[0] = slope.astype(BF)
    branch = dot(act, down_ref[...])
    branch5_ref[0] = branch.astype(BF)
    state = state + (keep * mod[5:6]) * branch
    sent_buf[step] = state.astype(BF)
    src, dst, _, sem, _ = state_copy(0, step)
    pltpu.make_async_copy(src, dst, sem).start()
    for turn in range(1, lay.n_ta):
        push(*state_copy(turn, step)).start()

    @pl.when(last)
    def _():
        for f in range(frames):
            for j in range(lay.clips_dev):
                end_push(me, *latent_copy(j, f))
            for turn in range(1, lay.group):
                push(*fellow_copy(turn, f)).wait_send()
            for turn in range(1, lay.n_ta):
                push(*state_copy(turn, f)).wait_send()
            for turn in range(lay.n_ta):
                src, dst, _, sem, _ = state_copy(turn, f)
                arrived(dst, sem)
        for j in range(lay.clips_dev):
            for s in range(lay.halves):
                end_push(me, *cot_copy(j, s))
        for t in range(lay.n_ta):
            arrived(moved_ref.at[pl.ds(t * frames, frames)], cot_recv.at[t])


def space_backward_kernel(
    lay,
    reducer,
    counts_ref,
    grad_ref,
    out_t_ref,
    exponent_ref,
    *refs,
):
    n_sources = len(reducer.shapes)
    sources, refs = refs[:n_sources], refs[n_sources:]
    (mod_ref, attn_ref, cross_ref, text_keys_t_ref, text_values_ref, up_ref, down_ref, own_ref, query_ref, keys_t_ref,
     value_ref, att_t_ref, inverse_ref, cross_query_ref, cross_exponent_ref, cross_att_t_ref, cross_inverse_ref,
     middle_ref, slope_ref, branch2_ref, branch5_ref) = refs[:21]
    (output_ref, lat_grad_ref, last_done_ref, reduced_ref, kept3_ref, d_lifted_ref, kept2_ref, d_cross_query_ref, kept1_ref,
     d_query_ref, d_pair_ref, d_text_keys_ref, d_text_values_ref, mods_ref) = refs[21:35]
    (exponent_buf, other_buf, fellow_buf, state_buf, own_buf, done_buf, exponent_sem, fellow_send, fellow_recv,
     out_send, out_recv, grad_send, grad_recv) = refs[35:48]
    reducer.bind(sources, reduced_ref, refs[48:])
    scale_by = HDIM ** (-0.5)
    me = lay.here()
    step = pl.program_id(0)
    frames = lay.frames
    rows = lay.space_rows
    mod = mod_ref[...]

    slots = frames * 3
    lengths = [0, 1] + [2] * 2 + [1] * (reducer.phases - 8) + [1, 2, 2]
    due_at, at = [], 0
    for length in lengths:
        at += length
        due_at.append(at)
    scale = min(1.0, (slots - 1) / at)
    due_at = [int(when * scale) for when in due_at]

    def hook(number):
        for f in range(frames):
            due = [k for k, when in enumerate(due_at) if when == f * 3 + number]
            if due:

                @pl.when(step == f)
                def _():
                    for k in due:
                        if k == 0:
                            reducer.prepare()
                        reducer.phase(k)

    def exponent_copy(head, f):
        return pltpu.make_async_copy(exponent_ref.at[f, head], exponent_buf.at[head], exponent_sem.at[head])

    def fellow_copy(turn, f):
        return (
            other_buf.at[f % 2, turn - 1], fellow_buf.at[f, turn - 1], fellow_send.at[turn - 1, f],
            fellow_recv.at[turn - 1, f], lay.fellow(me, -turn),
        )

    def out_copy(t):
        part, j = lay.own_chunk(me) % lay.halves, lay.clip(me) % lay.clips_dev
        return (
            out_t_ref.at[pl.ds(t * frames, frames)], output_ref.at[j, :, part], out_send.at[t],
            out_recv.at[j, part], lay.home(me, t),
        )

    def grad_copy(slot, f):
        j = lay.clip(me) % lay.clips_dev
        return (
            done_buf.at[f, slot], lat_grad_ref.at[j, f], grad_send.at[slot, f], grad_recv.at[j, f],
            lay.owner(me, me["ta"], slot),
        )

    @pl.when(step == 0)
    def _():
        for head in range(HEADS):
            exponent_copy(head, 0).start()
        fellows = [lay.fellow(me, turn) for turn in range(1, lay.group)]
        senders = [lay.space_target(me, j) for j in range(lay.clips_dev)]
        senders += [lay.time_target(me, j, s) for j in range(lay.clips_dev) for s in range(lay.halves)]
        for place in fellows + senders:
            greet(me, place)
        takers = [lay.owner(me, me["ta"], slot) for slot in range(lay.near)]
        takers += [lay.home(me, t) for t in range(lay.n_ta)]
        await_greetings(me, fellows + takers, reducer.greet())
        for t in range(lay.n_ta):
            start_push(me, *out_copy(t))

    mods_ref[0] = jnp.zeros(mods_ref.shape[1:], F32)

    @pl.when(step < frames)
    def _():
        hook(0)
        keep = (counts_ref[2] + step < counts_ref[0]).astype(F32)
        grad = grad_ref[0].astype(F32)
        kept = keep * grad
        d_gate5 = row_sums(kept * branch5_ref[0].astype(F32))
        d_branch = (kept * mod[5:6]).astype(BF)
        kept3_ref[0] = d_branch
        d_act = dot_nt(d_branch, down_ref[...])
        d_lifted = (d_act * slope_ref[0].astype(F32)).astype(BF)
        d_lifted_ref[0] = d_lifted
        d_normed = dot_nt(d_lifted, up_ref[...])
        hat, inverse = norm_parts(middle_ref[0])
        grad = grad + norm_back(d_normed, hat, inverse, mod[4:5])
        d_shift, d_scale = row_sums(d_normed), row_sums(d_normed * hat)
        kept = (keep * grad).astype(BF)
        kept2_ref[0] = kept
        d_att_t = dot_nt(cross_ref[1], kept)
        job = (
            lambda head, at: cross_exponent_ref[0, head, at, :],
            lambda pair: cross_query_ref[0, :, pair * LANES : (pair + 1) * LANES],
            lambda head, at: text_keys_t_ref[head * HDIM : (head + 1) * HDIM, at],
            lambda pair, at: text_values_ref[at, pair * LANES : (pair + 1) * LANES],
            d_att_t,
            cross_att_t_ref[0].astype(F32),
            lambda head: cross_inverse_ref[0, head : head + 1, :],
            text_values_ref.shape[0],
            None,
        )
        ((d_query_t, d_keys, d_values),) = attend_back([job], CROSS_AHEAD, KEY_CHUNK)
        d_text_keys_ref[0] = d_keys
        d_text_values_ref[0] = d_values
        d_query = (d_query_t.T * scale_by).astype(BF)
        d_cross_query_ref[0] = d_query
        grad = grad + dot_nt(d_query, cross_ref[0])
        state_buf[step % 2] = grad
        kept = keep * grad
        d_gate2 = row_sums(kept * branch2_ref[0].astype(F32))
        mods_ref[0, 2:6, :] = jnp.concatenate([d_gate2, d_shift, d_scale, d_gate5], axis=0)
        d_branch = (kept * mod[2:3]).astype(BF)
        kept1_ref[0] = d_branch
        hook(1)
        d_att_t = dot_nt(attn_ref[3], kept1_ref[0])
        later = jnp.minimum(step + 1, frames - 1)

        def end_head(head):
            exponent_copy(head, later).start()
            if head == HEADS // 2 - 1:
                hook(2)

        def exponent_of(head, at):
            if at.start == 0:
                exponent_copy(head, step).wait()
            return exponent_buf[head, at, :]

        job = (
            exponent_of,
            lambda pair: query_ref[0, :, pair * LANES : (pair + 1) * LANES],
            lambda head, at: keys_t_ref[0, head * HDIM : (head + 1) * HDIM, at],
            lambda pair, at: value_ref[0, at, pair * LANES : (pair + 1) * LANES],
            d_att_t,
            att_t_ref[0].astype(F32),
            lambda head: inverse_ref[0, head : head + 1, :],
            value_ref.shape[1],
            end_head,
        )
        ((d_query_t, d_keys, d_values),) = attend_back([job], BACK_STAGE, KEY_CHUNK)
        d_query = (d_query_t.T * scale_by).astype(BF)
        d_keys, d_values = d_keys.astype(BF), d_values.astype(BF)
        d_query_ref[0] = d_query
        d_pair_ref[0, :, : lay.width] = d_keys
        d_pair_ref[0, :, lay.width :] = d_values
        d_normed = dot_nt(d_keys, attn_ref[1]) + dot_nt(d_values, attn_ref[2])
        own_buf[step % 2] = d_normed[:rows] + dot_nt(d_query, attn_ref[0])

        @pl.when(step > 1)
        def _():
            for turn in range(1, lay.group):
                push(*fellow_copy(turn, step - 2)).wait_send()

        for turn in range(1, lay.group):
            other_buf[step % 2, turn - 1] = d_normed[turn * rows : (turn + 1) * rows].astype(BF)
            push(*fellow_copy(turn, step)).start()

    @pl.when(step > 0)
    def _():
        f = step - 1
        d_normed = own_buf[f % 2]
        for turn in range(1, lay.group):
            arrived(fellow_buf.at[f, turn - 1], fellow_recv.at[turn - 1, f])
            d_normed = d_normed + fellow_buf[f, turn - 1].astype(F32)
        hat, inverse = norm_parts(own_ref[0].astype(F32))
        grad = state_buf[f % 2] + norm_back(d_normed, hat, inverse, mod[1:2])
        done = grad.astype(BF).reshape(done_buf.shape[1:])
        done_buf[f] = done
        last_done_ref[...] = done
        mods_ref[0, 0:2, :] = jnp.concatenate([row_sums(d_normed), row_sums(d_normed * hat)], axis=0)

    @pl.when((step > 0) & (step < frames))
    def _():
        for slot in range(lay.near):
            start_push(me, *grad_copy(slot, step - 1))

    @pl.when(step == frames)
    def _():
        for k in range(len(due_at), reducer.phases):
            reducer.phase(k)
        for head in range(HEADS):
            exponent_copy(head, frames - 1).wait()
        for turn in range(1, lay.group):
            for f in range(max(frames - 2, 0), frames):
                push(*fellow_copy(turn, f)).wait_send()
        for t in range(lay.n_ta):
            end_push(me, *out_copy(t))
        for f in range(frames - 1):
            for slot in range(lay.near):
                end_push(me, *grad_copy(slot, f))
        for j in range(lay.clips_dev):
            for s in range(lay.halves):
                arrived(output_ref.at[j, :, s], out_recv.at[j, s])
            for f in range(frames - 1):
                arrived(lat_grad_ref.at[j, f], grad_recv.at[j, f])


def interleave(streams, lag):
    live, turn = list(enumerate(streams)), 0
    while live:
        left = []
        for i, stream in live:
            if turn < i * lag or next(stream, DONE) is not DONE:
                left.append((i, stream))
        live, turn = left, turn + 1


DONE = object()


def time_kernel(
    lay,
    counts_ref,
    state_ref,
    early_cot_ref,
    cotangent_ref,
    mod_ref,
    bias_ref,
    attn_ref,
    up_ref,
    down_ref,
    grad_s_ref,
    early_ref,
    late_ref,
    d_qkv_sum_ref,
    d_proj_sum_ref,
    d_up_sum_ref,
    d_down_sum_ref,
    mods_ref,
    exponent_ref,
    sent_buf,
    out_buf,
    d_qkv_sum,
    d_proj_sum,
    d_up_sum,
    d_down_sum,
    normed_ref,
    d_qkv_ref,
    att_ref,
    branch4_ref,
    normed2_ref,
    act_ref,
    d_lifted_ref,
    branch5_ref,
    grad_send,
    grad_recv,
    out_send,
    out_recv,
    cot_buf,
    cot_load,
    cot_send,
    cot_recv,
):
    frames, block, width = state_ref.shape
    me = lay.here()
    step = pl.program_id(0)
    last = pl.num_programs(0) - 1

    def grad_copy(turn, i):
        place = lay.across(me, turn)
        row = pl.multiple_of(lay.own_chunk(me) * lay.time_patches + i * block, TILE)
        return (
            sent_buf.at[i, pl.ds(place["ta"] * lay.frames, lay.frames)], grad_s_ref.at[:, pl.ds(row, block)],
            grad_send.at[turn, i], grad_recv.at[turn, i], place,
        )

    def out_copy(t, i):
        part, j = lay.own_chunk(me) % lay.halves, lay.clip(me) % lay.clips_dev
        return (
            out_buf.at[i, pl.ds(t * lay.frames, lay.frames)], early_ref.at[j, :, part, pl.ds(i * block, block)],
            out_send.at[t, i], out_recv.at[j, part, i], lay.home(me, t),
        )

    def cot_copy(j, s, b):
        row = s * lay.time_patches + (lay.early_cot + b) * block
        return (
            cotangent_ref.at[j, :, row : row + block], cot_buf.at[lay.early_cot + b, pl.ds(me["ta"] * lay.frames, lay.frames)],
            cot_send.at[j, s, b], cot_recv.at[me["ta"], b], lay.time_target(me, j, s),
        )

    def cot_here(i):
        return pltpu.make_async_copy(early_cot_ref.at[:, pl.ds(i * block, block)], cot_buf.at[i], cot_load.at[i])

    late_cot = lay.blocks - lay.early_cot
    early = lay.blocks - 1

    @pl.when(step == 0)
    def _():
        friends = [lay.across(me, turn) for turn in range(1, lay.n_ta)]
        for i in range(lay.early_cot):
            cot_here(i).start()
        parts = [(j, s) for j in range(lay.clips_dev) for s in range(lay.halves)]
        homes = [lay.home(me, t) for t in range(lay.n_ta)]
        places = [lay.time_target(me, j, s) for j, s in parts]
        senders = (places if early else []) + (homes if late_cot else [])
        takers = (homes if early else []) + (places if late_cot else [])
        for place in friends + senders:
            greet(me, place)
        await_greetings(me, friends + takers)
        for b in range(late_cot):
            for j, s in parts:
                start_push(me, *cot_copy(j, s, b))
        for total in (d_qkv_sum, d_proj_sum, d_up_sum, d_down_sum):
            total[...] = jnp.zeros_like(total)

    @pl.when(step > 0)
    def _():
        for t in range(lay.n_ta):
            start_push(me, *out_copy(t, step - 1))

    @pl.when(step < lay.early_cot)
    def _():
        cot_here(step).wait()

    if late_cot:

        @pl.when(step >= lay.early_cot)
        def _():
            for t in range(lay.n_ta):
                arrived(cot_buf.at[step, pl.ds(t * lay.frames, lay.frames)], cot_recv.at[t, step - lay.early_cot])

    scale_by = HDIM ** (-0.5)
    run_rows = frames * SUB
    runs = min(STREAM_RUNS, block // SUB)
    mod = mod_ref[...]
    totals = []

    def stream(first_run):
        patches = slice(first_run * SUB, (first_run + runs) * SUB)
        mine = slice(first_run * run_rows, (first_run + runs) * run_rows)

        def load(cube):
            cube = cube.astype(F32)
            parts = [cube[:, r * SUB : (r + 1) * SUB].reshape(run_rows, width) for r in range(runs)]
            return jnp.concatenate(parts, axis=0)

        def stored(value):
            parts = [value[r * run_rows : (r + 1) * run_rows].reshape(frames, SUB, width) for r in range(runs)]
            return jnp.concatenate(parts, axis=1).astype(BF)

        def run_of(value, r):
            return value[r * run_rows : (r + 1) * run_rows]

        state = load(state_ref[:, patches, :])
        frame = (lax.broadcasted_iota(jnp.int32, (runs * run_rows, 1), 0) // SUB) % frames
        keep = (frame < counts_ref[0]).astype(F32)
        hat1, inverse1 = norm_parts(state)
        normed = (hat1 * (1.0 + mod[1:2]) + mod[0:1]).astype(BF)
        normed_ref[mine] = normed
        yield
        queries = (dot(normed, attn_ref[0]).astype(BF) * scale_by).astype(BF)
        keys = dot(normed, attn_ref[1]).astype(BF)
        values = dot(normed, attn_ref[2]).astype(BF)
        yield
        keys_t_runs, jobs = [], []
        for r in range(runs):
            keys_t_runs.append(run_of(keys, r).T)
            jobs.append((run_of(queries, r), run_of(keys, r), run_of(values, r).T, bias_ref[...]))

        def keep_exponent(r, head, keys_span, span, exponent):
            exponent_ref[first_run + r, head, keys_span, span] = exponent

        att_t_runs, inverse_runs = attend(jobs, TIME_STAGE, keep_exponent)
        yield
        att = jnp.concatenate([att_t.T.astype(BF) for att_t in att_t_runs], axis=0)
        att_ref[mine] = att
        branch2 = dot(att, attn_ref[3])
        yield
        state = state + (keep * mod[2:3]) * branch2
        hat2, inverse2 = norm_parts(state)
        normed2 = (hat2 * (1.0 + mod[4:5]) + mod[3:4]).astype(BF)
        normed2_ref[mine] = normed2
        yield
        lifted = dot(normed2, up_ref[...])
        yield
        act, slope = gelu_parts(lifted)
        act = act.astype(BF)
        act_ref[mine] = act
        grad = load(cot_buf[step, :, patches, :])
        kept = keep * grad
        d_branch = (kept * mod[5:6]).astype(BF)
        branch5_ref[mine] = d_branch
        yield
        d_act = dot_nt(d_branch, down_ref[...])
        yield
        d_lifted = (d_act * slope).astype(BF)
        d_lifted_ref[mine] = d_lifted
        branch5 = dot(act, down_ref[...])
        yield
        final = stored(state + (keep * mod[5:6]) * branch5)
        out_buf[step, :, patches, :] = final
        late_ref[:, patches, :] = final
        d_gate5 = row_sums(kept * branch5)
        d_normed2 = dot_nt(d_lifted, up_ref[...])
        yield
        grad = grad + norm_back(d_normed2, hat2, inverse2, mod[4:5])
        kept = keep * grad
        d_gate2 = row_sums(kept * branch2)
        d_branch = (kept * mod[2:3]).astype(BF)
        branch4_ref[mine] = d_branch
        yield
        d_att_t_runs = [dot_nt(attn_ref[3], run_of(d_branch, r)) for r in range(runs)]
        yield

        def job(r):
            query_run, value_run = run_of(queries, r), run_of(values, r)
            return (
                lambda head, at: exponent_ref[first_run + r, head, at, :],
                lambda pair: pair_of(query_run, pair),
                lambda head, at: head_rows(keys_t_runs[r], head)[:, at],
                lambda pair, at: pair_of(value_run, pair)[at],
                d_att_t_runs[r],
                att_t_runs[r],
                lambda head: inverse_runs[r][head],
                run_rows,
                None,
            )

        backs = attend_back([job(r) for r in range(runs)], TIME_STAGE, run_rows)
        yield
        d_qkv = jnp.concatenate(
            [
                jnp.concatenate([(d_query_t.T * scale_by).astype(BF) for d_query_t, _, _ in backs], axis=0),
                jnp.concatenate([d_keys.astype(BF) for _, d_keys, _ in backs], axis=0),
                jnp.concatenate([d_values.astype(BF) for _, _, d_values in backs], axis=0),
            ],
            axis=1,
        )
        d_qkv_ref[mine] = d_qkv
        d_normed1 = sum(dot_nt(d_qkv[:, i * width : (i + 1) * width], attn_ref[i]) for i in range(3))
        yield
        grad = grad + norm_back(d_normed1, hat1, inverse1, mod[1:2])
        sent_buf[step, :, patches, :] = stored(grad)
        totals.append(
            jnp.concatenate(
                [
                    row_sums(d_normed1),
                    row_sums(d_normed1 * hat1),
                    d_gate2,
                    row_sums(d_normed2),
                    row_sums(d_normed2 * hat2),
                    d_gate5,
                    jnp.zeros((2, width), F32),
                ],
                axis=0,
            )
        )

    interleave([stream(first) for first in range(0, block // SUB, runs)], TIME_LAG)
    mods_ref[0] = sum(totals[1:], totals[0])
    src, dst, _, sem, _ = grad_copy(0, step)
    pltpu.make_async_copy(src, dst, sem).start()
    for turn in range(1, lay.n_ta):
        push(*grad_copy(turn, step)).start()

    d_qkv_sum[...] += dot_tn(normed_ref[...], d_qkv_ref[...])
    d_proj_sum[...] += dot_tn(att_ref[...], branch4_ref[...])
    d_up_sum[...] += dot_tn(normed2_ref[...], d_lifted_ref[...])
    d_down_sum[...] += dot_tn(branch5_ref[...], act_ref[...])

    @pl.when(step == last)
    def _():
        d_qkv_sum_ref[...] = d_qkv_sum[...].astype(BF)
        d_proj_sum_ref[...] = d_proj_sum[...].astype(BF)
        d_up_sum_ref[...] = d_up_sum[...].astype(BF)
        d_down_sum_ref[...] = d_down_sum[...].T.astype(BF)
        for b in range(late_cot):
            for j in range(lay.clips_dev):
                for s in range(lay.halves):
                    end_push(me, *cot_copy(j, s, b))
        for i in range(early):
            for t in range(lay.n_ta):
                end_push(me, *out_copy(t, i))
            for j in range(lay.clips_dev):
                for s in range(lay.halves):
                    arrived(early_ref.at[j, :, s, i * block : (i + 1) * block], out_recv.at[j, s, i])
        for i in range(lay.time_patches // block):
            for turn in range(lay.n_ta):
                src, dst, _, sem, place = grad_copy(turn, i)
                if turn:
                    push(*grad_copy(turn, i)).wait_send()
                arrived(dst, sem)


class Reducer:
    def __init__(self, shapes, small_rows, sizes, parts, direct=False):
        self.direct = direct
        self.width = width = shapes[0][1]
        self.shapes = shapes
        bits = {name: [(name, 1 << i) for i in range(sizes[name].bit_length() - 1)] for name in ("ta", "pa")}
        kinds = [bits["ta"] + bits["pa"], bits["ta"][::-1] + bits["pa"], bits["pa"] + bits["ta"]]
        self.ways = [("dev", 1)] + kinds[0]
        self.loads, row = [], 0
        for i, shape in enumerate(shapes):
            for column in range(shape[1] // width):
                self.loads.append((i, row, column * width, shape[0]))
                row += shape[0]
        self.total = row
        cut = TILE << sum(len(ways) for ways in bits.values())
        self.parts = next((n for n in parts if row % (2 * n * cut) == 0), 1)
        self.part_rows = row // 2 // self.parts
        self.half_rows = row // 2
        self.orders = [[("dev", 1)] + kinds[PATTERN[p % len(PATTERN)]] for p in range(self.parts)]
        self.steps = len(self.ways)
        self.small_rows = small_rows
        self.counts, self.halves, self.boxes, at = [self.part_rows], [True], [], 0
        for _ in range(1, self.steps):
            halve = (self.counts[-1] // 2) % TILE == 0
            self.halves.append(halve)
            self.counts.append(self.counts[-1] // 2 if halve else self.counts[-1])
        for p in range(self.parts):
            self.boxes.append([])
            for count in self.counts:
                self.boxes[p].append(at)
                at += count
        self.box_rows = at
        self.phases = 2 * self.steps + 1

    def scratch(self):
        shapes = [
            pltpu.VMEM((self.total, self.width), BF),
            pltpu.VMEM((self.total, self.width), BF),
            pltpu.VMEM((self.box_rows, self.width), BF),
            pltpu.SemaphoreType.DMA((len(self.loads),)),
            pltpu.SemaphoreType.DMA((self.parts, 2)),
            pltpu.SemaphoreType.DMA((self.parts, 2 * self.steps)),
            pltpu.SemaphoreType.DMA((self.parts, 2 * self.steps)),
        ]
        if self.small_rows:
            shapes += [
                pltpu.VMEM((self.steps, self.small_rows, self.width), F32),
                pltpu.SemaphoreType.DMA((self.steps,)),
                pltpu.SemaphoreType.DMA((self.steps,)),
            ]
        return shapes

    def bind(self, sources, out, scratch, small_in=None, small_out=None):
        self.sources, self.out = sources, out
        self.work, self.whole, self.inbox, self.in_sem, self.out_sem, self.send_sem, self.recv_sem = scratch[:7]
        self.small_in, self.small_out = small_in, small_out
        if self.small_rows:
            self.small_box, self.small_send, self.small_recv = scratch[7:]

    def bit(self, way):
        return (lax.axis_index(way[0]) // way[1]) % 2

    def peer(self, way):
        return {way[0]: lax.axis_index(way[0]) + way[1] - 2 * way[1] * self.bit(way)}

    def greet(self):
        barrier = pltpu.get_barrier_semaphore()
        for way in self.ways:
            pl.semaphore_signal(barrier, inc=1, device_id=self.peer(way), device_id_type=pl.DeviceIdType.MESH)
        return len(self.ways)

    def base(self, p, step):
        row = self.bit(self.orders[p][0]) * self.half_rows + p * self.part_rows
        for s in range(1, step + 1):
            if self.halves[s]:
                row = row + self.bit(self.orders[p][s]) * self.counts[s]
        return row

    def rows(self, ref, row, count):
        return ref.at[pl.ds(pl.multiple_of(row, TILE), count)]

    def load(self, i):
        source, row, column, rows = self.loads[i]
        view = self.sources[source].at[:, column : column + self.width]
        return pltpu.make_async_copy(view, self.work.at[row : row + rows], self.in_sem.at[i])

    def remote(self, src, dst, p, step, way):
        return pltpu.make_async_remote_copy(
            src_ref=src,
            dst_ref=dst,
            send_sem=self.send_sem.at[p, step],
            recv_sem=self.recv_sem.at[p, step],
            device_id=self.peer(way),
            device_id_type=pl.DeviceIdType.MESH,
        )

    def down(self, p, step):
        way, count = self.orders[p][step], self.counts[step]
        if step == 0:
            row = (1 - self.bit(way)) * self.half_rows + p * self.part_rows
        else:
            row = self.base(p, step - 1)
            if self.halves[step]:
                row = row + (1 - self.bit(way)) * count
        box = self.boxes[p][step]
        return self.remote(self.rows(self.work, row, count), self.inbox.at[box : box + count], p, step, way)

    def end_down(self, p, step):
        self.down(p, step).wait()
        count, base, box = self.counts[step], self.base(p, step), self.boxes[p][step]
        chunk = next(c for c in (96, 64, 48, 32, TILE) if count % c == 0)

        def body(i, carry):
            at = pl.ds(pl.multiple_of(base + i * chunk, TILE), chunk)
            got = self.inbox[pl.ds(pl.multiple_of(box + i * chunk, TILE), chunk), :]
            total = (self.work[at, :].astype(F32) + got.astype(F32)).astype(BF)
            if step == self.steps - 1:
                self.whole[at, :] = total
            else:
                self.work[at, :] = total
            return carry

        lax.fori_loop(0, count // chunk, body, 0)

    def up(self, p, turn):
        step = self.steps - 1 - turn
        if not self.halves[step]:
            return None
        rows = self.rows(self.whole, self.base(p, step), self.counts[step])
        return self.remote(rows, rows, p, self.steps + turn, self.orders[p][step])

    def store(self, p, side):
        rows = pl.ds(side * self.half_rows + p * self.part_rows, self.part_rows)
        return pltpu.make_async_copy(self.whole.at[rows], self.out.at[rows], self.out_sem.at[p, side])

    def small(self, step):
        return pltpu.make_async_remote_copy(
            src_ref=self.small_out,
            dst_ref=self.small_box.at[step],
            send_sem=self.small_send.at[step],
            recv_sem=self.small_recv.at[step],
            device_id=self.peer(self.ways[step]),
            device_id_type=pl.DeviceIdType.MESH,
        )

    def prepare(self):
        for i, (source, row, column, rows) in enumerate(self.loads):
            if self.direct:
                self.work[row : row + rows, :] = self.sources[source][:, column : column + self.width].astype(BF)
            else:
                self.load(i).start()
        if self.small_rows:
            self.small_out[...] = self.small_in[...]

    def phase(self, k):
        n = self.steps
        if k == 0 and not self.direct:
            for i in range(len(self.loads)):
                self.load(i).wait()
        for p in range(self.parts):
            if 1 <= k <= n:
                self.end_down(p, k - 1)
            elif k > n:
                before = self.up(p, k - n - 1)
                if before is not None:
                    before.wait()
            if k < n:
                self.down(p, k).start()
            elif k < 2 * n:
                after = self.up(p, k - n)
                if after is not None:
                    after.start()
            else:
                self.store(p, 0).start()
                self.store(p, 1).start()
        if k == 2 * n:
            for p in range(self.parts):
                self.store(p, 0).wait()
                self.store(p, 1).wait()
        if self.small_rows and k <= n:
            if k > 0:
                self.small(k - 1).wait()
                self.small_out[...] = self.small_out[...] + self.small_box[k - 1]
            if k < n:
                self.small(k).start()

    def unpack(self, reduced):
        results, at = [], 0
        for rows, columns in self.shapes:
            turns = columns // self.width
            blocks = [reduced[at + i * rows : at + (i + 1) * rows] for i in range(turns)]
            at += turns * rows
            results.append((blocks[0] if turns == 1 else jnp.concatenate(blocks, axis=1)).astype(F32))
        return results


def weights_kernel(
    lay,
    reducer,
    counts_ref,
    last_done_ref,
    small_ref,
    text_ref,
    normed_ref,
    d_query_ref,
    d_pair_ref,
    att_ref,
    branch2_ref,
    cross_in_ref,
    d_cross_query_ref,
    cross_att_ref,
    cross_branch_ref,
    normed2_ref,
    d_lifted_ref,
    branch5_ref,
    act_ref,
    d_text_keys_ref,
    d_text_values_ref,
    reduced_ref,
    lat_last_ref,
    small_out_ref,
    q_sum,
    pair_sum,
    proj_sum,
    cross_q_sum,
    cross_k_sum,
    cross_v_sum,
    cross_proj_sum,
    up_sum,
    turned_sum,
    down_sum,
    text_k_sum,
    text_v_sum,
    grad_send,
    grad_recv,
    *scratch,
):
    step = pl.program_id(0)
    sums = (q_sum, pair_sum, proj_sum, cross_q_sum, cross_proj_sum, up_sum, down_sum, text_k_sum, text_v_sum)
    grads = [q_sum, pair_sum, proj_sum, cross_q_sum, cross_k_sum, cross_v_sum, cross_proj_sum, up_sum, turned_sum]
    reducer.bind(grads, reduced_ref, scratch, small_ref, small_out_ref)

    me = lay.here()

    def grad_copy(slot):
        j = lay.clip(me) % lay.clips_dev
        return last_done_ref.at[slot], lat_last_ref.at[j], grad_send.at[slot], grad_recv.at[j], lay.owner(me, me["ta"], slot)

    @pl.when(step == 0)
    def _():
        for j in range(lay.clips_dev):
            greet(me, lay.space_target(me, j))
        amount = reducer.greet()
        await_greetings(me, [lay.owner(me, me["ta"], slot) for slot in range(lay.near)], amount)
        for slot in range(lay.near):
            start_push(me, *grad_copy(slot))
        for total in sums:
            total[...] = jnp.zeros_like(total)

    rows = d_query_ref.shape[1]
    q_sum[...] += dot_tn(normed_ref[0, :rows, :], d_query_ref[0])
    pair_sum[...] += dot_tn(normed_ref[0], d_pair_ref[0])
    proj_sum[...] += dot_tn(att_ref[0], branch2_ref[0])
    cross_q_sum[...] += dot_tn(cross_in_ref[0], d_cross_query_ref[0])
    cross_proj_sum[...] += dot_tn(cross_att_ref[0], cross_branch_ref[0])
    up_sum[...] += dot_tn(normed2_ref[0], d_lifted_ref[0])
    down_sum[...] += dot_tn(branch5_ref[0], act_ref[0])
    text_k_sum[...] += d_text_keys_ref[0]
    text_v_sum[...] += d_text_values_ref[0]

    @pl.when(step == pl.num_programs(0) - 1)
    def _():
        for total, result in ((text_k_sum, cross_k_sum), (text_v_sum, cross_v_sum)):
            value = total[...]
            head = value.astype(BF)
            rest = (value - head.astype(F32)).astype(BF)
            result[...] = dot_tn(text_ref[...], head) + dot_tn(text_ref[...], rest)
        turned_sum[...] = down_sum[...].T
        reducer.prepare()
        for k in range(reducer.phases):
            reducer.phase(k)
        for slot in range(lay.near):
            end_push(me, *grad_copy(slot))
        for j in range(lay.clips_dev):
            arrived(lat_last_ref.at[j], grad_recv.at[j])


def whole(array):
    zeros = (0,) * array.ndim
    return pl.BlockSpec(array.shape, lambda *grid: zeros)


def framed(array):
    tail = (0,) * (array.ndim - 1)
    return pl.BlockSpec((1,) + tuple(array.shape[1:]), lambda frame: (frame,) + tail)


SCALARS = pl.BlockSpec(memory_space=pltpu.SMEM)
HBM = pl.BlockSpec(memory_space=pl.ANY)


def shape_of(shape, dtype):
    return jax.ShapeDtypeStruct(shape, dtype)


def call(kernel, grid, inputs, in_specs, outputs, out_specs, flops, scratch=(), collective_id=None):
    moved = sum(math.prod(a.shape) * a.dtype.itemsize for a in (*inputs, *outputs))
    return pl.pallas_call(
        kernel,
        grid=grid,
        in_specs=in_specs,
        out_specs=out_specs,
        out_shape=outputs,
        scratch_shapes=list(scratch),
        compiler_params=pltpu.CompilerParams(
            vmem_limit_bytes=VMEM_BYTES, collective_id=collective_id, has_side_effects=collective_id is not None
        ),
        cost_estimate=pl.CostEstimate(flops=int(flops), bytes_accessed=int(moved), transcendentals=0),
    )(*inputs)


def make_per_device(sizes):
    n_ta, n_pa, n_dev = sizes["ta"], sizes["pa"], sizes["dev"]

    def per_device(
        latents,
        context,
        cotangent,
        timesteps,
        frame_counts,
        text_lengths,
        step_proj,
        mod_table,
        patch_attn,
        cross_attn,
        patch_up,
        patch_down,
        frame_attn,
        frame_up,
        frame_down,
    ):
        lay = Layout(sizes, latents.shape)
        clips_dev, frames, patches, width = latents.shape
        clips, run, group, near, halves = lay.clips, lay.run, lay.group, lay.near, lay.halves
        space_rows, other_rows, key_rows = lay.space_rows, lay.other_rows, lay.key_rows
        time_patches, all_frames = lay.time_patches, lay.all_frames
        ta, pa, dev = (lax.axis_index(name) for name in ("ta", "pa", "dev"))
        clip, member = lay.clip(lay.here()), lay.member(lay.here())

        def place(clip_id, member_id):
            return (clip_id * run + member_id % run) * n_dev + member_id // run

        def space_pairs(step):
            pairs = []
            for p in range(n_pa):
                for d in range(n_dev):
                    k = d * clips_dev + (p + step) % clips_dev
                    pairs.append((p * n_dev + d, place(k, p // near)))
            return pairs

        def time_pairs(step):
            u, w = step % halves, step // halves
            pairs = []
            for t in range(n_ta):
                for p in range(n_pa):
                    for d in range(n_dev):
                        s = (t % halves + u) % halves
                        j = (t // halves + w) % clips_dev
                        k = d * clips_dev + j
                        pairs.append(
                            (
                                (t * n_pa + p) * n_dev + d,
                                ((p % near) * halves + s) * n_pa * n_dev + place(k, p // near),
                            )
                        )
            return pairs

        def back(pairs):
            return [(b, a) for a, b in pairs]

        def group_pairs(step):
            return [
                (place(k, g), place(k, (g + step) % group)) for k in range(clips) for g in range(group)
            ]

        def ta_pairs(step):
            return [(t, t ^ step) for t in range(n_ta)]

        whole_axes = ("ta", "pa", "dev")
        pair_axes = ("pa", "dev")

        def of_clip(local):
            both = lax.all_gather(local, "dev", axis=0, tiled=True)
            return lax.dynamic_index_in_dim(both, clip, 0, keepdims=False)

        def sinusoid(steps):
            half = step_proj.shape[0] // 2
            frequency = jnp.exp(-math.log(10000.0) * jnp.arange(half, dtype=F32) / half)
            angles = steps.astype(F32)[:, None] * frequency[None, :]
            return jnp.concatenate([jnp.cos(angles), jnp.sin(angles)], axis=1)

        numbers = lax.all_gather(jnp.stack([timesteps, frame_counts, text_lengths], axis=1), "dev", axis=0, tiled=True)
        own_numbers = lax.dynamic_index_in_dim(numbers, clip, 0, keepdims=False)
        embeddings = sinusoid(numbers[:, 0])
        embedding = lax.dynamic_index_in_dim(embeddings, clip, 0, keepdims=True)
        timing = jnp.dot(embedding, step_proj.astype(F32), precision=HIGHEST).reshape(6, width)
        table = mod_table.astype(F32)
        pad = jnp.zeros((2, width), F32)
        space_mod = jnp.concatenate([timing + table[0], pad])
        frame_mod = jnp.concatenate([timing + table[1], pad])
        counts = jnp.stack([own_numbers[1], own_numbers[2], ta * frames, 0]).astype(jnp.int32)
        text = of_clip(context)
        text_count = text.shape[0]
        text_rows = -(-text_count // LANES) * LANES
        text_wide = jnp.pad(text, ((0, text_rows - text_count), (0, 0)))
        text_keys = dot(text_wide, cross_attn[1]).astype(BF)
        text_values = dot(text_wide, cross_attn[2]).astype(BF)
        cross_ends = jnp.stack([cross_attn[0], cross_attn[3]])

        def out(*shape, dtype=BF):
            return shape_of((frames,) + shape, dtype)

        def moved_tokens():
            return shape_of((all_frames, time_patches, width), BF)

        hidden = patch_up.shape[1]
        inputs = (
            counts, latents, cotangent, space_mod, patch_attn, cross_ends, text_keys, text_values.T,
            patch_up, patch_down,
        )
        outputs = (
            moved_tokens(),
            shape_of((all_frames, lay.early_cot * BLOCK, width), BF),
            out(space_rows, width),
            out(key_rows, width),
            out(space_rows, width),
            out(width, key_rows),
            out(key_rows, width),
            out(HEADS, key_rows, space_rows),
            out(width, space_rows),
            out(space_rows, width),
            out(8, space_rows, dtype=F32),
            out(space_rows, width),
            out(space_rows, width),
            out(HEADS, text_rows, space_rows),
            out(width, space_rows),
            out(space_rows, width),
            out(8, space_rows, dtype=F32),
            out(space_rows, width, dtype=F32),
            out(space_rows, width),
            out(space_rows, hidden),
            out(space_rows, hidden),
            out(space_rows, width),
            out(space_rows, width),
        )
        dense = 2 * frames * space_rows * width * (6 * width + 2 * hidden) + 8 * frames * key_rows * width * width
        dma = pltpu.SemaphoreType.DMA
        state, cot, *saved = call(
            lambda *refs: space_forward_kernel(lay, *refs),
            (frames,),
            inputs,
            [SCALARS, HBM, HBM] + [whole(a) for a in inputs[3:]],
            outputs,
            [HBM, HBM] + [framed(a) for a in outputs[2:]],
            dense + 16 * frames * space_rows * key_rows * width,
            [
                pltpu.VMEM((frames, near, patches, width), BF),
                pltpu.VMEM((frames, group - 1, near, patches, width), BF),
                pltpu.VMEM((frames, space_rows, width), BF),
                dma((clips_dev, frames)),
                dma((frames, near)),
                dma((group - 1, frames)),
                dma((group - 1, frames)),
                dma((n_ta, frames)),
                dma((n_ta, frames)),
                dma((clips_dev, halves)),
                dma((n_ta,)),
            ],
            collective_id=1,
        )

        block_rows = all_frames * BLOCK
        run_rows = all_frames * SUB
        ids = jnp.arange(run_rows, dtype=jnp.int32)
        same = (ids[:, None] % SUB == ids[None, :] % SUB) & (ids[:, None] // SUB < counts[0])
        bias = jnp.where(same, 0.0, MASKED_SCORE).astype(F32)
        hidden = frame_up.shape[1]
        n_blocks = time_patches // BLOCK

        early = max(n_blocks - 1, 1) * BLOCK
        time_inputs = (counts, state, cot, cotangent, frame_mod, bias, frame_attn, frame_up, frame_down)
        time_outputs = (
            out(space_rows, width),
            shape_of((clips_dev, frames, halves, early, width), BF),
            shape_of((all_frames, BLOCK, width), BF),
            shape_of((width, 3 * width), BF),
            shape_of((width, width), BF),
            shape_of((width, hidden), BF),
            shape_of((hidden, width), BF),
            shape_of((n_blocks, 8, width), F32),
        )

        def blocked(array):
            return pl.BlockSpec((all_frames, BLOCK, array.shape[2]), lambda at: (0, at, 0))

        def vmem(*shape, dtype=BF):
            return pltpu.VMEM(shape, dtype)

        (grad_s, early_out, late_out, d_frame_qkv, d_frame_proj, d_frame_up, d_frame_down, frame_six) = call(
            lambda *refs: time_kernel(lay, *refs),
            (n_blocks,),
            time_inputs,
            [SCALARS, blocked(state), HBM, HBM] + [whole(a) for a in time_inputs[4:]],
            time_outputs,
            [HBM, HBM] + [whole(a) for a in time_outputs[2:-1]] + [framed(time_outputs[-1])],
            all_frames * time_patches * width * (32 * width + 20 * hidden),
            [
                vmem(BLOCK // SUB, HEADS, run_rows, run_rows),
                vmem(n_blocks, all_frames, BLOCK, width),
                vmem(n_blocks, all_frames, BLOCK, width),
                vmem(width, 3 * width, dtype=F32),
                vmem(width, width, dtype=F32),
                vmem(width, hidden, dtype=F32),
                vmem(width, hidden, dtype=F32),
                vmem(block_rows, width),
                vmem(block_rows, 3 * width),
                vmem(block_rows, width),
                vmem(block_rows, width),
                vmem(block_rows, width),
                vmem(block_rows, hidden),
                vmem(block_rows, hidden),
                vmem(block_rows, width),
                dma((n_ta, n_blocks)),
                dma((n_ta, n_blocks)),
                dma((n_ta, n_blocks)),
                dma((clips_dev, halves, n_blocks)),
                vmem(n_blocks, all_frames, BLOCK, width),
                dma((n_blocks,)),
                dma((clips_dev, halves, n_blocks)),
                dma((n_ta, n_blocks)),
            ],
            collective_id=2,
        )

        (own, _, query, keys_t, value, exponent, att_t, _, inverse, _, cross_query, cross_exponent, cross_att_t, _,
         cross_inverse, middle, _, _, slope, branch2, branch5) = saved
        frame_grads = [d_frame_proj, d_frame_qkv, d_frame_up, d_frame_down]
        reducer = Reducer([a.shape for a in frame_grads], 0, sizes, HIDDEN_PARTS)
        fixed = (space_mod, patch_attn, cross_ends, text_keys.T, text_values, patch_up, patch_down)
        by_frame = (
            query, keys_t, value, att_t, inverse, cross_query, cross_exponent, cross_att_t, cross_inverse, middle,
            slope, branch2, branch5,
        )
        back_outputs = (
            shape_of((clips_dev, frames, halves, BLOCK, width), BF),
            shape_of((clips_dev, max(frames - 1, 1), patches, width), BF),
            shape_of((near, patches, width), BF),
            shape_of((reducer.total, width), BF),
            out(space_rows, width),
            out(space_rows, hidden),
            out(space_rows, width),
            out(space_rows, width),
            out(space_rows, width),
            out(space_rows, width),
            out(key_rows, 2 * width),
            out(text_rows, width, dtype=F32),
            out(text_rows, width, dtype=F32),
            shape_of((frames + 1, 8, width), F32),
        )

        def now(array):
            tail = (0,) * (array.ndim - 1)
            return pl.BlockSpec((1,) + tuple(array.shape[1:]), lambda at: (jnp.minimum(at, frames - 1),) + tail)

        def before(array):
            tail = (0,) * (array.ndim - 1)
            return pl.BlockSpec((1,) + tuple(array.shape[1:]), lambda at: (jnp.maximum(at, 1) - 1,) + tail)

        dense = 2 * frames * space_rows * width * (6 * width + 2 * hidden) + 8 * frames * key_rows * width * width
        output, lat_grad, last_done, frame_sums, *backs = call(
            lambda *refs: space_backward_kernel(lay, reducer, *refs),
            (frames + 1,),
            (counts, grad_s, late_out, exponent, *frame_grads, *fixed, own, *by_frame),
            [SCALARS, now(grad_s), HBM, HBM] + [HBM] * len(frame_grads) + [whole(a) for a in fixed] + [before(own)]
            + [now(a) for a in by_frame],
            back_outputs,
            [HBM, HBM, whole(back_outputs[2]), HBM] + [now(a) for a in back_outputs[4:-1]] + [framed(back_outputs[-1])],
            dense + 32 * frames * space_rows * key_rows * width,
            [
                pltpu.VMEM((HEADS, key_rows, space_rows), BF),
                pltpu.VMEM((2, group - 1, space_rows, width), BF),
                pltpu.VMEM((frames, group - 1, space_rows, width), BF),
                pltpu.VMEM((2, space_rows, width), F32),
                pltpu.VMEM((2, space_rows, width), F32),
                pltpu.VMEM((frames, near, patches, width), BF),
                dma((HEADS,)),
                dma((group - 1, frames)),
                dma((group - 1, frames)),
                dma((n_ta,)),
                dma((clips_dev, halves)),
                dma((near, frames)),
                dma((clips_dev, frames)),
                *reducer.scratch(),
            ],
            collective_id=3,
        )
        if n_blocks > 1:
            output = jnp.concatenate([early_out, output], axis=3)
        output = output.reshape(latents.shape)

        kept3, d_lifted2, kept2, d_cross_query, kept1, d_query, d_pair, d_tk, d_tv, space_six = backs
        mine = jnp.stack([jnp.sum(space_six, axis=0), jnp.sum(frame_six, axis=0)])
        spread = jnp.where(jnp.arange(clips)[:, None, None, None] == clip, mine[None], 0.0).reshape(-1, width)
        square, pair, lifted, lowered = (width, width), (width, 2 * width), (width, hidden), (hidden, width)
        shapes = [square, pair, square, square, square, square, square, lifted, lowered]
        tail = Reducer(shapes, spread.shape[0], sizes, PARTS, direct=True)
        by_frame = (
            saved[1], d_query, d_pair, saved[7], kept1, saved[9], d_cross_query, saved[13], kept2, saved[16], d_lifted2,
            kept3, saved[17], d_tk, d_tv,
        )
        tail_outputs = (
            shape_of((tail.total, width), BF),
            shape_of((clips_dev, patches, width), BF),
            shape_of(spread.shape, F32),
        )
        reduced, lat_last, by_clip = call(
            lambda *refs: weights_kernel(lay, tail, *refs),
            (frames,),
            (counts, last_done, spread, text_wide, *by_frame),
            [SCALARS, HBM, whole(spread), whole(text_wide)] + [framed(a) for a in by_frame],
            tail_outputs,
            [HBM, HBM, whole(spread)],
            2 * frames * space_rows * width * (4 * width + 2 * hidden) + 4 * frames * key_rows * width * width,
            [vmem(*shape, dtype=F32) for shape in shapes]
            + [vmem(width, hidden, dtype=F32)]
            + [vmem(text_rows, width, dtype=F32)] * 2
            + [dma((near,)), dma((clips_dev,))]
            + tail.scratch(),
            collective_id=0,
        )
        d_patch_q, d_patch_pair, d_patch_proj, *d_cross, d_patch_up, d_patch_down = tail.unpack(reduced)
        d_patch_attn = jnp.stack([d_patch_q, d_patch_pair[:, :width], d_patch_pair[:, width:], d_patch_proj])
        d_cross = jnp.stack(d_cross)
        lat_last = lat_last[:, None]
        latents_grad = jnp.concatenate([lat_grad, lat_last], axis=1) if frames > 1 else lat_last
        latents_grad = latents_grad.astype(F32)
        by_clip = by_clip.reshape(clips, 2, 8, width)[:, :, :6]
        d_frame_proj, d_frame_qkv, d_frame_up, d_frame_down = reducer.unpack(frame_sums)
        d_frame_qkv = d_frame_qkv.reshape(width, 3, width).swapaxes(0, 1)
        d_frame_attn = jnp.concatenate([d_frame_qkv, d_frame_proj[None]])
        d_table = jnp.sum(by_clip, axis=0)
        d_step = lax.dot_general(
            embeddings,
            jnp.sum(by_clip, axis=1).reshape(clips, -1),
            (((0,), (0,)), ((), ())),
            precision=HIGHEST,
        )
        return (
            output,
            latents_grad,
            d_step,
            d_table,
            d_patch_attn,
            d_cross,
            d_patch_up,
            d_patch_down,
            d_frame_attn,
            d_frame_up,
            d_frame_down,
        )

    return per_device


def solution(mesh):
    sizes = dict(mesh.shape)
    tokens = P("dev", "ta", "pa", None)
    in_specs = (tokens, P("dev", None, None), tokens, P("dev"), P("dev"), P("dev")) + (P(),) * 9
    out_specs = (tokens, tokens) + (P(),) * 9
    return jax.shard_map(
        make_per_device(sizes),
        mesh=mesh,
        in_specs=in_specs,
        out_specs=out_specs,
        check_vma=False,
    )
```
